32 devices in a mesh: rep: 8 (over z, x), shard: 4 (over y, core).
Axes of the slice: x: 2, y: 2, z: 4, core: 2. Of those that a mesh axis runs over, the one named last changes fastest.
Arguments:
- latents: float32 [64, 4096], P(('rep', 'shard')), may hold values from -6 to 6
- noises: float32 [64, 4096], P(('rep', 'shard')), may hold values from -6 to 6
- velocity: float32 [64, 4096], P(('rep', 'shard')), may hold values from -6 to 6
- times: int32 [64], P(('rep', 'shard')), may hold values from 0 to 988, as said below
- labels: int32 [64], P(('rep', 'shard')), may hold values from 0 to 999
- dropped: int32 [64], P(('rep', 'shard')), may hold values 0 or 1
- blocks_in: float32 [1, 768, 9984], P(None, None, 'shard'), may hold values from -0.21875 to 0.21875
- blocks_out: float32 [1, 3840, 768], P(None, None, 'shard'), may hold values from -0.21875 to 0.21875
- head_side: float32 [768, 2320], P(None, 'shard'), may hold values from -0.21875 to 0.21875
- embed_side: float32 [1273, 768], P(None, 'shard'), may hold values from -1.5 to 1.5
- state_in_row: float32 [1, 768], replicated, may hold values from 327.68 to 4915.2
- state_in_col: float32 [1, 9984], P(None, 'shard'), may hold values from 327.68 to 4915.2
- state_out_row: float32 [1, 3840], replicated, may hold values from 327.68 to 4915.2
- state_out_col: float32 [1, 768], P(None, 'shard'), may hold values from 327.68 to 4915.2
- state_head_row: float32 [768], replicated, may hold values from 327.68 to 4915.2
- state_head_col: float32 [2320], P('shard'), may hold values from 327.68 to 4915.2
- state_embed_row: float32 [1273], replicated, may hold values from 327.68 to 4915.2
- state_embed_col: float32 [768], P('shard'), may hold values from 327.68 to 4915.2
Outputs:
- loss_sum: float32 [], replicated
- update_rms: float32 [], replicated
- grad_in: float32 [1, 768, 9984], P(None, None, 'shard')
- grad_out: float32 [1, 3840, 768], P(None, None, 'shard')
- grad_head: float32 [768, 2320], P(None, 'shard')
- grad_embed: float32 [1273, 768], P(None, 'shard')
- new_in_row: float32 [1, 768], replicated
- new_in_col: float32 [1, 9984], P(None, 'shard')
- new_out_row: float32 [1, 3840], replicated
- new_out_col: float32 [1, 768], P(None, 'shard')
- new_head_row: float32 [768], replicated
- new_head_col: float32 [2320], P('shard')
- new_embed_row: float32 [1273], replicated
- new_embed_col: float32 [768], P('shard')
- new_in: float32 [1, 768, 9984], P(None, None, 'shard')
- new_out: float32 [1, 3840, 768], P(None, None, 'shard')
- new_head: float32 [768, 2320], P(None, 'shard')
- new_embed: float32 [1273, 768], P(None, 'shard')
The draws below stay inside these ranges and needn't reach their ends.
Inputs may be any that keep to these rules, and one draw needn't show every extreme that they name: `times`: the time index of latent i is below 1000 (64 + 2 i) / 192; the first latent's is 0 and the last latent's is the largest value.
All inputs are finite; a program needn't handle non-finite values. No bound on the sum of `dropped` on one device may be relied on, other than what follows from the above.
Results may differ from the reference program's by a relative error of at most 0.012.
The reference program's roundings to bfloat16 on the way count: a program that leaves them out, or rounds other values in their place, can miss the bound.
Values may be sent and summed in bfloat16 or wider, within the bound.
A program may use at most 704 MiB of HBM per device.

```python
import math
import jax
import jax.numpy as jnp
from jax import lax

D = 768
HEADS = 12
CLASSES = 1001
FREQ = 256
GRID = 16
PATCH = 16
LAYERS = 1
TOK = 256
IMAGES = 64
COLS_A = 9984
ROWS_B = 3840
COLS_C = 2320
ROWS_E = 1273


def draw_times(key, part):
    key = jax.random.fold_in(key, 7)
    raw = jax.random.randint(key, (IMAGES,), 0, 1000)
    order = jnp.arange(IMAGES, dtype=jnp.int32)
    raw = jnp.where(order == IMAGES - 1, 999, raw)
    raw = jnp.where(order == 0, 0, raw)
    return (raw * (IMAGES + 2 * order) // (3 * IMAGES)).astype(jnp.int32)


def place_ends(entries, key, smallest, high):
    longest = entries.shape.index(max(entries.shape))
    spots = []
    for shift in (0, 1):
        where = [jax.random.randint(jax.random.fold_in(key, axis), (), 0, length) for axis, length in enumerate(entries.shape)]
        where[longest] = (where[longest] + shift) % entries.shape[longest]
        spots.append(tuple(where))
    return entries.at[spots[0]].set(smallest).at[spots[1]].set(high)


def levels(rng, dims, cuts, low, largest):
    def one(position, blocks):
        steps = jax.random.uniform(jax.random.fold_in(jax.random.fold_in(rng, 6), position), (blocks,), jnp.float32, low / len(cuts), largest / len(cuts))
        return jnp.repeat(jnp.exp(steps), dims[position] // blocks).reshape((-1,) + (1,) * (len(dims) - position - 1))

    factor_of = one(*cuts[0])
    for cut in cuts[1:]:
        factor_of = factor_of * one(*cut)
    return factor_of


def bell_draw(rng, shape, scale, most, shards=(), kind=jnp.bfloat16):
    values = jax.random.normal(rng, shape, jnp.float32) * scale
    if len(shards) > 0:
        values = levels(rng, shape, shards, -0.22, 0.18) * values
    return jnp.clip(values, min=-most, max=most).astype(kind)


def setup_inputs(seed: int = 0) -> dict:
    seeds = jax.random.split(jax.random.key(seed), 19)
    return {
        "latents": bell_draw(seeds[0], (IMAGES, TOK * PATCH), 1.0, 6.0, ((0, 32),), jnp.float32),
        "noises": bell_draw(seeds[1], (IMAGES, TOK * PATCH), 1.0, 6.0, ((0, 32),), jnp.float32),
        "velocity": bell_draw(seeds[2], (IMAGES, TOK * PATCH), 1.0, 6.0, ((0, 32),), jnp.float32),
        "times": draw_times(jax.random.fold_in(seeds[18], 71), 0),
        "labels": place_ends(jax.random.randint(seeds[4], (IMAGES,), 0, CLASSES - 1), jax.random.fold_in(seeds[4], 1), 0, (CLASSES - 1) - 1).astype(jnp.int32),
        "dropped": place_ends((jax.random.randint(seeds[5], (IMAGES,), 0, 10) < 1).astype(jnp.int32), jax.random.fold_in(seeds[5], 1), 0, 1),
        "blocks_in": bell_draw(seeds[6], (LAYERS, D, COLS_A), D ** -0.5, 0.21875, ((2, 4),), jnp.float32),
        "blocks_out": bell_draw(seeds[7], (LAYERS, ROWS_B, D), D ** -0.5, 0.21875, ((2, 4),), jnp.float32),
        "head_side": bell_draw(seeds[8], (D, COLS_C), D ** -0.5, 0.21875, ((1, 4),), jnp.float32),
        "embed_side": bell_draw(seeds[9], (ROWS_E, D), 0.25, 1.5, ((1, 4),), jnp.float32),
        "state_in_row": jnp.clip(jnp.exp(jax.random.uniform(seeds[10], (LAYERS, D), jnp.float32, math.log(327.68), math.log(4915.2))), 327.68, 4915.2),
        "state_in_col": jnp.clip(jnp.exp(math.log(4915.2) - 2.7080503 * jax.random.uniform(seeds[11], (LAYERS, COLS_A), jnp.float32) ** levels(seeds[11], (LAYERS, COLS_A), ((1, 4),), -0.2, 0.2)), 327.68, 4915.2),
        "state_out_row": jnp.clip(jnp.exp(jax.random.uniform(seeds[12], (LAYERS, ROWS_B), jnp.float32, math.log(327.68), math.log(4915.2))), 327.68, 4915.2),
        "state_out_col": jnp.clip(jnp.exp(math.log(4915.2) - 2.7080503 * jax.random.uniform(seeds[13], (LAYERS, D), jnp.float32) ** levels(seeds[13], (LAYERS, D), ((1, 4),), -0.2, 0.2)), 327.68, 4915.2),
        "state_head_row": jnp.clip(jnp.exp(jax.random.uniform(seeds[14], (D,), jnp.float32, math.log(327.68), math.log(4915.2))), 327.68, 4915.2),
        "state_head_col": jnp.clip(jnp.exp(math.log(4915.2) - 2.7080503 * jax.random.uniform(seeds[15], (COLS_C,), jnp.float32) ** levels(seeds[15], (COLS_C,), ((0, 4),), -0.2, 0.2)), 327.68, 4915.2),
        "state_embed_row": jnp.clip(jnp.exp(jax.random.uniform(seeds[16], (ROWS_E,), jnp.float32, math.log(327.68), math.log(4915.2))), 327.68, 4915.2),
        "state_embed_col": jnp.clip(jnp.exp(math.log(4915.2) - 2.7080503 * jax.random.uniform(seeds[17], (D,), jnp.float32) ** levels(seeds[17], (D,), ((0, 4),), -0.2, 0.2)), 327.68, 4915.2),
    }


@jax.custom_vjp
def low(v):
    return lax.optimization_barrier(v.astype(jnp.bfloat16)).astype(jnp.float32)

@jax.custom_vjp
def low_back(v):
    return v

def low_keep(v):
    return (low(v), None)

def low_pass(kept, grad):
    return (grad,)

def back_keep(v):
    return (v, None)

def back_low(kept, grad):
    return (low(grad),)
low.defvjp(low_keep, low_pass)
low_back.defvjp(back_keep, back_low)
highest = lax.Precision.HIGHEST
eps_norm = 1e-06
decay = 0.5
eps_one = 1e-30
eps_two = 0.001
clip_level = 0.1
rate = 8.0
step_count = 1000.0

def mmul(left, right):
    return jnp.matmul(left, right, precision=highest)

def silu(value):
    return value * jax.nn.sigmoid(value)

def gelu(value):
    return 0.5 * value * (1.0 + jnp.tanh(0.7978845608 * (value + 0.044715 * value * value * value)))

def norm_mod(hidden, shift, scale):
    center = hidden - lax.optimization_barrier(jnp.mean(hidden, -1, keepdims=True))
    spread = lax.optimization_barrier(jnp.mean(center * center, -1, keepdims=True))
    return center * lax.rsqrt(spread + eps_norm) * (1.0 + scale[:, None, :]) + shift[:, None, :]

def positions(grid, width):
    quarter = width // 4
    omega = 1.0 / 10000.0 ** (jnp.arange(quarter, dtype=jnp.float32) / quarter)
    index = jnp.arange(grid * grid, dtype=jnp.int32)
    row_pos = (index // grid).astype(jnp.float32)[:, None] * omega[None, :]
    col_pos = (index % grid).astype(jnp.float32)[:, None] * omega[None, :]
    return jnp.concatenate([jnp.sin(row_pos), jnp.cos(row_pos), jnp.sin(col_pos), jnp.cos(col_pos)], 1)

def time_freq(t_value, width):
    half = width // 2
    freqs = jnp.exp(-math.log(10000.0) * jnp.arange(half, dtype=jnp.float32) / half)
    angles = (t_value * step_count)[:, None] * freqs[None, :]
    return jnp.concatenate([jnp.cos(angles), jnp.sin(angles)], -1)

def attend(qkv):
    batch, count, triple = qkv.shape
    width = triple // 3
    parts = qkv.reshape(batch, count, 3, HEADS, width // HEADS)
    query, key, value = (low(parts[:, :, 0]), low(parts[:, :, 1]), low(parts[:, :, 2]))
    score = low_back(jnp.einsum('bnhe,bmhe->bhnm', query, key, precision=highest) / math.sqrt(width // HEADS))
    expo = jnp.exp(score - lax.optimization_barrier(jnp.max(score, -1, keepdims=True)))
    probs = expo / lax.optimization_barrier(jnp.sum(expo, -1, keepdims=True))
    mixed = jnp.einsum('bhnm,bmhe->bnhe', low(probs), value, precision=highest)
    return low(low_back(mixed.reshape(batch, count, width)))

def block(hidden, cond, w_in, w_out):
    width = hidden.shape[-1]
    modul = low_back(mmul(cond, w_in[:, :6 * width]))
    pieces = jnp.split(modul, 6, axis=-1)
    normed = low(norm_mod(hidden, pieces[0], pieces[1]))
    qkv = low_back(mmul(normed, w_in[:, 6 * width:9 * width]))
    attn = jax.checkpoint(attend)(qkv)
    proj = low_back(mmul(attn, w_out[:width]))
    middle = hidden + pieces[2][:, None, :] * proj
    normed_two = low(norm_mod(middle, pieces[3], pieces[4]))
    upper = low_back(mmul(normed_two, w_in[:, 9 * width:]))
    active = low(gelu(upper))
    mlp = low_back(mmul(active, w_out[width:]))
    return middle + pieces[5][:, None, :] * mlp

def loss_of(weights, state, freq, onehot, target, weight_t):
    w_in, w_out, w_head, w_embed = [low(item) for item in weights]
    width = w_head.shape[0]
    w_patch = w_embed[:PATCH]
    w_time = w_embed[PATCH:PATCH + FREQ]
    table = w_embed[PATCH + FREQ:]
    hidden = low_back(mmul(low(state), w_patch)) + positions(GRID, width)[None]
    time_one = low_back(mmul(low(freq), w_time))
    time_two = low_back(mmul(low(silu(time_one)), w_head[:, :width]))
    cond = low(silu(time_two + mmul(onehot, table)))
    for layer_index in range(LAYERS):
        hidden = block(hidden, cond, w_in[layer_index], w_out[layer_index])
    final_mod = low_back(mmul(cond, w_head[:, width:3 * width]))
    final_low = low(norm_mod(hidden, final_mod[:, :width], final_mod[:, width:]))
    output = low_back(mmul(final_low, w_head[:, 3 * width:]))
    diff = output - target
    return 0.5 * jnp.sum(weight_t[:, None, None] * diff * diff)

def reference(latents, noises, velocity, times, labels, dropped, blocks_in, blocks_out, head_side, embed_side, state_in_row, state_in_col, state_out_row, state_out_col, state_head_row, state_head_col, state_embed_row, state_embed_col):
    weights = (blocks_in, blocks_out, head_side, embed_side)
    group = 16

    def one_group(carry, group_index):
        start = (group_index * group).astype(jnp.int32)

        def take(array):
            return lax.dynamic_slice_in_dim(array, start, group, 0)
        t_value = (take(times).astype(jnp.float32) + 1.0) / step_count
        classes = jnp.where(take(dropped) == 1, CLASSES - 1, take(labels))
        onehot = (classes[:, None] == jnp.arange(CLASSES, dtype=jnp.int32)[None, :]).astype(jnp.float32)
        clean = take(latents).reshape(group, TOK, PATCH)
        noise = take(noises).reshape(group, TOK, PATCH)
        target = take(velocity).reshape(group, TOK, PATCH)
        tcol = t_value[:, None, None]
        state = (1.0 - tcol) * clean + tcol * noise
        freq = time_freq(t_value, FREQ)

        def local_loss(w_a, w_b, w_c, w_e):
            return loss_of((w_a, w_b, w_c, w_e), state, freq, onehot, target, t_value)
        loss, pull = jax.vjp(local_loss, *weights)
        grads = pull(jnp.ones((), jnp.float32))
        return ((carry[0] + loss, tuple((old + new for old, new in zip(carry[1], grads)))), None)
    start_carry = (jnp.zeros((), jnp.float32), tuple((jnp.zeros_like(item) for item in weights)))
    (loss_sum, grads), _ = lax.scan(one_group, start_carry, jnp.arange(IMAGES // group, dtype=jnp.int32))
    rows_old = (state_in_row, state_out_row, state_head_row, state_embed_row)
    cols_old = (state_in_col, state_out_col, state_head_col, state_embed_col)
    updates, rows_new, cols_new = ([], [], [])
    for gradient, row_state, col_state in zip(grads, rows_old, cols_old):
        square = gradient * gradient
        row_next = decay * row_state + (1.0 - decay) * (lax.optimization_barrier(jnp.mean(square, -1)) + eps_one)
        col_next = decay * col_state + (1.0 - decay) * (lax.optimization_barrier(jnp.mean(square, -2)) + eps_one)
        second = row_next[..., :, None] * col_next[..., None, :] / lax.optimization_barrier(jnp.mean(row_next, -1))[..., None, None]
        updates.append(gradient * lax.rsqrt(second))
        rows_new.append(row_next)
        cols_new.append(col_next)
    total = sum((jnp.sum(item * item) for item in updates))
    count = sum((item.size for item in updates))
    update_rms = jnp.sqrt(total / count)
    factor = jnp.maximum(1.0, update_rms / clip_level)
    news = []
    for weight, update in zip(weights, updates):
        weight_rms = jnp.sqrt(lax.optimization_barrier(jnp.mean(weight * weight, axis=(-2, -1))))
        news.append(weight - rate * jnp.maximum(eps_two, weight_rms)[..., None, None] * update / factor)
    return (loss_sum, update_rms, grads[0], grads[1], grads[2], grads[3], rows_new[0], cols_new[0], rows_new[1], cols_new[1], rows_new[2], cols_new[2], rows_new[3], cols_new[3], news[0], news[1], news[2], news[3])
```

```python
import math

import jax
import jax.numpy as jnp
from jax import lax
from jax.sharding import PartitionSpec as P

HEADS = 12
CLASSES = 1001
FREQ = 256
GRID = 16
PATCH = 16
LAYERS = 1
TOK = 256


decay = 0.5
eps_norm = 1e-06
eps_one = 1e-30
eps_two = 0.001
clip_level = 0.1
rate = 8.0
step_count = 1000.0


def silu(value):
    return value * jax.nn.sigmoid(value)


def gelu(value):
    return 0.5 * value * (1.0 + jnp.tanh(0.7978845608 * (value + 0.044715 * value * value * value)))


def norm_mod(hidden, shift, scale):
    center = hidden - jnp.mean(hidden, -1, keepdims=True)
    spread = jnp.mean(center * center, -1, keepdims=True)
    return center * lax.rsqrt(spread + eps_norm) * (1.0 + scale[:, None, :]) + shift[:, None, :]


def positions(grid, width):
    quarter = width // 4
    omega = 1.0 / 10000.0 ** (jnp.arange(quarter, dtype=jnp.float32) / quarter)
    index = jnp.arange(grid * grid, dtype=jnp.int32)
    row_pos = (index // grid).astype(jnp.float32)[:, None] * omega[None, :]
    col_pos = (index % grid).astype(jnp.float32)[:, None] * omega[None, :]
    return jnp.concatenate(
        [jnp.sin(row_pos), jnp.cos(row_pos), jnp.sin(col_pos), jnp.cos(col_pos)], 1
    )


def time_freq(t_value, width):
    half = width // 2
    freqs = jnp.exp(-math.log(10000.0) * jnp.arange(half, dtype=jnp.float32) / half)
    angles = (t_value * step_count)[:, None] * freqs[None, :]
    return jnp.concatenate([jnp.cos(angles), jnp.sin(angles)], -1)


def forward_product(left, weight):
    return jnp.matmul(left, weight, preferred_element_type=jnp.float32)


def weight_grad(left, back):
    flat_left = left.reshape(-1, left.shape[-1])
    flat_back = back.reshape(-1, back.shape[-1])
    return lax.dot_general(
        flat_left, flat_back, (((0,), (0,)), ((), ())), preferred_element_type=jnp.float32
    )


def input_grad(back, weight):
    return lax.dot_general(
        back, weight, (((back.ndim - 1,), (1,)), ((), ())), preferred_element_type=jnp.float32
    )


def split_heads(qkv_low):
    batch, count, triple = qkv_low.shape
    width = triple // 3
    parts = qkv_low.reshape(batch, count, 3, HEADS, width // HEADS)
    return (parts[:, :, 0], parts[:, :, 1], parts[:, :, 2])


def probabilities(query, key):
    score = jnp.einsum(
        "bnhe,bmhe->bhnm", query, key, preferred_element_type=jnp.float32
    ) / math.sqrt(query.shape[-1])
    expo = jnp.exp(score - jnp.max(score, -1, keepdims=True))
    return expo / jnp.sum(expo, -1, keepdims=True)


def input_grad_t(back, weight_t):
    return jnp.matmul(back, weight_t, preferred_element_type=jnp.float32)


def forward_t(left, weight_t):
    return lax.dot_general(
        left, weight_t, (((left.ndim - 1,), (1,)), ((), ())), preferred_element_type=jnp.float32
    )


def attention_back(qkv_low, probs, d_attn):
    query, key, value = split_heads(qkv_low)
    scale = 1.0 / math.sqrt(query.shape[-1])
    d_mixed = d_attn.reshape(query.shape)
    d_value = jnp.einsum(
        "bhnm,bnhe->bmhe", probs.astype(jnp.bfloat16), d_mixed, preferred_element_type=jnp.float32
    )
    d_prob = jnp.einsum("bnhe,bmhe->bhnm", d_mixed, value, preferred_element_type=jnp.float32)
    d_score = (probs * (d_prob - jnp.sum(probs * d_prob, -1, keepdims=True))).astype(jnp.bfloat16)
    d_query = (
        jnp.einsum("bhnm,bmhe->bnhe", d_score, key, preferred_element_type=jnp.float32) * scale
    )
    d_key = (
        jnp.einsum("bhnm,bnhe->bmhe", d_score, query, preferred_element_type=jnp.float32) * scale
    )
    return jnp.concatenate(
        [item.reshape(item.shape[:2] + (-1,)) for item in (d_query, d_key, d_value)], -1
    ).astype(jnp.bfloat16)


def gather_heavy(in_low, out_low, shard_count):
    width = in_low.shape[0]
    all_in = lax.all_gather(in_low, "shard", axis=1, tiled=True)
    all_out = lax.all_gather(out_low, "shard", axis=1, tiled=True)
    return all_in[:, 6 * width : 9 * width].T, all_in[:, 9 * width :].T, all_out.T


def reduce_heavy(g_in_t, g_out_t, in_cols, out_cols):
    width = g_in_t.shape[1]
    total_in = lax.psum(g_in_t.astype(jnp.bfloat16), ("rep", "shard"))
    total_out = lax.psum(g_out_t.astype(jnp.bfloat16), ("rep", "shard"))
    place = lax.axis_index("shard")
    padded = jnp.pad(total_in, ((6 * width, 0), (0, 0)))
    own_in = lax.dynamic_slice_in_dim(padded, place * in_cols, in_cols, 0)
    own_out = lax.dynamic_slice_in_dim(total_out, place * out_cols, out_cols, 0)
    return own_in.T.astype(jnp.float32), own_out.T.astype(jnp.float32)


def on_device(
    latents,
    noises,
    velocity,
    times,
    labels,
    dropped,
    blocks_in,
    blocks_out,
    head_side,
    embed_side,
    state_in_row,
    state_in_col,
    state_out_row,
    state_out_col,
    state_head_row,
    state_head_col,
    state_embed_row,
    state_embed_col,
):
    both = ("rep", "shard")
    images = latents.shape[0]
    width = head_side.shape[0]
    shard_count = lax.axis_size("shard")
    place = lax.axis_index("shard")
    rep_place = lax.axis_index("rep")
    in_cols = blocks_in.shape[2]
    out_cols = blocks_out.shape[2]
    head_cols = head_side.shape[1]
    embed_cols = embed_side.shape[1]
    group = images * shard_count
    in_low = blocks_in[0].astype(jnp.bfloat16)
    out_low = blocks_out[0].astype(jnp.bfloat16)
    head_low = head_side.astype(jnp.bfloat16)
    embed_low = embed_side.astype(jnp.bfloat16)
    qkv_t, fc1_t, out_t = gather_heavy(in_low, out_low, shard_count)
    o_t, fc2_t = out_t[:, :width], out_t[:, width:]
    marks = lax.all_gather(jnp.stack([times, labels, dropped]), both, axis=1, tiled=True)
    t_all = (marks[0].astype(jnp.float32) + 1.0) / step_count
    classes = jnp.where(marks[2] == 1, CLASSES - 1, marks[1])
    onehot = (classes[:, None] == jnp.arange(CLASSES, dtype=jnp.int32)[None, :]).astype(
        jnp.bfloat16
    )
    freq_low = time_freq(t_all, FREQ).astype(jnp.bfloat16)
    time_one = forward_product(freq_low, embed_low[PATCH : PATCH + FREQ])
    table_part = forward_product(onehot, embed_low[PATCH + FREQ :])
    time_act = lax.all_gather(silu(time_one).astype(jnp.bfloat16), "shard", axis=1, tiled=True)
    two_part = forward_product(time_act, head_low)
    sides = lax.all_gather(
        jnp.concatenate([two_part, table_part], 1), "shard", axis=0, tiled=False
    )
    time_two = jnp.concatenate([sides[j, :, :head_cols] for j in range(shard_count)], 1)[:, :width]
    table_rows = jnp.concatenate([sides[j, :, head_cols:] for j in range(shard_count)], 1)
    cond_full = time_two + table_rows
    cond = silu(cond_full).astype(jnp.bfloat16)
    cond_group = lax.dynamic_slice_in_dim(cond, rep_place * group, group, 0)
    mod_part = jnp.concatenate(
        [forward_product(cond_group, in_low), forward_product(cond_group, head_low)], 1
    )
    mods = lax.all_gather(mod_part, "shard", axis=0, tiled=False)
    mods = lax.dynamic_slice_in_dim(mods, place * images, images, 1)
    modul = jnp.concatenate([mods[j, :, :in_cols] for j in range(shard_count)], 1)[:, : 6 * width]
    final_mod = jnp.concatenate([mods[j, :, in_cols:] for j in range(shard_count)], 1)
    final_mod = final_mod[:, width : 3 * width]
    small = jnp.concatenate(
        [
            lax.all_gather(embed_low[:PATCH], "shard", axis=1, tiled=True),
            lax.all_gather(head_low, "shard", axis=1, tiled=True)[:, 3 * width :].T,
        ],
        0,
    )
    patch_w, head_t = small[:PATCH], small[PATCH:]
    t_value = (times.astype(jnp.float32) + 1.0) / step_count
    tcol = t_value[:, None, None]
    state = (
        (1.0 - tcol) * latents.reshape(images, TOK, PATCH)
        + tcol * noises.reshape(images, TOK, PATCH)
    ).astype(jnp.bfloat16)
    target = velocity.reshape(images, TOK, PATCH)
    hidden = forward_product(state, patch_w) + positions(GRID, width)[None]
    pieces = jnp.split(modul, 6, axis=-1)
    normed, first_pull = jax.vjp(norm_mod, hidden, pieces[0], pieces[1])
    normed = normed.astype(jnp.bfloat16)
    qkv_low = forward_t(normed, qkv_t).astype(jnp.bfloat16)
    query, key, value = split_heads(qkv_low)
    probs = probabilities(query, key)
    mixed = jnp.einsum(
        "bhnm,bmhe->bnhe", probs.astype(jnp.bfloat16), value, preferred_element_type=jnp.float32
    )
    attn = mixed.reshape(hidden.shape).astype(jnp.bfloat16)
    proj = forward_t(attn, o_t)
    middle = hidden + pieces[2][:, None, :] * proj
    normed_two, norm_pull = jax.vjp(norm_mod, middle, pieces[3], pieces[4])
    normed_two = normed_two.astype(jnp.bfloat16)
    upper = forward_t(normed_two, fc1_t)
    active, gelu_pull = jax.vjp(gelu, upper)
    active = active.astype(jnp.bfloat16)
    mlp = forward_t(active, fc2_t)
    result = middle + pieces[5][:, None, :] * mlp
    final, final_pull = jax.vjp(norm_mod, result, final_mod[:, :width], final_mod[:, width:])
    final_low = final.astype(jnp.bfloat16)
    output = forward_t(final_low, head_t)
    diff = output - target
    loss_local = 0.5 * jnp.sum(tcol * diff * diff)
    d_output = (tcol * diff).astype(jnp.bfloat16)
    g_head_t = weight_grad(d_output, final_low)
    d_final = input_grad_t(d_output, head_t)
    back, d_shift, d_scale = final_pull(d_final)
    d_gate_two = jnp.sum(back * mlp, 1)
    d_mlp = (pieces[5][:, None, :] * back).astype(jnp.bfloat16)
    g_fc2_t = weight_grad(d_mlp, active)
    d_active = input_grad_t(d_mlp, fc2_t)
    d_upper = gelu_pull(d_active)[0].astype(jnp.bfloat16)
    g_fc1_t = weight_grad(d_upper, normed_two)
    d_normed_two = input_grad_t(d_upper, fc1_t)
    d_from_norm, d_shift_two, d_scale_two = norm_pull(d_normed_two)
    d_middle = back + d_from_norm
    d_gate_one = jnp.sum(d_middle * proj, 1)
    d_proj = (pieces[2][:, None, :] * d_middle).astype(jnp.bfloat16)
    g_o_t = weight_grad(d_proj, attn)
    d_attn = input_grad_t(d_proj, o_t).astype(jnp.bfloat16)
    d_qkv = attention_back(qkv_low, probs, d_attn)
    g_qkv_t = weight_grad(d_qkv, normed)
    d_normed = input_grad_t(d_qkv, qkv_t)
    d_from_first, d_shift_one, d_scale_one = first_pull(d_normed)
    d_hidden = d_middle + d_from_first
    g_patch = weight_grad(state, d_hidden.astype(jnp.bfloat16))
    heavy_in, heavy_out = reduce_heavy(
        jnp.concatenate([g_qkv_t, g_fc1_t], 0),
        jnp.concatenate([g_o_t, g_fc2_t], 1),
        in_cols,
        out_cols,
    )
    d_low = jnp.concatenate(
        [d_shift_one, d_scale_one, d_gate_one, d_shift_two, d_scale_two, d_gate_two, d_shift, d_scale],
        -1,
    ).astype(jnp.bfloat16)
    d_low = lax.all_gather(d_low, both, axis=0, tiled=True)
    full_in = in_cols * shard_count
    full_head = head_cols * shard_count
    d_in = jnp.pad(d_low[:, : 6 * width], ((0, 0), (0, full_in - 6 * width)))
    d_in = lax.dynamic_slice_in_dim(d_in, place * in_cols, in_cols, 1)
    d_fin = jnp.pad(d_low[:, 6 * width :], ((0, 0), (width, full_head - 3 * width)))
    d_fin = lax.dynamic_slice_in_dim(d_fin, place * head_cols, head_cols, 1)
    d_cond = lax.psum(input_grad(d_in, in_low) + input_grad(d_fin, head_low), "shard")
    _, silu_pull = jax.vjp(silu, cond_full)
    d_full = silu_pull(d_cond)[0]
    d_two = jnp.pad(d_full.astype(jnp.bfloat16), ((0, 0), (0, full_head - width)))
    d_two = lax.dynamic_slice_in_dim(d_two, place * head_cols, head_cols, 1)
    d_act = lax.psum_scatter(input_grad(d_two, head_low), "shard", scatter_dimension=1, tiled=True)
    _, time_pull = jax.vjp(silu, time_one)
    d_one = time_pull(d_act)[0].astype(jnp.bfloat16)
    d_full_own = lax.dynamic_slice_in_dim(d_full, place * embed_cols, embed_cols, 1)
    g_table = lax.dot_general(
        onehot.astype(jnp.float32),
        d_full_own,
        (((0,), (0,)), ((), ())),
        precision=lax.Precision.HIGHEST,
    )
    loss_sum, g_small = lax.psum((loss_local, jnp.concatenate([g_patch, g_head_t], 0)), both)
    own_patch = lax.dynamic_slice_in_dim(g_small[:PATCH], place * embed_cols, embed_cols, 1)
    own_head = jnp.pad(g_small[PATCH:].T, ((0, 0), (3 * width, 0)))
    own_head = lax.dynamic_slice_in_dim(own_head, place * head_cols, head_cols, 1)
    totals = (
        (weight_grad(cond, d_in) + heavy_in)[None],
        heavy_out[None],
        weight_grad(time_act, d_two) + weight_grad(cond, d_fin) + own_head,
        jnp.concatenate([own_patch, weight_grad(freq_low, d_one), g_table], 0),
    )
    weights = (blocks_in, blocks_out, head_side, embed_side)
    rows_old = (state_in_row, state_out_row, state_head_row, state_embed_row)
    cols_old = (state_in_col, state_out_col, state_head_col, state_embed_col)
    cols_new = [
        decay * col_state + (1.0 - decay) * (jnp.mean(gradient * gradient, -2) + eps_one)
        for gradient, col_state in zip(totals, cols_old)
    ]
    row_parts = [jnp.sum(gradient * gradient, -1) for gradient in totals]
    row_scaled = [
        jnp.sum(gradient * gradient / col_next[..., None, :], -1)
        for gradient, col_next in zip(totals, cols_new)
    ]
    weight_sq = [jnp.sum(weight * weight, axis=(-2, -1)) for weight in weights]
    row_sums, row_scaled, weight_sq = lax.psum((row_parts, row_scaled, weight_sq), "shard")
    rows_new = [
        decay * row_state
        + (1.0 - decay) * (row_sum / (gradient.shape[-1] * shard_count) + eps_one)
        for row_sum, gradient, row_state in zip(row_sums, totals, rows_old)
    ]
    row_means = [jnp.mean(row_next, -1) for row_next in rows_new]
    total_sq = sum(
        jnp.sum(row_mean * jnp.sum(scaled / row_next, -1))
        for scaled, row_next, row_mean in zip(row_scaled, rows_new, row_means)
    )
    count = sum((weight.size for weight in weights)) * shard_count
    update_rms = jnp.sqrt(total_sq / count)
    factor = jnp.maximum(1.0, update_rms / clip_level)
    news = []
    for index in range(4):
        numel = weights[index].shape[-2] * weights[index].shape[-1] * shard_count
        weight_rms = jnp.sqrt(weight_sq[index] / numel)
        step_size = rate * jnp.maximum(eps_two, weight_rms) / factor
        row_scale = jnp.asarray(step_size)[..., None] * lax.rsqrt(
            rows_new[index] / row_means[index][..., None]
        )
        news.append(
            weights[index]
            - totals[index] * row_scale[..., :, None] * lax.rsqrt(cols_new[index])[..., None, :]
        )
    return (
        loss_sum,
        update_rms,
        totals[0],
        totals[1],
        totals[2],
        totals[3],
        rows_new[0],
        cols_new[0],
        rows_new[1],
        cols_new[1],
        rows_new[2],
        cols_new[2],
        rows_new[3],
        cols_new[3],
        news[0],
        news[1],
        news[2],
        news[3],
    )


def solution(mesh):
    placed = (
        P(("rep", "shard"), None),
        P(("rep", "shard"), None),
        P(("rep", "shard"), None),
        P(("rep", "shard")),
        P(("rep", "shard")),
        P(("rep", "shard")),
        P(None, None, "shard"),
        P(None, None, "shard"),
        P(None, "shard"),
        P(None, "shard"),
        P(),
        P(None, "shard"),
        P(),
        P(None, "shard"),
        P(),
        P("shard"),
        P(),
        P("shard"),
    )
    return jax.shard_map(
        on_device,
        mesh=mesh,
        in_specs=placed,
        out_specs=(
            P(),
            P(),
            P(None, None, "shard"),
            P(None, None, "shard"),
            P(None, "shard"),
            P(None, "shard"),
            P(),
            P(None, "shard"),
            P(),
            P(None, "shard"),
            P(),
            P("shard"),
            P(),
            P("shard"),
            P(None, None, "shard"),
            P(None, None, "shard"),
            P(None, "shard"),
            P(None, "shard"),
        ),
        check_vma=False,
    )
```

```python
import functools
import math

import jax
import jax.numpy as jnp
from jax import lax
from jax.experimental import pallas as pl
from jax.experimental.pallas import tpu as pltpu
from jax.sharding import PartitionSpec as P

HEADS = 12
CLASSES = 1001
FREQ = 256
GRID = 16
PATCH = 16
LAYERS = 1
TOK = 256


decay = 0.5
eps_norm = 1e-06
eps_one = 1e-30
eps_two = 0.001
clip_level = 0.1
rate = 8.0
step_count = 1000.0


def silu(value):
    return value * jax.nn.sigmoid(value)


def gelu(value):
    return 0.5 * value * (1.0 + jnp.tanh(0.7978845608 * (value + 0.044715 * value * value * value)))


def norm_mod(hidden, shift, scale):
    center = hidden - jnp.mean(hidden, -1, keepdims=True)
    spread = jnp.mean(center * center, -1, keepdims=True)
    return center * lax.rsqrt(spread + eps_norm) * (1.0 + scale[:, None, :]) + shift[:, None, :]


def positions(grid, width):
    quarter = width // 4
    omega = 1.0 / 10000.0 ** (jnp.arange(quarter, dtype=jnp.float32) / quarter)
    index = jnp.arange(grid * grid, dtype=jnp.int32)
    row_pos = (index // grid).astype(jnp.float32)[:, None] * omega[None, :]
    col_pos = (index % grid).astype(jnp.float32)[:, None] * omega[None, :]
    return jnp.concatenate(
        [jnp.sin(row_pos), jnp.cos(row_pos), jnp.sin(col_pos), jnp.cos(col_pos)], 1
    )


def time_freq(t_value, width):
    half = width // 2
    freqs = jnp.exp(-math.log(10000.0) * jnp.arange(half, dtype=jnp.float32) / half)
    angles = (t_value * step_count)[:, None] * freqs[None, :]
    return jnp.concatenate([jnp.cos(angles), jnp.sin(angles)], -1)


def forward_product(left, weight):
    return jnp.matmul(left, weight, preferred_element_type=jnp.float32)


def weight_grad(left, back):
    flat_left = left.reshape(-1, left.shape[-1])
    flat_back = back.reshape(-1, back.shape[-1])
    return lax.dot_general(
        flat_left, flat_back, (((0,), (0,)), ((), ())), preferred_element_type=jnp.float32
    )


def input_grad(back, weight):
    return lax.dot_general(
        back, weight, (((back.ndim - 1,), (1,)), ((), ())), preferred_element_type=jnp.float32
    )


def split_heads(qkv_low):
    batch, count, triple = qkv_low.shape
    width = triple // 3
    parts = qkv_low.reshape(batch, count, 3, HEADS, width // HEADS)
    return (parts[:, :, 0], parts[:, :, 1], parts[:, :, 2])


def probabilities(query, key):
    score = jnp.einsum(
        "bnhe,bmhe->bhnm", query, key, preferred_element_type=jnp.float32
    ) / math.sqrt(query.shape[-1])
    expo = jnp.exp(score - jnp.max(score, -1, keepdims=True))
    return expo / jnp.sum(expo, -1, keepdims=True)


def input_grad_t(back, weight_t):
    return jnp.matmul(back, weight_t, preferred_element_type=jnp.float32)


def forward_t(left, weight_t):
    return lax.dot_general(
        left, weight_t, (((left.ndim - 1,), (1,)), ((), ())), preferred_element_type=jnp.float32
    )


def attention_back(qkv_low, probs, d_attn):
    query, key, value = split_heads(qkv_low)
    scale = 1.0 / math.sqrt(query.shape[-1])
    d_mixed = d_attn.reshape(query.shape)
    d_value = jnp.einsum(
        "bhnm,bnhe->bmhe", probs.astype(jnp.bfloat16), d_mixed, preferred_element_type=jnp.float32
    )
    d_prob = jnp.einsum("bnhe,bmhe->bhnm", d_mixed, value, preferred_element_type=jnp.float32)
    d_score = (probs * (d_prob - jnp.sum(probs * d_prob, -1, keepdims=True))).astype(jnp.bfloat16)
    d_query = (
        jnp.einsum("bhnm,bmhe->bnhe", d_score, key, preferred_element_type=jnp.float32) * scale
    )
    d_key = (
        jnp.einsum("bhnm,bnhe->bmhe", d_score, query, preferred_element_type=jnp.float32) * scale
    )
    return jnp.concatenate(
        [item.reshape(item.shape[:2] + (-1,)) for item in (d_query, d_key, d_value)], -1
    ).astype(jnp.bfloat16)


def gather_heavy(in_low, out_low, shard_count):
    width = in_low.shape[0]
    all_in = lax.all_gather(in_low, "shard", axis=1, tiled=True)
    all_out = lax.all_gather(out_low, "shard", axis=1, tiled=True)
    return all_in[:, 6 * width : 9 * width].T, all_in[:, 9 * width :].T, all_out.T


MESH = pl.DeviceIdType.MESH
PIECES = 4


def heavy_chunks(width):
    half = width // 2
    return (
        (0, 0, width, 0, width, False),
        (0, 0, width, 2 * width, width, False),
        (1, 0, 2 * width, 0, half, True),
        (1, 2 * width, 2 * width, 0, half, True),
        (2, 0, width, 0, half, False),
        (3, 0, width, 0, half, False),
        (3, width, width, 0, half, True),
        (3, 2 * width, width, 0, half, True),
    )


def add_rows(target, left, right, rows):
    block = 48

    def body(index, carry):
        span = pl.ds(pl.multiple_of(index * block, block), block)
        target[span] = left[span] + right[span]
        return carry

    lax.fori_loop(0, rows // block, body, 0)


def reduce_kernel(lines, chunks, g0, g1, g2, g3, f0, f1, f2, f3, *scratch):
    count = len(chunks)
    grads, finals = (g0, g1, g2, g3), (f0, f1, f2, f3)
    by_core, by_y, by_x, by_z = (scratch[k * count : (k + 1) * count] for k in range(4))
    send, recv, zsend, zrecv, wsend, wrecv = scratch[4 * count :]
    rep, shard = lax.axis_index("rep"), lax.axis_index("shard")
    x, z = lax.rem(rep, 2), lax.div(rep, 2)
    core, y = lax.rem(shard, 2), lax.div(shard, 2)
    to_core = (rep, shard + 1 - 2 * core)
    to_y = (rep, shard + 2 - 4 * y)
    to_x = (rep + 1 - 2 * x, shard)

    def line_peer(step):
        return lax.rem(z + step, lines)

    barrier = pltpu.get_barrier_semaphore()
    for peer in (to_core, to_y, to_x):
        pl.semaphore_signal(barrier, inc=1, device_id=peer, device_id_type=MESH)
    for step in range(1, lines):
        pl.semaphore_signal(
            barrier, inc=1, device_id=(line_peer(step) * 2 + x, shard), device_id_type=MESH
        )
    pl.semaphore_wait(barrier, 3 + lines - 1)

    stride = lines // PIECES
    owns = lax.rem(z, stride) == 0
    mine = lax.div(z, stride)
    sends = []

    def remote(source, target, send_sem, recv_sem, peer):
        return pltpu.make_async_remote_copy(
            src_ref=source,
            dst_ref=target,
            send_sem=send_sem,
            recv_sem=recv_sem,
            device_id=peer,
            device_id_type=MESH,
        )

    def rows_of(ref, start, size):
        return ref.at[pl.ds(pl.multiple_of(start, 16), size)]

    def lanes_at(index, ref, row, rows, which):
        _, _, _, lane, lanes, _ = chunks[index]
        return ref.at[
            pl.ds(pl.multiple_of(row, 16), rows), pl.ds(pl.multiple_of(lane + which * lanes, 128), lanes)
        ]

    def core_copy(i):
        array, row, rows = chunks[i][:3]
        return remote(
            lanes_at(i, grads[array], row, rows, 1 - core), by_core[i], send.at[i, 0], recv.at[i, 0], to_core
        )

    def y_copy(i):
        half = chunks[i][2] // 2
        return remote(
            rows_of(by_core[i], (1 - y) * half, half), by_y[i], send.at[i, 1], recv.at[i, 1], to_y
        )

    def x_copy(i):
        quarter = chunks[i][2] // 4
        return remote(
            rows_of(by_y[i], (1 - x) * quarter, quarter), by_x[i], send.at[i, 2], recv.at[i, 2], to_x
        )

    def z_copy(i, piece):
        size = chunks[i][2] // 4 // PIECES
        owner = piece * stride
        slot = lax.rem(z - owner - 1 + lines, lines)
        return remote(
            by_x[i].at[pl.ds(piece * size, size)],
            by_z[i].at[slot],
            zsend.at[i, piece],
            zrecv.at[i, slot],
            (owner * 2 + x, shard),
        )

    def final_rows(i, side, start, size, which):
        array, row, rows = chunks[i][:3]
        return lanes_at(i, finals[array], row + side * (rows // 2) + start, size, which)

    def cross_copy(i):
        size = chunks[i][2] // 4 // PIECES
        part = final_rows(i, 0, (x * PIECES + mine) * size, size, core)
        return remote(part, part, send.at[i, 3], recv.at[i, 3], to_y)

    def line_copy(i, which, side, step):
        size = chunks[i][2] // 4 // PIECES
        part = final_rows(i, side, (x * PIECES + mine) * size, size, core)
        return remote(
            part, part, wsend.at[i, which, step - 1], wrecv.at[i, which, mine], (line_peer(step) * 2 + x, shard)
        )

    def line_arrival(i, which, side, piece):
        size = chunks[i][2] // 4 // PIECES
        part = final_rows(i, side, (x * PIECES + piece) * size, size, core)
        return remote(part, part, wsend.at[i, which, 0], wrecv.at[i, which, piece], to_core)

    def pair_copy(i, which, side, column):
        quarter = chunks[i][2] // 4
        part = final_rows(i, side, column * quarter, quarter, core)
        return remote(part, part, send.at[i, 4 + which], recv.at[i, 4 + which], to_x)

    def last_copy(i, which, side, half):
        rows = chunks[i][2] // 2
        part = final_rows(i, side, 0, rows, half)
        return remote(part, part, send.at[i, 6 + which], recv.at[i, 6 + which], to_core)

    def sides(i, action):
        if chunks[i][5]:

            @pl.when(y == 1)
            def _():
                action(0, 1)
                action(1, 0)

        else:
            action(0, y)

    def stage0(i):
        core_copy(i).start()

    def stage1(i):
        array, row, rows = chunks[i][:3]
        core_copy(i).wait_recv()
        add_rows(by_core[i], by_core[i], lanes_at(i, grads[array], row, rows, core), rows)
        y_copy(i).start()

    def stage2(i):
        half = chunks[i][2] // 2
        y_copy(i).wait_recv()
        add_rows(by_y[i], by_y[i], rows_of(by_core[i], y * half, half), half)
        x_copy(i).start()

    def stage3(i):
        quarter = chunks[i][2] // 4
        x_copy(i).wait_recv()
        add_rows(by_x[i], by_x[i], rows_of(by_y[i], x * quarter, quarter), quarter)
        for piece in range(PIECES):

            @pl.when(z != piece * stride)
            def _():
                z_copy(i, piece).start()

    def stage4(i):
        size = chunks[i][2] // 4 // PIECES

        @pl.when(owns)
        def _():
            for slot in range(lines - 1):
                remote(
                    by_z[i].at[slot], by_z[i].at[slot], zsend.at[i, 0], zrecv.at[i, slot], to_core
                ).wait_recv()
            target = final_rows(i, y, (x * PIECES + mine) * size, size, core)

            def body(index, carry):
                total = by_x[i][
                    pl.ds(pl.multiple_of(mine * size + index * 16, 16), 16)
                ].astype(jnp.float32)
                for slot in range(lines - 1):
                    total += by_z[i][slot, pl.ds(pl.multiple_of(index * 16, 16), 16)].astype(jnp.float32)
                target[pl.ds(pl.multiple_of(index * 16, 16), 16)] = total.astype(jnp.bfloat16)
                return carry

            lax.fori_loop(0, size // 16, body, 0)
            if chunks[i][5]:

                @pl.when(y == 0)
                def _():
                    cross_copy(i).start()

                @pl.when(y == 1)
                def _():
                    for step in range(1, lines):
                        line_copy(i, 0, 1, step).start()
            else:
                for step in range(1, lines):
                    line_copy(i, 0, y, step).start()

    def stage5(i):
        if chunks[i][5]:

            @pl.when(jnp.logical_and(owns, y == 1))
            def _():
                cross_copy(i).wait_recv()
                for step in range(1, lines):
                    line_copy(i, 1, 0, step).start()

    def stage6(i):
        def action(which, side):
            for piece in range(PIECES):

                @pl.when(z != piece * stride)
                def _():
                    line_arrival(i, which, side, piece).wait_recv()

            pair_copy(i, which, side, x).start()

        sides(i, action)

    def stage7(i):
        def action(which, side):
            pair_copy(i, which, side, 1 - x).wait_recv()
            last_copy(i, which, side, core).start()

        sides(i, action)

    def stage8(i):
        sides(i, lambda which, side: last_copy(i, which, side, 1 - core).wait_recv())

    stages = (stage0, stage1, stage2, stage3, stage4, stage5, stage6, stage7, stage8)
    for tick in range(count + len(stages) - 1):
        for k, stage in enumerate(stages):
            if 0 <= tick - k < count:
                stage(tick - k)

    for i in range(count):
        core_copy(i).wait_send()
        y_copy(i).wait_send()
        x_copy(i).wait_send()
        for piece in range(PIECES):

            @pl.when(z != piece * stride)
            def _():
                z_copy(i, piece).wait_send()

        if chunks[i][5]:

            @pl.when(jnp.logical_and(owns, y == 0))
            def _():
                cross_copy(i).wait_send()

        def action(which, side):
            @pl.when(owns)
            def _():
                for step in range(1, lines):
                    line_copy(i, which, side, step).wait_send()

            pair_copy(i, which, side, x).wait_send()
            last_copy(i, which, side, core).wait_send()

        sides(i, action)


def reduce_call(lines, g_fc2_t, g_fc1_t, g_o_t, g_qkv_t):
    width = g_o_t.shape[0]
    chunks = heavy_chunks(width)
    count = len(chunks)
    grads = (g_fc2_t, g_fc1_t, g_o_t, g_qkv_t)
    low = jnp.bfloat16
    sizes = [(rows, lanes) for _, _, rows, _, lanes, _ in chunks]
    return pl.pallas_call(
        functools.partial(reduce_kernel, lines, chunks),
        out_shape=[jax.ShapeDtypeStruct(item.shape, low) for item in grads],
        in_specs=[pl.BlockSpec(memory_space=pltpu.VMEM)] * 4,
        out_specs=[pl.BlockSpec(memory_space=pltpu.VMEM)] * 4,
        scratch_shapes=[pltpu.VMEM((rows, lanes), low) for rows, lanes in sizes]
        + [pltpu.VMEM((rows // 2, lanes), low) for rows, lanes in sizes]
        + [pltpu.VMEM((rows // 4, lanes), low) for rows, lanes in sizes]
        + [pltpu.VMEM((lines - 1, rows // 4 // PIECES, lanes), low) for rows, lanes in sizes]
        + [
            pltpu.SemaphoreType.DMA((count, 8)),
            pltpu.SemaphoreType.DMA((count, 8)),
            pltpu.SemaphoreType.DMA((count, PIECES)),
            pltpu.SemaphoreType.DMA((count, lines - 1)),
            pltpu.SemaphoreType.DMA((count, 2, lines - 1)),
            pltpu.SemaphoreType.DMA((count, 2, PIECES)),
        ],
        compiler_params=pltpu.CompilerParams(
            collective_id=1, has_side_effects=True, vmem_limit_bytes=60 * 1024 * 1024
        ),
    )(*grads)


def reduce_heavy(g_fc2_t, g_fc1_t, g_o_t, g_qkv_t, in_cols, out_cols):
    width = g_o_t.shape[1]
    fc2, fc1, attn_out, qkv = reduce_call(
        lax.axis_size("rep") // 2,
        *(item.astype(jnp.bfloat16) for item in (g_fc2_t, g_fc1_t, g_o_t, g_qkv_t)),
    )
    place = lax.axis_index("shard")
    padded = jnp.concatenate([jnp.zeros((6 * width, width), jnp.bfloat16), qkv, fc1], 0)
    own_in = lax.dynamic_slice_in_dim(padded, place * in_cols, in_cols, 0)
    own_out = jnp.concatenate(
        [
            lax.dynamic_slice_in_dim(item, place * out_cols, out_cols, 0)
            for item in (attn_out, fc2)
        ],
        1,
    )
    return own_in.T.astype(jnp.float32), own_out.T.astype(jnp.float32)


def on_device(
    latents,
    noises,
    velocity,
    times,
    labels,
    dropped,
    blocks_in,
    blocks_out,
    head_side,
    embed_side,
    state_in_row,
    state_in_col,
    state_out_row,
    state_out_col,
    state_head_row,
    state_head_col,
    state_embed_row,
    state_embed_col,
):
    both = ("rep", "shard")
    images = latents.shape[0]
    width = head_side.shape[0]
    shard_count = lax.axis_size("shard")
    place = lax.axis_index("shard")
    rep_place = lax.axis_index("rep")
    in_cols = blocks_in.shape[2]
    out_cols = blocks_out.shape[2]
    head_cols = head_side.shape[1]
    embed_cols = embed_side.shape[1]
    group = images * shard_count
    in_low = blocks_in[0].astype(jnp.bfloat16)
    out_low = blocks_out[0].astype(jnp.bfloat16)
    head_low = head_side.astype(jnp.bfloat16)
    embed_low = embed_side.astype(jnp.bfloat16)
    qkv_t, fc1_t, out_t = gather_heavy(in_low, out_low, shard_count)
    o_t, fc2_t = out_t[:, :width], out_t[:, width:]
    marks = lax.all_gather(jnp.stack([times, labels, dropped]), both, axis=1, tiled=True)
    t_all = (marks[0].astype(jnp.float32) + 1.0) / step_count
    classes = jnp.where(marks[2] == 1, CLASSES - 1, marks[1])
    onehot = (classes[:, None] == jnp.arange(CLASSES, dtype=jnp.int32)[None, :]).astype(
        jnp.bfloat16
    )
    freq_low = time_freq(t_all, FREQ).astype(jnp.bfloat16)
    time_one = forward_product(freq_low, embed_low[PATCH : PATCH + FREQ])
    table_part = forward_product(onehot, embed_low[PATCH + FREQ :])
    time_act = lax.all_gather(silu(time_one).astype(jnp.bfloat16), "shard", axis=1, tiled=True)
    two_part = forward_product(time_act, head_low)
    sides = lax.all_gather(
        jnp.concatenate([two_part, table_part], 1), "shard", axis=0, tiled=False
    )
    time_two = jnp.concatenate([sides[j, :, :head_cols] for j in range(shard_count)], 1)[:, :width]
    table_rows = jnp.concatenate([sides[j, :, head_cols:] for j in range(shard_count)], 1)
    cond_full = time_two + table_rows
    cond = silu(cond_full).astype(jnp.bfloat16)
    cond_group = lax.dynamic_slice_in_dim(cond, rep_place * group, group, 0)
    mod_part = jnp.concatenate(
        [forward_product(cond_group, in_low), forward_product(cond_group, head_low)], 1
    )
    mods = lax.all_gather(mod_part, "shard", axis=0, tiled=False)
    mods = lax.dynamic_slice_in_dim(mods, place * images, images, 1)
    modul = jnp.concatenate([mods[j, :, :in_cols] for j in range(shard_count)], 1)[:, : 6 * width]
    final_mod = jnp.concatenate([mods[j, :, in_cols:] for j in range(shard_count)], 1)
    final_mod = final_mod[:, width : 3 * width]
    small = jnp.concatenate(
        [
            lax.all_gather(embed_low[:PATCH], "shard", axis=1, tiled=True),
            lax.all_gather(head_low, "shard", axis=1, tiled=True)[:, 3 * width :].T,
        ],
        0,
    )
    patch_w, head_t = small[:PATCH], small[PATCH:]
    t_value = (times.astype(jnp.float32) + 1.0) / step_count
    tcol = t_value[:, None, None]
    state = (
        (1.0 - tcol) * latents.reshape(images, TOK, PATCH)
        + tcol * noises.reshape(images, TOK, PATCH)
    ).astype(jnp.bfloat16)
    target = velocity.reshape(images, TOK, PATCH)
    hidden = forward_product(state, patch_w) + positions(GRID, width)[None]
    pieces = jnp.split(modul, 6, axis=-1)
    normed, first_pull = jax.vjp(norm_mod, hidden, pieces[0], pieces[1])
    normed = normed.astype(jnp.bfloat16)
    qkv_low = forward_t(normed, qkv_t).astype(jnp.bfloat16)
    query, key, value = split_heads(qkv_low)
    probs = probabilities(query, key)
    mixed = jnp.einsum(
        "bhnm,bmhe->bnhe", probs.astype(jnp.bfloat16), value, preferred_element_type=jnp.float32
    )
    attn = mixed.reshape(hidden.shape).astype(jnp.bfloat16)
    proj = forward_t(attn, o_t)
    middle = hidden + pieces[2][:, None, :] * proj
    normed_two, norm_pull = jax.vjp(norm_mod, middle, pieces[3], pieces[4])
    normed_two = normed_two.astype(jnp.bfloat16)
    upper = forward_t(normed_two, fc1_t)
    active, gelu_pull = jax.vjp(gelu, upper)
    active = active.astype(jnp.bfloat16)
    mlp = forward_t(active, fc2_t)
    result = middle + pieces[5][:, None, :] * mlp
    final, final_pull = jax.vjp(norm_mod, result, final_mod[:, :width], final_mod[:, width:])
    final_low = final.astype(jnp.bfloat16)
    output = forward_t(final_low, head_t)
    diff = output - target
    loss_local = 0.5 * jnp.sum(tcol * diff * diff)
    d_output = (tcol * diff).astype(jnp.bfloat16)
    g_head_t = weight_grad(d_output, final_low)
    d_final = input_grad_t(d_output, head_t)
    back, d_shift, d_scale = final_pull(d_final)
    d_gate_two = jnp.sum(back * mlp, 1)
    d_mlp = (pieces[5][:, None, :] * back).astype(jnp.bfloat16)
    g_fc2_t = weight_grad(d_mlp, active)
    d_active = input_grad_t(d_mlp, fc2_t)
    d_upper = gelu_pull(d_active)[0].astype(jnp.bfloat16)
    g_fc1_t = weight_grad(d_upper, normed_two)
    d_normed_two = input_grad_t(d_upper, fc1_t)
    d_from_norm, d_shift_two, d_scale_two = norm_pull(d_normed_two)
    d_middle = back + d_from_norm
    d_gate_one = jnp.sum(d_middle * proj, 1)
    d_proj = (pieces[2][:, None, :] * d_middle).astype(jnp.bfloat16)
    g_o_t = weight_grad(d_proj, attn)
    d_attn = input_grad_t(d_proj, o_t).astype(jnp.bfloat16)
    d_qkv = attention_back(qkv_low, probs, d_attn)
    g_qkv_t = weight_grad(d_qkv, normed)
    d_normed = input_grad_t(d_qkv, qkv_t)
    d_from_first, d_shift_one, d_scale_one = first_pull(d_normed)
    d_hidden = d_middle + d_from_first
    g_patch = weight_grad(state, d_hidden.astype(jnp.bfloat16))
    heavy_in, heavy_out = reduce_heavy(g_fc2_t, g_fc1_t, g_o_t, g_qkv_t, in_cols, out_cols)
    d_low = jnp.concatenate(
        [d_shift_one, d_scale_one, d_gate_one, d_shift_two, d_scale_two, d_gate_two, d_shift, d_scale],
        -1,
    ).astype(jnp.bfloat16)
    d_low = lax.all_gather(d_low, both, axis=0, tiled=True)
    full_in = in_cols * shard_count
    full_head = head_cols * shard_count
    d_in = jnp.pad(d_low[:, : 6 * width], ((0, 0), (0, full_in - 6 * width)))
    d_in = lax.dynamic_slice_in_dim(d_in, place * in_cols, in_cols, 1)
    d_fin = jnp.pad(d_low[:, 6 * width :], ((0, 0), (width, full_head - 3 * width)))
    d_fin = lax.dynamic_slice_in_dim(d_fin, place * head_cols, head_cols, 1)
    d_cond = lax.psum(input_grad(d_in, in_low) + input_grad(d_fin, head_low), "shard")
    _, silu_pull = jax.vjp(silu, cond_full)
    d_full = silu_pull(d_cond)[0]
    d_two = jnp.pad(d_full.astype(jnp.bfloat16), ((0, 0), (0, full_head - width)))
    d_two = lax.dynamic_slice_in_dim(d_two, place * head_cols, head_cols, 1)
    d_act = lax.psum_scatter(input_grad(d_two, head_low), "shard", scatter_dimension=1, tiled=True)
    _, time_pull = jax.vjp(silu, time_one)
    d_one = time_pull(d_act)[0].astype(jnp.bfloat16)
    d_full_own = lax.dynamic_slice_in_dim(d_full, place * embed_cols, embed_cols, 1)
    g_table = lax.dot_general(
        onehot.astype(jnp.float32),
        d_full_own,
        (((0,), (0,)), ((), ())),
        precision=lax.Precision.HIGHEST,
    )
    loss_sum, g_small = lax.psum((loss_local, jnp.concatenate([g_patch, g_head_t], 0)), both)
    own_patch = lax.dynamic_slice_in_dim(g_small[:PATCH], place * embed_cols, embed_cols, 1)
    own_head = jnp.pad(g_small[PATCH:].T, ((0, 0), (3 * width, 0)))
    own_head = lax.dynamic_slice_in_dim(own_head, place * head_cols, head_cols, 1)
    totals = (
        (weight_grad(cond, d_in) + heavy_in)[None],
        heavy_out[None],
        weight_grad(time_act, d_two) + weight_grad(cond, d_fin) + own_head,
        jnp.concatenate([own_patch, weight_grad(freq_low, d_one), g_table], 0),
    )
    weights = (blocks_in, blocks_out, head_side, embed_side)
    rows_old = (state_in_row, state_out_row, state_head_row, state_embed_row)
    cols_old = (state_in_col, state_out_col, state_head_col, state_embed_col)
    cols_new = [
        decay * col_state + (1.0 - decay) * (jnp.mean(gradient * gradient, -2) + eps_one)
        for gradient, col_state in zip(totals, cols_old)
    ]
    row_parts = [jnp.sum(gradient * gradient, -1) for gradient in totals]
    row_scaled = [
        jnp.sum(gradient * gradient / col_next[..., None, :], -1)
        for gradient, col_next in zip(totals, cols_new)
    ]
    weight_sq = [jnp.sum(weight * weight, axis=(-2, -1)) for weight in weights]
    row_sums, row_scaled, weight_sq = lax.psum((row_parts, row_scaled, weight_sq), "shard")
    rows_new = [
        decay * row_state
        + (1.0 - decay) * (row_sum / (gradient.shape[-1] * shard_count) + eps_one)
        for row_sum, gradient, row_state in zip(row_sums, totals, rows_old)
    ]
    row_means = [jnp.mean(row_next, -1) for row_next in rows_new]
    total_sq = sum(
        jnp.sum(row_mean * jnp.sum(scaled / row_next, -1))
        for scaled, row_next, row_mean in zip(row_scaled, rows_new, row_means)
    )
    count = sum((weight.size for weight in weights)) * shard_count
    update_rms = jnp.sqrt(total_sq / count)
    factor = jnp.maximum(1.0, update_rms / clip_level)
    news = []
    for index in range(4):
        numel = weights[index].shape[-2] * weights[index].shape[-1] * shard_count
        weight_rms = jnp.sqrt(weight_sq[index] / numel)
        step_size = rate * jnp.maximum(eps_two, weight_rms) / factor
        row_scale = jnp.asarray(step_size)[..., None] * lax.rsqrt(
            rows_new[index] / row_means[index][..., None]
        )
        news.append(
            weights[index]
            - totals[index] * row_scale[..., :, None] * lax.rsqrt(cols_new[index])[..., None, :]
        )
    return (
        loss_sum,
        update_rms,
        totals[0],
        totals[1],
        totals[2],
        totals[3],
        rows_new[0],
        cols_new[0],
        rows_new[1],
        cols_new[1],
        rows_new[2],
        cols_new[2],
        rows_new[3],
        cols_new[3],
        news[0],
        news[1],
        news[2],
        news[3],
    )


def solution(mesh):
    placed = (
        P(("rep", "shard"), None),
        P(("rep", "shard"), None),
        P(("rep", "shard"), None),
        P(("rep", "shard")),
        P(("rep", "shard")),
        P(("rep", "shard")),
        P(None, None, "shard"),
        P(None, None, "shard"),
        P(None, "shard"),
        P(None, "shard"),
        P(),
        P(None, "shard"),
        P(),
        P(None, "shard"),
        P(),
        P("shard"),
        P(),
        P("shard"),
    )
    return jax.shard_map(
        on_device,
        mesh=mesh,
        in_specs=placed,
        out_specs=(
            P(),
            P(),
            P(None, None, "shard"),
            P(None, None, "shard"),
            P(None, "shard"),
            P(None, "shard"),
            P(),
            P(None, "shard"),
            P(),
            P(None, "shard"),
            P(),
            P("shard"),
            P(),
            P("shard"),
            P(None, None, "shard"),
            P(None, None, "shard"),
            P(None, "shard"),
            P(None, "shard"),
        ),
        check_vma=False,
    )
```

```python
import functools
import math

import jax
import jax.numpy as jnp
from jax import lax
from jax.experimental import pallas as pl
from jax.experimental.pallas import tpu as pltpu
from jax.sharding import PartitionSpec as P

HEADS = 12
CLASSES = 1001
FREQ = 256
GRID = 16
PATCH = 16
LAYERS = 1
TOK = 256


decay = 0.5
eps_norm = 1e-06
eps_one = 1e-30
eps_two = 0.001
clip_level = 0.1
rate = 8.0
step_count = 1000.0


def silu(value):
    return value * jax.nn.sigmoid(value)


def positions(grid, width):
    quarter = width // 4
    omega = 1.0 / 10000.0 ** (jnp.arange(quarter, dtype=jnp.float32) / quarter)
    index = jnp.arange(grid * grid, dtype=jnp.int32)
    row_pos = (index // grid).astype(jnp.float32)[:, None] * omega[None, :]
    col_pos = (index % grid).astype(jnp.float32)[:, None] * omega[None, :]
    return jnp.concatenate(
        [jnp.sin(row_pos), jnp.cos(row_pos), jnp.sin(col_pos), jnp.cos(col_pos)], 1
    )


def time_freq(t_value, width):
    half = width // 2
    freqs = jnp.exp(-math.log(10000.0) * jnp.arange(half, dtype=jnp.float32) / half)
    angles = (t_value * step_count)[:, None] * freqs[None, :]
    return jnp.concatenate([jnp.cos(angles), jnp.sin(angles)], -1)


def weight_grad(left, back):
    flat_left = left.reshape(-1, left.shape[-1])
    flat_back = back.reshape(-1, back.shape[-1])
    return lax.dot_general(
        flat_left, flat_back, (((0,), (0,)), ((), ())), preferred_element_type=jnp.float32
    )


MESH = pl.DeviceIdType.MESH
LINE = 4
PIECES = 4


def heavy_chunks(width):
    half, third = width // 2, width // 3
    parts = [(0, 0, width, 2 * third * k, third, False) for k in range(6)]
    parts += [(1, 2 * third * k, 2 * third, 0, half, True) for k in range(6)]
    parts += [(2, 0, width, 0, half, False), (3, 0, width, 0, half, False)]
    parts += [(3, width + 2 * third * k, 2 * third, 0, half, True) for k in range(3)]
    return tuple(parts)


def add_rows(target, left, right, rows):
    block = 16

    def body(index, carry):
        span = pl.ds(pl.multiple_of(index * block, block), block)
        target[span] = left[span] + right[span]
        return carry

    lax.fori_loop(0, rows // block, body, 0)


def reduce_kernel(lines, chunks, tables, *refs):
    count = len(chunks)
    grads, refs = refs[:4], refs[4:]
    (d_mod, d_fm, few, in_t, head_t, cond_full, time_one), refs = refs[:7], refs[7:]
    finals, refs = refs[:4], refs[4:]
    (d_in, d_head, d_two, d_full, d_one, few_sum), scratch = refs[:6], refs[6:]
    by_core, by_y, by_x, by_z = (scratch[k * count : (k + 1) * count] for k in range(4))
    send, recv, zsend, zrecv, wsend, wrecv = scratch[4 * count : 4 * count + 6]
    (
        few_got, few_held, few_line, group_slot, pair_own, pair_got, line_slot, part_own, part_slot, act_own, act_slot,
        few_send, few_recv, group_send, group_recv, line_send, line_recv,
    ) = scratch[4 * count + 6 :]
    (in_starts, in_tiles), (head_starts, head_tiles), (embed_starts, embed_tiles), shards = tables
    rep, shard = lax.axis_index("rep"), lax.axis_index("shard")
    place = lax.rem(rep, 2 * lines)
    base = rep - place
    x, z = lax.rem(place, 2), lax.div(place, 2)
    core, y = lax.rem(shard, 2), lax.div(shard, 2)
    to_core = (rep, shard + 1 - 2 * core)
    to_y = (rep, shard + 2 - 4 * y)
    to_x = (rep + 1 - 2 * x, shard)

    def line_peer(step):
        return (base + lax.rem(z + step, lines) * 2 + x, shard)

    barrier = pltpu.get_barrier_semaphore()
    to_far = (rep, shards - 1 - shard)
    for peer in (to_core, to_y, to_x, to_far):
        pl.semaphore_signal(barrier, inc=1, device_id=peer, device_id_type=MESH)
    for step in range(1, lines):
        pl.semaphore_signal(
            barrier, inc=1, device_id=line_peer(step), device_id_type=MESH
        )
    pl.semaphore_wait(barrier, 4 + lines - 1)

    stride = lines // PIECES
    owns = lax.rem(z, stride) == 0
    mine = lax.div(z, stride)
    sends = []

    def remote(source, target, send_sem, recv_sem, peer):
        return pltpu.make_async_remote_copy(
            src_ref=source,
            dst_ref=target,
            send_sem=send_sem,
            recv_sem=recv_sem,
            device_id=peer,
            device_id_type=MESH,
        )

    def rows_of(ref, start, size):
        return ref.at[pl.ds(pl.multiple_of(start, 16), size)]

    def lanes_at(index, ref, row, rows, which):
        _, _, _, lane, lanes, _ = chunks[index]
        return ref.at[
            pl.ds(pl.multiple_of(row, 16), rows), pl.ds(pl.multiple_of(lane + which * lanes, 128), lanes)
        ]

    def core_copy(i):
        array, row, rows = chunks[i][:3]
        return remote(
            lanes_at(i, grads[array], row, rows, 1 - core), by_core[i], send.at[i, 0], recv.at[i, 0], to_core
        )

    def y_copy(i):
        half = chunks[i][2] // 2
        return remote(
            rows_of(by_core[i], (1 - y) * half, half), by_y[i], send.at[i, 1], recv.at[i, 1], to_y
        )

    def x_copy(i):
        quarter = chunks[i][2] // 4
        return remote(
            rows_of(by_y[i], (1 - x) * quarter, quarter), by_x[i], send.at[i, 2], recv.at[i, 2], to_x
        )

    def z_copy(i, piece):
        size = chunks[i][2] // 4 // PIECES
        owner = piece * stride
        slot = lax.rem(z - owner - 1 + lines, lines)
        return remote(
            by_x[i].at[pl.ds(piece * size, size)],
            by_z[i].at[slot],
            zsend.at[i, piece],
            zrecv.at[i, slot],
            (base + owner * 2 + x, shard),
        )

    def final_rows(i, side, start, size, which):
        array, row, rows = chunks[i][:3]
        return lanes_at(i, finals[array], row + side * (rows // 2) + start, size, which)

    def cross_copy(i):
        size = chunks[i][2] // 4 // PIECES
        part = final_rows(i, 0, (x * PIECES + mine) * size, size, core)
        return remote(part, part, send.at[i, 3], recv.at[i, 3], to_y)

    def line_copy(i, which, side, step):
        size = chunks[i][2] // 4 // PIECES
        part = final_rows(i, side, (x * PIECES + mine) * size, size, core)
        return remote(
            part, part, wsend.at[i, which, step - 1], wrecv.at[i, which, mine], line_peer(step)
        )

    def line_arrival(i, which, side, piece):
        size = chunks[i][2] // 4 // PIECES
        part = final_rows(i, side, (x * PIECES + piece) * size, size, core)
        return remote(part, part, wsend.at[i, which, 0], wrecv.at[i, which, piece], to_core)

    def pair_copy(i, which, side, column):
        quarter = chunks[i][2] // 4
        part = final_rows(i, side, column * quarter, quarter, core)
        return remote(part, part, send.at[i, 4 + which], recv.at[i, 4 + which], to_x)

    def last_copy(i, which, side, half):
        rows = chunks[i][2] // 2
        part = final_rows(i, side, 0, rows, half)
        return remote(part, part, send.at[i, 6 + which], recv.at[i, 6 + which], to_core)

    def sides(i, action):
        if chunks[i][5]:

            @pl.when(y == 1)
            def _():
                action(0, 1)
                action(1, 0)

        else:
            action(0, y)

    def stage0(i):
        core_copy(i).start()

    def stage1(i):
        array, row, rows = chunks[i][:3]
        core_copy(i).wait_recv()
        add_rows(by_core[i], by_core[i], lanes_at(i, grads[array], row, rows, core), rows)
        y_copy(i).start()

    def stage2(i):
        half = chunks[i][2] // 2
        y_copy(i).wait_recv()
        add_rows(by_y[i], by_y[i], rows_of(by_core[i], y * half, half), half)
        x_copy(i).start()

    def stage3(i):
        quarter = chunks[i][2] // 4
        x_copy(i).wait_recv()
        add_rows(by_x[i], by_x[i], rows_of(by_y[i], x * quarter, quarter), quarter)
        for piece in range(PIECES):

            @pl.when(z != piece * stride)
            def _():
                z_copy(i, piece).start()

    def stage4(i):
        size = chunks[i][2] // 4 // PIECES

        @pl.when(owns)
        def _():
            for slot in range(lines - 1):
                remote(
                    by_z[i].at[slot], by_z[i].at[slot], zsend.at[i, 0], zrecv.at[i, slot], to_core
                ).wait_recv()
            target = final_rows(i, y, (x * PIECES + mine) * size, size, core)

            def body(index, carry):
                total = by_x[i][
                    pl.ds(pl.multiple_of(mine * size + index * 16, 16), 16)
                ].astype(jnp.float32)
                for slot in range(lines - 1):
                    total += by_z[i][slot, pl.ds(pl.multiple_of(index * 16, 16), 16)].astype(jnp.float32)
                target[pl.ds(pl.multiple_of(index * 16, 16), 16)] = total.astype(jnp.bfloat16)
                return carry

            lax.fori_loop(0, size // 16, body, 0)
            if chunks[i][5]:

                @pl.when(y == 0)
                def _():
                    cross_copy(i).start()

                @pl.when(y == 1)
                def _():
                    for step in range(1, lines):
                        line_copy(i, 0, 1, step).start()
            else:
                for step in range(1, lines):
                    line_copy(i, 0, y, step).start()

    def stage5(i):
        if chunks[i][5]:

            @pl.when(jnp.logical_and(owns, y == 1))
            def _():
                cross_copy(i).wait_recv()
                for step in range(1, lines):
                    line_copy(i, 1, 0, step).start()

    def stage6(i):
        def action(which, side):
            for piece in range(PIECES):

                @pl.when(z != piece * stride)
                def _():
                    line_arrival(i, which, side, piece).wait_recv()

            pair_copy(i, which, side, x).start()

        sides(i, action)

    def stage7(i):
        def action(which, side):
            pair_copy(i, which, side, 1 - x).wait_recv()
            last_copy(i, which, side, core).start()

        sides(i, action)

    def stage8(i):
        sides(i, lambda which, side: last_copy(i, which, side, 1 - core).wait_recv())


    width = in_t.shape[1]
    mod_tiles, wide = 6 * width // 128, width // 128
    images = pair_own.shape[0]
    in_lanes = in_tiles * 128
    head_places = [o for o in range(shards) if head_starts[o] < wide]

    def few_copy(k, peer):
        return remote(few if k == 0 else few_held.at[k - 1], few_got.at[k], few_send.at[k], few_recv.at[k], peer)

    def few_line_copy(step):
        return remote(
            few_line.at[z], few_line.at[z], few_send.at[2 + step], few_recv.at[2 + step], line_peer(step)
        )

    def few_line_arrival(step):
        origin = lax.rem(z + lines - step, lines)
        return remote(few_line.at[origin], few_line.at[origin], few_send.at[2 + step], few_recv.at[2 + step], to_core)

    def group_parts(place):
        parts = []
        tiles = min(in_tiles, mod_tiles - in_starts[place])
        if tiles > 0:
            parts.append((0, in_starts[place] * 128, 0, tiles * 128))
        first, final = max(head_starts[place], wide), min(head_starts[place] + head_tiles, 3 * wide)
        if final > first:
            lead = (first - head_starts[place]) * 128
            parts.append((1, (first - wide) * 128, in_lanes + lead, (final - first) * 128))
        return parts

    def group_copy(place, k, origin):
        which, lane, own, lanes = group_parts(place)[k]
        step = lax.rem(place - origin + shards, shards) - 1
        return remote(
            (d_mod, d_fm)[which].at[:, pl.ds(lane, lanes)],
            group_slot.at[origin, :, pl.ds(own, lanes)],
            group_send.at[k, step],
            group_recv.at[k, step],
            (rep, jnp.int32(place)),
        )

    def to_others(kind, source, slots, step):
        return remote(
            source,
            slots.at[shard],
            group_send.at[kind, step - 1],
            group_recv.at[kind, step - 1],
            (rep, lax.rem(shard + step, shards)),
        )

    def from_others(kind, slots, step):
        origin = lax.rem(shard + shards - step, shards)
        return remote(slots.at[origin], slots.at[origin], group_send.at[kind, 0], group_recv.at[kind, step - 1], to_core)

    def pair_x_copy():
        return remote(pair_own, pair_got, few_send.at[lines + 2], few_recv.at[lines + 2], to_x)

    def line_d_copy(step):
        return remote(
            line_slot.at[z], line_slot.at[z], line_send.at[step - 1], line_recv.at[step - 1], line_peer(step)
        )

    def line_d_arrival(step):
        origin = lax.rem(z + lines - step, lines)
        return remote(line_slot.at[origin], line_slot.at[origin], line_send.at[0], line_recv.at[step - 1], to_core)

    def is_in(where, places):
        return functools.reduce(jnp.logical_or, [where == o for o in places])

    def side0():
        few_copy(0, to_core).start()
        for place in range(shards):
            for k, (which, lane, own, lanes) in enumerate(group_parts(place)):

                @pl.when(shard != place)
                def _():
                    group_copy(place, k, shard).start()

    def side1():
        few_copy(0, to_core).wait_recv()
        few_held[0] = few[...] + few_got[0]
        few_copy(1, to_y).start()
        pair_own[...] = jnp.zeros_like(pair_own)
        for place in range(shards):

            @pl.when(shard == place)
            def _():
                for k, (which, lane, own, lanes) in enumerate(group_parts(place)):
                    total = (d_mod, d_fm)[which][:, lane : lane + lanes]
                    for origin in range(shards):
                        if origin != place:
                            group_copy(place, k, jnp.int32(origin)).wait_recv()
                            total += group_slot[origin, :, own : own + lanes]
                    pair_own[:, own : own + lanes] = total

        pair_x_copy().start()

    def side2():
        few_copy(1, to_y).wait_recv()
        few_held[1] = few_held[0] + few_got[1]
        few_copy(2, to_x).start()
        pair_x_copy().wait_recv()
        own, got = pair_own[...], pair_got[...]
        both = jnp.concatenate([jnp.where(x == 0, own, got), jnp.where(x == 0, got, own)], 0)
        line_slot[z] = both.astype(jnp.bfloat16)
        for step in range(1, lines):
            line_d_copy(step).start()

    def side3():
        few_copy(2, to_x).wait_recv()
        few_line[z] = few_held[1] + few_got[2]
        for step in range(1, lines):
            few_line_copy(step).start()
        for step in range(1, lines):
            line_d_arrival(step).wait_recv()
        for at in range(lines):
            span = slice(at * 2 * images, (at + 1) * 2 * images)
            d_in[span, :] = line_slot[at, :, :in_lanes]
            d_head[span, :] = line_slot[at, :, in_lanes:]
        part_own[...] = jnp.dot(d_in[...], in_t[...], preferred_element_type=jnp.float32) + jnp.dot(
            d_head[...], head_t[...], preferred_element_type=jnp.float32
        )
        part_slot[shard] = part_own[...]
        for step in range(1, shards):
            to_others(2, part_own, part_slot, step).start()

    def side4():
        for step in range(1, lines):
            few_line_arrival(step).wait_recv()
        few_sum[...] = functools.reduce(jnp.add, [few_line[at] for at in range(lines)])
        for step in range(1, shards):
            from_others(2, part_slot, step).wait_recv()
        d_cond = functools.reduce(jnp.add, [part_slot[o] for o in range(shards)])
        value = cond_full[...]
        gate = jax.nn.sigmoid(value)
        d_full[...] = d_cond * (gate + value * gate * (1.0 - gate))
        d_two[...] = jnp.zeros_like(d_two)
        for place in head_places:

            @pl.when(shard == place)
            def _():
                lanes = min(head_tiles, wide - head_starts[place]) * 128
                first = head_starts[place] * 128
                d_two[:, :lanes] = d_full[:, first : first + lanes].astype(jnp.bfloat16)

        @pl.when(is_in(shard, head_places))
        def _():
            act_own[...] = jnp.dot(d_two[...], head_t[...], preferred_element_type=jnp.float32)
            act_slot[shard] = act_own[...]
            for step in range(1, shards):
                to_others(3, act_own, act_slot, step).start()

    def side5():
        for step in range(1, shards):

            @pl.when(is_in(lax.rem(shard + shards - step, shards), head_places))
            def _():
                from_others(3, act_slot, step).wait_recv()

        value = time_one[...]
        gate = jax.nn.sigmoid(value)
        slope = gate + value * gate * (1.0 - gate)
        for place in range(shards):

            @pl.when(shard == place)
            def _():
                first = embed_starts[place] * 128
                d_act = functools.reduce(
                    jnp.add, [act_slot[o, :, first : first + embed_tiles * 128] for o in head_places]
                )
                d_one[...] = (slope * d_act).astype(jnp.bfloat16)

    def side_end():
        for k, peer in enumerate((to_core, to_y, to_x)):
            few_copy(k, peer).wait_send()
        pair_x_copy().wait_send()
        for step in range(1, lines):
            few_line_copy(step).wait_send()
            line_d_copy(step).wait_send()
        for place in range(shards):
            for k in range(len(group_parts(place))):

                @pl.when(shard != place)
                def _():
                    group_copy(place, k, shard).wait_send()

        for step in range(1, shards):
            to_others(2, part_own, part_slot, step).wait_send()

        @pl.when(is_in(shard, head_places))
        def _():
            for step in range(1, shards):
                to_others(3, act_own, act_slot, step).wait_send()

    beside = (side0, side1, side2, side3, side4, side5)
    stages = (stage0, stage1, stage2, stage3, stage4, stage5, stage6, stage7, stage8)
    for tick in range(count + len(stages) - 1):
        if tick < len(beside):
            beside[tick]()
        for k, stage in enumerate(stages):
            if 0 <= tick - k < count:
                stage(tick - k)

    side_end()
    for i in range(count):
        core_copy(i).wait_send()
        y_copy(i).wait_send()
        x_copy(i).wait_send()
        for piece in range(PIECES):

            @pl.when(z != piece * stride)
            def _():
                z_copy(i, piece).wait_send()

        if chunks[i][5]:

            @pl.when(jnp.logical_and(owns, y == 0))
            def _():
                cross_copy(i).wait_send()

        def action(which, side):
            @pl.when(owns)
            def _():
                for step in range(1, lines):
                    line_copy(i, which, side, step).wait_send()

            pair_copy(i, which, side, x).wait_send()
            last_copy(i, which, side, core).wait_send()

        sides(i, action)


def reduce_call(lines, tables, heavy, light):
    width = heavy[2].shape[0]
    chunks = heavy_chunks(width)
    count = len(chunks)
    low, full = jnp.bfloat16, jnp.float32
    (_, in_tiles), (_, head_tiles), (_, embed_tiles), shards = tables
    few, cond_full = light[2], light[5]
    group, rows = light[0].shape[0], cond_full.shape[0]
    lanes = (in_tiles + head_tiles) * 128
    sizes = [(part_rows, part_lanes) for _, _, part_rows, _, part_lanes, _ in chunks]
    dma = pltpu.SemaphoreType.DMA
    shapes = [(item.shape, low) for item in heavy] + [
        ((rows, in_tiles * 128), low),
        ((rows, head_tiles * 128), low),
        ((rows, head_tiles * 128), low),
        ((rows, width), full),
        ((rows, embed_tiles * 128), low),
        (few.shape, full),
    ]
    scratch = [
        ((3,) + few.shape, full),
        ((2,) + few.shape, full),
        ((lines,) + few.shape, full),
        ((shards, group, lanes), full),
        ((group, lanes), full),
        ((group, lanes), full),
        ((lines, 2 * group, lanes), low),
        ((rows, width), full),
        ((shards, rows, width), full),
        ((rows, width), full),
        ((shards, rows, width), full),
    ]
    return pl.pallas_call(
        functools.partial(reduce_kernel, lines, chunks, tables),
        out_shape=[jax.ShapeDtypeStruct(*item) for item in shapes],
        in_specs=[pl.BlockSpec(memory_space=pltpu.VMEM)] * (4 + len(light)),
        out_specs=[pl.BlockSpec(memory_space=pltpu.VMEM)] * len(shapes),
        scratch_shapes=[pltpu.VMEM((r, c), low) for r, c in sizes]
        + [pltpu.VMEM((r // 2, c), low) for r, c in sizes]
        + [pltpu.VMEM((r // 4, c), low) for r, c in sizes]
        + [pltpu.VMEM((lines - 1, r // 4 // PIECES, c), low) for r, c in sizes]
        + [
            dma((count, 8)),
            dma((count, 8)),
            dma((count, PIECES)),
            dma((count, lines - 1)),
            dma((count, 2, lines - 1)),
            dma((count, 2, PIECES)),
        ]
        + [pltpu.VMEM(*item) for item in scratch]
        + [
            dma((lines + 3,)),
            dma((lines + 3,)),
            dma((4, shards - 1)),
            dma((4, shards - 1)),
            dma((lines - 1,)),
            dma((lines - 1,)),
        ],
        compiler_params=pltpu.CompilerParams(
            collective_id=1, has_side_effects=True, vmem_limit_bytes=63 * 1024 * 1024
        ),
    )(*heavy, *light)


def own_heavy(sums, in_cols, out_cols):
    fc2, fc1, attn_out, qkv = sums
    width = attn_out.shape[1]
    place = lax.axis_index("shard")
    padded = jnp.concatenate([jnp.zeros((6 * width, width), jnp.bfloat16), qkv, fc1], 0)
    own_in = lax.dynamic_slice_in_dim(padded, place * in_cols, in_cols, 0)
    own_out = jnp.concatenate(
        [
            lax.dynamic_slice_in_dim(item, place * out_cols, out_cols, 0)
            for item in (attn_out, fc2)
        ],
        1,
    )
    return own_in.T.astype(jnp.float32), own_out.T.astype(jnp.float32)


def windows(cols, shards):
    starts = [place * cols // 128 for place in range(shards)]
    tiles = max(-(-(place + 1) * cols // 128) - start for place, start in enumerate(starts))
    return starts, tiles


def heavy_segments(width, in_cols, in_starts, out_rows, shards):
    every = []
    for place in range(shards):
        parts = []
        for array, low, high, most in ((3, 6 * width, 9 * width, 960), (1, 9 * width, 13 * width, 832)):
            first, last = max(low, place * in_cols), min(high, (place + 1) * in_cols)
            while first < last:
                rows = min(most, last - first)
                parts.append((0, first - in_starts[place] * 128, array, first - low, rows, 0, 0, width))
                first += rows
            if array == 3:
                parts.append((1, 0, 2, place * out_rows, out_rows, 0, 0, width))
        parts.append((1, 0, 0, place * out_rows, out_rows, width, 0, 4 * width))
        every.append(parts)
    return every


def gather_kernel(
    plan, in_t, out_t, head_t, embed, traits,
    fc2, fc1, attn_out, qkv, cond_full, time_act, time_one, modul, fmod, patch, last, all_traits,
    s1_slot, tab_slot, patch_slot, two_slot, two_own, mod_slot, mod_own, fm_slot, fm_own, last_own,
    ysend, yrecv, xsend, xrecv, zsend, zrecv, csend, crecv, osend, orecv, small_send, small_recv, local_sem,
    trait_slot, trait_own, trait_got, line_slot, trait_send, trait_recv,
):
    segments, (in_starts, in_tiles), (head_starts, head_tiles), (embed_starts, embed_tiles), lines = plan
    shards = len(segments)
    arrays = (fc2, fc1, attn_out, qkv)
    sources = (in_t, out_t)
    rep, shard = lax.axis_index("rep"), lax.axis_index("shard")
    place_here = lax.rem(rep, 2 * lines)
    x, z = lax.rem(place_here, 2), lax.div(place_here, 2)
    zb = lax.rem(z, 2)
    core, y = lax.rem(shard, 2), lax.div(shard, 2)
    to_core = (rep, shard + 1 - 2 * core)
    to_y = (rep, shard + 2 - 4 * y)
    to_x = (rep + 1 - 2 * x, shard)
    to_z = (rep + 2 - 4 * zb, shard)
    width = head_t.shape[1]

    barrier = pltpu.get_barrier_semaphore()
    others = [(rep, lax.rem(shard + step, shards)) for step in range(1, shards)]

    def line_peer(step):
        return (rep - place_here + lax.rem(z + step, lines) * 2 + x, shard)

    for peer in others + [to_x] + [line_peer(step) for step in range(1, lines)]:
        pl.semaphore_signal(barrier, inc=1, device_id=peer, device_id_type=MESH)
    pl.semaphore_wait(barrier, shards + lines - 1)

    def remote(source, target, send_sem, recv_sem, peer):
        return pltpu.make_async_remote_copy(
            src_ref=source, dst_ref=target, send_sem=send_sem, recv_sem=recv_sem, device_id=peer, device_id_type=MESH
        )

    def small(kind, source, slots, step):
        return remote(
            source, slots.at[shard], small_send.at[kind, step - 1], small_recv.at[kind, step - 1], others[step - 1]
        )

    def small_arrival(kind, slots, step):
        origin = lax.rem(shard + shards - step, shards)
        return remote(
            slots.at[origin], slots.at[origin], small_send.at[kind, step - 1], small_recv.at[kind, step - 1], to_core
        )

    def exchange(kind, source, slots, origins=None):
        for step in range(1, shards):
            if origins is None:
                small(kind, source, slots, step).start()
            else:
                sends = functools.reduce(jnp.logical_or, [shard == o for o in origins])

                @pl.when(sends)
                def _():
                    small(kind, source, slots, step).start()

    def arrive(kind, slots, origins=None):
        for step in range(1, shards):
            if origins is None:
                small_arrival(kind, slots, step).wait_recv()
            else:
                origin = lax.rem(shard + shards - step, shards)

                @pl.when(functools.reduce(jnp.logical_or, [origin == o for o in origins]))
                def _():
                    small_arrival(kind, slots, step).wait_recv()

    def sent(kind, source, slots, origins=None):
        for step in range(1, shards):
            if origins is None:
                small(kind, source, slots, step).wait_send()
            else:

                @pl.when(functools.reduce(jnp.logical_or, [shard == o for o in origins]))
                def _():
                    small(kind, source, slots, step).wait_send()

    def place_tiles(target, slots, starts, tiles, origins, dtype, first=0):
        total = target.shape[1] // 128
        for tile in range(total):
            parts = [
                slots[o, :, (tile + first - starts[o]) * 128 : (tile + first - starts[o] + 1) * 128]
                for o in origins
                if 0 <= tile + first - starts[o] < tiles
            ]
            target[:, tile * 128 : (tile + 1) * 128] = functools.reduce(jnp.add, parts).astype(dtype)

    def source_part(place, k):
        source, row, array, _, rows, lane, _, lanes = segments[place][k]
        return sources[source].at[pl.ds(row, rows), pl.ds(lane, lanes)]

    def target_part(place, k, start=0, rows=None):
        _, _, array, row, total, _, lane, lanes = segments[place][k]
        start = row + start
        if not isinstance(start, int):
            start = pl.multiple_of(start, 16)
        return arrays[array].at[pl.ds(start, total if rows is None else rows), pl.ds(lane, lanes)]

    def quarter(place, k, index):
        size = segments[place][k][4] // 4
        return target_part(place, k, index * size, size)

    def half_of(place, k, index, second):
        size = segments[place][k][4] // 4
        cut = -(-size // 32) * 16
        return target_part(place, k, index * size + (cut if second else 0), size - cut if second else cut)

    me = x * 2 + zb
    across_x, along_z, corner = (1 - x) * 2 + zb, x * 2 + 1 - zb, (1 - x) * 2 + 1 - zb

    def y_copy(place, k):
        size = segments[place][k][4] // 4
        source, row, _, _, _, lane, _, lanes = segments[place][k]
        part = sources[source].at[pl.ds(pl.multiple_of(row + me * size, 16), size), pl.ds(lane, lanes)]
        return remote(part, quarter(place, k, me), ysend.at[k], yrecv.at[k], to_y)

    def owner_copy(place, k):
        return remote(source_part(place, k), target_part(place, k), osend.at[k], orecv.at[k], to_core)

    def own_copy(place, k):
        return pltpu.make_async_copy(source_part(place, k), target_part(place, k), local_sem.at[k])

    def hop(part, sems, k, slot, peer):
        return remote(part, part, sems[0].at[k, slot], sems[1].at[k, slot], peer)

    xs, zs, cs = (xsend, xrecv), (zsend, zrecv), (csend, crecv)

    for place in range(shards):

        @pl.when(shard == place)
        def _():
            for k in range(len(segments[place])):
                y_copy(place, k).start()
                owner_copy(place, k).start()
                own_copy(place, k).start()

    def trait_line(step):
        return remote(
            line_slot.at[z], line_slot.at[z], trait_send.at[step], trait_recv.at[step], line_peer(step)
        )

    def trait_line_arrival(step):
        origin = lax.rem(z + lines - step, lines)
        return remote(line_slot.at[origin], line_slot.at[origin], trait_send.at[step], trait_recv.at[step], to_core)

    trait_pair = remote(trait_own, trait_got, trait_send.at[0], trait_recv.at[0], to_x)
    trait_slot[shard] = traits[...]
    exchange(7, traits, trait_slot)
    arrive(7, trait_slot)
    trait_own[...] = functools.reduce(jnp.add, [trait_slot[o] for o in range(shards)])
    trait_pair.start()
    trait_pair.wait_recv()
    own, got = trait_own[...], trait_got[...]
    line_slot[z] = jnp.concatenate([jnp.where(x == 0, own, got), jnp.where(x == 0, got, own)], 0)
    for step in range(1, lines):
        trait_line(step).start()
    for step in range(1, lines):
        trait_line_arrival(step).wait_recv()
    count_in_line = 2 * traits.shape[0]
    for at in range(lines):
        all_traits[at * count_in_line : (at + 1) * count_in_line, :] = line_slot[at]
    freq = all_traits[:, :FREQ].astype(jnp.bfloat16)
    classes = embed.shape[0] - PATCH - FREQ
    named = lax.broadcasted_iota(jnp.int32, (all_traits.shape[0], classes), 1).astype(jnp.float32)
    onehot = jnp.where(named == all_traits[:, FREQ : FREQ + 1], 1.0, 0.0).astype(jnp.bfloat16)

    own_one = jnp.dot(freq, embed[PATCH : PATCH + FREQ, :], preferred_element_type=jnp.float32)
    time_one[...] = own_one
    s1_slot[shard] = (own_one * jax.nn.sigmoid(own_one)).astype(jnp.bfloat16)
    tab_slot[shard] = jnp.dot(onehot, embed[PATCH + FREQ :, :], preferred_element_type=jnp.float32)
    patch_slot[shard] = embed[0:PATCH, :]
    exchange(0, s1_slot.at[shard], s1_slot)
    exchange(1, tab_slot.at[shard], tab_slot)
    exchange(2, patch_slot.at[shard], patch_slot)
    last_place = [o for o in range(shards) if 0 <= 3 * width // 128 - head_starts[o] < head_tiles][-1]
    last_row = (3 * width // 128 - head_starts[last_place]) * 128
    last_own[...] = head_t[last_row : last_row + 16, :]

    @pl.when(shard == last_place)
    def _():
        last[...] = last_own[...]
        for step in range(1, shards):
            remote(last_own, last, small_send.at[6, step - 1], small_recv.at[6, 0], others[step - 1]).start()

    def relay(place, stage, k):
        if stage == 0:
            y_copy(place, k).wait_recv()
            hop(quarter(place, k, me), xs, k, 0, to_x).start()
            hop(quarter(place, k, me), zs, k, 0, to_z).start()
            hop(quarter(place, k, me), cs, k, 0, to_core).start()
        elif stage == 1:
            hop(quarter(place, k, across_x), xs, k, 0, to_x).wait_recv()
            hop(half_of(place, k, across_x, False), zs, k, 1, to_z).start()
            hop(quarter(place, k, along_z), zs, k, 0, to_z).wait_recv()
            hop(half_of(place, k, along_z, True), xs, k, 1, to_x).start()
            hop(quarter(place, k, across_x), cs, k, 1, to_core).start()
            hop(quarter(place, k, along_z), cs, k, 2, to_core).start()
        else:
            hop(half_of(place, k, corner, False), zs, k, 1, to_z).wait_recv()
            hop(half_of(place, k, corner, True), xs, k, 1, to_x).wait_recv()
            hop(quarter(place, k, corner), cs, k, 3, to_core).start()

    def relay_tick(tick):
        for place in range(shards):

            @pl.when(to_y[1] == place)
            def _():
                for stage in range(3):
                    if 0 <= tick - stage < len(segments[place]):
                        relay(place, stage, tick - stage)

    ticks = max(len(parts) for parts in segments) + 2
    head_places = [o for o in range(shards) if head_starts[o] * 128 < width]
    fm_places = [o for o in range(shards) if (head_starts[o] + head_tiles) * 128 > width]
    mod_places = [o for o in range(shards) if in_starts[o] * 128 < 6 * width]
    nt = (((1,), (1,)), ((), ()))
    group = modul.shape[0]

    arrive(0, s1_slot)
    place_tiles(time_act, s1_slot, embed_starts, embed_tiles, range(shards), jnp.bfloat16)
    two_own[...] = lax.dot_general(time_act[...], head_t[...], nt, preferred_element_type=jnp.float32)
    two_slot[shard] = two_own[...]
    exchange(3, two_own, two_slot, head_places)
    relay_tick(0)
    arrive(1, tab_slot)
    arrive(3, two_slot, head_places)
    place_tiles(cond_full, tab_slot, embed_starts, embed_tiles, range(shards), jnp.float32)
    for tile in range(width // 128):
        span = slice(tile * 128, (tile + 1) * 128)
        for o in head_places:
            if 0 <= tile - head_starts[o] < head_tiles:
                cond_full[:, span] += two_slot[o, :, (tile - head_starts[o]) * 128 : (tile - head_starts[o] + 1) * 128]
    mine = cond_full[pl.ds(pl.multiple_of(place_here * group, 8), group), :]
    cond = (mine * jax.nn.sigmoid(mine)).astype(jnp.bfloat16)
    mod_own[...] = lax.dot_general(cond, in_t[...], nt, preferred_element_type=jnp.float32)
    mod_slot[shard] = mod_own[...]
    exchange(4, mod_own, mod_slot, mod_places)
    fm_own[...] = lax.dot_general(cond, head_t[...], nt, preferred_element_type=jnp.float32)
    fm_slot[shard] = fm_own[...]
    exchange(5, fm_own, fm_slot, fm_places)
    relay_tick(1)
    arrive(2, patch_slot)
    place_tiles(patch, patch_slot, embed_starts, embed_tiles, range(shards), jnp.bfloat16)
    arrive(4, mod_slot, mod_places)
    arrive(5, fm_slot, fm_places)
    place_tiles(modul, mod_slot, in_starts, in_tiles, mod_places, jnp.float32)
    place_tiles(fmod, fm_slot, head_starts, head_tiles, fm_places, jnp.float32, width // 128)
    for tick in range(2, ticks):
        relay_tick(tick)

    for place in range(shards):
        count = len(segments[place])

        @pl.when(shard == place)
        def _():
            for k in range(count):
                y_copy(place, k).wait_send()
                owner_copy(place, k).wait_send()
                own_copy(place, k).wait()

        @pl.when(to_core[1] == place)
        def _():
            for k in range(count):
                remote(target_part(place, k), target_part(place, k), osend.at[k], orecv.at[k], to_core).wait_recv()

        @pl.when(to_y[1] == place)
        def _():
            for k in range(count):
                hop(quarter(place, k, me), xs, k, 0, to_x).wait_send()
                hop(quarter(place, k, me), zs, k, 0, to_z).wait_send()
                hop(half_of(place, k, across_x, False), zs, k, 1, to_z).wait_send()
                hop(half_of(place, k, along_z, True), xs, k, 1, to_x).wait_send()
                for slot, index in enumerate((me, across_x, along_z, corner)):
                    hop(quarter(place, k, index), cs, k, slot, to_core).wait_send()

        @pl.when(shards - 1 - shard == place)
        def _():
            for k in range(count):
                for slot, index in enumerate((me, across_x, along_z, corner)):
                    remote(
                        quarter(place, k, index), quarter(place, k, index), csend.at[k, slot], crecv.at[k, slot], to_core
                    ).wait_recv()

    trait_pair.wait_send()
    for step in range(1, lines):
        trait_line(step).wait_send()
    sent(7, traits, trait_slot)
    sent(0, s1_slot.at[shard], s1_slot)
    sent(1, tab_slot.at[shard], tab_slot)
    sent(2, patch_slot.at[shard], patch_slot)
    sent(3, two_own, two_slot, head_places)
    sent(4, mod_own, mod_slot, mod_places)
    sent(5, fm_own, fm_slot, fm_places)

    @pl.when(shard == last_place)
    def _():
        for step in range(1, shards):
            remote(last_own, last, small_send.at[6, step - 1], small_recv.at[6, 0], others[step - 1]).wait_send()

    @pl.when(shard != last_place)
    def _():
        remote(last_own, last, small_send.at[6, 0], small_recv.at[6, 0], to_core).wait_recv()


def gather_call(in_low, out_low, head_low, embed_low, traits, shards, lines):
    place = lax.axis_index("shard")
    width = head_low.shape[0]
    low, full = jnp.bfloat16, jnp.float32

    def window(item_t, starts, tiles, cols):
        offsets = jnp.asarray([o * cols - start * 128 for o, start in enumerate(starts)], jnp.int32)
        target = jnp.zeros((tiles * 128, item_t.shape[1]), item_t.dtype)
        return lax.dynamic_update_slice_in_dim(target, item_t, offsets[place], 0)

    in_cols, head_cols, embed_cols = in_low.shape[1], head_low.shape[1], embed_low.shape[1]
    in_starts, in_tiles = windows(in_cols, shards)
    head_starts, head_tiles = windows(head_cols, shards)
    embed_starts, embed_tiles = windows(embed_cols, shards)
    in_t = window(in_low.T, in_starts, in_tiles, in_cols)
    head_t = window(head_low.T, head_starts, head_tiles, head_cols)
    embed = window(embed_low.T, embed_starts, embed_tiles, embed_cols).T
    segments = heavy_segments(width, in_cols, in_starts, out_low.shape[1], shards)
    plan = (segments, (in_starts, in_tiles), (head_starts, head_tiles), (embed_starts, embed_tiles), lines)
    group = traits.shape[0]
    rows = 2 * lines * group
    most = max(len(parts) for parts in segments)
    shapes = [
        ((width, 4 * width), low),
        ((4 * width, width), low),
        ((width, width), low),
        ((3 * width, width), low),
        ((rows, width), full),
        ((rows, width), low),
        ((rows, embed_tiles * 128), full),
        ((group, 6 * width), full),
        ((group, 2 * width), full),
        ((PATCH, width), low),
        ((PATCH, width), low),
        ((rows, traits.shape[1]), full),
    ]
    scratch = [
        ((shards, rows, embed_tiles * 128), low),
        ((shards, rows, embed_tiles * 128), full),
        ((shards, PATCH, embed_tiles * 128), low),
        ((shards, rows, head_tiles * 128), full),
        ((rows, head_tiles * 128), full),
        ((shards, group, in_tiles * 128), full),
        ((group, in_tiles * 128), full),
        ((shards, group, head_tiles * 128), full),
        ((group, head_tiles * 128), full),
        ((PATCH, width), low),
    ]
    dma = pltpu.SemaphoreType.DMA
    outs = pl.pallas_call(
        functools.partial(gather_kernel, plan),
        out_shape=[jax.ShapeDtypeStruct(*item) for item in shapes],
        in_specs=[pl.BlockSpec(memory_space=pltpu.VMEM)] * 5,
        out_specs=[pl.BlockSpec(memory_space=pltpu.VMEM)] * len(shapes),
        scratch_shapes=[pltpu.VMEM(*item) for item in scratch]
        + [dma((most,)), dma((most,))]
        + [dma((most, 2))] * 4
        + [dma((most, 4))] * 2
        + [dma((most,)), dma((most,)), dma((8, shards - 1)), dma((8, shards - 1)), dma((most,))]
        + [
            pltpu.VMEM((shards,) + traits.shape, full),
            pltpu.VMEM(traits.shape, full),
            pltpu.VMEM(traits.shape, full),
            pltpu.VMEM((lines, 2 * group, traits.shape[1]), full),
            dma((lines,)),
            dma((lines,)),
        ],
        compiler_params=pltpu.CompilerParams(
            collective_id=2, has_side_effects=True, vmem_limit_bytes=60 * 1024 * 1024
        ),
    )(in_t, out_low.T, head_t, embed, traits)
    return in_t, head_t, outs


NN = (((1,), (0,)), ((), ()))
NT = (((1,), (1,)), ((), ()))
TN = (((0,), (0,)), ((), ()))


def mxu(left, right, kind):
    return lax.dot_general(left, right, kind, preferred_element_type=jnp.float32)


def blocks_of(total, size, body):
    def step(index, carry):
        body(pl.ds(pl.multiple_of(index * size, size), size))
        return carry

    lax.fori_loop(0, total // size, step, 0)


def pass_kernel(
    images, state, target, weight_t, pos, patch, last, modul, fmod, fc2, fc1, attn_out, qkv,
    g_fc2, g_fc1, g_o, g_qkv, few, d_mod, d_fm,
    stream, hat_one, hat_two, root_one, root_two, a_low, qkv_low, mixed, proj, b_low, upper, active, mlp, back, d_qkv,
):
    width = patch.shape[1]
    tokens = images * TOK
    low = jnp.bfloat16
    shard = lax.axis_index("shard")
    row = [shard * images + image for image in range(images)]
    span = [pl.ds(image * TOK, TOK) for image in range(images)]
    cut = 256

    def piece(ref, image, index):
        return ref[pl.ds(row[image], 1), pl.ds(index * width, width)]

    def normed(value):
        center = value - jnp.mean(value, -1, keepdims=True)
        root = lax.rsqrt(jnp.mean(center * center, -1, keepdims=True) + eps_norm)
        return center * root, root

    def norm_back(d_hat, hat, root):
        return root * (d_hat - jnp.mean(d_hat, -1, keepdims=True) - hat * jnp.mean(d_hat * hat, -1, keepdims=True))

    def put_row(ref, image, index, value):
        ref[pl.ds(row[image], 1), pl.ds(index * width, width)] = (
            jnp.sum(value, 0, keepdims=True).astype(low).astype(jnp.float32)
        )

    d_mod[...] = jnp.zeros_like(d_mod)
    d_fm[...] = jnp.zeros_like(d_fm)

    for image in range(images):
        value = mxu(state[span[image], :], patch[...], NN) + pos[...]
        stream[span[image], :] = value
        hat, root = normed(value)
        hat_one[span[image], :] = hat
        root_one[span[image], :] = root
        a_low[span[image], :] = (hat * (1.0 + piece(modul, image, 1)) + piece(modul, image, 0)).astype(low)

    def qkv_block(part):
        qkv_low[:, part] = mxu(a_low[...], qkv[part, :], NT).astype(low)

    blocks_of(3 * width, cut, qkv_block)
    lane = lax.broadcasted_iota(jnp.int32, (TOK, 128), 1)
    first = lane < 64
    scale = 0.125

    def softmax(query, key):
        score = mxu(query, key, NT) * scale
        expo = jnp.exp(score - jnp.max(score, -1, keepdims=True))
        return expo / jnp.sum(expo, -1, keepdims=True)

    def take(ref, image, start):
        return ref[span[image], pl.ds(pl.multiple_of(start, 128), 128)]

    def attend(pair, carry):
        for image in range(images):
            query, key, value = (take(qkv_low, image, index * width + pair * 128) for index in range(3))
            outs = []
            for side in (first, jnp.logical_not(first)):
                probs = softmax(jnp.where(side, query, jnp.zeros_like(query)), key)
                outs.append(mxu(probs.astype(low), value, NN))
            mixed[span[image], pl.ds(pl.multiple_of(pair * 128, 128), 128)] = jnp.where(first, outs[0], outs[1]).astype(low)
        return carry

    lax.fori_loop(0, width // 128, attend, 0)
    for image in range(images):
        got = mxu(mixed[span[image], :], attn_out[...], NT)
        proj[span[image], :] = got
        value = stream[span[image], :] + piece(modul, image, 2) * got
        stream[span[image], :] = value
        hat, root = normed(value)
        hat_two[span[image], :] = hat
        root_two[span[image], :] = root
        b_low[span[image], :] = (hat * (1.0 + piece(modul, image, 4)) + piece(modul, image, 3)).astype(low)

    def upper_block(part):
        value = mxu(b_low[...], fc1[part, :], NT)
        upper[:, part] = value
        active[:, part] = (
            0.5 * value * (1.0 + jnp.tanh(0.7978845608 * (value + 0.044715 * value * value * value)))
        ).astype(low)

    blocks_of(4 * width, cut, upper_block)

    def mlp_block(part):
        mlp[:, part] = mxu(active[...], fc2[part, :], NT)

    blocks_of(width, cut, mlp_block)
    loss = jnp.zeros((), jnp.float32)
    g_last = jnp.zeros((PATCH, width), jnp.float32)
    for image in range(images):
        value = stream[span[image], :] + piece(modul, image, 5) * mlp[span[image], :]
        hat, root = normed(value)
        gain = 1.0 + piece(fmod, image, 1)
        final = (hat * gain + piece(fmod, image, 0)).astype(low)
        diff = mxu(final, last[...], NT) - target[span[image], :]
        share = weight_t[span[image], :] * diff
        loss += 0.5 * jnp.sum(share * diff)
        d_out = share.astype(low)
        g_last += mxu(d_out, final, TN)
        d_final = mxu(d_out, last[...], NN)
        put_row(d_fm, image, 0, d_final)
        put_row(d_fm, image, 1, d_final * hat)
        d_value = norm_back(d_final * gain, hat, root)
        back[span[image], :] = d_value
        put_row(d_mod, image, 5, d_value * mlp[span[image], :])
        d_qkv[span[image], pl.ds(0, width)] = (piece(modul, image, 5) * d_value).astype(low)
    few[pl.ds(PATCH, PATCH), :] = g_last
    few[pl.ds(2 * PATCH, 8), :] = jnp.full((8, width), loss, jnp.float32)

    d_mlp = d_qkv.at[:, pl.ds(0, width)]

    def fc2_block(part):
        g_fc2[:, part] = mxu(d_mlp[...], active[:, part], TN).astype(low)
        value = upper[:, part]
        inner = jnp.tanh(0.7978845608 * (value + 0.044715 * value * value * value))
        slope = 0.5 * (1.0 + inner) + 0.5 * value * (1.0 - inner * inner) * 0.7978845608 * (
            1.0 + 3.0 * 0.044715 * value * value
        )
        active[:, part] = (slope * mxu(d_mlp[...], fc2[:, part], NN)).astype(low)

    blocks_of(4 * width, cut, fc2_block)

    def fc1_block(part):
        g_fc1[part, :] = mxu(active[:, part], b_low[...], TN).astype(low)

    blocks_of(4 * width, cut, fc1_block)
    for image in range(images):
        d_normed = mxu(active[span[image], :], fc1[...], NN)
        hat = hat_two[span[image], :]
        put_row(d_mod, image, 3, d_normed)
        put_row(d_mod, image, 4, d_normed * hat)
        d_value = back[span[image], :] + norm_back(
            d_normed * (1.0 + piece(modul, image, 4)), hat, root_two[span[image], :]
        )
        back[span[image], :] = d_value
        put_row(d_mod, image, 2, d_value * proj[span[image], :])
        b_low[span[image], :] = (piece(modul, image, 2) * d_value).astype(low)

    def o_block(part):
        g_o[part, :] = mxu(b_low[:, part], mixed[...], TN).astype(low)

    blocks_of(width, cut, o_block)
    d_mixed = active.at[:, pl.ds(0, width)]
    d_mixed[...] = mxu(b_low[...], attn_out[...], NN).astype(low)

    def attend_back(pair, carry):
        for image in range(images):
            query, key, value = (take(qkv_low, image, index * width + pair * 128) for index in range(3))
            d_out = take(active, image, pair * 128)
            d_query, d_key, d_value = [], [], []
            for side in (first, jnp.logical_not(first)):
                none = jnp.zeros_like(query)
                probs = softmax(jnp.where(side, query, none), key)
                d_prob = mxu(jnp.where(side, d_out, none), value, NT)
                d_score = (probs * (d_prob - jnp.sum(probs * d_prob, -1, keepdims=True))).astype(low)
                d_value.append(mxu(probs.astype(low), d_out, TN))
                d_query.append(mxu(d_score, key, NN) * scale)
                d_key.append(mxu(d_score, query, TN) * scale)
            for index, both in enumerate((d_query, d_key, d_value)):
                d_qkv[span[image], pl.ds(pl.multiple_of(index * width + pair * 128, 128), 128)] = jnp.where(
                    first, both[0], both[1]
                ).astype(low)
        return carry

    lax.fori_loop(0, width // 128, attend_back, 0)

    def g_qkv_block(part):
        g_qkv[part, :] = mxu(d_qkv[:, part], a_low[...], TN).astype(low)

    blocks_of(3 * width, cut, g_qkv_block)
    g_patch = jnp.zeros((PATCH, width), jnp.float32)
    for image in range(images):
        d_normed = mxu(d_qkv[span[image], :], qkv[...], NN)
        hat = hat_one[span[image], :]
        put_row(d_mod, image, 0, d_normed)
        put_row(d_mod, image, 1, d_normed * hat)
        d_value = back[span[image], :] + norm_back(
            d_normed * (1.0 + piece(modul, image, 1)), hat, root_one[span[image], :]
        )
        g_patch += mxu(state[span[image], :], d_value.astype(low), TN)
    few[pl.ds(0, PATCH), :] = g_patch


def pass_scratch(tokens, width):
    low, full = jnp.bfloat16, jnp.float32
    return [
        ((tokens, width), full),
        ((tokens, width), full),
        ((tokens, width), full),
        ((tokens, 1), full),
        ((tokens, 1), full),
        ((tokens, width), low),
        ((tokens, 3 * width), low),
        ((tokens, width), low),
        ((tokens, width), full),
        ((tokens, width), low),
        ((tokens, 4 * width), full),
        ((tokens, 4 * width), low),
        ((tokens, width), full),
        ((tokens, width), full),
        ((tokens, 3 * width), low),
    ]


def pass_call(images, state, target, weight_t, pos, patch, last, modul, fmod, heavy):
    width = patch.shape[1]
    low, full = jnp.bfloat16, jnp.float32
    shapes = [(item.shape, low) for item in heavy] + [
        ((2 * PATCH + 8, width), full),
        (modul.shape, full),
        (fmod.shape, full),
    ]
    return pl.pallas_call(
        functools.partial(pass_kernel, images),
        out_shape=[jax.ShapeDtypeStruct(*item) for item in shapes],
        in_specs=[pl.BlockSpec(memory_space=pltpu.VMEM)] * 12,
        out_specs=[pl.BlockSpec(memory_space=pltpu.VMEM)] * len(shapes),
        scratch_shapes=[pltpu.VMEM(*item) for item in pass_scratch(state.shape[0], width)],
        compiler_params=pltpu.CompilerParams(vmem_limit_bytes=63 * 1024 * 1024),
    )(state, target, weight_t, pos, patch, last, modul, fmod, *heavy)


def exchange_kernel(shards, own, total, slots, send, recv):
    rep, shard = lax.axis_index("rep"), lax.axis_index("shard")
    barrier = pltpu.get_barrier_semaphore()
    for step in range(1, shards):
        peer = (rep, lax.rem(shard + step, shards))
        pl.semaphore_signal(barrier, inc=1, device_id=peer, device_id_type=MESH)
    pl.semaphore_wait(barrier, shards - 1)

    def copy(step):
        return pltpu.make_async_remote_copy(
            src_ref=own,
            dst_ref=slots.at[shard],
            send_sem=send.at[step - 1],
            recv_sem=recv.at[step - 1],
            device_id=(rep, lax.rem(shard + step, shards)),
            device_id_type=MESH,
        )

    for step in range(1, shards):
        copy(step).start()
    slots[shard] = own[...]
    for step in range(1, shards):
        copy(step).wait()
    total[...] = functools.reduce(jnp.add, [slots[o] for o in range(shards)])


def sum_in_group(tree, shards):
    leaves, kind = jax.tree.flatten(tree)
    flat = jnp.concatenate([leaf.reshape(-1) for leaf in leaves])
    rows = -(-flat.shape[0] // 1024) * 8
    block = jnp.pad(flat, (0, rows * 128 - flat.shape[0])).reshape(rows, 128)
    total = pl.pallas_call(
        functools.partial(exchange_kernel, shards),
        out_shape=jax.ShapeDtypeStruct(block.shape, jnp.float32),
        in_specs=[pl.BlockSpec(memory_space=pltpu.VMEM)],
        out_specs=pl.BlockSpec(memory_space=pltpu.VMEM),
        scratch_shapes=[
            pltpu.VMEM((shards,) + block.shape, jnp.float32),
            pltpu.SemaphoreType.DMA((shards - 1,)),
            pltpu.SemaphoreType.DMA((shards - 1,)),
        ],
        compiler_params=pltpu.CompilerParams(collective_id=3, has_side_effects=True),
    )(block).reshape(-1)
    parts, first = [], 0
    for leaf in leaves:
        parts.append(total[first : first + leaf.size].reshape(leaf.shape))
        first += leaf.size
    return jax.tree.unflatten(kind, parts)


def on_device(
    latents,
    noises,
    velocity,
    times,
    labels,
    dropped,
    blocks_in,
    blocks_out,
    head_side,
    embed_side,
    state_in_row,
    state_in_col,
    state_out_row,
    state_out_col,
    state_head_row,
    state_head_col,
    state_embed_row,
    state_embed_col,
):
    images = latents.shape[0]
    width = head_side.shape[0]
    shard_count = lax.axis_size("shard")
    place = lax.axis_index("shard")
    in_cols = blocks_in.shape[2]
    out_cols = blocks_out.shape[2]
    head_cols = head_side.shape[1]
    embed_cols = embed_side.shape[1]
    group = images * shard_count
    in_low = blocks_in[0].astype(jnp.bfloat16)
    out_low = blocks_out[0].astype(jnp.bfloat16)
    head_low = head_side.astype(jnp.bfloat16)
    embed_low = embed_side.astype(jnp.bfloat16)
    t_value = (times.astype(jnp.float32) + 1.0) / step_count
    classes = jnp.where(dropped == 1, CLASSES - 1, labels).astype(jnp.float32)
    lines = LINE
    traits = jnp.zeros((group, FREQ + 128), jnp.float32)
    traits = lax.dynamic_update_slice(
        traits,
        jnp.concatenate([time_freq(t_value, FREQ), jnp.broadcast_to(classes[:, None], (images, 128))], 1),
        (place * images, 0),
    )
    in_t, head_win_t, gathered = gather_call(in_low, out_low, head_low, embed_low, traits, shard_count, lines)
    fc2_t, fc1_t, o_t, qkv_t, cond_full, time_act, time_one, modul, final_mod, patch_w, head_t, all_traits = gathered
    freq_low = all_traits[:, :FREQ].astype(jnp.bfloat16)
    onehot = all_traits[:, FREQ : FREQ + 1] == jnp.arange(CLASSES, dtype=jnp.float32)[None, :]
    cond = silu(cond_full).astype(jnp.bfloat16)
    tcol = t_value[:, None, None]
    state = (
        (1.0 - tcol) * latents.reshape(images, TOK, PATCH)
        + tcol * noises.reshape(images, TOK, PATCH)
    ).astype(jnp.bfloat16)
    *heavy, few, d_mod, d_fm = pass_call(
        images,
        state.reshape(images * TOK, PATCH),
        velocity.reshape(images * TOK, PATCH),
        jnp.repeat(t_value, TOK)[:, None],
        positions(GRID, width),
        patch_w,
        head_t,
        modul,
        final_mod,
        [fc2_t, fc1_t, o_t, qkv_t],
    )
    tables = (
        windows(in_cols, shard_count),
        windows(head_cols, shard_count),
        windows(embed_cols, shard_count),
        shard_count,
    )
    sums = reduce_call(
        lines,
        tables,
        heavy,
        [d_mod, d_fm, few, in_t, head_win_t, cond_full, time_one],
    )
    heavy_in, heavy_out = own_heavy(sums[:4], in_cols, out_cols)
    d_in, d_fin, d_two, d_full, d_one, few_sum = sums[4:]

    def own_columns(item, cols):
        return lax.dynamic_slice_in_dim(item, lax.rem(place * cols, 128), cols, 1)

    loss_sum = few_sum[2 * PATCH, 0]
    d_full_own = lax.dynamic_slice_in_dim(d_full, place * embed_cols, embed_cols, 1)
    g_table = lax.dot_general(
        onehot.astype(jnp.float32),
        d_full_own,
        (((0,), (0,)), ((), ())),
        precision=lax.Precision.HIGHEST,
    )
    own_patch = lax.dynamic_slice_in_dim(few_sum[:PATCH], place * embed_cols, embed_cols, 1)
    own_head = jnp.pad(few_sum[PATCH : 2 * PATCH].T, ((0, 0), (3 * width, 0)))
    own_head = lax.dynamic_slice_in_dim(own_head, place * head_cols, head_cols, 1)
    totals = (
        (own_columns(weight_grad(cond, d_in), in_cols) + heavy_in)[None],
        heavy_out[None],
        own_columns(weight_grad(time_act, d_two) + weight_grad(cond, d_fin), head_cols) + own_head,
        jnp.concatenate([own_patch, own_columns(weight_grad(freq_low, d_one), embed_cols), g_table], 0),
    )
    blocks = lax.axis_size("rep") // (2 * lines)
    if blocks > 1:
        apart = [[k * 2 * lines + j for k in range(blocks)] for j in range(2 * lines)]
        totals, loss_sum = lax.psum((totals, loss_sum), "rep", axis_index_groups=apart)
    weights = (blocks_in, blocks_out, head_side, embed_side)
    rows_old = (state_in_row, state_out_row, state_head_row, state_embed_row)
    cols_old = (state_in_col, state_out_col, state_head_col, state_embed_col)
    cols_new = [
        decay * col_state + (1.0 - decay) * (jnp.mean(gradient * gradient, -2) + eps_one)
        for gradient, col_state in zip(totals, cols_old)
    ]
    row_parts = [jnp.sum(gradient * gradient, -1) for gradient in totals]
    row_scaled = [
        jnp.sum(gradient * gradient / col_next[..., None, :], -1)
        for gradient, col_next in zip(totals, cols_new)
    ]
    weight_sq = [jnp.sum(weight * weight, axis=(-2, -1)) for weight in weights]
    row_sums, row_scaled, weight_sq = sum_in_group((row_parts, row_scaled, weight_sq), shard_count)
    rows_new = [
        decay * row_state
        + (1.0 - decay) * (row_sum / (gradient.shape[-1] * shard_count) + eps_one)
        for row_sum, gradient, row_state in zip(row_sums, totals, rows_old)
    ]
    row_means = [jnp.mean(row_next, -1) for row_next in rows_new]
    total_sq = sum(
        jnp.sum(row_mean * jnp.sum(scaled / row_next, -1))
        for scaled, row_next, row_mean in zip(row_scaled, rows_new, row_means)
    )
    count = sum((weight.size for weight in weights)) * shard_count
    update_rms = jnp.sqrt(total_sq / count)
    factor = jnp.maximum(1.0, update_rms / clip_level)
    news = []
    for index in range(4):
        numel = weights[index].shape[-2] * weights[index].shape[-1] * shard_count
        weight_rms = jnp.sqrt(weight_sq[index] / numel)
        step_size = rate * jnp.maximum(eps_two, weight_rms) / factor
        row_scale = jnp.asarray(step_size)[..., None] * lax.rsqrt(
            rows_new[index] / row_means[index][..., None]
        )
        news.append(
            weights[index]
            - totals[index] * row_scale[..., :, None] * lax.rsqrt(cols_new[index])[..., None, :]
        )
    return (
        loss_sum,
        update_rms,
        totals[0],
        totals[1],
        totals[2],
        totals[3],
        rows_new[0],
        cols_new[0],
        rows_new[1],
        cols_new[1],
        rows_new[2],
        cols_new[2],
        rows_new[3],
        cols_new[3],
        news[0],
        news[1],
        news[2],
        news[3],
    )


def solution(mesh):
    placed = (
        P(("rep", "shard"), None),
        P(("rep", "shard"), None),
        P(("rep", "shard"), None),
        P(("rep", "shard")),
        P(("rep", "shard")),
        P(("rep", "shard")),
        P(None, None, "shard"),
        P(None, None, "shard"),
        P(None, "shard"),
        P(None, "shard"),
        P(),
        P(None, "shard"),
        P(),
        P(None, "shard"),
        P(),
        P("shard"),
        P(),
        P("shard"),
    )
    return jax.shard_map(
        on_device,
        mesh=mesh,
        in_specs=placed,
        out_specs=(
            P(),
            P(),
            P(None, None, "shard"),
            P(None, None, "shard"),
            P(None, "shard"),
            P(None, "shard"),
            P(),
            P(None, "shard"),
            P(),
            P(None, "shard"),
            P(),
            P("shard"),
            P(),
            P("shard"),
            P(None, None, "shard"),
            P(None, None, "shard"),
            P(None, "shard"),
            P(None, "shard"),
        ),
        check_vma=False,
    )
```

```python
import functools
import math

import jax
import jax.numpy as jnp
from jax import lax
from jax.experimental import pallas as pl
from jax.experimental.pallas import tpu as pltpu
from jax.sharding import PartitionSpec as P

HEADS = 12
CLASSES = 1001
FREQ = 256
GRID = 16
PATCH = 16
LAYERS = 1
TOK = 256


decay = 0.5
eps_norm = 1e-06
eps_one = 1e-30
eps_two = 0.001
clip_level = 0.1
rate = 8.0
step_count = 1000.0


def silu(value):
    return value * jax.nn.sigmoid(value)


def positions(grid, width):
    quarter = width // 4
    omega = 1.0 / 10000.0 ** (jnp.arange(quarter, dtype=jnp.float32) / quarter)
    index = jnp.arange(grid * grid, dtype=jnp.int32)
    row_pos = (index // grid).astype(jnp.float32)[:, None] * omega[None, :]
    col_pos = (index % grid).astype(jnp.float32)[:, None] * omega[None, :]
    return jnp.concatenate(
        [jnp.sin(row_pos), jnp.cos(row_pos), jnp.sin(col_pos), jnp.cos(col_pos)], 1
    )


def time_freq(t_value, width):
    half = width // 2
    freqs = jnp.exp(-math.log(10000.0) * jnp.arange(half, dtype=jnp.float32) / half)
    angles = (t_value * step_count)[:, None] * freqs[None, :]
    return jnp.concatenate([jnp.cos(angles), jnp.sin(angles)], -1)


def weight_grad(left, back):
    flat_left = left.reshape(-1, left.shape[-1])
    flat_back = back.reshape(-1, back.shape[-1])
    return lax.dot_general(
        flat_left, flat_back, (((0,), (0,)), ((), ())), preferred_element_type=jnp.float32
    )


MESH = pl.DeviceIdType.MESH
LINE = 4
PIECES = 4


def heavy_chunks(width):
    half, third = width // 2, width // 3
    parts = [(0, 0, width, 2 * third * k, third, False) for k in range(6)]
    parts += [(1, 2 * third * k, 2 * third, 0, half, True) for k in range(6)]
    parts += [(2, 0, width, 0, half, False), (3, 0, width, 0, half, False)]
    parts += [(3, width + 2 * third * k, 2 * third, 0, half, True) for k in range(3)]
    return tuple(parts)


def add_rows(target, left, right, rows):
    block = 16

    def body(index, carry):
        span = pl.ds(pl.multiple_of(index * block, block), block)
        target[span] = left[span] + right[span]
        return carry

    lax.fori_loop(0, rows // block, body, 0)


def reduce_kernel(lines, chunks, tables, *refs):
    count = len(chunks)
    grads, refs = refs[:4], refs[4:]
    (d_mod, d_fm, few, in_t, head_t, cond_full, time_one), refs = refs[:7], refs[7:]
    finals, refs = refs[:4], refs[4:]
    (d_in, d_head, d_two, d_full, d_one, few_sum), scratch = refs[:6], refs[6:]
    by_core, by_y, by_x, by_z = (scratch[k * count : (k + 1) * count] for k in range(4))
    send, recv, zsend, zrecv, wsend, wrecv = scratch[4 * count : 4 * count + 6]
    (
        few_got, few_y, few_x, few_held, few_line, mod_got, fm_got, mod_sum, fm_sum, group_slot, part_own, part_slot,
        act_own, act_slot, pair_own, pair_got, line_in, line_rest, line_full,
        few_send, few_recv, group_send, group_recv, line_send, line_recv,
    ) = scratch[4 * count + 6 :]
    (in_starts, in_tiles), (head_starts, head_tiles), (embed_starts, embed_tiles), shards = tables
    rep, shard = lax.axis_index("rep"), lax.axis_index("shard")
    place_here = lax.rem(rep, 2 * lines)
    base = rep - place_here
    x, z = lax.rem(place_here, 2), lax.div(place_here, 2)
    core, y = lax.rem(shard, 2), lax.div(shard, 2)
    to_core = (rep, shard + 1 - 2 * core)
    to_y = (rep, shard + 2 - 4 * y)
    to_x = (rep + 1 - 2 * x, shard)

    def line_peer(step):
        return (base + lax.rem(z + step, lines) * 2 + x, shard)

    barrier = pltpu.get_barrier_semaphore()
    to_far = (rep, shards - 1 - shard)
    for peer in (to_core, to_y, to_x, to_far):
        pl.semaphore_signal(barrier, inc=1, device_id=peer, device_id_type=MESH)
    for step in range(1, lines):
        pl.semaphore_signal(
            barrier, inc=1, device_id=line_peer(step), device_id_type=MESH
        )
    pl.semaphore_wait(barrier, 4 + lines - 1)

    stride = lines // PIECES
    owns = lax.rem(z, stride) == 0
    mine = lax.div(z, stride)
    sends = []

    def remote(source, target, send_sem, recv_sem, peer):
        return pltpu.make_async_remote_copy(
            src_ref=source,
            dst_ref=target,
            send_sem=send_sem,
            recv_sem=recv_sem,
            device_id=peer,
            device_id_type=MESH,
        )

    def rows_of(ref, start, size):
        return ref.at[pl.ds(pl.multiple_of(start, 16), size)]

    def lanes_at(index, ref, row, rows, which):
        _, _, _, lane, lanes, _ = chunks[index]
        return ref.at[
            pl.ds(pl.multiple_of(row, 16), rows), pl.ds(pl.multiple_of(lane + which * lanes, 128), lanes)
        ]

    def core_copy(i):
        array, row, rows = chunks[i][:3]
        return remote(
            lanes_at(i, grads[array], row, rows, 1 - core), by_core[i], send.at[i, 0], recv.at[i, 0], to_core
        )

    def y_copy(i):
        half = chunks[i][2] // 2
        return remote(
            rows_of(by_core[i], (1 - y) * half, half), by_y[i], send.at[i, 1], recv.at[i, 1], to_y
        )

    def x_copy(i):
        quarter = chunks[i][2] // 4
        return remote(
            rows_of(by_y[i], (1 - x) * quarter, quarter), by_x[i], send.at[i, 2], recv.at[i, 2], to_x
        )

    def z_copy(i, piece):
        size = chunks[i][2] // 4 // PIECES
        owner = piece * stride
        slot = lax.rem(z - owner - 1 + lines, lines)
        return remote(
            by_x[i].at[pl.ds(piece * size, size)],
            by_z[i].at[slot],
            zsend.at[i, piece],
            zrecv.at[i, slot],
            (base + owner * 2 + x, shard),
        )

    def final_rows(i, side, start, size, which):
        array, row, rows = chunks[i][:3]
        return lanes_at(i, finals[array], row + side * (rows // 2) + start, size, which)

    def cross_copy(i):
        size = chunks[i][2] // 4 // PIECES
        part = final_rows(i, 0, (x * PIECES + mine) * size, size, core)
        return remote(part, part, send.at[i, 3], recv.at[i, 3], to_y)

    def line_copy(i, which, side, step):
        size = chunks[i][2] // 4 // PIECES
        part = final_rows(i, side, (x * PIECES + mine) * size, size, core)
        return remote(
            part, part, wsend.at[i, which, step - 1], wrecv.at[i, which, mine], line_peer(step)
        )

    def line_arrival(i, which, side, piece):
        size = chunks[i][2] // 4 // PIECES
        part = final_rows(i, side, (x * PIECES + piece) * size, size, core)
        return remote(part, part, wsend.at[i, which, 0], wrecv.at[i, which, piece], to_core)

    def pair_copy(i, which, side, column):
        quarter = chunks[i][2] // 4
        part = final_rows(i, side, column * quarter, quarter, core)
        return remote(part, part, send.at[i, 4 + which], recv.at[i, 4 + which], to_x)

    def last_copy(i, which, side, half):
        rows = chunks[i][2] // 2
        part = final_rows(i, side, 0, rows, half)
        return remote(part, part, send.at[i, 6 + which], recv.at[i, 6 + which], to_core)

    def sides(i, action):
        if chunks[i][5]:

            @pl.when(y == 1)
            def _():
                action(0, 1)
                action(1, 0)

        else:
            action(0, y)

    def stage0(i):
        core_copy(i).start()

    def stage1(i):
        array, row, rows = chunks[i][:3]
        core_copy(i).wait_recv()
        add_rows(by_core[i], by_core[i], lanes_at(i, grads[array], row, rows, core), rows)
        y_copy(i).start()

    def stage2(i):
        half = chunks[i][2] // 2
        y_copy(i).wait_recv()
        add_rows(by_y[i], by_y[i], rows_of(by_core[i], y * half, half), half)
        x_copy(i).start()

    def stage3(i):
        quarter = chunks[i][2] // 4
        x_copy(i).wait_recv()
        add_rows(by_x[i], by_x[i], rows_of(by_y[i], x * quarter, quarter), quarter)
        for piece in range(PIECES):

            @pl.when(z != piece * stride)
            def _():
                z_copy(i, piece).start()

    def stage4(i):
        size = chunks[i][2] // 4 // PIECES

        @pl.when(owns)
        def _():
            for slot in range(lines - 1):
                remote(
                    by_z[i].at[slot], by_z[i].at[slot], zsend.at[i, 0], zrecv.at[i, slot], to_core
                ).wait_recv()
            target = final_rows(i, y, (x * PIECES + mine) * size, size, core)

            def body(index, carry):
                total = by_x[i][
                    pl.ds(pl.multiple_of(mine * size + index * 16, 16), 16)
                ].astype(jnp.float32)
                for slot in range(lines - 1):
                    total += by_z[i][slot, pl.ds(pl.multiple_of(index * 16, 16), 16)].astype(jnp.float32)
                target[pl.ds(pl.multiple_of(index * 16, 16), 16)] = total.astype(jnp.bfloat16)
                return carry

            lax.fori_loop(0, size // 16, body, 0)
            if chunks[i][5]:

                @pl.when(y == 0)
                def _():
                    cross_copy(i).start()

                @pl.when(y == 1)
                def _():
                    for step in range(1, lines):
                        line_copy(i, 0, 1, step).start()
            else:
                for step in range(1, lines):
                    line_copy(i, 0, y, step).start()

    def stage5(i):
        if chunks[i][5]:

            @pl.when(jnp.logical_and(owns, y == 1))
            def _():
                cross_copy(i).wait_recv()
                for step in range(1, lines):
                    line_copy(i, 1, 0, step).start()

    def stage6(i):
        def action(which, side):
            for piece in range(PIECES):

                @pl.when(z != piece * stride)
                def _():
                    line_arrival(i, which, side, piece).wait_recv()

            pair_copy(i, which, side, x).start()

        sides(i, action)

    def stage7(i):
        def action(which, side):
            pair_copy(i, which, side, 1 - x).wait_recv()
            last_copy(i, which, side, core).start()

        sides(i, action)

    def stage8(i):
        sides(i, lambda which, side: last_copy(i, which, side, 1 - core).wait_recv())


    width = in_t.shape[1]
    mod_tiles, wide = 6 * width // 128, width // 128
    images = d_mod.shape[0]
    in_lanes, head_lanes, embed_lanes = in_tiles * 128, head_tiles * 128, embed_tiles * 128
    rest_lanes = 2 * head_lanes + embed_lanes
    head_places = [o for o in range(shards) if head_starts[o] < wide]
    mod_places = [o for o in range(shards) if in_starts[o] < mod_tiles]
    few_rows = few.shape[0] // 2
    half = pl.ds(pl.multiple_of(core * few_rows, 8), few_rows)
    other_half = pl.ds(pl.multiple_of((1 - core) * few_rows, 8), few_rows)

    def is_in(where, places):
        return functools.reduce(jnp.logical_or, [where == o for o in places])

    few_core = remote(few.at[other_half], few_got, few_send.at[0], few_recv.at[0], to_core)
    few_over_y = remote(few_held.at[0], few_y, few_send.at[1], few_recv.at[1], to_y)
    few_over_x = remote(few_held.at[1], few_x, few_send.at[2], few_recv.at[2], to_x)
    few_back = remote(few_sum.at[half], few_sum.at[half], few_send.at[3], few_recv.at[3], to_core)
    few_back_arrival = remote(few_sum.at[other_half], few_sum.at[other_half], few_send.at[3], few_recv.at[3], to_core)
    mod_core = remote(d_mod, mod_got, few_send.at[4], few_recv.at[4], to_core)
    fm_core = remote(d_fm, fm_got, few_send.at[5], few_recv.at[5], to_core)
    pair_copy_x = remote(pair_own, pair_got, few_send.at[6], few_recv.at[6], to_x)

    def few_line_copy(step):
        return remote(few_line.at[z], few_line.at[z], few_send.at[6 + step], few_recv.at[6 + step], line_peer(step))

    def few_line_arrival(step):
        origin = lax.rem(z + lines - step, lines)
        return remote(few_line.at[origin], few_line.at[origin], few_send.at[6 + step], few_recv.at[6 + step], to_core)

    def group_parts(place):
        parts = []
        tiles = min(in_tiles, mod_tiles - in_starts[place])
        if tiles > 0:
            parts.append((0, in_starts[place] * 128, 0, tiles * 128))
        first, final = max(head_starts[place], wide), min(head_starts[place] + head_tiles, 3 * wide)
        if final > first:
            lead = (first - head_starts[place]) * 128
            parts.append((1, (first - wide) * 128, in_lanes + lead, (final - first) * 128))
        return parts

    def group_copy(place, k):
        which, lane, own, lanes = group_parts(place)[k]
        return remote(
            (mod_sum, fm_sum)[which].at[:, pl.ds(lane, lanes)],
            group_slot.at[:, pl.ds(own, lanes)],
            group_send.at[k, 0],
            group_recv.at[k, 0],
            to_y,
        )

    def to_others(kind, source, slots, step):
        return remote(
            source,
            slots.at[shard],
            group_send.at[kind, step - 1],
            group_recv.at[kind, step - 1],
            (rep, lax.rem(shard + step, shards)),
        )

    def from_others(kind, slots, step):
        origin = lax.rem(shard + shards - step, shards)
        return remote(slots.at[origin], slots.at[origin], group_send.at[kind, 0], group_recv.at[kind, step - 1], to_core)

    slots_of = (line_rest, line_full, line_in)

    def line_copy_d(kind, step):
        slots = slots_of[kind]
        return remote(slots.at[z], slots.at[z], line_send.at[kind, step - 1], line_recv.at[kind, step - 1], line_peer(step))

    def line_arrival_d(kind, step):
        slots = slots_of[kind]
        origin = lax.rem(z + lines - step, lines)
        return remote(slots.at[origin], slots.at[origin], line_send.at[kind, 0], line_recv.at[kind, step - 1], to_core)

    def on_line(action):
        for step in range(1, lines):
            action(0, step)
            action(1, step)

            @pl.when(is_in(shard, mod_places))
            def _():
                action(2, step)

    def side0():
        mod_core.start()
        fm_core.start()
        few_core.start()

    def side1():
        mod_core.wait_recv()
        mod_sum[...] = d_mod[...] + mod_got[...]
        fm_core.wait_recv()
        fm_sum[...] = d_fm[...] + fm_got[...]
        for place in range(shards):

            @pl.when(to_y[1] == place)
            def _():
                for k in range(len(group_parts(place))):
                    group_copy(place, k).start()

        few_core.wait_recv()
        few_held[0] = few[half] + few_got[...]
        few_over_y.start()

    def side2():
        pair_own[...] = jnp.zeros_like(pair_own)
        for place in range(shards):

            @pl.when(shard == place)
            def _():
                for k, (which, lane, own, lanes) in enumerate(group_parts(place)):
                    group_copy(place, k).wait_recv()
                    pair_own[:, own : own + lanes] = (
                        (mod_sum, fm_sum)[which][:, lane : lane + lanes] + group_slot[:, own : own + lanes]
                    )

        part_own[...] = jnp.dot(
            pair_own[:, in_lanes : in_lanes + head_lanes].astype(jnp.bfloat16),
            head_t[...],
            preferred_element_type=jnp.float32,
        )

        @pl.when(is_in(shard, mod_places))
        def _():
            part_own[...] += jnp.dot(
                pair_own[:, :in_lanes].astype(jnp.bfloat16), in_t[...], preferred_element_type=jnp.float32
            )

        part_slot[shard] = part_own[...]
        for step in range(1, shards):
            to_others(2, part_own, part_slot, step).start()
        few_over_y.wait_recv()
        few_held[1] = few_held[0] + few_y[...]
        few_over_x.start()

    def side3():
        for step in range(1, shards):
            from_others(2, part_slot, step).wait_recv()
        d_cond = functools.reduce(jnp.add, [part_slot[o] for o in range(shards)])
        value = cond_full[pl.ds(pl.multiple_of(place_here * images, 8), images), :]
        gate = jax.nn.sigmoid(value)
        d_value = d_cond * (gate + value * gate * (1.0 - gate))
        for place in range(shards):

            @pl.when(shard == place)
            def _():
                first = embed_starts[place] * 128
                pair_own[:, in_lanes + rest_lanes :] = d_value[:, first : first + embed_lanes]
                if place in head_places:
                    lanes = min(head_tiles, wide - head_starts[place]) * 128
                    first = head_starts[place] * 128
                    start = in_lanes + head_lanes
                    d_two_own = d_value[:, first : first + lanes].astype(jnp.bfloat16)
                    pair_own[:, start : start + lanes] = d_two_own.astype(jnp.float32)
                    act_own[...] = jnp.dot(d_two_own, head_t[:lanes, :], preferred_element_type=jnp.float32)
                    act_slot[shard] = act_own[...]
                    for step in range(1, shards):
                        to_others(3, act_own, act_slot, step).start()

        few_over_x.wait_recv()
        few_line[z] = few_held[1] + few_x[...]
        for step in range(1, lines):
            few_line_copy(step).start()

    def side4():
        for step in range(1, shards):

            @pl.when(is_in(lax.rem(shard + shards - step, shards), head_places))
            def _():
                from_others(3, act_slot, step).wait_recv()

        value = time_one[pl.ds(pl.multiple_of(place_here * images, 8), images), :]
        gate = jax.nn.sigmoid(value)
        slope = gate + value * gate * (1.0 - gate)
        for place in range(shards):

            @pl.when(shard == place)
            def _():
                first = embed_starts[place] * 128
                d_act = functools.reduce(jnp.add, [act_slot[o, :, first : first + embed_lanes] for o in head_places])
                start = in_lanes + 2 * head_lanes
                pair_own[:, start : start + embed_lanes] = (slope * d_act).astype(jnp.bfloat16).astype(jnp.float32)

        pair_copy_x.start()
        for step in range(1, lines):
            few_line_arrival(step).wait_recv()
        few_sum[half] = functools.reduce(jnp.add, [few_line[at] for at in range(lines)])
        few_back.start()

    def side5():
        pair_copy_x.wait_recv()
        own, got = pair_own[...], pair_got[...]
        both = jnp.concatenate([jnp.where(x == 0, own, got), jnp.where(x == 0, got, own)], 0)
        line_in[z] = both[:, :in_lanes].astype(jnp.bfloat16)
        line_rest[z] = both[:, in_lanes : in_lanes + rest_lanes].astype(jnp.bfloat16)
        line_full[z] = both[:, in_lanes + rest_lanes :]
        on_line(lambda kind, step: line_copy_d(kind, step).start())

    def side6():
        on_line(lambda kind, step: line_arrival_d(kind, step).wait_recv())
        for at in range(lines):
            span = slice(at * 2 * images, (at + 1) * 2 * images)
            d_head[span, :] = line_rest[at, :, :head_lanes]
            d_two[span, :] = line_rest[at, :, head_lanes : 2 * head_lanes]
            d_one[span, :] = line_rest[at, :, 2 * head_lanes :]
            d_full[span, :] = line_full[at]
        d_in[...] = jnp.zeros_like(d_in)

        @pl.when(is_in(shard, mod_places))
        def _():
            for at in range(lines):
                d_in[at * 2 * images : (at + 1) * 2 * images, :] = line_in[at]

        few_back_arrival.wait_recv()

    def side_end():
        for copy in (few_core, few_over_y, few_over_x, few_back, mod_core, fm_core, pair_copy_x):
            copy.wait_send()
        for step in range(1, lines):
            few_line_copy(step).wait_send()
        on_line(lambda kind, step: line_copy_d(kind, step).wait_send())
        for place in range(shards):

            @pl.when(to_y[1] == place)
            def _():
                for k in range(len(group_parts(place))):
                    group_copy(place, k).wait_send()

        for step in range(1, shards):
            to_others(2, part_own, part_slot, step).wait_send()

        @pl.when(is_in(shard, head_places))
        def _():
            for step in range(1, shards):
                to_others(3, act_own, act_slot, step).wait_send()

    beside = (side0, side1, side2, side3, side4, side5, side6)
    beside_at = (12, 14, 16, 18, 20, 22, 24)
    stages = (stage0, stage1, stage2, stage3, stage4, stage5, stage6, stage7, stage8)
    for tick in range(count + len(stages) - 1):
        if tick in beside_at:
            beside[beside_at.index(tick)]()
        for k, stage in enumerate(stages):
            if 0 <= tick - k < count:
                stage(tick - k)

    side_end()
    for i in range(count):
        core_copy(i).wait_send()
        y_copy(i).wait_send()
        x_copy(i).wait_send()
        for piece in range(PIECES):

            @pl.when(z != piece * stride)
            def _():
                z_copy(i, piece).wait_send()

        if chunks[i][5]:

            @pl.when(jnp.logical_and(owns, y == 0))
            def _():
                cross_copy(i).wait_send()

        def action(which, side):
            @pl.when(owns)
            def _():
                for step in range(1, lines):
                    line_copy(i, which, side, step).wait_send()

            pair_copy(i, which, side, x).wait_send()
            last_copy(i, which, side, core).wait_send()

        sides(i, action)


def reduce_call(lines, tables, heavy, light):
    width = heavy[2].shape[0]
    chunks = heavy_chunks(width)
    count = len(chunks)
    low, full = jnp.bfloat16, jnp.float32
    (_, in_tiles), (_, head_tiles), (_, embed_tiles), shards = tables
    few, cond_full = light[2], light[5]
    group, rows = light[0].shape[0], cond_full.shape[0]
    in_lanes, head_lanes, embed_lanes = in_tiles * 128, head_tiles * 128, embed_tiles * 128
    rest_lanes = 2 * head_lanes + embed_lanes
    few_half = (few.shape[0] // 2, width)
    pair = (group, in_lanes + rest_lanes + embed_lanes)
    sizes = [(part_rows, part_lanes) for _, _, part_rows, _, part_lanes, _ in chunks]
    dma = pltpu.SemaphoreType.DMA
    shapes = [(item.shape, low) for item in heavy] + [
        ((rows, in_tiles * 128), low),
        ((rows, head_tiles * 128), low),
        ((rows, head_tiles * 128), low),
        ((rows, embed_lanes), full),
        ((rows, embed_lanes), low),
        (few.shape, full),
    ]
    scratch = [
        (few_half, full),
        (few_half, full),
        (few_half, full),
        ((2,) + few_half, full),
        ((lines,) + few_half, full),
        (light[0].shape, full),
        (light[1].shape, full),
        (light[0].shape, full),
        (light[1].shape, full),
        ((group, in_lanes + head_lanes), full),
        ((group, width), full),
        ((shards, group, width), full),
        ((group, width), full),
        ((shards, group, width), full),
        (pair, full),
        (pair, full),
        ((lines, 2 * group, in_lanes), low),
        ((lines, 2 * group, rest_lanes), low),
        ((lines, 2 * group, embed_lanes), full),
    ]
    return pl.pallas_call(
        functools.partial(reduce_kernel, lines, chunks, tables),
        out_shape=[jax.ShapeDtypeStruct(*item) for item in shapes],
        in_specs=[pl.BlockSpec(memory_space=pltpu.VMEM)] * (4 + len(light)),
        out_specs=[pl.BlockSpec(memory_space=pltpu.VMEM)] * len(shapes),
        scratch_shapes=[pltpu.VMEM((r, c), low) for r, c in sizes]
        + [pltpu.VMEM((r // 2, c), low) for r, c in sizes]
        + [pltpu.VMEM((r // 4, c), low) for r, c in sizes]
        + [pltpu.VMEM((lines - 1, r // 4 // PIECES, c), low) for r, c in sizes]
        + [
            dma((count, 8)),
            dma((count, 8)),
            dma((count, PIECES)),
            dma((count, lines - 1)),
            dma((count, 2, lines - 1)),
            dma((count, 2, PIECES)),
        ]
        + [pltpu.VMEM(*item) for item in scratch]
        + [
            dma((lines + 6,)),
            dma((lines + 6,)),
            dma((4, shards - 1)),
            dma((4, shards - 1)),
            dma((3, lines - 1)),
            dma((3, lines - 1)),
        ],
        compiler_params=pltpu.CompilerParams(
            collective_id=1, has_side_effects=True, vmem_limit_bytes=63 * 1024 * 1024
        ),
    )(*heavy, *light)


def placed_traits(traits, lanes):
    lead = -(-(PATCH + FREQ) // 128) * 128
    lane = lax.broadcasted_iota(jnp.int32, (traits.shape[0], lead), 1)
    here = jnp.logical_and(lane >= PATCH, lane < PATCH + FREQ)
    freq = jnp.where(here, traits[:, :lead], 0.0).astype(jnp.bfloat16)
    named = lax.broadcasted_iota(jnp.int32, (traits.shape[0], lanes), 1).astype(jnp.float32)
    onehot = jnp.where(named == traits[:, lead : lead + 1], 1.0, 0.0).astype(jnp.bfloat16)
    return freq, onehot


def windows(cols, shards):
    starts = [place * cols // 128 for place in range(shards)]
    tiles = max(-(-(place + 1) * cols // 128) - start for place, start in enumerate(starts))
    return starts, tiles


def heavy_segments(width, in_cols, in_starts, out_rows, shards):
    every = []
    for place in range(shards):
        parts = []
        for array, low, high, most in ((3, 6 * width, 9 * width, 640), (1, 9 * width, 13 * width, 640)):
            first, last = max(low, place * in_cols), min(high, (place + 1) * in_cols)
            while first < last:
                rows = min(most, last - first)
                parts.append((0, first - in_starts[place] * 128, array, first - low, rows, 0, 0, width))
                first += rows
            if array == 3:
                parts.append((1, 0, 2, place * out_rows, out_rows, 0, 0, width))
        parts.append((1, 0, 0, place * out_rows, out_rows, width, 0, 4 * width))
        every.append(parts)
    return every


def gather_kernel(
    plan, in_t, out_t, head_t, embed, traits,
    fc2, fc1, attn_out, qkv, cond_full, time_act, time_one, modul, fmod, patch, last, all_traits,
    s1_slot, tab_slot, patch_slot, two_slot, two_own, mod_slot, mod_own, fm_slot, fm_own, last_own,
    ysend, yrecv, xsend, xrecv, zsend, zrecv, csend, crecv, osend, orecv, small_send, small_recv, local_sem,
    trait_slot, trait_own, trait_got, line_slot, trait_send, trait_recv,
):
    segments, (in_starts, in_tiles), (head_starts, head_tiles), (embed_starts, embed_tiles), lines = plan
    shards = len(segments)
    arrays = (fc2, fc1, attn_out, qkv)
    sources = (in_t, out_t)
    rep, shard = lax.axis_index("rep"), lax.axis_index("shard")
    place_here = lax.rem(rep, 2 * lines)
    x, z = lax.rem(place_here, 2), lax.div(place_here, 2)
    zb = lax.rem(z, 2)
    core, y = lax.rem(shard, 2), lax.div(shard, 2)
    to_core = (rep, shard + 1 - 2 * core)
    to_y = (rep, shard + 2 - 4 * y)
    to_x = (rep + 1 - 2 * x, shard)
    to_z = (rep + 2 - 4 * zb, shard)
    width = head_t.shape[1]

    barrier = pltpu.get_barrier_semaphore()
    others = [(rep, lax.rem(shard + step, shards)) for step in range(1, shards)]

    def line_peer(step):
        return (rep - place_here + lax.rem(z + step, lines) * 2 + x, shard)

    for peer in others + [to_x] + [line_peer(step) for step in range(1, lines)]:
        pl.semaphore_signal(barrier, inc=1, device_id=peer, device_id_type=MESH)
    pl.semaphore_wait(barrier, shards + lines - 1)

    def remote(source, target, send_sem, recv_sem, peer):
        return pltpu.make_async_remote_copy(
            src_ref=source, dst_ref=target, send_sem=send_sem, recv_sem=recv_sem, device_id=peer, device_id_type=MESH
        )

    def small(kind, source, slots, step):
        return remote(
            source, slots.at[shard], small_send.at[kind, step - 1], small_recv.at[kind, step - 1], others[step - 1]
        )

    def small_arrival(kind, slots, step):
        origin = lax.rem(shard + shards - step, shards)
        return remote(
            slots.at[origin], slots.at[origin], small_send.at[kind, step - 1], small_recv.at[kind, step - 1], to_core
        )

    def exchange(kind, source, slots, origins=None):
        for step in range(1, shards):
            if origins is None:
                small(kind, source, slots, step).start()
            else:
                sends = functools.reduce(jnp.logical_or, [shard == o for o in origins])

                @pl.when(sends)
                def _():
                    small(kind, source, slots, step).start()

    def arrive(kind, slots, origins=None):
        for step in range(1, shards):
            if origins is None:
                small_arrival(kind, slots, step).wait_recv()
            else:
                origin = lax.rem(shard + shards - step, shards)

                @pl.when(functools.reduce(jnp.logical_or, [origin == o for o in origins]))
                def _():
                    small_arrival(kind, slots, step).wait_recv()

    def sent(kind, source, slots, origins=None):
        for step in range(1, shards):
            if origins is None:
                small(kind, source, slots, step).wait_send()
            else:

                @pl.when(functools.reduce(jnp.logical_or, [shard == o for o in origins]))
                def _():
                    small(kind, source, slots, step).wait_send()

    def place_tiles(target, slots, starts, tiles, origins, dtype, first=0):
        total = target.shape[1] // 128
        for tile in range(total):
            parts = [
                slots[o, :, (tile + first - starts[o]) * 128 : (tile + first - starts[o] + 1) * 128]
                for o in origins
                if 0 <= tile + first - starts[o] < tiles
            ]
            target[:, tile * 128 : (tile + 1) * 128] = functools.reduce(jnp.add, parts).astype(dtype)

    def source_part(place, k):
        source, row, array, _, rows, lane, _, lanes = segments[place][k]
        return sources[source].at[pl.ds(row, rows), pl.ds(lane, lanes)]

    def target_part(place, k, start=0, rows=None):
        _, _, array, row, total, _, lane, lanes = segments[place][k]
        start = row + start
        if not isinstance(start, int):
            start = pl.multiple_of(start, 16)
        return arrays[array].at[pl.ds(start, total if rows is None else rows), pl.ds(lane, lanes)]

    def quarter(place, k, index):
        size = segments[place][k][4] // 4
        return target_part(place, k, index * size, size)

    def half_of(place, k, index, second):
        size = segments[place][k][4] // 4
        cut = -(-size // 32) * 16
        return target_part(place, k, index * size + (cut if second else 0), size - cut if second else cut)

    me = x * 2 + zb
    across_x, along_z, corner = (1 - x) * 2 + zb, x * 2 + 1 - zb, (1 - x) * 2 + 1 - zb

    def y_copy(place, k):
        size = segments[place][k][4] // 4
        source, row, _, _, _, lane, _, lanes = segments[place][k]
        part = sources[source].at[pl.ds(pl.multiple_of(row + me * size, 16), size), pl.ds(lane, lanes)]
        return remote(part, quarter(place, k, me), ysend.at[k], yrecv.at[k], to_y)

    def owner_copy(place, k):
        return remote(source_part(place, k), target_part(place, k), osend.at[k], orecv.at[k], to_core)

    def own_copy(place, k):
        return pltpu.make_async_copy(source_part(place, k), target_part(place, k), local_sem.at[k])

    def hop(part, sems, k, slot, peer):
        return remote(part, part, sems[0].at[k, slot], sems[1].at[k, slot], peer)

    xs, zs, cs = (xsend, xrecv), (zsend, zrecv), (csend, crecv)

    def begin(k, across):
        for place in range(shards):
            if k < len(segments[place]):

                @pl.when(shard == place)
                def _():
                    if across:
                        y_copy(place, k).start()
                    else:
                        owner_copy(place, k).start()
                        own_copy(place, k).start()

    def relay(place, stage, k):
        if stage == 0:
            y_copy(place, k).wait_recv()
            hop(quarter(place, k, me), xs, k, 0, to_x).start()
            hop(quarter(place, k, me), zs, k, 0, to_z).start()
            hop(quarter(place, k, me), cs, k, 0, to_core).start()
        elif stage == 1:
            hop(quarter(place, k, across_x), xs, k, 0, to_x).wait_recv()
            hop(half_of(place, k, across_x, False), zs, k, 1, to_z).start()
            hop(quarter(place, k, along_z), zs, k, 0, to_z).wait_recv()
            hop(half_of(place, k, along_z, True), xs, k, 1, to_x).start()
            hop(quarter(place, k, across_x), cs, k, 1, to_core).start()
            hop(quarter(place, k, along_z), cs, k, 2, to_core).start()
        else:
            hop(half_of(place, k, corner, False), zs, k, 1, to_z).wait_recv()
            hop(half_of(place, k, corner, True), xs, k, 1, to_x).wait_recv()
            hop(quarter(place, k, corner), cs, k, 3, to_core).start()

    def relay_tick(tick):
        for place in range(shards):

            @pl.when(to_y[1] == place)
            def _():
                for stage in range(3):
                    if 0 <= tick - stage < len(segments[place]):
                        relay(place, stage, tick - stage)

    def trait_line(step):
        return remote(
            line_slot.at[z], line_slot.at[z], trait_send.at[step], trait_recv.at[step], line_peer(step)
        )

    def trait_line_arrival(step):
        origin = lax.rem(z + lines - step, lines)
        return remote(line_slot.at[origin], line_slot.at[origin], trait_send.at[step], trait_recv.at[step], to_core)

    trait_pair = remote(trait_own, trait_got, trait_send.at[0], trait_recv.at[0], to_x)
    trait_slot[shard] = traits[...]
    exchange(7, traits, trait_slot)
    begin(0, True)
    arrive(7, trait_slot)
    trait_own[...] = functools.reduce(jnp.add, [trait_slot[o] for o in range(shards)])
    trait_pair.start()
    begin(1, True)
    trait_pair.wait_recv()
    own, got = trait_own[...], trait_got[...]
    line_slot[z] = jnp.concatenate([jnp.where(x == 0, own, got), jnp.where(x == 0, got, own)], 0)
    for step in range(1, lines):
        trait_line(step).start()
    relay_tick(0)
    begin(2, True)
    for step in range(1, lines):
        trait_line_arrival(step).wait_recv()
    count_in_line = 2 * traits.shape[0]
    for at in range(lines):
        all_traits[at * count_in_line : (at + 1) * count_in_line, :] = line_slot[at]
    freq, onehot = placed_traits(all_traits[...], embed.shape[1])

    nt = (((1,), (1,)), ((), ()))
    own_one = lax.dot_general(freq, embed[:, : freq.shape[1]], nt, preferred_element_type=jnp.float32)
    time_one[...] = own_one
    s1_slot[shard] = (own_one * jax.nn.sigmoid(own_one)).astype(jnp.bfloat16)
    tab_slot[shard] = lax.dot_general(onehot, embed[...], nt, preferred_element_type=jnp.float32)
    eye = lax.broadcasted_iota(jnp.int32, (PATCH, 128), 0) == lax.broadcasted_iota(jnp.int32, (PATCH, 128), 1)
    eye = jnp.where(eye, 1.0, 0.0).astype(jnp.bfloat16)
    patch_slot[shard] = lax.dot_general(eye, embed[:, :128], nt, preferred_element_type=jnp.float32).astype(jnp.bfloat16)
    exchange(0, s1_slot.at[shard], s1_slot)
    exchange(1, tab_slot.at[shard], tab_slot)
    exchange(2, patch_slot.at[shard], patch_slot)
    relay_tick(1)
    begin(3, True)
    last_place = [o for o in range(shards) if 0 <= 3 * width // 128 - head_starts[o] < head_tiles][-1]
    last_row = (3 * width // 128 - head_starts[last_place]) * 128
    last_own[...] = head_t[last_row : last_row + 16, :]

    @pl.when(shard == last_place)
    def _():
        last[...] = last_own[...]
        for step in range(1, shards):
            remote(last_own, last, small_send.at[6, step - 1], small_recv.at[6, 0], others[step - 1]).start()

    head_places = [o for o in range(shards) if head_starts[o] * 128 < width]
    fm_places = [o for o in range(shards) if (head_starts[o] + head_tiles) * 128 > width]
    mod_places = [o for o in range(shards) if in_starts[o] * 128 < 6 * width]
    group = modul.shape[0]

    arrive(0, s1_slot)
    place_tiles(time_act, s1_slot, embed_starts, embed_tiles, range(shards), jnp.bfloat16)
    two_own[...] = lax.dot_general(time_act[...], head_t[...], nt, preferred_element_type=jnp.float32)
    two_slot[shard] = two_own[...]
    exchange(3, two_own, two_slot, head_places)
    relay_tick(2)
    begin(4, True)
    arrive(1, tab_slot)
    arrive(3, two_slot, head_places)
    place_tiles(cond_full, tab_slot, embed_starts, embed_tiles, range(shards), jnp.float32)
    for tile in range(width // 128):
        span = slice(tile * 128, (tile + 1) * 128)
        for o in head_places:
            if 0 <= tile - head_starts[o] < head_tiles:
                cond_full[:, span] += two_slot[o, :, (tile - head_starts[o]) * 128 : (tile - head_starts[o] + 1) * 128]
    mine = cond_full[pl.ds(pl.multiple_of(place_here * group, 8), group), :]
    cond = (mine * jax.nn.sigmoid(mine)).astype(jnp.bfloat16)
    mod_own[...] = lax.dot_general(cond, in_t[...], nt, preferred_element_type=jnp.float32)
    mod_slot[shard] = mod_own[...]
    exchange(4, mod_own, mod_slot, mod_places)
    fm_own[...] = lax.dot_general(cond, head_t[...], nt, preferred_element_type=jnp.float32)
    fm_slot[shard] = fm_own[...]
    exchange(5, fm_own, fm_slot, fm_places)
    relay_tick(3)
    begin(5, True)
    begin(0, False)
    begin(1, False)
    begin(2, False)
    begin(3, False)
    begin(4, False)
    begin(5, False)
    arrive(2, patch_slot)
    place_tiles(patch, patch_slot, embed_starts, embed_tiles, range(shards), jnp.bfloat16)
    arrive(4, mod_slot, mod_places)
    arrive(5, fm_slot, fm_places)
    place_tiles(modul, mod_slot, in_starts, in_tiles, mod_places, jnp.float32)
    place_tiles(fmod, fm_slot, head_starts, head_tiles, fm_places, jnp.float32, width // 128)
    relay_tick(4)
    relay_tick(5)
    relay_tick(6)
    relay_tick(7)

    for place in range(shards):
        count = len(segments[place])

        @pl.when(shard == place)
        def _():
            for k in range(count):
                y_copy(place, k).wait_send()
                owner_copy(place, k).wait_send()
                own_copy(place, k).wait()

        @pl.when(to_core[1] == place)
        def _():
            for k in range(count):
                remote(target_part(place, k), target_part(place, k), osend.at[k], orecv.at[k], to_core).wait_recv()

        @pl.when(to_y[1] == place)
        def _():
            for k in range(count):
                hop(quarter(place, k, me), xs, k, 0, to_x).wait_send()
                hop(quarter(place, k, me), zs, k, 0, to_z).wait_send()
                hop(half_of(place, k, across_x, False), zs, k, 1, to_z).wait_send()
                hop(half_of(place, k, along_z, True), xs, k, 1, to_x).wait_send()
                for slot, index in enumerate((me, across_x, along_z, corner)):
                    hop(quarter(place, k, index), cs, k, slot, to_core).wait_send()

        @pl.when(shards - 1 - shard == place)
        def _():
            for k in range(count):
                for slot, index in enumerate((me, across_x, along_z, corner)):
                    remote(
                        quarter(place, k, index), quarter(place, k, index), csend.at[k, slot], crecv.at[k, slot], to_core
                    ).wait_recv()

    trait_pair.wait_send()
    for step in range(1, lines):
        trait_line(step).wait_send()
    sent(7, traits, trait_slot)
    sent(0, s1_slot.at[shard], s1_slot)
    sent(1, tab_slot.at[shard], tab_slot)
    sent(2, patch_slot.at[shard], patch_slot)
    sent(3, two_own, two_slot, head_places)
    sent(4, mod_own, mod_slot, mod_places)
    sent(5, fm_own, fm_slot, fm_places)

    @pl.when(shard == last_place)
    def _():
        for step in range(1, shards):
            remote(last_own, last, small_send.at[6, step - 1], small_recv.at[6, 0], others[step - 1]).wait_send()

    @pl.when(shard != last_place)
    def _():
        remote(last_own, last, small_send.at[6, 0], small_recv.at[6, 0], to_core).wait_recv()


def gather_call(in_t, out_t, head_t, embed_t, traits, shards, lines):
    place = lax.axis_index("shard")
    width = head_t.shape[1]
    low, full = jnp.bfloat16, jnp.float32

    def window(item_t, starts, tiles, lanes):
        rows = item_t.shape[0]
        offsets = [o * rows - start * 128 for o, start in enumerate(starts)]
        most = max(offsets)
        padded = jnp.pad(item_t, ((most, tiles * 128 - rows), (0, lanes - item_t.shape[1])))
        begin = most - jnp.asarray(offsets, jnp.int32)[place]
        return lax.dynamic_slice_in_dim(padded, begin, tiles * 128, 0).astype(low)

    in_cols, head_cols, embed_cols = in_t.shape[0], head_t.shape[0], embed_t.shape[0]
    in_starts, in_tiles = windows(in_cols, shards)
    head_starts, head_tiles = windows(head_cols, shards)
    embed_starts, embed_tiles = windows(embed_cols, shards)
    in_t = window(in_t, in_starts, in_tiles, width)
    head_t = window(head_t, head_starts, head_tiles, width)
    embed = window(embed_t, embed_starts, embed_tiles, -(-embed_t.shape[1] // 128) * 128)
    segments = heavy_segments(width, in_cols, in_starts, out_t.shape[0], shards)
    plan = (segments, (in_starts, in_tiles), (head_starts, head_tiles), (embed_starts, embed_tiles), lines)
    group = traits.shape[0]
    rows = 2 * lines * group
    most = max(len(parts) for parts in segments)
    shapes = [
        ((width, 4 * width), low),
        ((4 * width, width), low),
        ((width, width), low),
        ((3 * width, width), low),
        ((rows, width), full),
        ((rows, width), low),
        ((rows, embed_tiles * 128), full),
        ((group, 6 * width), full),
        ((group, 2 * width), full),
        ((PATCH, width), low),
        ((PATCH, width), low),
        ((rows, traits.shape[1]), full),
    ]
    scratch = [
        ((shards, rows, embed_tiles * 128), low),
        ((shards, rows, embed_tiles * 128), full),
        ((shards, PATCH, embed_tiles * 128), low),
        ((shards, rows, head_tiles * 128), full),
        ((rows, head_tiles * 128), full),
        ((shards, group, in_tiles * 128), full),
        ((group, in_tiles * 128), full),
        ((shards, group, head_tiles * 128), full),
        ((group, head_tiles * 128), full),
        ((PATCH, width), low),
    ]
    dma = pltpu.SemaphoreType.DMA
    outs = pl.pallas_call(
        functools.partial(gather_kernel, plan),
        out_shape=[jax.ShapeDtypeStruct(*item) for item in shapes],
        in_specs=[pl.BlockSpec(memory_space=pltpu.VMEM)] * 5,
        out_specs=[pl.BlockSpec(memory_space=pltpu.VMEM)] * len(shapes),
        scratch_shapes=[pltpu.VMEM(*item) for item in scratch]
        + [dma((most,)), dma((most,))]
        + [dma((most, 2))] * 4
        + [dma((most, 4))] * 2
        + [dma((most,)), dma((most,)), dma((8, shards - 1)), dma((8, shards - 1)), dma((most,))]
        + [
            pltpu.VMEM((shards,) + traits.shape, full),
            pltpu.VMEM(traits.shape, full),
            pltpu.VMEM(traits.shape, full),
            pltpu.VMEM((lines, 2 * group, traits.shape[1]), full),
            dma((lines,)),
            dma((lines,)),
        ],
        compiler_params=pltpu.CompilerParams(
            collective_id=2, has_side_effects=True, vmem_limit_bytes=60 * 1024 * 1024
        ),
    )(in_t, out_t.astype(low), head_t, embed, traits)
    return in_t, head_t, outs


NN = (((1,), (0,)), ((), ()))
NT = (((1,), (1,)), ((), ()))
TN = (((0,), (0,)), ((), ()))


def mxu(left, right, kind):
    return lax.dot_general(left, right, kind, preferred_element_type=jnp.float32)


def blocks_of(total, size, body):
    def step(index, carry):
        body(pl.ds(pl.multiple_of(index * size, size), size))
        return carry

    lax.fori_loop(0, total // size, step, 0)


def pass_kernel(
    images, state, target, weight_t, pos, patch, last, modul, fmod, fc2, fc1, attn_out, qkv,
    g_fc2, g_fc1, g_o, g_qkv, few, d_mod, d_fm,
    stream, hat_one, hat_two, root_one, root_two, a_low, qkv_low, mixed, proj, b_low, upper, active, mlp, back, d_qkv,
):
    width = patch.shape[1]
    tokens = images * TOK
    low = jnp.bfloat16
    shard = lax.axis_index("shard")
    row = [shard * images + image for image in range(images)]
    span = [pl.ds(image * TOK, TOK) for image in range(images)]
    cut = 256

    def piece(ref, image, index):
        return ref[pl.ds(row[image], 1), pl.ds(index * width, width)]

    def normed(value):
        center = value - jnp.mean(value, -1, keepdims=True)
        root = lax.rsqrt(jnp.mean(center * center, -1, keepdims=True) + eps_norm)
        return center * root, root

    def norm_back(d_hat, hat, root):
        return root * (d_hat - jnp.mean(d_hat, -1, keepdims=True) - hat * jnp.mean(d_hat * hat, -1, keepdims=True))

    def put_row(ref, image, index, value):
        ref[pl.ds(row[image], 1), pl.ds(index * width, width)] = (
            jnp.sum(value, 0, keepdims=True).astype(low).astype(jnp.float32)
        )

    d_mod[...] = jnp.zeros_like(d_mod)
    d_fm[...] = jnp.zeros_like(d_fm)

    for image in range(images):
        value = mxu(state[span[image], :], patch[...], NN) + pos[...]
        stream[span[image], :] = value
        hat, root = normed(value)
        hat_one[span[image], :] = hat
        root_one[span[image], :] = root
        a_low[span[image], :] = (hat * (1.0 + piece(modul, image, 1)) + piece(modul, image, 0)).astype(low)

    def qkv_block(part):
        qkv_low[:, part] = mxu(a_low[...], qkv[part, :], NT).astype(low)

    blocks_of(3 * width, cut, qkv_block)
    lane = lax.broadcasted_iota(jnp.int32, (TOK, 128), 1)
    first = lane < 64
    scale = 0.125

    def softmax(query, key):
        score = mxu(query, key, NT) * scale
        expo = jnp.exp(score - jnp.max(score, -1, keepdims=True))
        return expo / jnp.sum(expo, -1, keepdims=True)

    def take(ref, image, start):
        return ref[span[image], pl.ds(pl.multiple_of(start, 128), 128)]

    def attend(pair, carry):
        for image in range(images):
            query, key, value = (take(qkv_low, image, index * width + pair * 128) for index in range(3))
            outs = []
            for side in (first, jnp.logical_not(first)):
                probs = softmax(jnp.where(side, query, jnp.zeros_like(query)), key)
                outs.append(mxu(probs.astype(low), value, NN))
            mixed[span[image], pl.ds(pl.multiple_of(pair * 128, 128), 128)] = jnp.where(first, outs[0], outs[1]).astype(low)
        return carry

    lax.fori_loop(0, width // 128, attend, 0)
    for image in range(images):
        got = mxu(mixed[span[image], :], attn_out[...], NT)
        proj[span[image], :] = got
        value = stream[span[image], :] + piece(modul, image, 2) * got
        stream[span[image], :] = value
        hat, root = normed(value)
        hat_two[span[image], :] = hat
        root_two[span[image], :] = root
        b_low[span[image], :] = (hat * (1.0 + piece(modul, image, 4)) + piece(modul, image, 3)).astype(low)

    def upper_block(part):
        value = mxu(b_low[...], fc1[part, :], NT)
        upper[:, part] = value
        active[:, part] = (
            0.5 * value * (1.0 + jnp.tanh(0.7978845608 * (value + 0.044715 * value * value * value)))
        ).astype(low)

    blocks_of(4 * width, cut, upper_block)

    def mlp_block(part):
        mlp[:, part] = mxu(active[...], fc2[part, :], NT)

    blocks_of(width, cut, mlp_block)
    loss = jnp.zeros((), jnp.float32)
    g_last = jnp.zeros((PATCH, width), jnp.float32)
    for image in range(images):
        value = stream[span[image], :] + piece(modul, image, 5) * mlp[span[image], :]
        hat, root = normed(value)
        gain = 1.0 + piece(fmod, image, 1)
        final = (hat * gain + piece(fmod, image, 0)).astype(low)
        diff = mxu(final, last[...], NT) - target[span[image], :]
        share = weight_t[span[image], :] * diff
        loss += 0.5 * jnp.sum(share * diff)
        d_out = share.astype(low)
        g_last += mxu(d_out, final, TN)
        d_final = mxu(d_out, last[...], NN)
        put_row(d_fm, image, 0, d_final)
        put_row(d_fm, image, 1, d_final * hat)
        d_value = norm_back(d_final * gain, hat, root)
        back[span[image], :] = d_value
        put_row(d_mod, image, 5, d_value * mlp[span[image], :])
        d_qkv[span[image], pl.ds(0, width)] = (piece(modul, image, 5) * d_value).astype(low)
    few[pl.ds(PATCH, 8), :] = jnp.full((8, width), loss, jnp.float32)
    few[pl.ds(PATCH + 8, PATCH), :] = g_last
    few[pl.ds(2 * PATCH + 8, 8), :] = jnp.zeros((8, width), jnp.float32)

    d_mlp = d_qkv.at[:, pl.ds(0, width)]

    def fc2_block(part):
        g_fc2[:, part] = mxu(d_mlp[...], active[:, part], TN).astype(low)
        value = upper[:, part]
        inner = jnp.tanh(0.7978845608 * (value + 0.044715 * value * value * value))
        slope = 0.5 * (1.0 + inner) + 0.5 * value * (1.0 - inner * inner) * 0.7978845608 * (
            1.0 + 3.0 * 0.044715 * value * value
        )
        active[:, part] = (slope * mxu(d_mlp[...], fc2[:, part], NN)).astype(low)

    blocks_of(4 * width, cut, fc2_block)

    def fc1_block(part):
        g_fc1[part, :] = mxu(active[:, part], b_low[...], TN).astype(low)

    blocks_of(4 * width, cut, fc1_block)
    for image in range(images):
        d_normed = mxu(active[span[image], :], fc1[...], NN)
        hat = hat_two[span[image], :]
        put_row(d_mod, image, 3, d_normed)
        put_row(d_mod, image, 4, d_normed * hat)
        d_value = back[span[image], :] + norm_back(
            d_normed * (1.0 + piece(modul, image, 4)), hat, root_two[span[image], :]
        )
        back[span[image], :] = d_value
        put_row(d_mod, image, 2, d_value * proj[span[image], :])
        b_low[span[image], :] = (piece(modul, image, 2) * d_value).astype(low)

    def o_block(part):
        g_o[part, :] = mxu(b_low[:, part], mixed[...], TN).astype(low)

    blocks_of(width, cut, o_block)
    d_mixed = active.at[:, pl.ds(0, width)]
    d_mixed[...] = mxu(b_low[...], attn_out[...], NN).astype(low)

    def attend_back(pair, carry):
        for image in range(images):
            query, key, value = (take(qkv_low, image, index * width + pair * 128) for index in range(3))
            d_out = take(active, image, pair * 128)
            d_query, d_key, d_value = [], [], []
            for side in (first, jnp.logical_not(first)):
                none = jnp.zeros_like(query)
                probs = softmax(jnp.where(side, query, none), key)
                d_prob = mxu(jnp.where(side, d_out, none), value, NT)
                d_score = (probs * (d_prob - jnp.sum(probs * d_prob, -1, keepdims=True))).astype(low)
                d_value.append(mxu(probs.astype(low), d_out, TN))
                d_query.append(mxu(d_score, key, NN) * scale)
                d_key.append(mxu(d_score, query, TN) * scale)
            for index, both in enumerate((d_query, d_key, d_value)):
                d_qkv[span[image], pl.ds(pl.multiple_of(index * width + pair * 128, 128), 128)] = jnp.where(
                    first, both[0], both[1]
                ).astype(low)
        return carry

    lax.fori_loop(0, width // 128, attend_back, 0)

    def g_qkv_block(part):
        g_qkv[part, :] = mxu(d_qkv[:, part], a_low[...], TN).astype(low)

    blocks_of(3 * width, cut, g_qkv_block)
    g_patch = jnp.zeros((PATCH, width), jnp.float32)
    for image in range(images):
        d_normed = mxu(d_qkv[span[image], :], qkv[...], NN)
        hat = hat_one[span[image], :]
        put_row(d_mod, image, 0, d_normed)
        put_row(d_mod, image, 1, d_normed * hat)
        d_value = back[span[image], :] + norm_back(
            d_normed * (1.0 + piece(modul, image, 1)), hat, root_one[span[image], :]
        )
        g_patch += mxu(state[span[image], :], d_value.astype(low), TN)
    few[pl.ds(0, PATCH), :] = g_patch


def pass_scratch(tokens, width):
    low, full = jnp.bfloat16, jnp.float32
    return [
        ((tokens, width), full),
        ((tokens, width), full),
        ((tokens, width), full),
        ((tokens, 1), full),
        ((tokens, 1), full),
        ((tokens, width), low),
        ((tokens, 3 * width), low),
        ((tokens, width), low),
        ((tokens, width), full),
        ((tokens, width), low),
        ((tokens, 4 * width), full),
        ((tokens, 4 * width), low),
        ((tokens, width), full),
        ((tokens, width), full),
        ((tokens, 3 * width), low),
    ]


def pass_call(images, state, target, weight_t, pos, patch, last, modul, fmod, heavy):
    width = patch.shape[1]
    low, full = jnp.bfloat16, jnp.float32
    shapes = [(item.shape, low) for item in heavy] + [
        ((2 * PATCH + 16, width), full),
        (modul.shape, full),
        (fmod.shape, full),
    ]
    return pl.pallas_call(
        functools.partial(pass_kernel, images),
        out_shape=[jax.ShapeDtypeStruct(*item) for item in shapes],
        in_specs=[pl.BlockSpec(memory_space=pltpu.VMEM)] * 12,
        out_specs=[pl.BlockSpec(memory_space=pltpu.VMEM)] * len(shapes),
        scratch_shapes=[pltpu.VMEM(*item) for item in pass_scratch(state.shape[0], width)],
        compiler_params=pltpu.CompilerParams(vmem_limit_bytes=63 * 1024 * 1024),
    )(state, target, weight_t, pos, patch, last, modul, fmod, *heavy)


def own_segments(width, in_cols, in_starts, out_rows, shards):
    every = []
    for place in range(shards):
        parts = []
        for array, low, high in ((3, 6 * width, 9 * width), (1, 9 * width, 13 * width)):
            first, last = max(low, place * in_cols), min(high, (place + 1) * in_cols)
            if first < last:
                parts.append((array, first - low, last - first, first - in_starts[place] * 128))
        every.append(parts)
    return every


def total_kernel(
    tables, segments, fc2, fc1, attn_out, qkv, w_in, w_out, w_head, w_embed,
    d_in, d_fin, d_two, d_one, d_full, few, cond_full, time_act, traits, c_in, c_out, c_head, c_embed,
    g_in, g_out, g_head, g_embed, n_in, n_out, n_head, n_embed, stats,
    own_t, own_out, grad_t, head_t, t_out, t_head, t_embed, v_in, v_out, v_head, v_embed,
    load, write, fetch,
):
    (in_starts, in_tiles), (head_starts, head_tiles), (embed_starts, embed_tiles), shards = tables
    arrays = (fc2, fc1, attn_out, qkv)
    shard = lax.axis_index("shard")
    width = cond_full.shape[1]
    in_cols, head_cols, embed_cols, out_cols = (item.shape[0] for item in (w_in, w_head, w_embed, w_out))
    full, low = jnp.float32, jnp.bfloat16
    span = lane_span(width, w_embed.shape[1])

    weights = ((w_in, v_in), (w_out, v_out), (w_head, v_head), (w_embed, v_embed))
    reads = [pltpu.make_async_copy(source, target, load.at[k]) for k, (source, target) in enumerate(weights)]
    for copy in reads:
        copy.start()

    def heavy_copies(place):
        copies = []
        for k, (array, row, rows, at) in enumerate(segments[place]):
            copies.append(
                pltpu.make_async_copy(
                    arrays[array].at[pl.ds(row, rows), :], own_t.at[pl.ds(at, rows), :], fetch.at[k]
                )
            )
        for k, array in ((2, 2), (3, 0)):
            lane = 0 if array == 2 else width
            copies.append(
                pltpu.make_async_copy(
                    arrays[array].at[pl.ds(place * out_cols, out_cols), :],
                    own_out.at[:, pl.ds(lane, arrays[array].shape[1])],
                    fetch.at[k],
                )
            )
        return copies

    for place in range(shards):

        @pl.when(shard == place)
        def _():
            for copy in heavy_copies(place):
                copy.start()
            edges = [0]
            for _, _, rows, at in segments[place]:
                edges += [at, at + rows]
            edges.append(in_tiles * 128)
            for start, stop in zip(edges[0::2], edges[1::2]):
                if start < stop:
                    own_t[start:stop, :] = jnp.zeros((stop - start, width), low)

    def decayed(state, total, count):
        return decay * state + (1.0 - decay) * (total / count + eps_one)

    def to_lanes(column):
        return jnp.broadcast_to(column, (column.shape[0], 128)).T[:1, :]

    def to_column(lanes):
        return jnp.broadcast_to(lanes, (128, lanes.shape[1])).T[:, :1]

    def squares_of(value, state, fresh_out, start, size):
        square = value * value
        sums = to_lanes(jnp.sum(square, -1, keepdims=True))[:, :size]
        fresh = decayed(state[:, start : start + size], sums, value.shape[1])
        fresh_out[:, start : start + size] = fresh
        inverse = 1.0 / fresh
        if size < value.shape[0]:
            inverse = jnp.concatenate([inverse, jnp.zeros((1, value.shape[0] - size), full)], 1)
        return jnp.sum(square, 0, keepdims=True), jnp.sum(square * to_column(inverse), 0, keepdims=True)

    def put(start, plain, scaled):
        stats[:, start : start + plain.shape[1]] = plain
        stats[:, span + start : span + start + plain.shape[1]] = scaled

    def column_blocks(total):
        return [(start, min(128, total - start)) for start in range(0, total, 128)]

    def by_blocks(take, total, state, fresh_out, place):
        plain, scaled = jnp.zeros((1, width), full), jnp.zeros((1, width), full)
        for start, size in column_blocks(total):
            value = take(start, size)
            if size < 128:
                value = jnp.concatenate([value, jnp.zeros((128 - size, width), full)], 0)
            more, more_scaled = squares_of(value, state, fresh_out, start, size)
            plain, scaled = plain + more, scaled + more_scaled
        put(place, plain, scaled)

    cond = cond_full[...]
    cond = (cond * jax.nn.sigmoid(cond)).astype(low)

    lanes_all = -(-w_embed.shape[1] // 128) * 128
    freq, onehot = placed_traits(traits[...], lanes_all)
    square_one = lax.broadcasted_iota(jnp.int32, (PATCH, lanes_all), 0)
    eye = jnp.where(square_one == lax.broadcasted_iota(jnp.int32, (PATCH, lanes_all), 1), 1.0, 0.0).astype(low)

    def exact(value, picks):
        total = None
        for _ in range(3):
            part = value.astype(low)
            value = value - part.astype(full)
            term = mxu(part, picks, TN)
            total = term if total is None else total + term
        return total

    for place in range(shards):

        @pl.when(shard == place)
        def _():
            lead = place * embed_cols - embed_starts[place] * 128
            lanes = slice(embed_starts[place] * 128, (embed_starts[place] + embed_tiles) * 128)
            value = exact(d_full[...], onehot) + exact(few[0:PATCH, lanes], eye)
            value = value[lead : lead + embed_cols, :]
            time = mxu(d_one[...], freq, TN)[lead : lead + embed_cols, :]
            t_embed[:, : freq.shape[1]] = value[:, : freq.shape[1]] + time
            t_embed[:, freq.shape[1] :] = value[:, freq.shape[1] : w_embed.shape[1]]

    pltpu.make_async_copy(t_embed, g_embed, write.at[3]).start()
    value = jnp.concatenate([t_embed[...], jnp.zeros((embed_cols, lanes_all - w_embed.shape[1]), full)], 1)
    square = value * value
    fresh = decayed(c_embed[...], to_lanes(jnp.sum(square, -1, keepdims=True)), w_embed.shape[1])
    n_embed[...] = fresh
    put(7 * width, jnp.sum(square, 0, keepdims=True), jnp.sum(square * to_column(1.0 / fresh), 0, keepdims=True))

    head_t[...] = mxu(d_two[...], time_act[...], TN) + mxu(d_fin[...], cond, TN)
    last_place = [o for o in range(shards) if 0 <= 3 * width // 128 - head_starts[o] < head_tiles][-1]
    last_row = (3 * width // 128 - head_starts[last_place]) * 128

    @pl.when(shard == last_place)
    def _():
        head_t[last_row : last_row + PATCH, :] = few[PATCH + 8 : 2 * PATCH + 8, :]

    for place in range(shards):

        @pl.when(shard == place)
        def _():
            lead = place * head_cols - head_starts[place] * 128
            t_head[...] = head_t[lead : lead + head_cols, :]

    pltpu.make_async_copy(t_head, g_head, write.at[2]).start()
    by_blocks(lambda start, size: t_head[start : start + size, :], head_cols, c_head, n_head, 6 * width)

    for place in range(shards):

        @pl.when(shard == place)
        def _():
            for copy in heavy_copies(place):
                copy.wait()

    def light(index, carry):
        part = pl.ds(pl.multiple_of(index * 128, 128), 128)
        grad_t[part, :] = mxu(d_in[:, part], cond, TN) + own_t[part, :].astype(full)
        return carry

    lax.fori_loop(0, in_tiles, light, 0)
    lead = lax.rem(shard * in_cols, 128)
    write_in = pltpu.make_async_copy(grad_t.at[pl.ds(pl.multiple_of(lead, 64), in_cols), :], g_in, write.at[0])
    write_in.start()
    by_blocks(
        lambda start, size: grad_t[pl.ds(pl.multiple_of(lead + start, 64), size), :], in_cols, c_in, n_in, 0
    )

    sums = jnp.zeros((out_cols, 1), full)
    for index in range(5):
        value = own_out[:, index * width : (index + 1) * width].astype(full)
        t_out[:, index * width : (index + 1) * width] = value
        sums += jnp.sum(value * value, -1, keepdims=True)
    pltpu.make_async_copy(t_out, g_out, write.at[1]).start()
    fresh = decayed(c_out[...], to_lanes(sums), 5 * width)
    n_out[...] = fresh
    column = to_column(1.0 / fresh)
    for index in range(5):
        value = t_out[:, index * width : (index + 1) * width]
        square = value * value
        put(width + index * width, jnp.sum(square, 0, keepdims=True), jnp.sum(square * column, 0, keepdims=True))

    for copy in reads:
        copy.wait()
    for k, (_, value) in enumerate(weights):
        rows, cols = value.shape

        def squares(index, carry):
            block = value[pl.ds(pl.multiple_of(index * 64, 64), 64), :]
            return carry + jnp.sum(block * block, 0, keepdims=True)

        total = lax.fori_loop(0, rows // 64, squares, jnp.zeros((1, cols), full))
        if rows % 64:
            block = value[rows // 64 * 64 :, :]
            total += jnp.sum(block * block, 0, keepdims=True)
        start = 2 * span + k * 128
        stats[:, start : start + 128] = jnp.broadcast_to(jnp.sum(total, -1, keepdims=True) / 128.0, (1, 128))
    write_in.wait()
    for k, (source, target) in enumerate(((t_out, g_out), (t_head, g_head), (t_embed, g_embed))):
        pltpu.make_async_copy(source, target, write.at[k + 1]).wait()


def lane_span(width, embed_rows):
    return 7 * width + -(-embed_rows // 128) * 128


def total_call(tables, heavy, weights, light, cols):
    (in_starts, in_tiles), (_, head_tiles), _, shards = tables
    low, full = jnp.bfloat16, jnp.float32
    width = heavy[2].shape[0]
    w_in, w_out, w_head, w_embed = weights
    lanes = 2 * lane_span(width, w_embed.shape[1]) + 4 * 128
    segments = own_segments(width, w_in.shape[0], in_starts, w_out.shape[0], shards)
    shapes = [(item.shape, full) for item in weights] + [(item.shape, full) for item in cols] + [((1, lanes), full)]
    anywhere, vmem = pl.BlockSpec(memory_space=pl.ANY), pl.BlockSpec(memory_space=pltpu.VMEM)
    scratch = [
        ((in_tiles * 128, width), low),
        (w_out.shape, low),
        ((in_tiles * 128, width), full),
        ((head_tiles * 128, width), full),
    ]
    scratch += [(item.shape, full) for item in weights[1:]] + [(item.shape, full) for item in weights]
    return pl.pallas_call(
        functools.partial(total_kernel, tables, segments),
        out_shape=[jax.ShapeDtypeStruct(*item) for item in shapes],
        in_specs=[anywhere] * 8 + [vmem] * (len(light) + 4),
        out_specs=[anywhere] * 4 + [vmem] * 5,
        scratch_shapes=[pltpu.VMEM(*item) for item in scratch] + [pltpu.SemaphoreType.DMA((4,))] * 3,
        compiler_params=pltpu.CompilerParams(vmem_limit_bytes=60 * 1024 * 1024),
    )(*heavy, *weights, *light, *cols)


def finish_kernel(shards, sizes, own, r_in, r_out, r_head, r_embed, n_in, n_out, n_head, n_embed, s_in, s_out, s_head, s_embed, rms, slots, send, recv):
    rep, shard = lax.axis_index("rep"), lax.axis_index("shard")
    barrier = pltpu.get_barrier_semaphore()
    for step in range(1, shards):
        peer = (rep, lax.rem(shard + step, shards))
        pl.semaphore_signal(barrier, inc=1, device_id=peer, device_id_type=MESH)
    pl.semaphore_wait(barrier, shards - 1)

    def copy(step):
        return pltpu.make_async_remote_copy(
            src_ref=own,
            dst_ref=slots.at[shard],
            send_sem=send.at[step - 1],
            recv_sem=recv.at[step - 1],
            device_id=(rep, lax.rem(shard + step, shards)),
            device_id_type=MESH,
        )

    for step in range(1, shards):
        copy(step).start()
    slots[shard] = own[...]
    for step in range(1, shards):
        copy(step).wait()
    total = functools.reduce(jnp.add, [slots[o] for o in range(shards)])
    states, fresh, scales = (r_in, r_out, r_head, r_embed), (n_in, n_out, n_head, n_embed), (s_in, s_out, s_head, s_embed)
    starts, start = [], 0
    for rows, _ in sizes:
        starts.append(start)
        start += -(-rows // 128) * 128
    update, means = jnp.zeros((1, 1), jnp.float32), []
    for k, (rows, cols) in enumerate(sizes):
        row = decay * states[k][...] + (1.0 - decay) * (total[:, starts[k] : starts[k] + rows] / cols + eps_one)
        fresh[k][...] = row
        mean = jnp.mean(row, -1, keepdims=True)
        means.append(mean)
        update += mean * jnp.sum(total[:, start + starts[k] : start + starts[k] + rows] / row, -1, keepdims=True)
    update = jnp.sqrt(update / sum(rows * cols for rows, cols in sizes))
    rms[...] = jnp.broadcast_to(update, rms.shape)
    factor = jnp.maximum(1.0, update / clip_level)
    for k, (rows, cols) in enumerate(sizes):
        first = 2 * start + k * 128
        weight = jnp.sqrt(jnp.sum(total[:, first : first + 128], -1, keepdims=True) / (rows * cols))
        scales[k][...] = rate * jnp.maximum(eps_two, weight) / factor * lax.rsqrt(fresh[k][...] / means[k])


def finish_call(shards, sizes, stats, rows_old):
    full = jnp.float32
    shapes = [((1, rows), full) for rows, _ in sizes] * 2 + [((1, 128), full)]
    return pl.pallas_call(
        functools.partial(finish_kernel, shards, sizes),
        out_shape=[jax.ShapeDtypeStruct(*item) for item in shapes],
        in_specs=[pl.BlockSpec(memory_space=pltpu.VMEM)] * 5,
        out_specs=[pl.BlockSpec(memory_space=pltpu.VMEM)] * len(shapes),
        scratch_shapes=[
            pltpu.VMEM((shards,) + stats.shape, full),
            pltpu.SemaphoreType.DMA((shards - 1,)),
            pltpu.SemaphoreType.DMA((shards - 1,)),
        ],
        compiler_params=pltpu.CompilerParams(collective_id=3, has_side_effects=True),
    )(stats, *rows_old)


def on_device(
    latents,
    noises,
    velocity,
    times,
    labels,
    dropped,
    blocks_in,
    blocks_out,
    head_side,
    embed_side,
    state_in_row,
    state_in_col,
    state_out_row,
    state_out_col,
    state_head_row,
    state_head_col,
    state_embed_row,
    state_embed_col,
):
    images = latents.shape[0]
    width = head_side.shape[0]
    shard_count = lax.axis_size("shard")
    place = lax.axis_index("shard")
    in_cols = blocks_in.shape[2]
    head_cols = head_side.shape[1]
    embed_cols = embed_side.shape[1]
    group = images * shard_count
    weights = (blocks_in[0].T, blocks_out[0].T, head_side.T, embed_side.T)
    t_value = (times.astype(jnp.float32) + 1.0) / step_count
    classes = (PATCH + FREQ + jnp.where(dropped == 1, CLASSES - 1, labels)).astype(jnp.float32)
    lines = LINE
    lead = -(-(PATCH + FREQ) // 128) * 128
    own_traits = jnp.concatenate(
        [
            jnp.zeros((images, PATCH), jnp.float32),
            time_freq(t_value, FREQ),
            jnp.zeros((images, lead - PATCH - FREQ), jnp.float32),
            jnp.broadcast_to(classes[:, None], (images, 128)),
        ],
        1,
    )
    traits = lax.dynamic_update_slice(
        jnp.zeros((group, lead + 128), jnp.float32), own_traits, (place * images, 0)
    )
    in_t, head_win_t, gathered = gather_call(*weights, traits, shard_count, lines)
    fc2_t, fc1_t, o_t, qkv_t, cond_full, time_act, time_one, modul, final_mod, patch_w, head_t, all_traits = gathered
    tcol = t_value[:, None, None]
    state = (
        (1.0 - tcol) * latents.reshape(images, TOK, PATCH)
        + tcol * noises.reshape(images, TOK, PATCH)
    ).astype(jnp.bfloat16)
    *heavy, few, d_mod, d_fm = pass_call(
        images,
        state.reshape(images * TOK, PATCH),
        velocity.reshape(images * TOK, PATCH),
        jnp.repeat(t_value, TOK)[:, None],
        positions(GRID, width),
        patch_w,
        head_t,
        modul,
        final_mod,
        [fc2_t, fc1_t, o_t, qkv_t],
    )
    tables = (
        windows(in_cols, shard_count),
        windows(head_cols, shard_count),
        windows(embed_cols, shard_count),
        shard_count,
    )
    sums = reduce_call(
        lines,
        tables,
        heavy,
        [d_mod, d_fm, few, in_t, head_win_t, cond_full, time_one],
    )
    d_in, d_fin, d_two, d_full, d_one, few_sum = sums[4:]
    loss_sum = few_sum[PATCH, 0]
    rows_old = (state_in_row, state_out_row, state_head_row[None], state_embed_row[None])
    cols_old = (state_in_col, state_out_col, state_head_col[None], state_embed_col[None])
    *outs, stats = total_call(
        tables,
        sums[:4],
        weights,
        [d_in, d_fin, d_two, d_one, d_full, few_sum, cond_full, time_act, all_traits],
        cols_old,
    )
    totals, cols_new = outs[:4], outs[4:]
    blocks = lax.axis_size("rep") // (2 * lines)
    if blocks > 1:
        apart = [[k * 2 * lines + j for k in range(blocks)] for j in range(2 * lines)]
        totals, loss_sum = lax.psum((totals, loss_sum), "rep", axis_index_groups=apart)
        cols_new, plain, scaled = [], [], []
        for gradient, col_state in zip(totals, cols_old):
            square = gradient * gradient
            fresh = decay * col_state + (1.0 - decay) * (jnp.mean(square, 1)[None] + eps_one)
            pad = (0, -gradient.shape[1] % 128)
            cols_new.append(fresh)
            plain.append(jnp.pad(jnp.sum(square, 0), pad))
            scaled.append(jnp.pad(jnp.sum(square / fresh[0][:, None], 0), pad))
        spans = sum(item.shape[0] for item in plain) * 2
        stats = jnp.concatenate(plain + scaled + [stats[0, spans:]])[None]
    sizes = [(weight.shape[1], weight.shape[0] * shard_count) for weight in weights]
    *outs, rms = finish_call(shard_count, sizes, stats, rows_old)
    rows_new, scales = outs[:4], outs[4:]
    update_rms = rms[0, 0]
    news = [
        (weight - gradient * scale * lax.rsqrt(col_next[0])[:, None]).T
        for weight, gradient, scale, col_next in zip(weights, totals, scales, cols_new)
    ]
    return (
        loss_sum,
        update_rms,
        totals[0].T[None],
        totals[1].T[None],
        totals[2].T,
        totals[3].T,
        rows_new[0],
        cols_new[0],
        rows_new[1],
        cols_new[1],
        rows_new[2][0],
        cols_new[2][0],
        rows_new[3][0],
        cols_new[3][0],
        news[0][None],
        news[1][None],
        news[2],
        news[3],
    )


def solution(mesh):
    placed = (
        P(("rep", "shard"), None),
        P(("rep", "shard"), None),
        P(("rep", "shard"), None),
        P(("rep", "shard")),
        P(("rep", "shard")),
        P(("rep", "shard")),
        P(None, None, "shard"),
        P(None, None, "shard"),
        P(None, "shard"),
        P(None, "shard"),
        P(),
        P(None, "shard"),
        P(),
        P(None, "shard"),
        P(),
        P("shard"),
        P(),
        P("shard"),
    )
    return jax.shard_map(
        on_device,
        mesh=mesh,
        in_specs=placed,
        out_specs=(
            P(),
            P(),
            P(None, None, "shard"),
            P(None, None, "shard"),
            P(None, "shard"),
            P(None, "shard"),
            P(),
            P(None, "shard"),
            P(),
            P(None, "shard"),
            P(),
            P("shard"),
            P(),
            P("shard"),
            P(None, None, "shard"),
            P(None, None, "shard"),
            P(None, "shard"),
            P(None, "shard"),
        ),
        check_vma=False,
    )
```

```python
import functools
import math

import jax
import jax.numpy as jnp
from jax import lax
from jax.experimental import pallas as pl
from jax.experimental.pallas import tpu as pltpu
from jax.sharding import PartitionSpec as P

HEADS = 12
CLASSES = 1001
FREQ = 256
GRID = 16
PATCH = 16
LAYERS = 1
TOK = 256


decay = 0.5
eps_norm = 1e-06
eps_one = 1e-30
eps_two = 0.001
clip_level = 0.1
rate = 8.0
step_count = 1000.0


def silu(value):
    return value * jax.nn.sigmoid(value)


def positions(grid, width):
    quarter = width // 4
    omega = 1.0 / 10000.0 ** (jnp.arange(quarter, dtype=jnp.float32) / quarter)
    index = jnp.arange(grid * grid, dtype=jnp.int32)
    row_pos = (index // grid).astype(jnp.float32)[:, None] * omega[None, :]
    col_pos = (index % grid).astype(jnp.float32)[:, None] * omega[None, :]
    return jnp.concatenate(
        [jnp.sin(row_pos), jnp.cos(row_pos), jnp.sin(col_pos), jnp.cos(col_pos)], 1
    )


def time_freq(t_value, width):
    half = width // 2
    freqs = jnp.exp(-math.log(10000.0) * jnp.arange(half, dtype=jnp.float32) / half)
    angles = (t_value * step_count)[:, None] * freqs[None, :]
    return jnp.concatenate([jnp.cos(angles), jnp.sin(angles)], -1)


def weight_grad(left, back):
    flat_left = left.reshape(-1, left.shape[-1])
    flat_back = back.reshape(-1, back.shape[-1])
    return lax.dot_general(
        flat_left, flat_back, (((0,), (0,)), ((), ())), preferred_element_type=jnp.float32
    )


MESH = pl.DeviceIdType.MESH
LINE = 4
PIECES = 4
PARTS = (4, 4, 2)
ORDER = (
    (0, 0), (0, 1), (0, 2), (1, 0), (9, 0), (1, 1), (0, 3), (9, 1), (1, 2), (0, 4), (0, 5), (1, 3), (9, 2),
    (2, 0), (0, 6), (1, 4), (1, 5), (0, 7), (9, 4), (2, 1), (1, 6), (3, 0), (0, 8), (1, 7), (9, 5), (2, 2),
    (0, 9), (3, 1), (0, 10), (1, 8), (4, 0), (9, 6), (2, 4), (0, 11), (3, 2), (0, 12), (0, 13), (0, 14), (4, 1),
    (9, 7), (2, 5), (3, 4), (6, 0), (0, 15), (9, 3), (2, 6), (2, 7), (3, 5), (4, 2), (4, 4), (9, 8), (6, 1),
    (1, 9), (7, 0), (0, 16), (0, 17), (3, 6), (2, 3), (9, 9), (3, 7), (4, 5), (1, 10), (1, 11), (6, 2), (7, 1),
    (8, 0), (2, 8), (9, 10), (3, 3), (5, 4), (8, 1), (4, 6), (7, 2), (2, 9), (4, 7), (3, 8), (8, 2), (9, 11),
    (5, 5), (2, 10), (4, 3), (3, 9), (6, 4), (5, 6), (5, 7), (3, 10), (2, 11), (4, 8), (6, 5), (6, 3), (7, 4),
    (6, 6), (4, 9), (3, 11), (8, 4), (6, 7), (4, 10), (6, 8), (7, 5), (6, 9), (7, 3), (8, 5), (4, 11), (8, 3),
    (5, 10), (7, 6), (8, 6), (5, 11), (7, 7), (6, 10), (7, 8), (8, 7), (7, 9), (6, 11), (8, 8), (8, 9), (7, 10),
    (8, 10), (7, 11), (8, 11),
)
BESIDE_AT = (44, 54, 65, 76, 87, 97, 108)
SLOTS = 3
NN = (((1,), (0,)), ((), ()))
NT = (((1,), (1,)), ((), ()))
TN = (((0,), (0,)), ((), ()))


def mxu(left, right, kind):
    return lax.dot_general(left, right, kind, preferred_element_type=jnp.float32)


def blocks_of(total, size, body):
    def step(index, carry):
        body(pl.ds(pl.multiple_of(index * size, size), size))
        return carry

    lax.fori_loop(0, total // size, step, 0)


def heavy_chunks(width):
    half = width // 2
    fc2, fc1, kv = PARTS
    parts = [(0, 0, width, 4 * width // fc2 * k, 2 * width // fc2, False) for k in range(fc2)]
    parts += [(1, 4 * width // fc1 * k, 4 * width // fc1, 0, half, True) for k in range(fc1)]
    parts += [(2, 0, width, 0, half, False), (3, 0, width, 0, half, False)]
    parts += [(3, width + 2 * width // kv * k, 2 * width // kv, 0, half, True) for k in range(kv)]
    return tuple(parts)


def add_rows(target, left, right, rows):
    block = 16

    def body(index, carry):
        span = pl.ds(pl.multiple_of(index * block, block), block)
        target[span] = left[span] + right[span]
        return carry

    lax.fori_loop(0, rows // block, body, 0)


def step_kernel(lines, chunks, tables, *refs):
    count = len(chunks)
    heavy, refs = refs[:4], refs[4:]
    (in_far, state, target, weight_t, pos, patch, last, modul, fmod, head_t, cond_full, time_one), refs = refs[:12], refs[12:]
    finals, refs = refs[:4], refs[4:]
    (d_in, d_head, d_two, d_full, d_one, few_sum), scratch = refs[:6], refs[6:]
    held, by_y, by_x, by_z = (scratch[k * count : (k + 1) * count] for k in range(4))
    send, recv, zsend, zrecv, wsend, wrecv = scratch[4 * count : 4 * count + 6]
    scratch = scratch[4 * count + 6 :]
    (stage_wide, stage_tall, land_wide, land_tall, free_wide, free_tall, fetch, d_mod, d_fm, few), scratch = scratch[:10], scratch[10:]
    (
        stream, hat_one, hat_two, root_one, root_two, a_low, qkv_low, mixed, proj, b_low, active, mlp, d_mlp,
    ), scratch = scratch[:13], scratch[13:]
    (
        few_got, few_y, few_x, few_held, few_line, mod_got, fm_got, mod_sum, fm_sum, group_slot, part_own, part_slot,
        act_own, act_slot, pair_own, pair_got, line_in, line_rest, line_full,
        few_send, few_recv, group_send, group_recv, line_send, line_recv,
    ) = scratch
    (in_starts, in_tiles), (head_starts, head_tiles), (embed_starts, embed_tiles), shards = tables
    rep, shard = lax.axis_index("rep"), lax.axis_index("shard")
    place_here = lax.rem(rep, 2 * lines)
    base = rep - place_here
    x, z = lax.rem(place_here, 2), lax.div(place_here, 2)
    core, y = lax.rem(shard, 2), lax.div(shard, 2)
    to_core = (rep, shard + 1 - 2 * core)
    to_y = (rep, shard + 2 - 4 * y)
    to_x = (rep + 1 - 2 * x, shard)

    def line_peer(step):
        return (base + lax.rem(z + step, lines) * 2 + x, shard)

    barrier = pltpu.get_barrier_semaphore()
    to_far = (rep, shards - 1 - shard)
    for peer in (to_core, to_y, to_x, to_far):
        pl.semaphore_signal(barrier, inc=1, device_id=peer, device_id_type=MESH)
    for step in range(1, lines):
        pl.semaphore_signal(
            barrier, inc=1, device_id=line_peer(step), device_id_type=MESH
        )
    pl.semaphore_wait(barrier, 4 + lines - 1)

    width, tokens = head_t.shape[1], state.shape[0]
    in_blocks = [active.at[:, pl.ds(k * width, width)] for k in range(4)] + [d_mlp]

    def far_copy(k):
        return pltpu.make_async_copy(in_far.at[pl.ds(k * tokens, tokens), :], in_blocks[k], fetch.at[4 + k])

    stride = lines // PIECES
    owns = lax.rem(z, stride) == 0
    mine = lax.div(z, stride)
    def remote(source, target, send_sem, recv_sem, peer):
        return pltpu.make_async_remote_copy(
            src_ref=source,
            dst_ref=target,
            send_sem=send_sem,
            recv_sem=recv_sem,
            device_id=peer,
            device_id_type=MESH,
        )

    def rows_of(ref, start, size):
        return ref.at[pl.ds(pl.multiple_of(start, 16), size)]

    def lanes_at(index, ref, row, rows, which):
        _, _, _, lane, lanes, _ = chunks[index]
        return ref.at[
            pl.ds(pl.multiple_of(row, 16), rows), pl.ds(pl.multiple_of(lane + which * lanes, 128), lanes)
        ]

    turn = {i: sum(chunks[j][0] == 0 for j in range(i)) if chunks[i][0] == 0 else sum(chunks[j][0] != 0 for j in range(i)) for i in range(count)}

    def slot_of(i, wide, tall):
        if chunks[i][0] == 0:
            return wide.at[turn[i] % SLOTS]
        return tall.at[turn[i] % SLOTS, pl.ds(0, chunks[i][2])]

    def turn_away(i, steps):
        for j in range(count):
            if (chunks[j][0] == 0) == (chunks[i][0] == 0) and turn[j] == turn[i] + steps:
                return j
        return None

    def core_copy(i):
        return remote(
            slot_of(i, stage_wide, stage_tall), slot_of(i, land_wide, land_tall), send.at[i, 0], recv.at[i, 0], to_core
        )

    def free_of(i):
        return free_wide if chunks[i][0] == 0 else free_tall

    def y_copy(i):
        half = chunks[i][2] // 2
        return remote(
            rows_of(held[i], (1 - y) * half, half), by_y[i], send.at[i, 1], recv.at[i, 1], to_y
        )

    def x_copy(i):
        quarter = chunks[i][2] // 4
        return remote(
            rows_of(by_y[i], (1 - x) * quarter, quarter), by_x[i], send.at[i, 2], recv.at[i, 2], to_x
        )

    def z_copy(i, piece):
        size = chunks[i][2] // 4 // PIECES
        owner = piece * stride
        slot = lax.rem(z - owner - 1 + lines, lines)
        return remote(
            by_x[i].at[pl.ds(piece * size, size)],
            by_z[i].at[slot],
            zsend.at[i, piece],
            zrecv.at[i, slot],
            (base + owner * 2 + x, shard),
        )

    def final_rows(i, side, start, size, which):
        array, row, rows = chunks[i][:3]
        return lanes_at(i, finals[array], row + side * (rows // 2) + start, size, which)

    def cross_copy(i):
        quarter = chunks[i][2] // 4
        part = final_rows(i, 0, x * quarter, quarter, core)
        return remote(part, part, send.at[i, 3], recv.at[i, 3], to_y)

    def line_copy(i, which, side, step):
        size = chunks[i][2] // 4 // PIECES
        part = final_rows(i, side, (x * PIECES + mine) * size, size, core)
        return remote(
            part, part, wsend.at[i, which, step - 1], wrecv.at[i, which, mine], line_peer(step)
        )

    def line_arrival(i, which, side, piece):
        size = chunks[i][2] // 4 // PIECES
        part = final_rows(i, side, (x * PIECES + piece) * size, size, core)
        return remote(part, part, wsend.at[i, which, 0], wrecv.at[i, which, piece], to_core)

    def pair_copy(i, which, side, column):
        quarter = chunks[i][2] // 4
        part = final_rows(i, side, column * quarter, quarter, core)
        return remote(part, part, send.at[i, 4 + which], recv.at[i, 4 + which], to_x)

    def last_copy(i, which, side, half):
        rows = chunks[i][2] // 2
        part = final_rows(i, side, 0, rows, half)
        return remote(part, part, send.at[i, 6 + which], recv.at[i, 6 + which], to_core)

    def sides(i, action):
        if chunks[i][5]:

            @pl.when(y == 1)
            def _():
                action(0, 1)
                action(1, 0)

        else:
            action(0, y)

    def produce(i, left, right):
        rows, lanes = chunks[i][2], chunks[i][4]
        before, after = turn_away(i, -SLOTS), turn_away(i, SLOTS)
        if before is not None:
            core_copy(before).wait_send()
        staged = slot_of(i, stage_wide, stage_tall)

        def block(part):
            value = mxu(left[:, part], right[...], TN)
            first, second = value[:, :lanes], value[:, lanes:]
            held[i][part, :] = jnp.where(core == 0, first, second).astype(jnp.bfloat16)
            staged[part, :] = jnp.where(core == 0, second, first).astype(jnp.bfloat16)

        blocks_of(rows, 256, block)
        if before is not None:
            pl.semaphore_wait(free_of(i), 1)
        core_copy(i).start()

    def stage1(i):
        core_copy(i).wait_recv()
        add_rows(held[i], held[i], slot_of(i, land_wide, land_tall), chunks[i][2])
        if turn_away(i, SLOTS) is not None:
            pl.semaphore_signal(free_of(i), inc=1, device_id=to_core, device_id_type=MESH)

    def stage2(i):
        half = chunks[i][2] // 2
        y_copy(i).wait_recv()
        add_rows(by_y[i], by_y[i], rows_of(held[i], y * half, half), half)
        x_copy(i).start()

    def stage3(i):
        quarter = chunks[i][2] // 4
        x_copy(i).wait_recv()
        add_rows(by_x[i], by_x[i], rows_of(by_y[i], x * quarter, quarter), quarter)
        for piece in range(PIECES):

            @pl.when(z != piece * stride)
            def _():
                z_copy(i, piece).start()

    def stage4(i):
        size = chunks[i][2] // 4 // PIECES

        @pl.when(owns)
        def _():
            for slot in range(lines - 1):
                remote(
                    by_z[i].at[slot], by_z[i].at[slot], zsend.at[i, 0], zrecv.at[i, slot], to_core
                ).wait_recv()
            target = final_rows(i, y, (x * PIECES + mine) * size, size, core)

            def body(index, carry):
                total = by_x[i][
                    pl.ds(pl.multiple_of(mine * size + index * 16, 16), 16)
                ].astype(jnp.float32)
                for slot in range(lines - 1):
                    total += by_z[i][slot, pl.ds(pl.multiple_of(index * 16, 16), 16)].astype(jnp.float32)
                target[pl.ds(pl.multiple_of(index * 16, 16), 16)] = total.astype(jnp.bfloat16)
                return carry

            lax.fori_loop(0, size // 16, body, 0)
            for step in range(1, lines):
                line_copy(i, 0, y, step).start()

    def line_wait(i):
        for piece in range(PIECES):

            @pl.when(z != piece * stride)
            def _():
                line_arrival(i, 0, y, piece).wait_recv()

    def stage5(i):
        @pl.when(y == 0)
        def _():
            line_wait(i)
            cross_copy(i).start()

    def stage6(i):
        if chunks[i][5]:

            @pl.when(y == 1)
            def _():
                line_wait(i)
                pair_copy(i, 0, 1, x).start()
                cross_copy(i).wait_recv()
                pair_copy(i, 1, 0, x).start()

        else:
            line_wait(i)
            pair_copy(i, 0, y, x).start()

    def stage7(i):
        def action(which, side):
            pair_copy(i, which, side, 1 - x).wait_recv()
            last_copy(i, which, side, core).start()

        sides(i, action)

    def stage8(i):
        sides(i, lambda which, side: last_copy(i, which, side, 1 - core).wait_recv())


    mod_tiles, wide = 6 * width // 128, width // 128
    images = d_mod.shape[0]
    in_lanes, head_lanes, embed_lanes = in_tiles * 128, head_tiles * 128, embed_tiles * 128
    rest_lanes = 2 * head_lanes + embed_lanes
    head_places = [o for o in range(shards) if head_starts[o] < wide]
    mod_places = [o for o in range(shards) if in_starts[o] < mod_tiles]
    few_rows = few.shape[0] // 2
    half = pl.ds(pl.multiple_of(core * few_rows, 8), few_rows)
    other_half = pl.ds(pl.multiple_of((1 - core) * few_rows, 8), few_rows)

    def is_in(where, places):
        return functools.reduce(jnp.logical_or, [where == o for o in places])

    few_core = remote(few.at[other_half], few_got, few_send.at[0], few_recv.at[0], to_core)
    few_over_y = remote(few_held.at[0], few_y, few_send.at[1], few_recv.at[1], to_y)
    few_over_x = remote(few_held.at[1], few_x, few_send.at[2], few_recv.at[2], to_x)
    few_back = remote(few_sum.at[half], few_sum.at[half], few_send.at[3], few_recv.at[3], to_core)
    few_back_arrival = remote(few_sum.at[other_half], few_sum.at[other_half], few_send.at[3], few_recv.at[3], to_core)
    mod_core = remote(d_mod, mod_got, few_send.at[4], few_recv.at[4], to_core)
    fm_core = remote(d_fm, fm_got, few_send.at[5], few_recv.at[5], to_core)
    pair_copy_x = remote(pair_own, pair_got, few_send.at[6], few_recv.at[6], to_x)

    def few_line_copy(step):
        return remote(few_line.at[z], few_line.at[z], few_send.at[6 + step], few_recv.at[6 + step], line_peer(step))

    def few_line_arrival(step):
        origin = lax.rem(z + lines - step, lines)
        return remote(few_line.at[origin], few_line.at[origin], few_send.at[6 + step], few_recv.at[6 + step], to_core)

    def group_parts(place):
        parts = []
        tiles = min(in_tiles, mod_tiles - in_starts[place])
        if tiles > 0:
            parts.append((0, in_starts[place] * 128, 0, tiles * 128))
        first, final = max(head_starts[place], wide), min(head_starts[place] + head_tiles, 3 * wide)
        if final > first:
            lead = (first - head_starts[place]) * 128
            parts.append((1, (first - wide) * 128, in_lanes + lead, (final - first) * 128))
        return parts

    def group_copy(place, k):
        which, lane, own, lanes = group_parts(place)[k]
        return remote(
            (mod_sum, fm_sum)[which].at[:, pl.ds(lane, lanes)],
            group_slot.at[:, pl.ds(own, lanes)],
            group_send.at[k, 0],
            group_recv.at[k, 0],
            to_y,
        )

    def to_others(kind, source, slots, step):
        return remote(
            source,
            slots.at[shard],
            group_send.at[kind, step - 1],
            group_recv.at[kind, step - 1],
            (rep, lax.rem(shard + step, shards)),
        )

    def from_others(kind, slots, step):
        origin = lax.rem(shard + shards - step, shards)
        return remote(slots.at[origin], slots.at[origin], group_send.at[kind, 0], group_recv.at[kind, step - 1], to_core)

    slots_of = (line_rest, line_full, line_in)

    def line_copy_d(kind, step):
        slots = slots_of[kind]
        return remote(slots.at[z], slots.at[z], line_send.at[kind, step - 1], line_recv.at[kind, step - 1], line_peer(step))

    def line_arrival_d(kind, step):
        slots = slots_of[kind]
        origin = lax.rem(z + lines - step, lines)
        return remote(slots.at[origin], slots.at[origin], line_send.at[kind, 0], line_recv.at[kind, step - 1], to_core)

    def on_line(action):
        for step in range(1, lines):
            action(0, step)
            action(1, step)

            @pl.when(is_in(shard, mod_places))
            def _():
                action(2, step)

    def side0():
        mod_core.start()
        fm_core.start()
        few_core.start()

    def side1():
        mod_core.wait_recv()
        mod_sum[...] = d_mod[...] + mod_got[...]
        fm_core.wait_recv()
        fm_sum[...] = d_fm[...] + fm_got[...]
        for place in range(shards):

            @pl.when(to_y[1] == place)
            def _():
                for k in range(len(group_parts(place))):
                    group_copy(place, k).start()

        few_core.wait_recv()
        few_held[0] = few[half] + few_got[...]
        few_over_y.start()

    def side2():
        pair_own[...] = jnp.zeros_like(pair_own)
        for place in range(shards):

            @pl.when(shard == place)
            def _():
                for k, (which, lane, own, lanes) in enumerate(group_parts(place)):
                    group_copy(place, k).wait_recv()
                    pair_own[:, own : own + lanes] = (
                        (mod_sum, fm_sum)[which][:, lane : lane + lanes] + group_slot[:, own : own + lanes]
                    )

        part_own[...] = jnp.dot(
            pair_own[:, in_lanes : in_lanes + head_lanes].astype(jnp.bfloat16),
            head_t[...],
            preferred_element_type=jnp.float32,
        )

        @pl.when(is_in(shard, mod_places))
        def _():
            for k in range(len(in_blocks)):
                far_copy(k).wait()
                lanes = pair_own[:, k * tokens : (k + 1) * tokens].astype(jnp.bfloat16)
                part_own[...] += jnp.dot(lanes, in_blocks[k][...], preferred_element_type=jnp.float32)

        part_slot[shard] = part_own[...]
        for step in range(1, shards):
            to_others(2, part_own, part_slot, step).start()
        few_over_y.wait_recv()
        few_held[1] = few_held[0] + few_y[...]
        few_over_x.start()

    def side3():
        for step in range(1, shards):
            from_others(2, part_slot, step).wait_recv()
        d_cond = functools.reduce(jnp.add, [part_slot[o] for o in range(shards)])
        value = cond_full[pl.ds(pl.multiple_of(place_here * images, 8), images), :]
        gate = jax.nn.sigmoid(value)
        d_value = d_cond * (gate + value * gate * (1.0 - gate))
        for place in range(shards):

            @pl.when(shard == place)
            def _():
                first = embed_starts[place] * 128
                pair_own[:, in_lanes + rest_lanes :] = d_value[:, first : first + embed_lanes]
                if place in head_places:
                    lanes = min(head_tiles, wide - head_starts[place]) * 128
                    first = head_starts[place] * 128
                    start = in_lanes + head_lanes
                    d_two_own = d_value[:, first : first + lanes].astype(jnp.bfloat16)
                    pair_own[:, start : start + lanes] = d_two_own.astype(jnp.float32)
                    act_own[...] = jnp.dot(d_two_own, head_t[:lanes, :], preferred_element_type=jnp.float32)
                    act_slot[shard] = act_own[...]
                    for step in range(1, shards):
                        to_others(3, act_own, act_slot, step).start()

        few_over_x.wait_recv()
        few_line[z] = few_held[1] + few_x[...]
        for step in range(1, lines):
            few_line_copy(step).start()

    def side4():
        for step in range(1, shards):

            @pl.when(is_in(lax.rem(shard + shards - step, shards), head_places))
            def _():
                from_others(3, act_slot, step).wait_recv()

        value = time_one[pl.ds(pl.multiple_of(place_here * images, 8), images), :]
        gate = jax.nn.sigmoid(value)
        slope = gate + value * gate * (1.0 - gate)
        for place in range(shards):

            @pl.when(shard == place)
            def _():
                first = embed_starts[place] * 128
                d_act = functools.reduce(jnp.add, [act_slot[o, :, first : first + embed_lanes] for o in head_places])
                start = in_lanes + 2 * head_lanes
                pair_own[:, start : start + embed_lanes] = (slope * d_act).astype(jnp.bfloat16).astype(jnp.float32)

        pair_copy_x.start()
        for step in range(1, lines):
            few_line_arrival(step).wait_recv()
        few_sum[half] = functools.reduce(jnp.add, [few_line[at] for at in range(lines)])
        few_back.start()

    def side5():
        pair_copy_x.wait_recv()
        own, got = pair_own[...], pair_got[...]
        both = jnp.concatenate([jnp.where(x == 0, own, got), jnp.where(x == 0, got, own)], 0)
        line_in[z] = both[:, :in_lanes].astype(jnp.bfloat16)
        line_rest[z] = both[:, in_lanes : in_lanes + rest_lanes].astype(jnp.bfloat16)
        line_full[z] = both[:, in_lanes + rest_lanes :]
        on_line(lambda kind, step: line_copy_d(kind, step).start())

    def side6():
        on_line(lambda kind, step: line_arrival_d(kind, step).wait_recv())
        for at in range(lines):
            span = slice(at * 2 * images, (at + 1) * 2 * images)
            d_head[span, :] = line_rest[at, :, :head_lanes]
            d_two[span, :] = line_rest[at, :, head_lanes : 2 * head_lanes]
            d_one[span, :] = line_rest[at, :, 2 * head_lanes :]
            d_full[span, :] = line_full[at]
        d_in[...] = jnp.zeros_like(d_in)

        @pl.when(is_in(shard, mod_places))
        def _():
            for at in range(lines):
                d_in[at * 2 * images : (at + 1) * 2 * images, :] = line_in[at]

        few_back_arrival.wait_recv()

    def side_end():
        for copy in (few_core, few_over_y, few_over_x, few_back, mod_core, fm_core, pair_copy_x):
            copy.wait_send()
        for step in range(1, lines):
            few_line_copy(step).wait_send()
        on_line(lambda kind, step: line_copy_d(kind, step).wait_send())
        for place in range(shards):

            @pl.when(to_y[1] == place)
            def _():
                for k in range(len(group_parts(place))):
                    group_copy(place, k).wait_send()

        for step in range(1, shards):
            to_others(2, part_own, part_slot, step).wait_send()

        @pl.when(is_in(shard, head_places))
        def _():
            for step in range(1, shards):
                to_others(3, act_own, act_slot, step).wait_send()

    beside = (side0, side1, side2, side3, side4, side5, side6)
    low = jnp.bfloat16
    per = tokens // TOK
    row = [shard * per + image for image in range(per)]
    span = [pl.ds(image * TOK, TOK) for image in range(per)]
    cut = 256

    def piece(ref, image, index):
        return ref[pl.ds(row[image], 1), pl.ds(index * width, width)]

    def normed(value):
        center = value - jnp.mean(value, -1, keepdims=True)
        root = lax.rsqrt(jnp.mean(center * center, -1, keepdims=True) + eps_norm)
        return center * root, root

    def norm_back(d_hat, hat, root):
        return root * (d_hat - jnp.mean(d_hat, -1, keepdims=True) - hat * jnp.mean(d_hat * hat, -1, keepdims=True))

    def put_row(ref, image, index, value):
        ref[pl.ds(row[image], 1), pl.ds(index * width, width)] = (
            jnp.sum(value, 0, keepdims=True).astype(low).astype(jnp.float32)
        )

    fc2, fc1, attn_out, qkv = finals

    def load(k):
        return pltpu.make_async_copy(heavy[k], finals[k], fetch.at[k])

    for k in (3, 2, 1, 0):
        load(k).start()
    d_mod[...] = jnp.zeros_like(d_mod)
    d_fm[...] = jnp.zeros_like(d_fm)

    for image in range(per):
        value = mxu(state[span[image], :], patch[...], NN) + pos[...]
        stream[span[image], :] = value
        hat, root = normed(value)
        hat_one[span[image], :] = hat
        root_one[span[image], :] = root
        a_low[span[image], :] = (hat * (1.0 + piece(modul, image, 1)) + piece(modul, image, 0)).astype(low)

    def qkv_block(part):
        qkv_low[:, part] = mxu(a_low[...], qkv[part, :], NT).astype(low)

    load(3).wait()
    blocks_of(3 * width, cut, qkv_block)
    load(2).wait()
    lane = lax.broadcasted_iota(jnp.int32, (TOK, 128), 1)
    first = lane < 64
    scale = 0.125

    def softmax(query, key):
        score = mxu(query, key, NT) * scale
        expo = jnp.exp(score - jnp.max(score, -1, keepdims=True))
        return expo / jnp.sum(expo, -1, keepdims=True)

    def take(ref, image, start):
        return ref[span[image], pl.ds(pl.multiple_of(start, 128), 128)]

    def attend(pair, carry):
        for image in range(per):
            query, key, value = (take(qkv_low, image, index * width + pair * 128) for index in range(3))
            outs = []
            for side in (first, jnp.logical_not(first)):
                probs = softmax(jnp.where(side, query, jnp.zeros_like(query)), key)
                outs.append(mxu(probs.astype(low), value, NN))
            mixed[span[image], pl.ds(pl.multiple_of(pair * 128, 128), 128)] = jnp.where(first, outs[0], outs[1]).astype(low)
        return carry

    lax.fori_loop(0, width // 128, attend, 0)
    for image in range(per):
        got = mxu(mixed[span[image], :], attn_out[...], NT)
        proj[span[image], :] = got
        value = stream[span[image], :] + piece(modul, image, 2) * got
        stream[span[image], :] = value
        hat, root = normed(value)
        hat_two[span[image], :] = hat
        root_two[span[image], :] = root
        b_low[span[image], :] = (hat * (1.0 + piece(modul, image, 4)) + piece(modul, image, 3)).astype(low)

    def upper_block(part):
        value = mxu(b_low[...], fc1[part, :], NT)
        active[:, part] = (
            0.5 * value * (1.0 + jnp.tanh(0.7978845608 * (value + 0.044715 * value * value * value)))
        ).astype(low)

    load(1).wait()
    blocks_of(4 * width, cut, upper_block)
    load(0).wait()

    def mlp_block(part):
        mlp[:, part] = mxu(active[...], fc2[part, :], NT)

    blocks_of(width, cut, mlp_block)
    loss = jnp.zeros((), jnp.float32)
    g_last = jnp.zeros((PATCH, width), jnp.float32)
    for image in range(per):
        value = stream[span[image], :] + piece(modul, image, 5) * mlp[span[image], :]
        hat, root = normed(value)
        gain = 1.0 + piece(fmod, image, 1)
        final = (hat * gain + piece(fmod, image, 0)).astype(low)
        diff = mxu(final, last[...], NT) - target[span[image], :]
        share = weight_t[span[image], :] * diff
        loss += 0.5 * jnp.sum(share * diff)
        d_out = share.astype(low)
        g_last += mxu(d_out, final, TN)
        d_final = mxu(d_out, last[...], NN)
        put_row(d_fm, image, 0, d_final)
        put_row(d_fm, image, 1, d_final * hat)
        d_value = norm_back(d_final * gain, hat, root)
        stream[span[image], :] = d_value
        put_row(d_mod, image, 5, d_value * mlp[span[image], :])
        d_mlp[span[image], :] = (piece(modul, image, 5) * d_value).astype(low)
    few[pl.ds(PATCH, 8), :] = jnp.full((8, width), loss, jnp.float32)
    few[pl.ds(PATCH + 8, PATCH), :] = g_last
    few[pl.ds(2 * PATCH + 8, 8), :] = jnp.zeros((8, width), jnp.float32)

    of_fc2 = [i for i in range(count) if chunks[i][0] == 0]
    of_fc1 = [i for i in range(count) if chunks[i][0] == 1]
    of_o = [i for i in range(count) if chunks[i][0] == 2]
    of_qkv = [i for i in range(count) if chunks[i][0] == 3]

    def fc2_step(i):
        first, lanes = chunks[i][3], 2 * chunks[i][4]
        part = pl.ds(first, lanes)
        value = mxu(b_low[...], fc1[part, :], NT)
        inner = jnp.tanh(0.7978845608 * (value + 0.044715 * value * value * value))
        slope = 0.5 * (1.0 + inner) + 0.5 * value * (1.0 - inner * inner) * 0.7978845608 * (
            1.0 + 3.0 * 0.044715 * value * value
        )
        d_upper = (slope * mxu(d_mlp[...], fc2[:, part], NN)).astype(low)
        produce(i, d_mlp, active.at[:, part])
        active[:, part] = d_upper

    def fc1_step(i):
        part = pl.ds(chunks[i][1], chunks[i][2])
        more = mxu(active[:, part], fc1[part, :], NN)
        if i == of_fc1[0]:
            mlp[...] = more
        else:
            mlp[...] += more
        produce(i, active.at[:, part], b_low)

    def o_step(i):
        for image in range(per):
            d_normed = mlp[span[image], :]
            hat = hat_two[span[image], :]
            put_row(d_mod, image, 3, d_normed)
            put_row(d_mod, image, 4, d_normed * hat)
            d_value = stream[span[image], :] + norm_back(
                d_normed * (1.0 + piece(modul, image, 4)), hat, root_two[span[image], :]
            )
            stream[span[image], :] = d_value
            put_row(d_mod, image, 2, d_value * proj[span[image], :])
            b_low[span[image], :] = (piece(modul, image, 2) * d_value).astype(low)
        active[:, pl.ds(0, width)] = mxu(b_low[...], attn_out[...], NN).astype(low)
        produce(i, b_low, mixed)

    def attend_back(pair):
        for image in range(per):
            query, key, value = (take(qkv_low, image, index * width + pair * 128) for index in range(3))
            d_out = take(active, image, pair * 128)
            d_query, d_key, d_value = [], [], []
            for side in (first, jnp.logical_not(first)):
                none = jnp.zeros_like(query)
                probs = softmax(jnp.where(side, query, none), key)
                d_prob = mxu(jnp.where(side, d_out, none), value, NT)
                d_score = (probs * (d_prob - jnp.sum(probs * d_prob, -1, keepdims=True))).astype(low)
                d_value.append(mxu(probs.astype(low), d_out, TN))
                d_query.append(mxu(d_score, key, NN) * scale)
                d_key.append(mxu(d_score, query, TN) * scale)
            for index, both in enumerate((d_query, d_key, d_value)):
                qkv_low[span[image], pl.ds(pl.multiple_of(index * width + pair * 128, 128), 128)] = jnp.where(
                    first, both[0], both[1]
                ).astype(low)

    def norm_one_step():
        @pl.when(is_in(shard, mod_places))
        def _():
            for k in range(len(in_blocks)):
                far_copy(k).start()

        g_patch = jnp.zeros((PATCH, width), jnp.float32)
        for image in range(per):
            d_normed = mxu(qkv_low[span[image], :], qkv[...], NN)
            hat = hat_one[span[image], :]
            put_row(d_mod, image, 0, d_normed)
            put_row(d_mod, image, 1, d_normed * hat)
            d_value = stream[span[image], :] + norm_back(
                d_normed * (1.0 + piece(modul, image, 1)), hat, root_one[span[image], :]
            )
            g_patch += mxu(state[span[image], :], d_value.astype(low), TN)
        few[pl.ds(0, PATCH), :] = g_patch

    def qkv_step(i):
        if i == of_qkv[0]:
            norm_one_step()
        produce(i, qkv_low.at[:, pl.ds(chunks[i][1], chunks[i][2])], a_low)

    def over_y(i):
        y_copy(i).start()

    stages = (None, stage1, stage2, stage3, stage4, stage5, stage6, stage7, stage8, over_y)
    steps = [(fc2_step, i) for i in of_fc2] + [(fc1_step, i) for i in of_fc1] + [(o_step, i) for i in of_o]
    steps += [(attend_back, pair) for pair in range(width // 128)] + [(qkv_step, i) for i in of_qkv]
    for j, (k, i) in enumerate(ORDER):
        if j in BESIDE_AT:
            beside[BESIDE_AT.index(j)]()
        if k == 0:
            step, arg = steps[i]
            step(arg)
        else:
            stages[k](i)

    side_end()
    for i in range(count):
        if turn_away(i, SLOTS) is None:
            core_copy(i).wait_send()
        y_copy(i).wait_send()
        x_copy(i).wait_send()
        for piece in range(PIECES):

            @pl.when(z != piece * stride)
            def _():
                z_copy(i, piece).wait_send()

        if chunks[i][5]:

            @pl.when(y == 0)
            def _():
                cross_copy(i).wait_send()

        @pl.when(owns)
        def _():
            for step in range(1, lines):
                line_copy(i, 0, y, step).wait_send()

        def action(which, side):
            pair_copy(i, which, side, x).wait_send()
            last_copy(i, which, side, core).wait_send()

        sides(i, action)


def step_call(lines, tables, images, heavy, in_t, light):
    width = heavy[2].shape[0]
    chunks = heavy_chunks(width)
    count = len(chunks)
    low, full = jnp.bfloat16, jnp.float32
    (_, in_tiles), (_, head_tiles), (_, embed_tiles), shards = tables
    state, modul, fmod, cond_full = light[0], light[6], light[7], light[9]
    tokens, group, rows = state.shape[0], modul.shape[0], cond_full.shape[0]
    in_lanes, head_lanes, embed_lanes = in_tiles * 128, head_tiles * 128, embed_tiles * 128
    rest_lanes = 2 * head_lanes + embed_lanes
    few = (2 * PATCH + 16, width)
    few_half = (few[0] // 2, width)
    pair = (group, in_lanes + rest_lanes + embed_lanes)
    sizes = [(part_rows, part_lanes) for _, _, part_rows, _, part_lanes, _ in chunks]
    wide = [item for item, chunk in zip(sizes, chunks) if chunk[0] == 0][0]
    tall = max(item for item, chunk in zip(sizes, chunks) if chunk[0] != 0)
    dma = pltpu.SemaphoreType.DMA
    shapes = [(item.shape, low) for item in heavy] + [
        ((rows, in_lanes), low),
        ((rows, head_lanes), low),
        ((rows, head_lanes), low),
        ((rows, embed_lanes), full),
        ((rows, embed_lanes), low),
        (few, full),
    ]
    pass_scratch = [
        ((tokens, width), full),
        ((tokens, width), full),
        ((tokens, width), full),
        ((tokens, 1), full),
        ((tokens, 1), full),
        ((tokens, width), low),
        ((tokens, 3 * width), low),
        ((tokens, width), low),
        ((tokens, width), full),
        ((tokens, width), low),
        ((tokens, 4 * width), low),
        ((tokens, width), full),
        ((tokens, width), low),
    ]
    scratch = [
        (few_half, full),
        (few_half, full),
        (few_half, full),
        ((2,) + few_half, full),
        ((lines,) + few_half, full),
        (modul.shape, full),
        (fmod.shape, full),
        (modul.shape, full),
        (fmod.shape, full),
        ((group, in_lanes + head_lanes), full),
        ((group, width), full),
        ((shards, group, width), full),
        ((group, width), full),
        ((shards, group, width), full),
        (pair, full),
        (pair, full),
        ((lines, 2 * group, in_lanes), low),
        ((lines, 2 * group, rest_lanes), low),
        ((lines, 2 * group, embed_lanes), full),
    ]
    vmem, anywhere = pl.BlockSpec(memory_space=pltpu.VMEM), pl.BlockSpec(memory_space=pl.ANY)
    return pl.pallas_call(
        functools.partial(step_kernel, lines, chunks, tables),
        out_shape=[jax.ShapeDtypeStruct(*item) for item in shapes],
        in_specs=[anywhere] * 5 + [vmem] * len(light),
        out_specs=[vmem] * len(shapes),
        scratch_shapes=[pltpu.VMEM((r, c), low) for r, c in sizes]
        + [pltpu.VMEM((r // 2, c), low) for r, c in sizes]
        + [pltpu.VMEM((r // 4, c), low) for r, c in sizes]
        + [pltpu.VMEM((lines - 1, r // 4 // PIECES, c), low) for r, c in sizes]
        + [
            dma((count, 8)),
            dma((count, 8)),
            dma((count, PIECES)),
            dma((count, lines - 1)),
            dma((count, 2, lines - 1)),
            dma((count, 2, PIECES)),
        ]
        + [pltpu.VMEM((SLOTS,) + item, low) for item in (wide, tall)] * 2
        + [pltpu.SemaphoreType.REGULAR, pltpu.SemaphoreType.REGULAR, dma((9,))]
        + [pltpu.VMEM(*item) for item in ((modul.shape, full), (fmod.shape, full), (few, full))]
        + [pltpu.VMEM(*item) for item in pass_scratch]
        + [pltpu.VMEM(*item) for item in scratch]
        + [
            dma((lines + 6,)),
            dma((lines + 6,)),
            dma((4, shards - 1)),
            dma((4, shards - 1)),
            dma((3, lines - 1)),
            dma((3, lines - 1)),
        ],
        compiler_params=pltpu.CompilerParams(
            collective_id=1, has_side_effects=True, vmem_limit_bytes=64 * 1024 * 1024 - 65536
        ),
    )(*heavy, in_t, *light)


def placed_traits(traits, lanes):
    lead = -(-(PATCH + FREQ) // 128) * 128
    lane = lax.broadcasted_iota(jnp.int32, (traits.shape[0], lead), 1)
    here = jnp.logical_and(lane >= PATCH, lane < PATCH + FREQ)
    freq = jnp.where(here, traits[:, :lead], 0.0).astype(jnp.bfloat16)
    named = lax.broadcasted_iota(jnp.int32, (traits.shape[0], lanes), 1).astype(jnp.float32)
    onehot = jnp.where(named == traits[:, lead : lead + 1], 1.0, 0.0).astype(jnp.bfloat16)
    return freq, onehot


def windows(cols, shards):
    starts = [place * cols // 128 for place in range(shards)]
    tiles = max(-(-(place + 1) * cols // 128) - start for place, start in enumerate(starts))
    return starts, tiles


def heavy_segments(width, in_cols, in_starts, out_rows, shards):
    every = []
    for place in range(shards):
        parts = []
        for array, low, high, most in ((3, 6 * width, 9 * width, 640), (1, 9 * width, 13 * width, 640)):
            first, last = max(low, place * in_cols), min(high, (place + 1) * in_cols)
            while first < last:
                rows = min(most, last - first)
                parts.append((0, first - in_starts[place] * 128, array, first - low, rows, 0, 0, width))
                first += rows
            if array == 3:
                parts.append((1, 0, 2, place * out_rows, out_rows, 0, 0, width))
        parts.append((1, 0, 0, place * out_rows, out_rows, width, 0, 4 * width))
        every.append(parts)
    return every


def gather_kernel(
    plan, in_t, out_t, head_t, embed, traits,
    fc2, fc1, attn_out, qkv, cond_full, time_act, time_one, modul, fmod, patch, last, all_traits,
    s1_slot, tab_slot, patch_slot, two_slot, two_own, mod_slot, mod_own, fm_slot, fm_own, last_own,
    ysend, yrecv, xsend, xrecv, zsend, zrecv, csend, crecv, osend, orecv, small_send, small_recv, local_sem,
    trait_slot, trait_own, trait_got, line_slot, trait_send, trait_recv,
):
    segments, (in_starts, in_tiles), (head_starts, head_tiles), (embed_starts, embed_tiles), lines = plan
    shards = len(segments)
    arrays = (fc2, fc1, attn_out, qkv)
    sources = (in_t, out_t)
    rep, shard = lax.axis_index("rep"), lax.axis_index("shard")
    place_here = lax.rem(rep, 2 * lines)
    x, z = lax.rem(place_here, 2), lax.div(place_here, 2)
    zb = lax.rem(z, 2)
    core, y = lax.rem(shard, 2), lax.div(shard, 2)
    to_core = (rep, shard + 1 - 2 * core)
    to_y = (rep, shard + 2 - 4 * y)
    to_x = (rep + 1 - 2 * x, shard)
    to_z = (rep + 2 - 4 * zb, shard)
    width = head_t.shape[1]

    barrier = pltpu.get_barrier_semaphore()
    others = [(rep, lax.rem(shard + step, shards)) for step in range(1, shards)]

    def line_peer(step):
        return (rep - place_here + lax.rem(z + step, lines) * 2 + x, shard)

    for peer in others + [to_x] + [line_peer(step) for step in range(1, lines)]:
        pl.semaphore_signal(barrier, inc=1, device_id=peer, device_id_type=MESH)
    pl.semaphore_wait(barrier, shards + lines - 1)

    def remote(source, target, send_sem, recv_sem, peer):
        return pltpu.make_async_remote_copy(
            src_ref=source, dst_ref=target, send_sem=send_sem, recv_sem=recv_sem, device_id=peer, device_id_type=MESH
        )

    def small(kind, source, slots, step):
        return remote(
            source, slots.at[shard], small_send.at[kind, step - 1], small_recv.at[kind, step - 1], others[step - 1]
        )

    def small_arrival(kind, slots, step):
        origin = lax.rem(shard + shards - step, shards)
        return remote(
            slots.at[origin], slots.at[origin], small_send.at[kind, step - 1], small_recv.at[kind, step - 1], to_core
        )

    def exchange(kind, source, slots, origins=None):
        for step in range(1, shards):
            if origins is None:
                small(kind, source, slots, step).start()
            else:
                sends = functools.reduce(jnp.logical_or, [shard == o for o in origins])

                @pl.when(sends)
                def _():
                    small(kind, source, slots, step).start()

    def arrive(kind, slots, origins=None):
        for step in range(1, shards):
            if origins is None:
                small_arrival(kind, slots, step).wait_recv()
            else:
                origin = lax.rem(shard + shards - step, shards)

                @pl.when(functools.reduce(jnp.logical_or, [origin == o for o in origins]))
                def _():
                    small_arrival(kind, slots, step).wait_recv()

    def sent(kind, source, slots, origins=None):
        for step in range(1, shards):
            if origins is None:
                small(kind, source, slots, step).wait_send()
            else:

                @pl.when(functools.reduce(jnp.logical_or, [shard == o for o in origins]))
                def _():
                    small(kind, source, slots, step).wait_send()

    def place_tiles(target, slots, starts, tiles, origins, dtype, first=0):
        total = target.shape[1] // 128
        for tile in range(total):
            parts = [
                slots[o, :, (tile + first - starts[o]) * 128 : (tile + first - starts[o] + 1) * 128]
                for o in origins
                if 0 <= tile + first - starts[o] < tiles
            ]
            target[:, tile * 128 : (tile + 1) * 128] = functools.reduce(jnp.add, parts).astype(dtype)

    def source_part(place, k):
        source, row, array, _, rows, lane, _, lanes = segments[place][k]
        return sources[source].at[pl.ds(row, rows), pl.ds(lane, lanes)]

    def target_part(place, k, start=0, rows=None):
        _, _, array, row, total, _, lane, lanes = segments[place][k]
        start = row + start
        if not isinstance(start, int):
            start = pl.multiple_of(start, 16)
        return arrays[array].at[pl.ds(start, total if rows is None else rows), pl.ds(lane, lanes)]

    def quarter(place, k, index):
        size = segments[place][k][4] // 4
        return target_part(place, k, index * size, size)

    def half_of(place, k, index, second):
        size = segments[place][k][4] // 4
        cut = -(-size // 32) * 16
        return target_part(place, k, index * size + (cut if second else 0), size - cut if second else cut)

    me = x * 2 + zb
    across_x, along_z, corner = (1 - x) * 2 + zb, x * 2 + 1 - zb, (1 - x) * 2 + 1 - zb

    def y_copy(place, k):
        size = segments[place][k][4] // 4
        source, row, _, _, _, lane, _, lanes = segments[place][k]
        part = sources[source].at[pl.ds(pl.multiple_of(row + me * size, 16), size), pl.ds(lane, lanes)]
        return remote(part, quarter(place, k, me), ysend.at[k], yrecv.at[k], to_y)

    def owner_copy(place, k):
        return remote(source_part(place, k), target_part(place, k), osend.at[k], orecv.at[k], to_core)

    def own_copy(place, k):
        return pltpu.make_async_copy(source_part(place, k), target_part(place, k), local_sem.at[k])

    def hop(part, sems, k, slot, peer):
        return remote(part, part, sems[0].at[k, slot], sems[1].at[k, slot], peer)

    xs, zs, cs = (xsend, xrecv), (zsend, zrecv), (csend, crecv)

    def begin(k, across):
        for place in range(shards):
            if k < len(segments[place]):

                @pl.when(shard == place)
                def _():
                    if across:
                        y_copy(place, k).start()
                    else:
                        owner_copy(place, k).start()
                        own_copy(place, k).start()

    def relay(place, stage, k):
        if stage == 0:
            y_copy(place, k).wait_recv()
            hop(quarter(place, k, me), xs, k, 0, to_x).start()
            hop(quarter(place, k, me), zs, k, 0, to_z).start()
            hop(quarter(place, k, me), cs, k, 0, to_core).start()
        elif stage == 1:
            hop(quarter(place, k, across_x), xs, k, 0, to_x).wait_recv()
            hop(half_of(place, k, across_x, False), zs, k, 1, to_z).start()
            hop(quarter(place, k, along_z), zs, k, 0, to_z).wait_recv()
            hop(half_of(place, k, along_z, True), xs, k, 1, to_x).start()
            hop(quarter(place, k, across_x), cs, k, 1, to_core).start()
            hop(quarter(place, k, along_z), cs, k, 2, to_core).start()
        else:
            hop(half_of(place, k, corner, False), zs, k, 1, to_z).wait_recv()
            hop(half_of(place, k, corner, True), xs, k, 1, to_x).wait_recv()
            hop(quarter(place, k, corner), cs, k, 3, to_core).start()

    def relay_tick(tick):
        for place in range(shards):

            @pl.when(to_y[1] == place)
            def _():
                for stage in range(3):
                    if 0 <= tick - stage < len(segments[place]):
                        relay(place, stage, tick - stage)

    def trait_line(step):
        return remote(
            line_slot.at[z], line_slot.at[z], trait_send.at[step], trait_recv.at[step], line_peer(step)
        )

    def trait_line_arrival(step):
        origin = lax.rem(z + lines - step, lines)
        return remote(line_slot.at[origin], line_slot.at[origin], trait_send.at[step], trait_recv.at[step], to_core)

    trait_pair = remote(trait_own, trait_got, trait_send.at[0], trait_recv.at[0], to_x)
    trait_slot[shard] = traits[...]
    exchange(7, traits, trait_slot)
    begin(0, True)
    arrive(7, trait_slot)
    trait_own[...] = functools.reduce(jnp.add, [trait_slot[o] for o in range(shards)])
    trait_pair.start()
    begin(1, True)
    trait_pair.wait_recv()
    own, got = trait_own[...], trait_got[...]
    line_slot[z] = jnp.concatenate([jnp.where(x == 0, own, got), jnp.where(x == 0, got, own)], 0)
    for step in range(1, lines):
        trait_line(step).start()
    relay_tick(0)
    begin(2, True)
    for step in range(1, lines):
        trait_line_arrival(step).wait_recv()
    count_in_line = 2 * traits.shape[0]
    for at in range(lines):
        all_traits[at * count_in_line : (at + 1) * count_in_line, :] = line_slot[at]
    freq, onehot = placed_traits(all_traits[...], embed.shape[1])

    nt = (((1,), (1,)), ((), ()))
    own_one = lax.dot_general(freq, embed[:, : freq.shape[1]], nt, preferred_element_type=jnp.float32)
    time_one[...] = own_one
    s1_slot[shard] = (own_one * jax.nn.sigmoid(own_one)).astype(jnp.bfloat16)
    tab_slot[shard] = lax.dot_general(onehot, embed[...], nt, preferred_element_type=jnp.float32)
    eye = lax.broadcasted_iota(jnp.int32, (PATCH, 128), 0) == lax.broadcasted_iota(jnp.int32, (PATCH, 128), 1)
    eye = jnp.where(eye, 1.0, 0.0).astype(jnp.bfloat16)
    patch_slot[shard] = lax.dot_general(eye, embed[:, :128], nt, preferred_element_type=jnp.float32).astype(jnp.bfloat16)
    exchange(0, s1_slot.at[shard], s1_slot)
    exchange(1, tab_slot.at[shard], tab_slot)
    exchange(2, patch_slot.at[shard], patch_slot)
    relay_tick(1)
    begin(3, True)
    last_place = [o for o in range(shards) if 0 <= 3 * width // 128 - head_starts[o] < head_tiles][-1]
    last_row = (3 * width // 128 - head_starts[last_place]) * 128
    last_own[...] = head_t[last_row : last_row + 16, :]

    @pl.when(shard == last_place)
    def _():
        last[...] = last_own[...]
        for step in range(1, shards):
            remote(last_own, last, small_send.at[6, step - 1], small_recv.at[6, 0], others[step - 1]).start()

    head_places = [o for o in range(shards) if head_starts[o] * 128 < width]
    fm_places = [o for o in range(shards) if (head_starts[o] + head_tiles) * 128 > width]
    mod_places = [o for o in range(shards) if in_starts[o] * 128 < 6 * width]
    group = modul.shape[0]

    arrive(0, s1_slot)
    place_tiles(time_act, s1_slot, embed_starts, embed_tiles, range(shards), jnp.bfloat16)
    two_own[...] = lax.dot_general(time_act[...], head_t[...], nt, preferred_element_type=jnp.float32)
    two_slot[shard] = two_own[...]
    exchange(3, two_own, two_slot, head_places)
    relay_tick(2)
    begin(4, True)
    arrive(1, tab_slot)
    arrive(3, two_slot, head_places)
    place_tiles(cond_full, tab_slot, embed_starts, embed_tiles, range(shards), jnp.float32)
    for tile in range(width // 128):
        span = slice(tile * 128, (tile + 1) * 128)
        for o in head_places:
            if 0 <= tile - head_starts[o] < head_tiles:
                cond_full[:, span] += two_slot[o, :, (tile - head_starts[o]) * 128 : (tile - head_starts[o] + 1) * 128]
    mine = cond_full[pl.ds(pl.multiple_of(place_here * group, 8), group), :]
    cond = (mine * jax.nn.sigmoid(mine)).astype(jnp.bfloat16)
    mod_own[...] = lax.dot_general(cond, in_t[...], nt, preferred_element_type=jnp.float32)
    mod_slot[shard] = mod_own[...]
    exchange(4, mod_own, mod_slot, mod_places)
    fm_own[...] = lax.dot_general(cond, head_t[...], nt, preferred_element_type=jnp.float32)
    fm_slot[shard] = fm_own[...]
    exchange(5, fm_own, fm_slot, fm_places)
    relay_tick(3)
    begin(5, True)
    begin(0, False)
    begin(1, False)
    begin(2, False)
    begin(3, False)
    begin(4, False)
    begin(5, False)
    arrive(2, patch_slot)
    place_tiles(patch, patch_slot, embed_starts, embed_tiles, range(shards), jnp.bfloat16)
    arrive(4, mod_slot, mod_places)
    arrive(5, fm_slot, fm_places)
    place_tiles(modul, mod_slot, in_starts, in_tiles, mod_places, jnp.float32)
    place_tiles(fmod, fm_slot, head_starts, head_tiles, fm_places, jnp.float32, width // 128)
    relay_tick(4)
    relay_tick(5)
    relay_tick(6)
    relay_tick(7)

    for place in range(shards):
        count = len(segments[place])

        @pl.when(shard == place)
        def _():
            for k in range(count):
                y_copy(place, k).wait_send()
                owner_copy(place, k).wait_send()
                own_copy(place, k).wait()

        @pl.when(to_core[1] == place)
        def _():
            for k in range(count):
                remote(target_part(place, k), target_part(place, k), osend.at[k], orecv.at[k], to_core).wait_recv()

        @pl.when(to_y[1] == place)
        def _():
            for k in range(count):
                hop(quarter(place, k, me), xs, k, 0, to_x).wait_send()
                hop(quarter(place, k, me), zs, k, 0, to_z).wait_send()
                hop(half_of(place, k, across_x, False), zs, k, 1, to_z).wait_send()
                hop(half_of(place, k, along_z, True), xs, k, 1, to_x).wait_send()
                for slot, index in enumerate((me, across_x, along_z, corner)):
                    hop(quarter(place, k, index), cs, k, slot, to_core).wait_send()

        @pl.when(shards - 1 - shard == place)
        def _():
            for k in range(count):
                for slot, index in enumerate((me, across_x, along_z, corner)):
                    remote(
                        quarter(place, k, index), quarter(place, k, index), csend.at[k, slot], crecv.at[k, slot], to_core
                    ).wait_recv()

    trait_pair.wait_send()
    for step in range(1, lines):
        trait_line(step).wait_send()
    sent(7, traits, trait_slot)
    sent(0, s1_slot.at[shard], s1_slot)
    sent(1, tab_slot.at[shard], tab_slot)
    sent(2, patch_slot.at[shard], patch_slot)
    sent(3, two_own, two_slot, head_places)
    sent(4, mod_own, mod_slot, mod_places)
    sent(5, fm_own, fm_slot, fm_places)

    @pl.when(shard == last_place)
    def _():
        for step in range(1, shards):
            remote(last_own, last, small_send.at[6, step - 1], small_recv.at[6, 0], others[step - 1]).wait_send()

    @pl.when(shard != last_place)
    def _():
        remote(last_own, last, small_send.at[6, 0], small_recv.at[6, 0], to_core).wait_recv()


def gather_call(in_t, out_t, head_t, embed_t, traits, shards, lines):
    place = lax.axis_index("shard")
    width = head_t.shape[1]
    low, full = jnp.bfloat16, jnp.float32

    def window(item_t, starts, tiles, lanes):
        rows = item_t.shape[0]
        offsets = [o * rows - start * 128 for o, start in enumerate(starts)]
        most = max(offsets)
        padded = jnp.pad(item_t, ((most, tiles * 128 - rows), (0, lanes - item_t.shape[1])))
        begin = most - jnp.asarray(offsets, jnp.int32)[place]
        return lax.dynamic_slice_in_dim(padded, begin, tiles * 128, 0).astype(low)

    in_cols, head_cols, embed_cols = in_t.shape[0], head_t.shape[0], embed_t.shape[0]
    in_starts, in_tiles = windows(in_cols, shards)
    head_starts, head_tiles = windows(head_cols, shards)
    embed_starts, embed_tiles = windows(embed_cols, shards)
    in_t = window(in_t, in_starts, in_tiles, width)
    head_t = window(head_t, head_starts, head_tiles, width)
    embed = window(embed_t, embed_starts, embed_tiles, -(-embed_t.shape[1] // 128) * 128)
    segments = heavy_segments(width, in_cols, in_starts, out_t.shape[0], shards)
    plan = (segments, (in_starts, in_tiles), (head_starts, head_tiles), (embed_starts, embed_tiles), lines)
    group = traits.shape[0]
    rows = 2 * lines * group
    most = max(len(parts) for parts in segments)
    shapes = [
        ((width, 4 * width), low),
        ((4 * width, width), low),
        ((width, width), low),
        ((3 * width, width), low),
        ((rows, width), full),
        ((rows, width), low),
        ((rows, embed_tiles * 128), full),
        ((group, 6 * width), full),
        ((group, 2 * width), full),
        ((PATCH, width), low),
        ((PATCH, width), low),
        ((rows, traits.shape[1]), full),
    ]
    scratch = [
        ((shards, rows, embed_tiles * 128), low),
        ((shards, rows, embed_tiles * 128), full),
        ((shards, PATCH, embed_tiles * 128), low),
        ((shards, rows, head_tiles * 128), full),
        ((rows, head_tiles * 128), full),
        ((shards, group, in_tiles * 128), full),
        ((group, in_tiles * 128), full),
        ((shards, group, head_tiles * 128), full),
        ((group, head_tiles * 128), full),
        ((PATCH, width), low),
    ]
    dma = pltpu.SemaphoreType.DMA
    outs = pl.pallas_call(
        functools.partial(gather_kernel, plan),
        out_shape=[jax.ShapeDtypeStruct(*item) for item in shapes],
        in_specs=[pl.BlockSpec(memory_space=pltpu.VMEM)] * 5,
        out_specs=[pl.BlockSpec(memory_space=pltpu.VMEM)] * len(shapes),
        scratch_shapes=[pltpu.VMEM(*item) for item in scratch]
        + [dma((most,)), dma((most,))]
        + [dma((most, 2))] * 4
        + [dma((most, 4))] * 2
        + [dma((most,)), dma((most,)), dma((8, shards - 1)), dma((8, shards - 1)), dma((most,))]
        + [
            pltpu.VMEM((shards,) + traits.shape, full),
            pltpu.VMEM(traits.shape, full),
            pltpu.VMEM(traits.shape, full),
            pltpu.VMEM((lines, 2 * group, traits.shape[1]), full),
            dma((lines,)),
            dma((lines,)),
        ],
        compiler_params=pltpu.CompilerParams(
            collective_id=2, has_side_effects=True, vmem_limit_bytes=60 * 1024 * 1024
        ),
    )(in_t, out_t.astype(low), head_t, embed, traits)
    return in_t, head_t, outs


def own_segments(width, in_cols, in_starts, out_rows, shards):
    every = []
    for place in range(shards):
        parts = []
        for array, low, high in ((3, 6 * width, 9 * width), (1, 9 * width, 13 * width)):
            first, last = max(low, place * in_cols), min(high, (place + 1) * in_cols)
            if first < last:
                parts.append((array, first - low, last - first, first - in_starts[place] * 128))
        every.append(parts)
    return every


def total_kernel(
    tables, segments, fc2, fc1, attn_out, qkv, w_in, w_out, w_head, w_embed,
    d_in, d_fin, d_two, d_one, d_full, few, cond_full, time_act, traits, c_in, c_out, c_head, c_embed,
    g_in, g_out, g_head, g_embed, n_in, n_out, n_head, n_embed, stats,
    own_t, own_out, grad_t, head_t, t_out, t_head, t_embed, v_in, v_out, v_head, v_embed,
    load, write, fetch,
):
    (in_starts, in_tiles), (head_starts, head_tiles), (embed_starts, embed_tiles), shards = tables
    arrays = (fc2, fc1, attn_out, qkv)
    shard = lax.axis_index("shard")
    width = cond_full.shape[1]
    in_cols, head_cols, embed_cols, out_cols = (item.shape[0] for item in (w_in, w_head, w_embed, w_out))
    full, low = jnp.float32, jnp.bfloat16
    span = lane_span(width, w_embed.shape[1])

    weights = ((w_in, v_in), (w_out, v_out), (w_head, v_head), (w_embed, v_embed))
    reads = [pltpu.make_async_copy(source, target, load.at[k]) for k, (source, target) in enumerate(weights)]
    for copy in reads:
        copy.start()

    def heavy_copies(place):
        copies = []
        for k, (array, row, rows, at) in enumerate(segments[place]):
            copies.append(
                pltpu.make_async_copy(
                    arrays[array].at[pl.ds(row, rows), :], own_t.at[pl.ds(at, rows), :], fetch.at[k]
                )
            )
        for k, array in ((2, 2), (3, 0)):
            lane = 0 if array == 2 else width
            copies.append(
                pltpu.make_async_copy(
                    arrays[array].at[pl.ds(place * out_cols, out_cols), :],
                    own_out.at[:, pl.ds(lane, arrays[array].shape[1])],
                    fetch.at[k],
                )
            )
        return copies

    for place in range(shards):

        @pl.when(shard == place)
        def _():
            for copy in heavy_copies(place):
                copy.start()
            edges = [0]
            for _, _, rows, at in segments[place]:
                edges += [at, at + rows]
            edges.append(in_tiles * 128)
            for start, stop in zip(edges[0::2], edges[1::2]):
                if start < stop:
                    own_t[start:stop, :] = jnp.zeros((stop - start, width), low)

    def decayed(state, total, count):
        return decay * state + (1.0 - decay) * (total / count + eps_one)

    def to_lanes(column):
        return jnp.broadcast_to(column, (column.shape[0], 128)).T[:1, :]

    def to_column(lanes):
        return jnp.broadcast_to(lanes, (128, lanes.shape[1])).T[:, :1]

    def squares_of(value, state, fresh_out, start, size):
        square = value * value
        sums = to_lanes(jnp.sum(square, -1, keepdims=True))[:, :size]
        fresh = decayed(state[:, start : start + size], sums, value.shape[1])
        fresh_out[:, start : start + size] = fresh
        inverse = 1.0 / fresh
        if size < value.shape[0]:
            inverse = jnp.concatenate([inverse, jnp.zeros((1, value.shape[0] - size), full)], 1)
        return jnp.sum(square, 0, keepdims=True), jnp.sum(square * to_column(inverse), 0, keepdims=True)

    def put(start, plain, scaled):
        stats[:, start : start + plain.shape[1]] = plain
        stats[:, span + start : span + start + plain.shape[1]] = scaled

    def column_blocks(total):
        return [(start, min(128, total - start)) for start in range(0, total, 128)]

    def by_blocks(take, total, state, fresh_out, place):
        plain, scaled = jnp.zeros((1, width), full), jnp.zeros((1, width), full)
        for start, size in column_blocks(total):
            value = take(start, size)
            if size < 128:
                value = jnp.concatenate([value, jnp.zeros((128 - size, width), full)], 0)
            more, more_scaled = squares_of(value, state, fresh_out, start, size)
            plain, scaled = plain + more, scaled + more_scaled
        put(place, plain, scaled)

    cond = cond_full[...]
    cond = (cond * jax.nn.sigmoid(cond)).astype(low)

    lanes_all = -(-w_embed.shape[1] // 128) * 128
    freq, onehot = placed_traits(traits[...], lanes_all)
    square_one = lax.broadcasted_iota(jnp.int32, (PATCH, lanes_all), 0)
    eye = jnp.where(square_one == lax.broadcasted_iota(jnp.int32, (PATCH, lanes_all), 1), 1.0, 0.0).astype(low)

    def exact(value, picks):
        total = None
        for _ in range(3):
            part = value.astype(low)
            value = value - part.astype(full)
            term = mxu(part, picks, TN)
            total = term if total is None else total + term
        return total

    for place in range(shards):

        @pl.when(shard == place)
        def _():
            lead = place * embed_cols - embed_starts[place] * 128
            lanes = slice(embed_starts[place] * 128, (embed_starts[place] + embed_tiles) * 128)
            value = exact(d_full[...], onehot) + exact(few[0:PATCH, lanes], eye)
            value = value[lead : lead + embed_cols, :]
            time = mxu(d_one[...], freq, TN)[lead : lead + embed_cols, :]
            t_embed[:, : freq.shape[1]] = value[:, : freq.shape[1]] + time
            t_embed[:, freq.shape[1] :] = value[:, freq.shape[1] : w_embed.shape[1]]

    pltpu.make_async_copy(t_embed, g_embed, write.at[3]).start()
    value = jnp.concatenate([t_embed[...], jnp.zeros((embed_cols, lanes_all - w_embed.shape[1]), full)], 1)
    square = value * value
    fresh = decayed(c_embed[...], to_lanes(jnp.sum(square, -1, keepdims=True)), w_embed.shape[1])
    n_embed[...] = fresh
    put(7 * width, jnp.sum(square, 0, keepdims=True), jnp.sum(square * to_column(1.0 / fresh), 0, keepdims=True))

    head_t[...] = mxu(d_two[...], time_act[...], TN) + mxu(d_fin[...], cond, TN)
    last_place = [o for o in range(shards) if 0 <= 3 * width // 128 - head_starts[o] < head_tiles][-1]
    last_row = (3 * width // 128 - head_starts[last_place]) * 128

    @pl.when(shard == last_place)
    def _():
        head_t[last_row : last_row + PATCH, :] = few[PATCH + 8 : 2 * PATCH + 8, :]

    for place in range(shards):

        @pl.when(shard == place)
        def _():
            lead = place * head_cols - head_starts[place] * 128
            t_head[...] = head_t[lead : lead + head_cols, :]

    pltpu.make_async_copy(t_head, g_head, write.at[2]).start()
    by_blocks(lambda start, size: t_head[start : start + size, :], head_cols, c_head, n_head, 6 * width)

    for place in range(shards):

        @pl.when(shard == place)
        def _():
            for copy in heavy_copies(place):
                copy.wait()

    def light(index, carry):
        part = pl.ds(pl.multiple_of(index * 128, 128), 128)
        grad_t[part, :] = mxu(d_in[:, part], cond, TN) + own_t[part, :].astype(full)
        return carry

    lax.fori_loop(0, in_tiles, light, 0)
    lead = lax.rem(shard * in_cols, 128)
    write_in = pltpu.make_async_copy(grad_t.at[pl.ds(pl.multiple_of(lead, 64), in_cols), :], g_in, write.at[0])
    write_in.start()
    by_blocks(
        lambda start, size: grad_t[pl.ds(pl.multiple_of(lead + start, 64), size), :], in_cols, c_in, n_in, 0
    )

    sums = jnp.zeros((out_cols, 1), full)
    for index in range(5):
        value = own_out[:, index * width : (index + 1) * width].astype(full)
        t_out[:, index * width : (index + 1) * width] = value
        sums += jnp.sum(value * value, -1, keepdims=True)
    pltpu.make_async_copy(t_out, g_out, write.at[1]).start()
    fresh = decayed(c_out[...], to_lanes(sums), 5 * width)
    n_out[...] = fresh
    column = to_column(1.0 / fresh)
    for index in range(5):
        value = t_out[:, index * width : (index + 1) * width]
        square = value * value
        put(width + index * width, jnp.sum(square, 0, keepdims=True), jnp.sum(square * column, 0, keepdims=True))

    for copy in reads:
        copy.wait()
    for k, (_, value) in enumerate(weights):
        rows, cols = value.shape

        def squares(index, carry):
            block = value[pl.ds(pl.multiple_of(index * 64, 64), 64), :]
            return carry + jnp.sum(block * block, 0, keepdims=True)

        total = lax.fori_loop(0, rows // 64, squares, jnp.zeros((1, cols), full))
        if rows % 64:
            block = value[rows // 64 * 64 :, :]
            total += jnp.sum(block * block, 0, keepdims=True)
        start = 2 * span + k * 128
        stats[:, start : start + 128] = jnp.broadcast_to(jnp.sum(total, -1, keepdims=True) / 128.0, (1, 128))
    write_in.wait()
    for k, (source, target) in enumerate(((t_out, g_out), (t_head, g_head), (t_embed, g_embed))):
        pltpu.make_async_copy(source, target, write.at[k + 1]).wait()


def lane_span(width, embed_rows):
    return 7 * width + -(-embed_rows // 128) * 128


def total_call(tables, heavy, weights, light, cols):
    (in_starts, in_tiles), (_, head_tiles), _, shards = tables
    low, full = jnp.bfloat16, jnp.float32
    width = heavy[2].shape[0]
    w_in, w_out, w_head, w_embed = weights
    lanes = 2 * lane_span(width, w_embed.shape[1]) + 4 * 128
    segments = own_segments(width, w_in.shape[0], in_starts, w_out.shape[0], shards)
    shapes = [(item.shape, full) for item in weights] + [(item.shape, full) for item in cols] + [((1, lanes), full)]
    anywhere, vmem = pl.BlockSpec(memory_space=pl.ANY), pl.BlockSpec(memory_space=pltpu.VMEM)
    scratch = [
        ((in_tiles * 128, width), low),
        (w_out.shape, low),
        ((in_tiles * 128, width), full),
        ((head_tiles * 128, width), full),
    ]
    scratch += [(item.shape, full) for item in weights[1:]] + [(item.shape, full) for item in weights]
    return pl.pallas_call(
        functools.partial(total_kernel, tables, segments),
        out_shape=[jax.ShapeDtypeStruct(*item) for item in shapes],
        in_specs=[anywhere] * 8 + [vmem] * (len(light) + 4),
        out_specs=[anywhere] * 4 + [vmem] * 5,
        scratch_shapes=[pltpu.VMEM(*item) for item in scratch] + [pltpu.SemaphoreType.DMA((4,))] * 3,
        compiler_params=pltpu.CompilerParams(vmem_limit_bytes=60 * 1024 * 1024),
    )(*heavy, *weights, *light, *cols)


def finish_kernel(shards, sizes, own, r_in, r_out, r_head, r_embed, n_in, n_out, n_head, n_embed, s_in, s_out, s_head, s_embed, rms, slots, send, recv):
    rep, shard = lax.axis_index("rep"), lax.axis_index("shard")
    barrier = pltpu.get_barrier_semaphore()
    for step in range(1, shards):
        peer = (rep, lax.rem(shard + step, shards))
        pl.semaphore_signal(barrier, inc=1, device_id=peer, device_id_type=MESH)
    pl.semaphore_wait(barrier, shards - 1)

    def copy(step):
        return pltpu.make_async_remote_copy(
            src_ref=own,
            dst_ref=slots.at[shard],
            send_sem=send.at[step - 1],
            recv_sem=recv.at[step - 1],
            device_id=(rep, lax.rem(shard + step, shards)),
            device_id_type=MESH,
        )

    for step in range(1, shards):
        copy(step).start()
    slots[shard] = own[...]
    for step in range(1, shards):
        copy(step).wait()
    total = functools.reduce(jnp.add, [slots[o] for o in range(shards)])
    states, fresh, scales = (r_in, r_out, r_head, r_embed), (n_in, n_out, n_head, n_embed), (s_in, s_out, s_head, s_embed)
    starts, start = [], 0
    for rows, _ in sizes:
        starts.append(start)
        start += -(-rows // 128) * 128
    update, means = jnp.zeros((1, 1), jnp.float32), []
    for k, (rows, cols) in enumerate(sizes):
        row = decay * states[k][...] + (1.0 - decay) * (total[:, starts[k] : starts[k] + rows] / cols + eps_one)
        fresh[k][...] = row
        mean = jnp.mean(row, -1, keepdims=True)
        means.append(mean)
        update += mean * jnp.sum(total[:, start + starts[k] : start + starts[k] + rows] / row, -1, keepdims=True)
    update = jnp.sqrt(update / sum(rows * cols for rows, cols in sizes))
    rms[...] = jnp.broadcast_to(update, rms.shape)
    factor = jnp.maximum(1.0, update / clip_level)
    for k, (rows, cols) in enumerate(sizes):
        first = 2 * start + k * 128
        weight = jnp.sqrt(jnp.sum(total[:, first : first + 128], -1, keepdims=True) / (rows * cols))
        scales[k][...] = rate * jnp.maximum(eps_two, weight) / factor * lax.rsqrt(fresh[k][...] / means[k])


def finish_call(shards, sizes, stats, rows_old):
    full = jnp.float32
    shapes = [((1, rows), full) for rows, _ in sizes] * 2 + [((1, 128), full)]
    return pl.pallas_call(
        functools.partial(finish_kernel, shards, sizes),
        out_shape=[jax.ShapeDtypeStruct(*item) for item in shapes],
        in_specs=[pl.BlockSpec(memory_space=pltpu.VMEM)] * 5,
        out_specs=[pl.BlockSpec(memory_space=pltpu.VMEM)] * len(shapes),
        scratch_shapes=[
            pltpu.VMEM((shards,) + stats.shape, full),
            pltpu.SemaphoreType.DMA((shards - 1,)),
            pltpu.SemaphoreType.DMA((shards - 1,)),
        ],
        compiler_params=pltpu.CompilerParams(collective_id=3, has_side_effects=True),
    )(stats, *rows_old)


def on_device(
    latents,
    noises,
    velocity,
    times,
    labels,
    dropped,
    blocks_in,
    blocks_out,
    head_side,
    embed_side,
    state_in_row,
    state_in_col,
    state_out_row,
    state_out_col,
    state_head_row,
    state_head_col,
    state_embed_row,
    state_embed_col,
):
    images = latents.shape[0]
    width = head_side.shape[0]
    shard_count = lax.axis_size("shard")
    place = lax.axis_index("shard")
    in_cols = blocks_in.shape[2]
    head_cols = head_side.shape[1]
    embed_cols = embed_side.shape[1]
    group = images * shard_count
    weights = (blocks_in[0].T, blocks_out[0].T, head_side.T, embed_side.T)
    t_value = (times.astype(jnp.float32) + 1.0) / step_count
    classes = (PATCH + FREQ + jnp.where(dropped == 1, CLASSES - 1, labels)).astype(jnp.float32)
    lines = LINE
    lead = -(-(PATCH + FREQ) // 128) * 128
    own_traits = jnp.concatenate(
        [
            jnp.zeros((images, PATCH), jnp.float32),
            time_freq(t_value, FREQ),
            jnp.zeros((images, lead - PATCH - FREQ), jnp.float32),
            jnp.broadcast_to(classes[:, None], (images, 128)),
        ],
        1,
    )
    traits = lax.dynamic_update_slice(
        jnp.zeros((group, lead + 128), jnp.float32), own_traits, (place * images, 0)
    )
    in_t, head_win_t, gathered = gather_call(*weights, traits, shard_count, lines)
    fc2_t, fc1_t, o_t, qkv_t, cond_full, time_act, time_one, modul, final_mod, patch_w, head_t, all_traits = gathered
    tcol = t_value[:, None, None]
    state = (
        (1.0 - tcol) * latents.reshape(images, TOK, PATCH)
        + tcol * noises.reshape(images, TOK, PATCH)
    ).astype(jnp.bfloat16)
    tables = (
        windows(in_cols, shard_count),
        windows(head_cols, shard_count),
        windows(embed_cols, shard_count),
        shard_count,
    )
    sums = step_call(
        lines,
        tables,
        images,
        [fc2_t, fc1_t, o_t, qkv_t],
        in_t,
        [
            state.reshape(images * TOK, PATCH),
            velocity.reshape(images * TOK, PATCH),
            jnp.repeat(t_value, TOK)[:, None],
            positions(GRID, width),
            patch_w,
            head_t,
            modul,
            final_mod,
            head_win_t,
            cond_full,
            time_one,
        ],
    )
    d_in, d_fin, d_two, d_full, d_one, few_sum = sums[4:]
    loss_sum = few_sum[PATCH, 0]
    rows_old = (state_in_row, state_out_row, state_head_row[None], state_embed_row[None])
    cols_old = (state_in_col, state_out_col, state_head_col[None], state_embed_col[None])
    *outs, stats = total_call(
        tables,
        sums[:4],
        weights,
        [d_in, d_fin, d_two, d_one, d_full, few_sum, cond_full, time_act, all_traits],
        cols_old,
    )
    totals, cols_new = outs[:4], outs[4:]
    blocks = lax.axis_size("rep") // (2 * lines)
    if blocks > 1:
        apart = [[k * 2 * lines + j for k in range(blocks)] for j in range(2 * lines)]
        totals, loss_sum = lax.psum((totals, loss_sum), "rep", axis_index_groups=apart)
        cols_new, plain, scaled = [], [], []
        for gradient, col_state in zip(totals, cols_old):
            square = gradient * gradient
            fresh = decay * col_state + (1.0 - decay) * (jnp.mean(square, 1)[None] + eps_one)
            pad = (0, -gradient.shape[1] % 128)
            cols_new.append(fresh)
            plain.append(jnp.pad(jnp.sum(square, 0), pad))
            scaled.append(jnp.pad(jnp.sum(square / fresh[0][:, None], 0), pad))
        spans = sum(item.shape[0] for item in plain) * 2
        stats = jnp.concatenate(plain + scaled + [stats[0, spans:]])[None]
    sizes = [(weight.shape[1], weight.shape[0] * shard_count) for weight in weights]
    *outs, rms = finish_call(shard_count, sizes, stats, rows_old)
    rows_new, scales = outs[:4], outs[4:]
    update_rms = rms[0, 0]
    news = [
        (weight - gradient * scale * lax.rsqrt(col_next[0])[:, None]).T
        for weight, gradient, scale, col_next in zip(weights, totals, scales, cols_new)
    ]
    return (
        loss_sum,
        update_rms,
        totals[0].T[None],
        totals[1].T[None],
        totals[2].T,
        totals[3].T,
        rows_new[0],
        cols_new[0],
        rows_new[1],
        cols_new[1],
        rows_new[2][0],
        cols_new[2][0],
        rows_new[3][0],
        cols_new[3][0],
        news[0][None],
        news[1][None],
        news[2],
        news[3],
    )


def solution(mesh):
    placed = (
        P(("rep", "shard"), None),
        P(("rep", "shard"), None),
        P(("rep", "shard"), None),
        P(("rep", "shard")),
        P(("rep", "shard")),
        P(("rep", "shard")),
        P(None, None, "shard"),
        P(None, None, "shard"),
        P(None, "shard"),
        P(None, "shard"),
        P(),
        P(None, "shard"),
        P(),
        P(None, "shard"),
        P(),
        P("shard"),
        P(),
        P("shard"),
    )
    return jax.shard_map(
        on_device,
        mesh=mesh,
        in_specs=placed,
        out_specs=(
            P(),
            P(),
            P(None, None, "shard"),
            P(None, None, "shard"),
            P(None, "shard"),
            P(None, "shard"),
            P(),
            P(None, "shard"),
            P(),
            P(None, "shard"),
            P(),
            P("shard"),
            P(),
            P("shard"),
            P(None, None, "shard"),
            P(None, None, "shard"),
            P(None, "shard"),
            P(None, "shard"),
        ),
        check_vma=False,
    )
```

```python
import functools
import math

import jax
import jax.numpy as jnp
import numpy as np
from jax import lax
from jax.experimental import pallas as pl
from jax.experimental.pallas import tpu as pltpu
from jax.sharding import PartitionSpec as P

HEADS = 12
CLASSES = 1001
FREQ = 256
GRID = 16
PATCH = 16
LAYERS = 1
TOK = 256


decay = 0.5
eps_norm = 1e-06
eps_one = 1e-30
eps_two = 0.001
clip_level = 0.1
rate = 8.0
step_count = 1000.0


def silu(value):
    return value * jax.nn.sigmoid(value)


def positions(grid, width):
    quarter = width // 4
    omega = (1.0 / 10000.0 ** (np.arange(quarter, dtype=np.float32) / quarter)).astype(np.float32)
    index = np.arange(grid * grid)
    row_pos = (index // grid).astype(np.float32)[:, None] * omega[None, :]
    col_pos = (index % grid).astype(np.float32)[:, None] * omega[None, :]
    return np.concatenate([np.sin(row_pos), np.cos(row_pos), np.sin(col_pos), np.cos(col_pos)], 1)


def time_freq(t_value, width):
    half = width // 2
    freqs = jnp.exp(-math.log(10000.0) * jnp.arange(half, dtype=jnp.float32) / half)
    angles = (t_value * step_count)[:, None] * freqs[None, :]
    return jnp.concatenate([jnp.cos(angles), jnp.sin(angles)], -1)


def weight_grad(left, back):
    flat_left = left.reshape(-1, left.shape[-1])
    flat_back = back.reshape(-1, back.shape[-1])
    return lax.dot_general(
        flat_left, flat_back, (((0,), (0,)), ((), ())), preferred_element_type=jnp.float32
    )


MESH = pl.DeviceIdType.MESH
LINE = 4
PIECES = 4
PARTS = (4, 4, 2)
ORDER = (
    (0, 0), (0, 1), (0, 2), (1, 0), (9, 0), (1, 1), (0, 3), (9, 1), (1, 2), (0, 4), (0, 5), (1, 3), (9, 2),
    (2, 0), (0, 6), (1, 4), (1, 5), (0, 7), (9, 4), (2, 1), (1, 6), (3, 0), (0, 8), (1, 7), (9, 5), (2, 2),
    (0, 9), (3, 1), (0, 10), (1, 8), (4, 0), (9, 6), (2, 4), (0, 11), (3, 2), (0, 12), (0, 13), (0, 14), (4, 1),
    (9, 7), (2, 5), (3, 4), (6, 0), (0, 15), (9, 3), (2, 6), (2, 7), (3, 5), (4, 2), (4, 4), (9, 8), (6, 1),
    (1, 9), (7, 0), (0, 16), (0, 17), (3, 6), (2, 3), (9, 9), (3, 7), (4, 5), (1, 10), (1, 11), (6, 2), (7, 1),
    (8, 0), (2, 8), (9, 10), (3, 3), (5, 4), (8, 1), (4, 6), (7, 2), (2, 9), (4, 7), (3, 8), (8, 2), (9, 11),
    (5, 5), (2, 10), (4, 3), (3, 9), (6, 4), (5, 6), (5, 7), (3, 10), (2, 11), (4, 8), (6, 5), (6, 3), (7, 4),
    (6, 6), (4, 9), (3, 11), (8, 4), (6, 7), (4, 10), (6, 8), (7, 5), (6, 9), (7, 3), (8, 5), (4, 11), (8, 3),
    (5, 10), (7, 6), (8, 6), (5, 11), (7, 7), (6, 10), (7, 8), (8, 7), (7, 9), (6, 11), (8, 8), (8, 9), (7, 10),
    (8, 10), (7, 11), (8, 11),
)
BESIDE_AT = (44, 54, 65, 76, 87, 97, 108)
SLOTS = 3
NN = (((1,), (0,)), ((), ()))
NT = (((1,), (1,)), ((), ()))
TN = (((0,), (0,)), ((), ()))


def mxu(left, right, kind):
    return lax.dot_general(left, right, kind, preferred_element_type=jnp.float32)


def blocks_of(total, size, body):
    def step(index, carry):
        body(pl.ds(pl.multiple_of(index * size, size), size))
        return carry

    lax.fori_loop(0, total // size, step, 0)


def heavy_chunks(width):
    half = width // 2
    fc2, fc1, kv = PARTS
    parts = [(0, 0, width, 4 * width // fc2 * k, 2 * width // fc2, False) for k in range(fc2)]
    parts += [(1, 4 * width // fc1 * k, 4 * width // fc1, 0, half, True) for k in range(fc1)]
    parts += [(2, 0, width, 0, half, False), (3, 0, width, 0, half, False)]
    parts += [(3, width + 2 * width // kv * k, 2 * width // kv, 0, half, True) for k in range(kv)]
    return tuple(parts)


def add_rows(target, left, right, rows):
    block = 16

    def body(index, carry):
        span = pl.ds(pl.multiple_of(index * block, block), block)
        target[span] = left[span] + right[span]
        return carry

    lax.fori_loop(0, rows // block, body, 0)


def step_kernel(lines, chunks, tables, in_cols, *refs):
    count = len(chunks)
    (in_far, out_far, state, target, weight_t, pos, head_t, embed, traits), refs = refs[:9], refs[9:]
    finals, refs = refs[:4], refs[4:]
    (d_in, d_head, d_two, d_full, d_one, few_sum, cond_full, time_act, all_traits), scratch = refs[:9], refs[9:]
    held, by_y, by_x, by_z = (scratch[k * count : (k + 1) * count] for k in range(4))
    send, recv, zsend, zrecv, wsend, wrecv = scratch[4 * count : 4 * count + 6]
    scratch = scratch[4 * count + 6 :]
    (stage_wide, stage_tall, land_wide, land_tall, free_wide, free_tall, fetch, d_mod, d_fm, few), scratch = scratch[:10], scratch[10:]
    (
        stream, hat_one, hat_two, root_one, root_two, a_low, qkv_low, mixed, proj, b_low, active, mlp, d_mlp,
    ), scratch = scratch[:13], scratch[13:]
    (
        few_got, few_y, few_x, few_held, few_line, mod_got, fm_got, mod_sum, fm_sum, group_slot, part_own, part_slot,
        act_own, act_slot, pair_own, pair_got, line_in, line_rest, line_full,
        few_send, few_recv, group_send, group_recv, line_send, line_recv,
    ) = scratch[:25]
    gather_refs = scratch[25:]
    (in_starts, in_tiles), (head_starts, head_tiles), (embed_starts, embed_tiles), shards = tables
    time_one, modul, fmod, patch, last = gather_refs[:5]
    rep, shard = lax.axis_index("rep"), lax.axis_index("shard")
    place_here = lax.rem(rep, 2 * lines)
    base = rep - place_here
    x, z = lax.rem(place_here, 2), lax.div(place_here, 2)
    core, y = lax.rem(shard, 2), lax.div(shard, 2)
    to_core = (rep, shard + 1 - 2 * core)
    to_y = (rep, shard + 2 - 4 * y)
    to_x = (rep + 1 - 2 * x, shard)

    def line_peer(step):
        return (base + lax.rem(z + step, lines) * 2 + x, shard)

    barrier = pltpu.get_barrier_semaphore()
    to_far = (rep, shards - 1 - shard)
    for peer in (to_core, to_y, to_x, to_far):
        pl.semaphore_signal(barrier, inc=1, device_id=peer, device_id_type=MESH)
    for step in range(1, lines):
        pl.semaphore_signal(
            barrier, inc=1, device_id=line_peer(step), device_id_type=MESH
        )
    pl.semaphore_wait(barrier, 4 + lines - 1)

    width, tokens = head_t.shape[1], state.shape[0]
    in_blocks = [active.at[:, pl.ds(k * width, width)] for k in range(4)] + [d_mlp]

    def far_copy(k):
        return pltpu.make_async_copy(in_far.at[pl.ds(k * tokens, tokens), :], in_blocks[k], fetch.at[4 + k])

    stride = lines // PIECES
    owns = lax.rem(z, stride) == 0
    mine = lax.div(z, stride)
    def remote(source, target, send_sem, recv_sem, peer):
        return pltpu.make_async_remote_copy(
            src_ref=source,
            dst_ref=target,
            send_sem=send_sem,
            recv_sem=recv_sem,
            device_id=peer,
            device_id_type=MESH,
        )

    def rows_of(ref, start, size):
        return ref.at[pl.ds(pl.multiple_of(start, 16), size)]

    def lanes_at(index, ref, row, rows, which):
        _, _, _, lane, lanes, _ = chunks[index]
        return ref.at[
            pl.ds(pl.multiple_of(row, 16), rows), pl.ds(pl.multiple_of(lane + which * lanes, 128), lanes)
        ]

    turn = {i: sum(chunks[j][0] == 0 for j in range(i)) if chunks[i][0] == 0 else sum(chunks[j][0] != 0 for j in range(i)) for i in range(count)}

    def slot_of(i, wide, tall):
        if chunks[i][0] == 0:
            return wide.at[turn[i] % SLOTS]
        return tall.at[turn[i] % SLOTS, pl.ds(0, chunks[i][2])]

    def turn_away(i, steps):
        for j in range(count):
            if (chunks[j][0] == 0) == (chunks[i][0] == 0) and turn[j] == turn[i] + steps:
                return j
        return None

    def core_copy(i):
        return remote(
            slot_of(i, stage_wide, stage_tall), slot_of(i, land_wide, land_tall), send.at[i, 0], recv.at[i, 0], to_core
        )

    def free_of(i):
        return free_wide if chunks[i][0] == 0 else free_tall

    def y_copy(i):
        half = chunks[i][2] // 2
        return remote(
            rows_of(held[i], (1 - y) * half, half), by_y[i], send.at[i, 1], recv.at[i, 1], to_y
        )

    def x_copy(i):
        quarter = chunks[i][2] // 4
        return remote(
            rows_of(by_y[i], (1 - x) * quarter, quarter), by_x[i], send.at[i, 2], recv.at[i, 2], to_x
        )

    def z_copy(i, piece):
        size = chunks[i][2] // 4 // PIECES
        owner = piece * stride
        slot = lax.rem(z - owner - 1 + lines, lines)
        return remote(
            by_x[i].at[pl.ds(piece * size, size)],
            by_z[i].at[slot],
            zsend.at[i, piece],
            zrecv.at[i, slot],
            (base + owner * 2 + x, shard),
        )

    def final_rows(i, side, start, size, which):
        array, row, rows = chunks[i][:3]
        return lanes_at(i, finals[array], row + side * (rows // 2) + start, size, which)

    def cross_copy(i):
        quarter = chunks[i][2] // 4
        part = final_rows(i, 0, x * quarter, quarter, core)
        return remote(part, part, send.at[i, 3], recv.at[i, 3], to_y)

    def line_copy(i, which, side, step):
        size = chunks[i][2] // 4 // PIECES
        part = final_rows(i, side, (x * PIECES + mine) * size, size, core)
        return remote(
            part, part, wsend.at[i, which, step - 1], wrecv.at[i, which, mine], line_peer(step)
        )

    def line_arrival(i, which, side, piece):
        size = chunks[i][2] // 4 // PIECES
        part = final_rows(i, side, (x * PIECES + piece) * size, size, core)
        return remote(part, part, wsend.at[i, which, 0], wrecv.at[i, which, piece], to_core)

    def pair_copy(i, which, side, column):
        quarter = chunks[i][2] // 4
        part = final_rows(i, side, column * quarter, quarter, core)
        return remote(part, part, send.at[i, 4 + which], recv.at[i, 4 + which], to_x)

    def last_copy(i, which, side, half):
        rows = chunks[i][2] // 2
        part = final_rows(i, side, 0, rows, half)
        return remote(part, part, send.at[i, 6 + which], recv.at[i, 6 + which], to_core)

    def sides(i, action):
        if chunks[i][5]:

            @pl.when(y == 1)
            def _():
                action(0, 1)
                action(1, 0)

        else:
            action(0, y)

    def produce(i, left, right):
        rows, lanes = chunks[i][2], chunks[i][4]
        before, after = turn_away(i, -SLOTS), turn_away(i, SLOTS)
        if before is not None:
            core_copy(before).wait_send()
        staged = slot_of(i, stage_wide, stage_tall)

        def block(part):
            value = mxu(left[:, part], right[...], TN)
            first, second = value[:, :lanes], value[:, lanes:]
            held[i][part, :] = jnp.where(core == 0, first, second).astype(jnp.bfloat16)
            staged[part, :] = jnp.where(core == 0, second, first).astype(jnp.bfloat16)

        blocks_of(rows, 256, block)
        if before is not None:
            pl.semaphore_wait(free_of(i), 1)
        core_copy(i).start()

    def stage1(i):
        core_copy(i).wait_recv()
        add_rows(held[i], held[i], slot_of(i, land_wide, land_tall), chunks[i][2])
        if turn_away(i, SLOTS) is not None:
            pl.semaphore_signal(free_of(i), inc=1, device_id=to_core, device_id_type=MESH)

    def stage2(i):
        half = chunks[i][2] // 2
        y_copy(i).wait_recv()
        add_rows(by_y[i], by_y[i], rows_of(held[i], y * half, half), half)
        x_copy(i).start()

    def stage3(i):
        quarter = chunks[i][2] // 4
        x_copy(i).wait_recv()
        add_rows(by_x[i], by_x[i], rows_of(by_y[i], x * quarter, quarter), quarter)
        for piece in range(PIECES):

            @pl.when(z != piece * stride)
            def _():
                z_copy(i, piece).start()

    def stage4(i):
        size = chunks[i][2] // 4 // PIECES

        @pl.when(owns)
        def _():
            for slot in range(lines - 1):
                remote(
                    by_z[i].at[slot], by_z[i].at[slot], zsend.at[i, 0], zrecv.at[i, slot], to_core
                ).wait_recv()
            target = final_rows(i, y, (x * PIECES + mine) * size, size, core)

            def body(index, carry):
                total = by_x[i][
                    pl.ds(pl.multiple_of(mine * size + index * 16, 16), 16)
                ].astype(jnp.float32)
                for slot in range(lines - 1):
                    total += by_z[i][slot, pl.ds(pl.multiple_of(index * 16, 16), 16)].astype(jnp.float32)
                target[pl.ds(pl.multiple_of(index * 16, 16), 16)] = total.astype(jnp.bfloat16)
                return carry

            lax.fori_loop(0, size // 16, body, 0)
            for step in range(1, lines):
                line_copy(i, 0, y, step).start()

    def line_wait(i):
        for piece in range(PIECES):

            @pl.when(z != piece * stride)
            def _():
                line_arrival(i, 0, y, piece).wait_recv()

    def stage5(i):
        @pl.when(y == 0)
        def _():
            line_wait(i)
            cross_copy(i).start()

    def stage6(i):
        if chunks[i][5]:

            @pl.when(y == 1)
            def _():
                line_wait(i)
                pair_copy(i, 0, 1, x).start()
                cross_copy(i).wait_recv()
                pair_copy(i, 1, 0, x).start()

        else:
            line_wait(i)
            pair_copy(i, 0, y, x).start()

    def stage7(i):
        def action(which, side):
            pair_copy(i, which, side, 1 - x).wait_recv()
            last_copy(i, which, side, core).start()

        sides(i, action)

    def stage8(i):
        sides(i, lambda which, side: last_copy(i, which, side, 1 - core).wait_recv())


    mod_tiles, wide = 6 * width // 128, width // 128
    images = d_mod.shape[0]
    in_lanes, head_lanes, embed_lanes = in_tiles * 128, head_tiles * 128, embed_tiles * 128
    rest_lanes = 2 * head_lanes + embed_lanes
    head_places = [o for o in range(shards) if head_starts[o] < wide]
    mod_places = [o for o in range(shards) if in_starts[o] < mod_tiles]
    few_rows = few.shape[0] // 2
    half = pl.ds(pl.multiple_of(core * few_rows, 8), few_rows)
    other_half = pl.ds(pl.multiple_of((1 - core) * few_rows, 8), few_rows)

    def is_in(where, places):
        return functools.reduce(jnp.logical_or, [where == o for o in places])

    few_core = remote(few.at[other_half], few_got, few_send.at[0], few_recv.at[0], to_core)
    few_over_y = remote(few_held.at[0], few_y, few_send.at[1], few_recv.at[1], to_y)
    few_over_x = remote(few_held.at[1], few_x, few_send.at[2], few_recv.at[2], to_x)
    few_back = remote(few_sum.at[half], few_sum.at[half], few_send.at[3], few_recv.at[3], to_core)
    few_back_arrival = remote(few_sum.at[other_half], few_sum.at[other_half], few_send.at[3], few_recv.at[3], to_core)
    mod_core = remote(d_mod, mod_got, few_send.at[4], few_recv.at[4], to_core)
    fm_core = remote(d_fm, fm_got, few_send.at[5], few_recv.at[5], to_core)
    pair_copy_x = remote(pair_own, pair_got, few_send.at[6], few_recv.at[6], to_x)

    def few_line_copy(step):
        return remote(few_line.at[z], few_line.at[z], few_send.at[6 + step], few_recv.at[6 + step], line_peer(step))

    def few_line_arrival(step):
        origin = lax.rem(z + lines - step, lines)
        return remote(few_line.at[origin], few_line.at[origin], few_send.at[6 + step], few_recv.at[6 + step], to_core)

    def group_parts(place):
        parts = []
        tiles = min(in_tiles, mod_tiles - in_starts[place])
        if tiles > 0:
            parts.append((0, in_starts[place] * 128, 0, tiles * 128))
        first, final = max(head_starts[place], wide), min(head_starts[place] + head_tiles, 3 * wide)
        if final > first:
            lead = (first - head_starts[place]) * 128
            parts.append((1, (first - wide) * 128, in_lanes + lead, (final - first) * 128))
        return parts

    def group_copy(place, k):
        which, lane, own, lanes = group_parts(place)[k]
        return remote(
            (mod_sum, fm_sum)[which].at[:, pl.ds(lane, lanes)],
            group_slot.at[:, pl.ds(own, lanes)],
            group_send.at[k, 0],
            group_recv.at[k, 0],
            to_y,
        )

    def to_others(kind, source, slots, step):
        return remote(
            source,
            slots.at[shard],
            group_send.at[kind, step - 1],
            group_recv.at[kind, step - 1],
            (rep, lax.rem(shard + step, shards)),
        )

    def from_others(kind, slots, step):
        origin = lax.rem(shard + shards - step, shards)
        return remote(slots.at[origin], slots.at[origin], group_send.at[kind, 0], group_recv.at[kind, step - 1], to_core)

    slots_of = (line_rest, line_full, line_in)

    def line_copy_d(kind, step):
        slots = slots_of[kind]
        return remote(slots.at[z], slots.at[z], line_send.at[kind, step - 1], line_recv.at[kind, step - 1], line_peer(step))

    def line_arrival_d(kind, step):
        slots = slots_of[kind]
        origin = lax.rem(z + lines - step, lines)
        return remote(slots.at[origin], slots.at[origin], line_send.at[kind, 0], line_recv.at[kind, step - 1], to_core)

    def on_line(action):
        for step in range(1, lines):
            action(0, step)
            action(1, step)

            @pl.when(is_in(shard, mod_places))
            def _():
                action(2, step)

    def side0():
        mod_core.start()
        fm_core.start()
        few_core.start()

    def side1():
        mod_core.wait_recv()
        mod_sum[...] = d_mod[...] + mod_got[...]
        fm_core.wait_recv()
        fm_sum[...] = d_fm[...] + fm_got[...]
        for place in range(shards):

            @pl.when(to_y[1] == place)
            def _():
                for k in range(len(group_parts(place))):
                    group_copy(place, k).start()

        few_core.wait_recv()
        few_held[0] = few[half] + few_got[...]
        few_over_y.start()

    def side2():
        pair_own[...] = jnp.zeros_like(pair_own)
        for place in range(shards):

            @pl.when(shard == place)
            def _():
                for k, (which, lane, own, lanes) in enumerate(group_parts(place)):
                    group_copy(place, k).wait_recv()
                    pair_own[:, own : own + lanes] = (
                        (mod_sum, fm_sum)[which][:, lane : lane + lanes] + group_slot[:, own : own + lanes]
                    )

        part_own[...] = jnp.dot(
            pair_own[:, in_lanes : in_lanes + head_lanes].astype(jnp.bfloat16),
            head_t[...],
            preferred_element_type=jnp.float32,
        )

        @pl.when(is_in(shard, mod_places))
        def _():
            for k in range(len(in_blocks)):
                far_copy(k).wait()
                lanes = pair_own[:, k * tokens : (k + 1) * tokens].astype(jnp.bfloat16)
                part_own[...] += jnp.dot(lanes, in_blocks[k][...], preferred_element_type=jnp.float32)

        part_slot[shard] = part_own[...]
        for step in range(1, shards):
            to_others(2, part_own, part_slot, step).start()
        few_over_y.wait_recv()
        few_held[1] = few_held[0] + few_y[...]
        few_over_x.start()

    def side3():
        for step in range(1, shards):
            from_others(2, part_slot, step).wait_recv()
        d_cond = functools.reduce(jnp.add, [part_slot[o] for o in range(shards)])
        value = cond_full[pl.ds(pl.multiple_of(place_here * images, 8), images), :]
        gate = jax.nn.sigmoid(value)
        d_value = d_cond * (gate + value * gate * (1.0 - gate))
        for place in range(shards):

            @pl.when(shard == place)
            def _():
                first = embed_starts[place] * 128
                pair_own[:, in_lanes + rest_lanes :] = d_value[:, first : first + embed_lanes]
                if place in head_places:
                    lanes = min(head_tiles, wide - head_starts[place]) * 128
                    first = head_starts[place] * 128
                    start = in_lanes + head_lanes
                    d_two_own = d_value[:, first : first + lanes].astype(jnp.bfloat16)
                    pair_own[:, start : start + lanes] = d_two_own.astype(jnp.float32)
                    act_own[...] = jnp.dot(d_two_own, head_t[:lanes, :], preferred_element_type=jnp.float32)
                    act_slot[shard] = act_own[...]
                    for step in range(1, shards):
                        to_others(3, act_own, act_slot, step).start()

        few_over_x.wait_recv()
        few_line[z] = few_held[1] + few_x[...]
        for step in range(1, lines):
            few_line_copy(step).start()

    def side4():
        for step in range(1, shards):

            @pl.when(is_in(lax.rem(shard + shards - step, shards), head_places))
            def _():
                from_others(3, act_slot, step).wait_recv()

        value = time_one[pl.ds(pl.multiple_of(place_here * images, 8), images), :]
        gate = jax.nn.sigmoid(value)
        slope = gate + value * gate * (1.0 - gate)
        for place in range(shards):

            @pl.when(shard == place)
            def _():
                first = embed_starts[place] * 128
                d_act = functools.reduce(jnp.add, [act_slot[o, :, first : first + embed_lanes] for o in head_places])
                start = in_lanes + 2 * head_lanes
                pair_own[:, start : start + embed_lanes] = (slope * d_act).astype(jnp.bfloat16).astype(jnp.float32)

        pair_copy_x.start()
        for step in range(1, lines):
            few_line_arrival(step).wait_recv()
        few_sum[half] = functools.reduce(jnp.add, [few_line[at] for at in range(lines)])
        few_back.start()

    def side5():
        pair_copy_x.wait_recv()
        own, got = pair_own[...], pair_got[...]
        both = jnp.concatenate([jnp.where(x == 0, own, got), jnp.where(x == 0, got, own)], 0)
        line_in[z] = both[:, :in_lanes].astype(jnp.bfloat16)
        line_rest[z] = both[:, in_lanes : in_lanes + rest_lanes].astype(jnp.bfloat16)
        line_full[z] = both[:, in_lanes + rest_lanes :]
        on_line(lambda kind, step: line_copy_d(kind, step).start())

    def side6():
        on_line(lambda kind, step: line_arrival_d(kind, step).wait_recv())
        for at in range(lines):
            span = slice(at * 2 * images, (at + 1) * 2 * images)
            d_head[span, :] = line_rest[at, :, :head_lanes]
            d_two[span, :] = line_rest[at, :, head_lanes : 2 * head_lanes]
            d_one[span, :] = line_rest[at, :, 2 * head_lanes :]
            d_full[span, :] = line_full[at]
        d_in[...] = jnp.zeros_like(d_in)

        @pl.when(is_in(shard, mod_places))
        def _():
            for at in range(lines):
                d_in[at * 2 * images : (at + 1) * 2 * images, :] = line_in[at]

        few_back_arrival.wait_recv()

    def side_end():
        for copy in (few_core, few_over_y, few_over_x, few_back, mod_core, fm_core, pair_copy_x):
            copy.wait_send()
        for step in range(1, lines):
            few_line_copy(step).wait_send()
        on_line(lambda kind, step: line_copy_d(kind, step).wait_send())
        for place in range(shards):

            @pl.when(to_y[1] == place)
            def _():
                for k in range(len(group_parts(place))):
                    group_copy(place, k).wait_send()

        for step in range(1, shards):
            to_others(2, part_own, part_slot, step).wait_send()

        @pl.when(is_in(shard, head_places))
        def _():
            for step in range(1, shards):
                to_others(3, act_own, act_slot, step).wait_send()

    beside = (side0, side1, side2, side3, side4, side5, side6)
    low = jnp.bfloat16
    per = tokens // TOK
    row = [shard * per + image for image in range(per)]
    span = [pl.ds(image * TOK, TOK) for image in range(per)]
    cut = 256

    def piece(ref, image, index):
        return ref[pl.ds(row[image], 1), pl.ds(index * width, width)]

    def normed(value):
        center = value - jnp.mean(value, -1, keepdims=True)
        root = lax.rsqrt(jnp.mean(center * center, -1, keepdims=True) + eps_norm)
        return center * root, root

    def norm_back(d_hat, hat, root):
        return root * (d_hat - jnp.mean(d_hat, -1, keepdims=True) - hat * jnp.mean(d_hat * hat, -1, keepdims=True))

    def put_row(ref, image, index, value):
        ref[pl.ds(row[image], 1), pl.ds(index * width, width)] = (
            jnp.sum(value, 0, keepdims=True).astype(low).astype(jnp.float32)
        )

    fc2, fc1, attn_out, qkv = finals
    segments = heavy_segments(width, in_cols, in_starts, out_far.shape[0], shards)
    plan = (segments,) + tables[:3] + (lines,)
    relay_tick, arrived, finish = gather_steps(
        plan, remote, line_peer, in_blocks, far_copy, out_far, in_far, head_t, embed, traits,
        *finals, cond_full, time_act, time_one, modul, fmod, patch, last, all_traits, *gather_refs[5:],
    )
    d_mod[...] = jnp.zeros_like(d_mod)
    d_fm[...] = jnp.zeros_like(d_fm)

    for image in range(per):
        value = mxu(state[span[image], :], patch[...], NN) + pos[...]
        stream[span[image], :] = value
        hat, root = normed(value)
        hat_one[span[image], :] = hat
        root_one[span[image], :] = root
        a_low[span[image], :] = (hat * (1.0 + piece(modul, image, 1)) + piece(modul, image, 0)).astype(low)

    def qkv_block(part):
        qkv_low[:, part] = mxu(a_low[...], qkv[part, :], NT).astype(low)

    relay_tick(4)
    arrived(3)
    relay_tick(5)
    blocks_of(3 * width, cut, qkv_block)
    relay_tick(6)
    lane = lax.broadcasted_iota(jnp.int32, (TOK, 128), 1)
    first = lane < 64
    scale = 0.125

    def softmax(query, key):
        score = mxu(query, key, NT) * scale
        expo = jnp.exp(score - jnp.max(score, -1, keepdims=True))
        return expo / jnp.sum(expo, -1, keepdims=True)

    def take(ref, image, start):
        return ref[span[image], pl.ds(pl.multiple_of(start, 128), 128)]

    def attend(pair, carry):
        for image in range(per):
            query, key, value = (take(qkv_low, image, index * width + pair * 128) for index in range(3))
            outs = []
            for side in (first, jnp.logical_not(first)):
                probs = softmax(jnp.where(side, query, jnp.zeros_like(query)), key)
                outs.append(mxu(probs.astype(low), value, NN))
            mixed[span[image], pl.ds(pl.multiple_of(pair * 128, 128), 128)] = jnp.where(first, outs[0], outs[1]).astype(low)
        return carry

    lax.fori_loop(0, width // 128, attend, 0)
    relay_tick(7)
    arrived(2)
    for image in range(per):
        got = mxu(mixed[span[image], :], attn_out[...], NT)
        proj[span[image], :] = got
        value = stream[span[image], :] + piece(modul, image, 2) * got
        stream[span[image], :] = value
        hat, root = normed(value)
        hat_two[span[image], :] = hat
        root_two[span[image], :] = root
        b_low[span[image], :] = (hat * (1.0 + piece(modul, image, 4)) + piece(modul, image, 3)).astype(low)

    def upper_block(part):
        value = mxu(b_low[...], fc1[part, :], NT)
        active[:, part] = (
            0.5 * value * (1.0 + jnp.tanh(0.7978845608 * (value + 0.044715 * value * value * value)))
        ).astype(low)

    arrived(1)
    blocks_of(4 * width, cut, upper_block)
    arrived(0)
    finish()

    def mlp_block(part):
        mlp[:, part] = mxu(active[...], fc2[part, :], NT)

    blocks_of(width, cut, mlp_block)
    loss = jnp.zeros((), jnp.float32)
    g_last = jnp.zeros((PATCH, width), jnp.float32)
    for image in range(per):
        value = stream[span[image], :] + piece(modul, image, 5) * mlp[span[image], :]
        hat, root = normed(value)
        gain = 1.0 + piece(fmod, image, 1)
        final = (hat * gain + piece(fmod, image, 0)).astype(low)
        diff = mxu(final, last[...], NT) - target[span[image], :]
        share = weight_t[span[image], :] * diff
        loss += 0.5 * jnp.sum(share * diff)
        d_out = share.astype(low)
        g_last += mxu(d_out, final, TN)
        d_final = mxu(d_out, last[...], NN)
        put_row(d_fm, image, 0, d_final)
        put_row(d_fm, image, 1, d_final * hat)
        d_value = norm_back(d_final * gain, hat, root)
        stream[span[image], :] = d_value
        put_row(d_mod, image, 5, d_value * mlp[span[image], :])
        d_mlp[span[image], :] = (piece(modul, image, 5) * d_value).astype(low)
    few[pl.ds(PATCH, 8), :] = jnp.full((8, width), loss, jnp.float32)
    few[pl.ds(PATCH + 8, PATCH), :] = g_last
    few[pl.ds(2 * PATCH + 8, 8), :] = jnp.zeros((8, width), jnp.float32)

    of_fc2 = [i for i in range(count) if chunks[i][0] == 0]
    of_fc1 = [i for i in range(count) if chunks[i][0] == 1]
    of_o = [i for i in range(count) if chunks[i][0] == 2]
    of_qkv = [i for i in range(count) if chunks[i][0] == 3]

    def fc2_step(i):
        first, lanes = chunks[i][3], 2 * chunks[i][4]
        part = pl.ds(first, lanes)
        value = mxu(b_low[...], fc1[part, :], NT)
        inner = jnp.tanh(0.7978845608 * (value + 0.044715 * value * value * value))
        slope = 0.5 * (1.0 + inner) + 0.5 * value * (1.0 - inner * inner) * 0.7978845608 * (
            1.0 + 3.0 * 0.044715 * value * value
        )
        d_upper = (slope * mxu(d_mlp[...], fc2[:, part], NN)).astype(low)
        produce(i, d_mlp, active.at[:, part])
        active[:, part] = d_upper

    def fc1_step(i):
        part = pl.ds(chunks[i][1], chunks[i][2])
        more = mxu(active[:, part], fc1[part, :], NN)
        if i == of_fc1[0]:
            mlp[...] = more
        else:
            mlp[...] += more
        produce(i, active.at[:, part], b_low)

    def o_step(i):
        for image in range(per):
            d_normed = mlp[span[image], :]
            hat = hat_two[span[image], :]
            put_row(d_mod, image, 3, d_normed)
            put_row(d_mod, image, 4, d_normed * hat)
            d_value = stream[span[image], :] + norm_back(
                d_normed * (1.0 + piece(modul, image, 4)), hat, root_two[span[image], :]
            )
            stream[span[image], :] = d_value
            put_row(d_mod, image, 2, d_value * proj[span[image], :])
            b_low[span[image], :] = (piece(modul, image, 2) * d_value).astype(low)
        active[:, pl.ds(0, width)] = mxu(b_low[...], attn_out[...], NN).astype(low)
        produce(i, b_low, mixed)

    def attend_back(pair):
        for image in range(per):
            query, key, value = (take(qkv_low, image, index * width + pair * 128) for index in range(3))
            d_out = take(active, image, pair * 128)
            d_query, d_key, d_value = [], [], []
            for side in (first, jnp.logical_not(first)):
                none = jnp.zeros_like(query)
                probs = softmax(jnp.where(side, query, none), key)
                d_prob = mxu(jnp.where(side, d_out, none), value, NT)
                d_score = (probs * (d_prob - jnp.sum(probs * d_prob, -1, keepdims=True))).astype(low)
                d_value.append(mxu(probs.astype(low), d_out, TN))
                d_query.append(mxu(d_score, key, NN) * scale)
                d_key.append(mxu(d_score, query, TN) * scale)
            for index, both in enumerate((d_query, d_key, d_value)):
                qkv_low[span[image], pl.ds(pl.multiple_of(index * width + pair * 128, 128), 128)] = jnp.where(
                    first, both[0], both[1]
                ).astype(low)

    def norm_one_step():
        @pl.when(is_in(shard, mod_places))
        def _():
            for k in range(len(in_blocks)):
                far_copy(k).start()

        g_patch = jnp.zeros((PATCH, width), jnp.float32)
        for image in range(per):
            d_normed = mxu(qkv_low[span[image], :], qkv[...], NN)
            hat = hat_one[span[image], :]
            put_row(d_mod, image, 0, d_normed)
            put_row(d_mod, image, 1, d_normed * hat)
            d_value = stream[span[image], :] + norm_back(
                d_normed * (1.0 + piece(modul, image, 1)), hat, root_one[span[image], :]
            )
            g_patch += mxu(state[span[image], :], d_value.astype(low), TN)
        few[pl.ds(0, PATCH), :] = g_patch

    def qkv_step(i):
        if i == of_qkv[0]:
            norm_one_step()
        produce(i, qkv_low.at[:, pl.ds(chunks[i][1], chunks[i][2])], a_low)

    def over_y(i):
        y_copy(i).start()

    stages = (None, stage1, stage2, stage3, stage4, stage5, stage6, stage7, stage8, over_y)
    steps = [(fc2_step, i) for i in of_fc2] + [(fc1_step, i) for i in of_fc1] + [(o_step, i) for i in of_o]
    steps += [(attend_back, pair) for pair in range(width // 128)] + [(qkv_step, i) for i in of_qkv]
    for j, (k, i) in enumerate(ORDER):
        if j in BESIDE_AT:
            beside[BESIDE_AT.index(j)]()
        if k == 0:
            step, arg = steps[i]
            step(arg)
        else:
            stages[k](i)

    side_end()
    for i in range(count):
        if turn_away(i, SLOTS) is None:
            core_copy(i).wait_send()
        y_copy(i).wait_send()
        x_copy(i).wait_send()
        for piece in range(PIECES):

            @pl.when(z != piece * stride)
            def _():
                z_copy(i, piece).wait_send()

        if chunks[i][5]:

            @pl.when(y == 0)
            def _():
                cross_copy(i).wait_send()

        @pl.when(owns)
        def _():
            for step in range(1, lines):
                line_copy(i, 0, y, step).wait_send()

        def action(which, side):
            pair_copy(i, which, side, x).wait_send()
            last_copy(i, which, side, core).wait_send()

        sides(i, action)


def step_call(lines, tables, in_cols, far, light):
    width = far[0].shape[1]
    chunks = heavy_chunks(width)
    count = len(chunks)
    low, full = jnp.bfloat16, jnp.float32
    (_, in_tiles), (_, head_tiles), (_, embed_tiles), shards = tables
    state, traits = light[0], light[6]
    tokens, group = state.shape[0], traits.shape[0]
    rows = 2 * lines * group
    modul_shape, fmod_shape = (group, 6 * width), (group, 2 * width)
    segments = heavy_segments(width, in_cols, tables[0][0], far[1].shape[0], shards)
    most = max(len(parts) for parts in segments)
    in_lanes, head_lanes, embed_lanes = in_tiles * 128, head_tiles * 128, embed_tiles * 128
    rest_lanes = 2 * head_lanes + embed_lanes
    few = (2 * PATCH + 16, width)
    few_half = (few[0] // 2, width)
    pair = (group, in_lanes + rest_lanes + embed_lanes)
    sizes = [(part_rows, part_lanes) for _, _, part_rows, _, part_lanes, _ in chunks]
    wide = [item for item, chunk in zip(sizes, chunks) if chunk[0] == 0][0]
    tall = max(item for item, chunk in zip(sizes, chunks) if chunk[0] != 0)
    dma = pltpu.SemaphoreType.DMA
    heavy = [(width, 4 * width), (4 * width, width), (width, width), (3 * width, width)]
    shapes = [(item, low) for item in heavy] + [
        ((rows, in_lanes), low),
        ((rows, head_lanes), low),
        ((rows, head_lanes), low),
        ((rows, embed_lanes), full),
        ((rows, embed_lanes), low),
        (few, full),
        ((rows, width), full),
        ((rows, width), low),
        ((rows, traits.shape[1]), full),
    ]
    pass_scratch = [
        ((tokens, width), full),
        ((tokens, width), full),
        ((tokens, width), full),
        ((tokens, 1), full),
        ((tokens, 1), full),
        ((tokens, width), low),
        ((tokens, 3 * width), low),
        ((tokens, width), low),
        ((tokens, width), full),
        ((tokens, width), low),
        ((tokens, 4 * width), low),
        ((tokens, width), full),
        ((tokens, width), low),
    ]
    scratch = [
        (few_half, full),
        (few_half, full),
        (few_half, full),
        ((2,) + few_half, full),
        ((lines,) + few_half, full),
        (modul_shape, full),
        (fmod_shape, full),
        (modul_shape, full),
        (fmod_shape, full),
        ((group, in_lanes + head_lanes), full),
        ((group, width), full),
        ((shards, group, width), full),
        ((group, width), full),
        ((shards, group, width), full),
        (pair, full),
        (pair, full),
        ((lines, 2 * group, in_lanes), low),
        ((lines, 2 * group, rest_lanes), low),
        ((lines, 2 * group, embed_lanes), full),
    ]
    gather_scratch = [
        ((rows, embed_lanes), full),
        (modul_shape, full),
        (fmod_shape, full),
        ((PATCH, width), low),
        ((PATCH, width), low),
        ((shards, rows, embed_lanes), low),
        ((shards, rows, embed_lanes), full),
        ((shards, PATCH, embed_lanes), low),
        ((shards, rows, head_lanes), full),
        ((rows, head_lanes), full),
        ((shards, group, in_lanes), full),
        ((group, in_lanes), full),
        ((shards, group, head_lanes), full),
        ((group, head_lanes), full),
        ((PATCH, width), low),
        ((shards,) + traits.shape, full),
        (traits.shape, full),
        (traits.shape, full),
        ((lines, 2 * group, traits.shape[1]), full),
    ]
    vmem, anywhere = pl.BlockSpec(memory_space=pltpu.VMEM), pl.BlockSpec(memory_space=pl.ANY)
    return pl.pallas_call(
        functools.partial(step_kernel, lines, chunks, tables, in_cols),
        out_shape=[jax.ShapeDtypeStruct(*item) for item in shapes],
        in_specs=[anywhere] * len(far) + [vmem] * len(light),
        out_specs=[vmem] * len(shapes),
        scratch_shapes=[pltpu.VMEM((r, c), low) for r, c in sizes]
        + [pltpu.VMEM((r // 2, c), low) for r, c in sizes]
        + [pltpu.VMEM((r // 4, c), low) for r, c in sizes]
        + [pltpu.VMEM((lines - 1, r // 4 // PIECES, c), low) for r, c in sizes]
        + [
            dma((count, 8)),
            dma((count, 8)),
            dma((count, PIECES)),
            dma((count, lines - 1)),
            dma((count, 2, lines - 1)),
            dma((count, 2, PIECES)),
        ]
        + [pltpu.VMEM((SLOTS,) + item, low) for item in (wide, tall)] * 2
        + [pltpu.SemaphoreType.REGULAR, pltpu.SemaphoreType.REGULAR, dma((9,))]
        + [pltpu.VMEM(*item) for item in ((modul_shape, full), (fmod_shape, full), (few, full))]
        + [pltpu.VMEM(*item) for item in pass_scratch]
        + [pltpu.VMEM(*item) for item in scratch]
        + [
            dma((lines + 6,)),
            dma((lines + 6,)),
            dma((4, shards - 1)),
            dma((4, shards - 1)),
            dma((3, lines - 1)),
            dma((3, lines - 1)),
        ]
        + [pltpu.VMEM(*item) for item in gather_scratch]
        + [dma((most,)), dma((most,))]
        + [dma((most, 2))] * 4
        + [dma((most, 4))] * 2
        + [dma((most,)), dma((most,)), dma((8, shards - 1)), dma((8, shards - 1)), dma((most,)), dma((lines,)), dma((lines,))],
        compiler_params=pltpu.CompilerParams(
            collective_id=1, has_side_effects=True, vmem_limit_bytes=64 * 1024 * 1024 - 65536
        ),
    )(*far, *light)


def placed_traits(traits, lanes):
    lead = -(-(PATCH + FREQ) // 128) * 128
    lane = lax.broadcasted_iota(jnp.int32, (traits.shape[0], lead), 1)
    here = jnp.logical_and(lane >= PATCH, lane < PATCH + FREQ)
    freq = jnp.where(here, traits[:, :lead], 0.0).astype(jnp.bfloat16)
    named = lax.broadcasted_iota(jnp.int32, (traits.shape[0], lanes), 1).astype(jnp.float32)
    onehot = jnp.where(named == traits[:, lead : lead + 1], 1.0, 0.0).astype(jnp.bfloat16)
    return freq, onehot


def windows(cols, shards):
    starts = [place * cols // 128 for place in range(shards)]
    tiles = max(-(-(place + 1) * cols // 128) - start for place, start in enumerate(starts))
    return starts, tiles


def heavy_segments(width, in_cols, in_starts, out_rows, shards):
    every = []
    for place in range(shards):
        parts = []
        for array, low, high, most in ((3, 6 * width, 9 * width, 640), (1, 9 * width, 13 * width, 640)):
            first, last = max(low, place * in_cols), min(high, (place + 1) * in_cols)
            while first < last:
                rows = min(most, last - first)
                parts.append((0, first - in_starts[place] * 128, array, first - low, rows, 0, 0, width))
                first += rows
            if array == 3:
                parts.append((1, 0, 2, place * out_rows, out_rows, 0, 0, width))
        parts.append((1, 0, 0, place * out_rows, out_rows, width, 0, 4 * width))
        every.append(parts)
    return every


def gather_steps(
    plan, remote, line_peer, in_blocks, far_copy,
    out_t, in_t, head_t, embed, traits,
    fc2, fc1, attn_out, qkv, cond_full, time_act, time_one, modul, fmod, patch, last, all_traits,
    s1_slot, tab_slot, patch_slot, two_slot, two_own, mod_slot, mod_own, fm_slot, fm_own, last_own,
    trait_slot, trait_own, trait_got, line_slot,
    ysend, yrecv, xsend, xrecv, zsend, zrecv, csend, crecv, osend, orecv, small_send, small_recv, local_sem,
    trait_send, trait_recv,
):
    segments, (in_starts, in_tiles), (head_starts, head_tiles), (embed_starts, embed_tiles), lines = plan
    shards = len(segments)
    arrays = (fc2, fc1, attn_out, qkv)
    sources = (in_t, out_t)
    rep, shard = lax.axis_index("rep"), lax.axis_index("shard")
    place_here = lax.rem(rep, 2 * lines)
    x, z = lax.rem(place_here, 2), lax.div(place_here, 2)
    zb = lax.rem(z, 2)
    core, y = lax.rem(shard, 2), lax.div(shard, 2)
    to_core = (rep, shard + 1 - 2 * core)
    to_y = (rep, shard + 2 - 4 * y)
    to_x = (rep + 1 - 2 * x, shard)
    to_z = (rep + 2 - 4 * zb, shard)
    width = head_t.shape[1]
    others = [(rep, lax.rem(shard + step, shards)) for step in range(1, shards)]
    mod_places = [o for o in range(shards) if in_starts[o] * 128 < 6 * width]
    computes_mod = functools.reduce(jnp.logical_or, [shard == o for o in mod_places])

    @pl.when(computes_mod)
    def _():
        for k in range(len(in_blocks)):
            far_copy(k).start()

    def small(kind, source, slots, step):
        return remote(
            source, slots.at[shard], small_send.at[kind, step - 1], small_recv.at[kind, step - 1], others[step - 1]
        )

    def small_arrival(kind, slots, step):
        origin = lax.rem(shard + shards - step, shards)
        return remote(
            slots.at[origin], slots.at[origin], small_send.at[kind, step - 1], small_recv.at[kind, step - 1], to_core
        )

    def exchange(kind, source, slots, origins=None):
        for step in range(1, shards):
            if origins is None:
                small(kind, source, slots, step).start()
            else:
                sends = functools.reduce(jnp.logical_or, [shard == o for o in origins])

                @pl.when(sends)
                def _():
                    small(kind, source, slots, step).start()

    def arrive(kind, slots, origins=None):
        for step in range(1, shards):
            if origins is None:
                small_arrival(kind, slots, step).wait_recv()
            else:
                origin = lax.rem(shard + shards - step, shards)

                @pl.when(functools.reduce(jnp.logical_or, [origin == o for o in origins]))
                def _():
                    small_arrival(kind, slots, step).wait_recv()

    def sent(kind, source, slots, origins=None):
        for step in range(1, shards):
            if origins is None:
                small(kind, source, slots, step).wait_send()
            else:

                @pl.when(functools.reduce(jnp.logical_or, [shard == o for o in origins]))
                def _():
                    small(kind, source, slots, step).wait_send()

    def place_tiles(target, slots, starts, tiles, origins, dtype, first=0):
        total = target.shape[1] // 128
        for tile in range(total):
            parts = [
                slots[o, :, (tile + first - starts[o]) * 128 : (tile + first - starts[o] + 1) * 128]
                for o in origins
                if 0 <= tile + first - starts[o] < tiles
            ]
            target[:, tile * 128 : (tile + 1) * 128] = functools.reduce(jnp.add, parts).astype(dtype)

    def source_part(place, k):
        source, row, array, _, rows, lane, _, lanes = segments[place][k]
        return sources[source].at[pl.ds(row, rows), pl.ds(lane, lanes)]

    def target_part(place, k, start=0, rows=None):
        _, _, array, row, total, _, lane, lanes = segments[place][k]
        start = row + start
        if not isinstance(start, int):
            start = pl.multiple_of(start, 16)
        return arrays[array].at[pl.ds(start, total if rows is None else rows), pl.ds(lane, lanes)]

    def quarter(place, k, index):
        size = segments[place][k][4] // 4
        return target_part(place, k, index * size, size)

    def half_of(place, k, index, second):
        size = segments[place][k][4] // 4
        cut = -(-size // 32) * 16
        return target_part(place, k, index * size + (cut if second else 0), size - cut if second else cut)

    me = x * 2 + zb
    across_x, along_z, corner = (1 - x) * 2 + zb, x * 2 + 1 - zb, (1 - x) * 2 + 1 - zb

    def y_copy(place, k):
        size = segments[place][k][4] // 4
        source, row, _, _, _, lane, _, lanes = segments[place][k]
        part = sources[source].at[pl.ds(pl.multiple_of(row + me * size, 16), size), pl.ds(lane, lanes)]
        return remote(part, quarter(place, k, me), ysend.at[k], yrecv.at[k], to_y)

    def owner_copy(place, k):
        return remote(source_part(place, k), target_part(place, k), osend.at[k], orecv.at[k], to_core)

    def own_copy(place, k):
        return pltpu.make_async_copy(source_part(place, k), target_part(place, k), local_sem.at[k])

    def hop(part, sems, k, slot, peer):
        return remote(part, part, sems[0].at[k, slot], sems[1].at[k, slot], peer)

    xs, zs, cs = (xsend, xrecv), (zsend, zrecv), (csend, crecv)

    def begin(k, across):
        for place in range(shards):
            if k < len(segments[place]):

                @pl.when(shard == place)
                def _():
                    if across:
                        y_copy(place, k).start()
                    else:
                        owner_copy(place, k).start()
                        own_copy(place, k).start()

    def relay(place, stage, k):
        if stage == 0:
            y_copy(place, k).wait_recv()
            hop(quarter(place, k, me), xs, k, 0, to_x).start()
            hop(quarter(place, k, me), zs, k, 0, to_z).start()
            hop(quarter(place, k, me), cs, k, 0, to_core).start()
        elif stage == 1:
            hop(quarter(place, k, across_x), xs, k, 0, to_x).wait_recv()
            hop(half_of(place, k, across_x, False), zs, k, 1, to_z).start()
            hop(quarter(place, k, along_z), zs, k, 0, to_z).wait_recv()
            hop(half_of(place, k, along_z, True), xs, k, 1, to_x).start()
            hop(quarter(place, k, across_x), cs, k, 1, to_core).start()
            hop(quarter(place, k, along_z), cs, k, 2, to_core).start()
        else:
            hop(half_of(place, k, corner, False), zs, k, 1, to_z).wait_recv()
            hop(half_of(place, k, corner, True), xs, k, 1, to_x).wait_recv()
            hop(quarter(place, k, corner), cs, k, 3, to_core).start()

    def relay_tick(tick):
        for place in range(shards):

            @pl.when(to_y[1] == place)
            def _():
                for stage in range(3):
                    if 0 <= tick - stage < len(segments[place]):
                        relay(place, stage, tick - stage)

    def trait_line(step):
        return remote(
            line_slot.at[z], line_slot.at[z], trait_send.at[step], trait_recv.at[step], line_peer(step)
        )

    def trait_line_arrival(step):
        origin = lax.rem(z + lines - step, lines)
        return remote(line_slot.at[origin], line_slot.at[origin], trait_send.at[step], trait_recv.at[step], to_core)

    trait_pair = remote(trait_own, trait_got, trait_send.at[0], trait_recv.at[0], to_x)
    trait_slot[shard] = traits[...]
    exchange(7, traits, trait_slot)
    begin(0, True)
    arrive(7, trait_slot)
    trait_own[...] = functools.reduce(jnp.add, [trait_slot[o] for o in range(shards)])
    trait_pair.start()
    begin(1, True)
    trait_pair.wait_recv()
    own, got = trait_own[...], trait_got[...]
    line_slot[z] = jnp.concatenate([jnp.where(x == 0, own, got), jnp.where(x == 0, got, own)], 0)
    for step in range(1, lines):
        trait_line(step).start()
    relay_tick(0)
    begin(2, True)
    for step in range(1, lines):
        trait_line_arrival(step).wait_recv()
    count_in_line = 2 * traits.shape[0]
    for at in range(lines):
        all_traits[at * count_in_line : (at + 1) * count_in_line, :] = line_slot[at]
    freq, onehot = placed_traits(all_traits[...], embed.shape[1])

    nt = (((1,), (1,)), ((), ()))
    own_one = lax.dot_general(freq, embed[:, : freq.shape[1]], nt, preferred_element_type=jnp.float32)
    time_one[...] = own_one
    s1_slot[shard] = (own_one * jax.nn.sigmoid(own_one)).astype(jnp.bfloat16)
    tab_slot[shard] = lax.dot_general(onehot, embed[...], nt, preferred_element_type=jnp.float32)
    eye = lax.broadcasted_iota(jnp.int32, (PATCH, 128), 0) == lax.broadcasted_iota(jnp.int32, (PATCH, 128), 1)
    eye = jnp.where(eye, 1.0, 0.0).astype(jnp.bfloat16)
    patch_slot[shard] = lax.dot_general(eye, embed[:, :128], nt, preferred_element_type=jnp.float32).astype(jnp.bfloat16)
    exchange(0, s1_slot.at[shard], s1_slot)
    exchange(1, tab_slot.at[shard], tab_slot)
    exchange(2, patch_slot.at[shard], patch_slot)
    relay_tick(1)
    begin(3, True)
    last_place = [o for o in range(shards) if 0 <= 3 * width // 128 - head_starts[o] < head_tiles][-1]
    last_row = (3 * width // 128 - head_starts[last_place]) * 128
    last_own[...] = head_t[last_row : last_row + 16, :]

    @pl.when(shard == last_place)
    def _():
        last[...] = last_own[...]
        for step in range(1, shards):
            remote(last_own, last, small_send.at[6, step - 1], small_recv.at[6, 0], others[step - 1]).start()

    head_places = [o for o in range(shards) if head_starts[o] * 128 < width]
    fm_places = [o for o in range(shards) if (head_starts[o] + head_tiles) * 128 > width]
    group = modul.shape[0]

    arrive(0, s1_slot)
    place_tiles(time_act, s1_slot, embed_starts, embed_tiles, range(shards), jnp.bfloat16)
    two_own[...] = lax.dot_general(time_act[...], head_t[...], nt, preferred_element_type=jnp.float32)
    two_slot[shard] = two_own[...]
    exchange(3, two_own, two_slot, head_places)
    relay_tick(2)
    begin(4, True)
    arrive(1, tab_slot)
    arrive(3, two_slot, head_places)
    place_tiles(cond_full, tab_slot, embed_starts, embed_tiles, range(shards), jnp.float32)
    for tile in range(width // 128):
        span = slice(tile * 128, (tile + 1) * 128)
        for o in head_places:
            if 0 <= tile - head_starts[o] < head_tiles:
                cond_full[:, span] += two_slot[o, :, (tile - head_starts[o]) * 128 : (tile - head_starts[o] + 1) * 128]
    mine = cond_full[pl.ds(pl.multiple_of(place_here * group, 8), group), :]
    cond = (mine * jax.nn.sigmoid(mine)).astype(jnp.bfloat16)

    @pl.when(computes_mod)
    def _():
        for k, block in enumerate(in_blocks):
            far_copy(k).wait()
            span = slice(k * block.shape[0], (k + 1) * block.shape[0])
            mod_own[:, span] = lax.dot_general(cond, block[...], nt, preferred_element_type=jnp.float32)
        mod_slot[shard] = mod_own[...]

    exchange(4, mod_own, mod_slot, mod_places)
    fm_own[...] = lax.dot_general(cond, head_t[...], nt, preferred_element_type=jnp.float32)
    fm_slot[shard] = fm_own[...]
    exchange(5, fm_own, fm_slot, fm_places)
    relay_tick(3)
    begin(5, True)
    begin(0, False)
    begin(1, False)
    begin(2, False)
    begin(3, False)
    begin(4, False)
    begin(5, False)
    arrive(2, patch_slot)
    place_tiles(patch, patch_slot, embed_starts, embed_tiles, range(shards), jnp.bfloat16)
    arrive(4, mod_slot, mod_places)
    arrive(5, fm_slot, fm_places)
    place_tiles(modul, mod_slot, in_starts, in_tiles, mod_places, jnp.float32)
    place_tiles(fmod, fm_slot, head_starts, head_tiles, fm_places, jnp.float32, width // 128)

    @pl.when(shard != last_place)
    def _():
        remote(last_own, last, small_send.at[6, 0], small_recv.at[6, 0], to_core).wait_recv()

    def arrived(array):
        for place in range(shards):
            of_array = [k for k, part in enumerate(segments[place]) if part[2] == array]

            @pl.when(shard == place)
            def _():
                for k in of_array:
                    own_copy(place, k).wait()

            @pl.when(to_core[1] == place)
            def _():
                for k in of_array:
                    remote(target_part(place, k), target_part(place, k), osend.at[k], orecv.at[k], to_core).wait_recv()

            @pl.when(shards - 1 - shard == place)
            def _():
                for k in of_array:
                    for slot, index in enumerate((me, across_x, along_z, corner)):
                        part = quarter(place, k, index)
                        remote(part, part, csend.at[k, slot], crecv.at[k, slot], to_core).wait_recv()

    def finish():
        for place in range(shards):
            count = len(segments[place])

            @pl.when(shard == place)
            def _():
                for k in range(count):
                    y_copy(place, k).wait_send()
                    owner_copy(place, k).wait_send()

            @pl.when(to_y[1] == place)
            def _():
                for k in range(count):
                    hop(quarter(place, k, me), xs, k, 0, to_x).wait_send()
                    hop(quarter(place, k, me), zs, k, 0, to_z).wait_send()
                    hop(half_of(place, k, across_x, False), zs, k, 1, to_z).wait_send()
                    hop(half_of(place, k, along_z, True), xs, k, 1, to_x).wait_send()
                    for slot, index in enumerate((me, across_x, along_z, corner)):
                        hop(quarter(place, k, index), cs, k, slot, to_core).wait_send()

        trait_pair.wait_send()
        for step in range(1, lines):
            trait_line(step).wait_send()
        sent(7, traits, trait_slot)
        sent(0, s1_slot.at[shard], s1_slot)
        sent(1, tab_slot.at[shard], tab_slot)
        sent(2, patch_slot.at[shard], patch_slot)
        sent(3, two_own, two_slot, head_places)
        sent(4, mod_own, mod_slot, mod_places)
        sent(5, fm_own, fm_slot, fm_places)

        @pl.when(shard == last_place)
        def _():
            for step in range(1, shards):
                remote(last_own, last, small_send.at[6, step - 1], small_recv.at[6, 0], others[step - 1]).wait_send()

    return relay_tick, arrived, finish


def windowed(in_t, out_t, head_t, embed_t, shards):
    place = lax.axis_index("shard")
    width = head_t.shape[1]
    low = jnp.bfloat16

    def window(item_t, starts, tiles, lanes):
        rows = item_t.shape[0]
        offsets = [o * rows - start * 128 for o, start in enumerate(starts)]
        most = max(offsets)
        padded = jnp.pad(item_t, ((most, tiles * 128 - rows), (0, lanes - item_t.shape[1])))
        begin = most - jnp.asarray(offsets, jnp.int32)[place]
        return lax.dynamic_slice_in_dim(padded, begin, tiles * 128, 0).astype(low)

    in_cols, head_cols, embed_cols = in_t.shape[0], head_t.shape[0], embed_t.shape[0]
    in_starts, in_tiles = windows(in_cols, shards)
    head_starts, head_tiles = windows(head_cols, shards)
    embed_starts, embed_tiles = windows(embed_cols, shards)
    in_t = window(in_t, in_starts, in_tiles, width)
    head_t = window(head_t, head_starts, head_tiles, width)
    embed = window(embed_t, embed_starts, embed_tiles, -(-embed_t.shape[1] // 128) * 128)
    return in_t, out_t.astype(low), head_t, embed


def own_segments(width, in_cols, in_starts, out_rows, shards):
    every = []
    for place in range(shards):
        parts = []
        for array, low, high in ((3, 6 * width, 9 * width), (1, 9 * width, 13 * width)):
            first, last = max(low, place * in_cols), min(high, (place + 1) * in_cols)
            if first < last:
                parts.append((array, first - low, last - first, first - in_starts[place] * 128))
        every.append(parts)
    return every


def total_kernel(
    tables, segments, fc2, fc1, attn_out, qkv, w_in, w_out, w_head, w_embed,
    d_in, d_fin, d_two, d_one, d_full, few, cond_full, time_act, traits, c_in, c_out, c_head, c_embed,
    g_in, g_out, g_head, g_embed, n_in, n_out, n_head, n_embed, stats,
    own_t, own_out, grad_t, head_t, t_out, t_head, t_embed, v_in, v_out, v_head, v_embed,
    load, write, fetch,
):
    (in_starts, in_tiles), (head_starts, head_tiles), (embed_starts, embed_tiles), shards = tables
    arrays = (fc2, fc1, attn_out, qkv)
    shard = lax.axis_index("shard")
    width = cond_full.shape[1]
    in_cols, head_cols, embed_cols, out_cols = (item.shape[0] for item in (w_in, w_head, w_embed, w_out))
    full, low = jnp.float32, jnp.bfloat16
    span = lane_span(width, w_embed.shape[1])

    weights = ((w_in, v_in), (w_out, v_out), (w_head, v_head), (w_embed, v_embed))
    reads = [pltpu.make_async_copy(source, target, load.at[k]) for k, (source, target) in enumerate(weights)]
    for copy in reads:
        copy.start()

    def heavy_copies(place):
        copies = []
        for k, (array, row, rows, at) in enumerate(segments[place]):
            copies.append(
                pltpu.make_async_copy(
                    arrays[array].at[pl.ds(row, rows), :], own_t.at[pl.ds(at, rows), :], fetch.at[k]
                )
            )
        for k, array in ((2, 2), (3, 0)):
            lane = 0 if array == 2 else width
            copies.append(
                pltpu.make_async_copy(
                    arrays[array].at[pl.ds(place * out_cols, out_cols), :],
                    own_out.at[:, pl.ds(lane, arrays[array].shape[1])],
                    fetch.at[k],
                )
            )
        return copies

    for place in range(shards):

        @pl.when(shard == place)
        def _():
            for copy in heavy_copies(place):
                copy.start()
            edges = [0]
            for _, _, rows, at in segments[place]:
                edges += [at, at + rows]
            edges.append(in_tiles * 128)
            for start, stop in zip(edges[0::2], edges[1::2]):
                if start < stop:
                    own_t[start:stop, :] = jnp.zeros((stop - start, width), low)

    def decayed(state, total, count):
        return decay * state + (1.0 - decay) * (total / count + eps_one)

    def to_lanes(column):
        return jnp.broadcast_to(column, (column.shape[0], 128)).T[:1, :]

    def to_column(lanes):
        return jnp.broadcast_to(lanes, (128, lanes.shape[1])).T[:, :1]

    def squares_of(value, state, fresh_out, start, size):
        square = value * value
        sums = to_lanes(jnp.sum(square, -1, keepdims=True))[:, :size]
        fresh = decayed(state[:, start : start + size], sums, value.shape[1])
        fresh_out[:, start : start + size] = fresh
        inverse = 1.0 / fresh
        if size < value.shape[0]:
            inverse = jnp.concatenate([inverse, jnp.zeros((1, value.shape[0] - size), full)], 1)
        return jnp.sum(square, 0, keepdims=True), jnp.sum(square * to_column(inverse), 0, keepdims=True)

    def put(start, plain, scaled):
        stats[:, start : start + plain.shape[1]] = plain
        stats[:, span + start : span + start + plain.shape[1]] = scaled

    def column_blocks(total):
        return [(start, min(128, total - start)) for start in range(0, total, 128)]

    def by_blocks(take, total, state, fresh_out, place):
        plain, scaled = jnp.zeros((1, width), full), jnp.zeros((1, width), full)
        for start, size in column_blocks(total):
            value = take(start, size)
            if size < 128:
                value = jnp.concatenate([value, jnp.zeros((128 - size, width), full)], 0)
            more, more_scaled = squares_of(value, state, fresh_out, start, size)
            plain, scaled = plain + more, scaled + more_scaled
        put(place, plain, scaled)

    cond = cond_full[...]
    cond = (cond * jax.nn.sigmoid(cond)).astype(low)

    lanes_all = -(-w_embed.shape[1] // 128) * 128
    freq, onehot = placed_traits(traits[...], lanes_all)
    square_one = lax.broadcasted_iota(jnp.int32, (PATCH, lanes_all), 0)
    eye = jnp.where(square_one == lax.broadcasted_iota(jnp.int32, (PATCH, lanes_all), 1), 1.0, 0.0).astype(low)

    def exact(value, picks):
        total = None
        for _ in range(3):
            part = value.astype(low)
            value = value - part.astype(full)
            term = mxu(part, picks, TN)
            total = term if total is None else total + term
        return total

    for place in range(shards):

        @pl.when(shard == place)
        def _():
            lead = place * embed_cols - embed_starts[place] * 128
            lanes = slice(embed_starts[place] * 128, (embed_starts[place] + embed_tiles) * 128)
            value = exact(d_full[...], onehot) + exact(few[0:PATCH, lanes], eye)
            value = value[lead : lead + embed_cols, :]
            time = mxu(d_one[...], freq, TN)[lead : lead + embed_cols, :]
            t_embed[:, : freq.shape[1]] = value[:, : freq.shape[1]] + time
            t_embed[:, freq.shape[1] :] = value[:, freq.shape[1] : w_embed.shape[1]]

    pltpu.make_async_copy(t_embed, g_embed, write.at[3]).start()
    value = jnp.concatenate([t_embed[...], jnp.zeros((embed_cols, lanes_all - w_embed.shape[1]), full)], 1)
    square = value * value
    fresh = decayed(c_embed[...], to_lanes(jnp.sum(square, -1, keepdims=True)), w_embed.shape[1])
    n_embed[...] = fresh
    put(7 * width, jnp.sum(square, 0, keepdims=True), jnp.sum(square * to_column(1.0 / fresh), 0, keepdims=True))

    head_t[...] = mxu(d_two[...], time_act[...], TN) + mxu(d_fin[...], cond, TN)
    last_place = [o for o in range(shards) if 0 <= 3 * width // 128 - head_starts[o] < head_tiles][-1]
    last_row = (3 * width // 128 - head_starts[last_place]) * 128

    @pl.when(shard == last_place)
    def _():
        head_t[last_row : last_row + PATCH, :] = few[PATCH + 8 : 2 * PATCH + 8, :]

    for place in range(shards):

        @pl.when(shard == place)
        def _():
            lead = place * head_cols - head_starts[place] * 128
            t_head[...] = head_t[lead : lead + head_cols, :]

    pltpu.make_async_copy(t_head, g_head, write.at[2]).start()
    by_blocks(lambda start, size: t_head[start : start + size, :], head_cols, c_head, n_head, 6 * width)

    for place in range(shards):

        @pl.when(shard == place)
        def _():
            for copy in heavy_copies(place):
                copy.wait()

    def light(index, carry):
        part = pl.ds(pl.multiple_of(index * 128, 128), 128)
        grad_t[part, :] = mxu(d_in[:, part], cond, TN) + own_t[part, :].astype(full)
        return carry

    lax.fori_loop(0, in_tiles, light, 0)
    lead = lax.rem(shard * in_cols, 128)
    write_in = pltpu.make_async_copy(grad_t.at[pl.ds(pl.multiple_of(lead, 64), in_cols), :], g_in, write.at[0])
    write_in.start()
    by_blocks(
        lambda start, size: grad_t[pl.ds(pl.multiple_of(lead + start, 64), size), :], in_cols, c_in, n_in, 0
    )

    sums = jnp.zeros((out_cols, 1), full)
    for index in range(5):
        value = own_out[:, index * width : (index + 1) * width].astype(full)
        t_out[:, index * width : (index + 1) * width] = value
        sums += jnp.sum(value * value, -1, keepdims=True)
    pltpu.make_async_copy(t_out, g_out, write.at[1]).start()
    fresh = decayed(c_out[...], to_lanes(sums), 5 * width)
    n_out[...] = fresh
    column = to_column(1.0 / fresh)
    for index in range(5):
        value = t_out[:, index * width : (index + 1) * width]
        square = value * value
        put(width + index * width, jnp.sum(square, 0, keepdims=True), jnp.sum(square * column, 0, keepdims=True))

    for copy in reads:
        copy.wait()
    for k, (_, value) in enumerate(weights):
        rows, cols = value.shape

        def squares(index, carry):
            block = value[pl.ds(pl.multiple_of(index * 64, 64), 64), :]
            return carry + jnp.sum(block * block, 0, keepdims=True)

        total = lax.fori_loop(0, rows // 64, squares, jnp.zeros((1, cols), full))
        if rows % 64:
            block = value[rows // 64 * 64 :, :]
            total += jnp.sum(block * block, 0, keepdims=True)
        start = 2 * span + k * 128
        stats[:, start : start + 128] = jnp.broadcast_to(jnp.sum(total, -1, keepdims=True) / 128.0, (1, 128))
    write_in.wait()
    for k, (source, target) in enumerate(((t_out, g_out), (t_head, g_head), (t_embed, g_embed))):
        pltpu.make_async_copy(source, target, write.at[k + 1]).wait()


def lane_span(width, embed_rows):
    return 7 * width + -(-embed_rows // 128) * 128


def total_call(tables, heavy, weights, light, cols):
    (in_starts, in_tiles), (_, head_tiles), _, shards = tables
    low, full = jnp.bfloat16, jnp.float32
    width = heavy[2].shape[0]
    w_in, w_out, w_head, w_embed = weights
    lanes = 2 * lane_span(width, w_embed.shape[1]) + 4 * 128
    segments = own_segments(width, w_in.shape[0], in_starts, w_out.shape[0], shards)
    shapes = [(item.shape, full) for item in weights] + [(item.shape, full) for item in cols] + [((1, lanes), full)]
    anywhere, vmem = pl.BlockSpec(memory_space=pl.ANY), pl.BlockSpec(memory_space=pltpu.VMEM)
    scratch = [
        ((in_tiles * 128, width), low),
        (w_out.shape, low),
        ((in_tiles * 128, width), full),
        ((head_tiles * 128, width), full),
    ]
    scratch += [(item.shape, full) for item in weights[1:]] + [(item.shape, full) for item in weights]
    return pl.pallas_call(
        functools.partial(total_kernel, tables, segments),
        out_shape=[jax.ShapeDtypeStruct(*item) for item in shapes],
        in_specs=[anywhere] * 8 + [vmem] * (len(light) + 4),
        out_specs=[anywhere] * 4 + [vmem] * 5,
        scratch_shapes=[pltpu.VMEM(*item) for item in scratch] + [pltpu.SemaphoreType.DMA((4,))] * 3,
        compiler_params=pltpu.CompilerParams(vmem_limit_bytes=60 * 1024 * 1024),
    )(*heavy, *weights, *light, *cols)


def finish_kernel(shards, sizes, own, r_in, r_out, r_head, r_embed, n_in, n_out, n_head, n_embed, s_in, s_out, s_head, s_embed, rms, slots, send, recv):
    rep, shard = lax.axis_index("rep"), lax.axis_index("shard")
    barrier = pltpu.get_barrier_semaphore()
    for step in range(1, shards):
        peer = (rep, lax.rem(shard + step, shards))
        pl.semaphore_signal(barrier, inc=1, device_id=peer, device_id_type=MESH)
    pl.semaphore_wait(barrier, shards - 1)

    def copy(step):
        return pltpu.make_async_remote_copy(
            src_ref=own,
            dst_ref=slots.at[shard],
            send_sem=send.at[step - 1],
            recv_sem=recv.at[step - 1],
            device_id=(rep, lax.rem(shard + step, shards)),
            device_id_type=MESH,
        )

    for step in range(1, shards):
        copy(step).start()
    slots[shard] = own[...]
    for step in range(1, shards):
        copy(step).wait()
    total = functools.reduce(jnp.add, [slots[o] for o in range(shards)])
    states, fresh, scales = (r_in, r_out, r_head, r_embed), (n_in, n_out, n_head, n_embed), (s_in, s_out, s_head, s_embed)
    starts, start = [], 0
    for rows, _ in sizes:
        starts.append(start)
        start += -(-rows // 128) * 128
    update, means = jnp.zeros((1, 1), jnp.float32), []
    for k, (rows, cols) in enumerate(sizes):
        row = decay * states[k][...] + (1.0 - decay) * (total[:, starts[k] : starts[k] + rows] / cols + eps_one)
        fresh[k][...] = row
        mean = jnp.mean(row, -1, keepdims=True)
        means.append(mean)
        update += mean * jnp.sum(total[:, start + starts[k] : start + starts[k] + rows] / row, -1, keepdims=True)
    update = jnp.sqrt(update / sum(rows * cols for rows, cols in sizes))
    rms[...] = jnp.broadcast_to(update, rms.shape)
    factor = jnp.maximum(1.0, update / clip_level)
    for k, (rows, cols) in enumerate(sizes):
        first = 2 * start + k * 128
        weight = jnp.sqrt(jnp.sum(total[:, first : first + 128], -1, keepdims=True) / (rows * cols))
        scales[k][...] = rate * jnp.maximum(eps_two, weight) / factor * lax.rsqrt(fresh[k][...] / means[k])


def finish_call(shards, sizes, stats, rows_old):
    full = jnp.float32
    shapes = [((1, rows), full) for rows, _ in sizes] * 2 + [((1, 128), full)]
    return pl.pallas_call(
        functools.partial(finish_kernel, shards, sizes),
        out_shape=[jax.ShapeDtypeStruct(*item) for item in shapes],
        in_specs=[pl.BlockSpec(memory_space=pltpu.VMEM)] * 5,
        out_specs=[pl.BlockSpec(memory_space=pltpu.VMEM)] * len(shapes),
        scratch_shapes=[
            pltpu.VMEM((shards,) + stats.shape, full),
            pltpu.SemaphoreType.DMA((shards - 1,)),
            pltpu.SemaphoreType.DMA((shards - 1,)),
        ],
        compiler_params=pltpu.CompilerParams(collective_id=3, has_side_effects=True),
    )(stats, *rows_old)


def on_device(
    latents,
    noises,
    velocity,
    times,
    labels,
    dropped,
    blocks_in,
    blocks_out,
    head_side,
    embed_side,
    state_in_row,
    state_in_col,
    state_out_row,
    state_out_col,
    state_head_row,
    state_head_col,
    state_embed_row,
    state_embed_col,
):
    images = latents.shape[0]
    width = head_side.shape[0]
    shard_count = lax.axis_size("shard")
    place = lax.axis_index("shard")
    in_cols = blocks_in.shape[2]
    head_cols = head_side.shape[1]
    embed_cols = embed_side.shape[1]
    group = images * shard_count
    weights = (blocks_in[0].T, blocks_out[0].T, head_side.T, embed_side.T)
    t_value = (times.astype(jnp.float32) + 1.0) / step_count
    classes = (PATCH + FREQ + jnp.where(dropped == 1, CLASSES - 1, labels)).astype(jnp.float32)
    lines = LINE
    lead = -(-(PATCH + FREQ) // 128) * 128
    own_traits = jnp.concatenate(
        [
            jnp.zeros((images, PATCH), jnp.float32),
            time_freq(t_value, FREQ),
            jnp.zeros((images, lead - PATCH - FREQ), jnp.float32),
            jnp.broadcast_to(classes[:, None], (images, 128)),
        ],
        1,
    )
    traits = lax.dynamic_update_slice(
        jnp.zeros((group, lead + 128), jnp.float32), own_traits, (place * images, 0)
    )
    in_t, out_t, head_t, embed = windowed(*weights, shard_count)
    tcol = t_value[:, None, None]
    state = (
        (1.0 - tcol) * latents.reshape(images, TOK, PATCH)
        + tcol * noises.reshape(images, TOK, PATCH)
    ).astype(jnp.bfloat16)
    tables = (
        windows(in_cols, shard_count),
        windows(head_cols, shard_count),
        windows(embed_cols, shard_count),
        shard_count,
    )
    sums = step_call(
        lines,
        tables,
        in_cols,
        [in_t, out_t],
        [
            state.reshape(images * TOK, PATCH),
            velocity.reshape(images * TOK, PATCH),
            jnp.repeat(t_value, TOK)[:, None],
            jnp.asarray(positions(GRID, width)),
            head_t,
            embed,
            traits,
        ],
    )
    d_in, d_fin, d_two, d_full, d_one, few_sum, cond_full, time_act, all_traits = sums[4:]
    loss_sum = few_sum[PATCH, 0]
    rows_old = (state_in_row, state_out_row, state_head_row[None], state_embed_row[None])
    cols_old = (state_in_col, state_out_col, state_head_col[None], state_embed_col[None])
    *outs, stats = total_call(
        tables,
        sums[:4],
        weights,
        [d_in, d_fin, d_two, d_one, d_full, few_sum, cond_full, time_act, all_traits],
        cols_old,
    )
    totals, cols_new = outs[:4], outs[4:]
    blocks = lax.axis_size("rep") // (2 * lines)
    if blocks > 1:
        apart = [[k * 2 * lines + j for k in range(blocks)] for j in range(2 * lines)]
        totals, loss_sum = lax.psum((totals, loss_sum), "rep", axis_index_groups=apart)
        cols_new, plain, scaled = [], [], []
        for gradient, col_state in zip(totals, cols_old):
            square = gradient * gradient
            fresh = decay * col_state + (1.0 - decay) * (jnp.mean(square, 1)[None] + eps_one)
            pad = (0, -gradient.shape[1] % 128)
            cols_new.append(fresh)
            plain.append(jnp.pad(jnp.sum(square, 0), pad))
            scaled.append(jnp.pad(jnp.sum(square / fresh[0][:, None], 0), pad))
        spans = sum(item.shape[0] for item in plain) * 2
        stats = jnp.concatenate(plain + scaled + [stats[0, spans:]])[None]
    sizes = [(weight.shape[1], weight.shape[0] * shard_count) for weight in weights]
    *outs, rms = finish_call(shard_count, sizes, stats, rows_old)
    rows_new, scales = outs[:4], outs[4:]
    update_rms = rms[0, 0]
    news = [
        (weight - gradient * scale * lax.rsqrt(col_next[0])[:, None]).T
        for weight, gradient, scale, col_next in zip(weights, totals, scales, cols_new)
    ]
    return (
        loss_sum,
        update_rms,
        totals[0].T[None],
        totals[1].T[None],
        totals[2].T,
        totals[3].T,
        rows_new[0],
        cols_new[0],
        rows_new[1],
        cols_new[1],
        rows_new[2][0],
        cols_new[2][0],
        rows_new[3][0],
        cols_new[3][0],
        news[0][None],
        news[1][None],
        news[2],
        news[3],
    )


def solution(mesh):
    placed = (
        P(("rep", "shard"), None),
        P(("rep", "shard"), None),
        P(("rep", "shard"), None),
        P(("rep", "shard")),
        P(("rep", "shard")),
        P(("rep", "shard")),
        P(None, None, "shard"),
        P(None, None, "shard"),
        P(None, "shard"),
        P(None, "shard"),
        P(),
        P(None, "shard"),
        P(),
        P(None, "shard"),
        P(),
        P("shard"),
        P(),
        P("shard"),
    )
    return jax.shard_map(
        on_device,
        mesh=mesh,
        in_specs=placed,
        out_specs=(
            P(),
            P(),
            P(None, None, "shard"),
            P(None, None, "shard"),
            P(None, "shard"),
            P(None, "shard"),
            P(),
            P(None, "shard"),
            P(),
            P(None, "shard"),
            P(),
            P("shard"),
            P(),
            P("shard"),
            P(None, None, "shard"),
            P(None, None, "shard"),
            P(None, "shard"),
            P(None, "shard"),
        ),
        check_vma=False,
    )
```

```python
import functools
import math

import jax
import jax.numpy as jnp
import numpy as np
from jax import lax
from jax.experimental import pallas as pl
from jax.experimental.pallas import tpu as pltpu
from jax.sharding import PartitionSpec as P

HEADS = 12
CLASSES = 1001
FREQ = 256
GRID = 16
PATCH = 16
LAYERS = 1
TOK = 256


decay = 0.5
eps_norm = 1e-06
eps_one = 1e-30
eps_two = 0.001
clip_level = 0.1
rate = 8.0
step_count = 1000.0


def silu(value):
    return value * jax.nn.sigmoid(value)


def positions(grid, width):
    quarter = width // 4
    omega = (1.0 / 10000.0 ** (np.arange(quarter, dtype=np.float32) / quarter)).astype(np.float32)
    index = np.arange(grid * grid)
    row_pos = (index // grid).astype(np.float32)[:, None] * omega[None, :]
    col_pos = (index % grid).astype(np.float32)[:, None] * omega[None, :]
    return np.concatenate([np.sin(row_pos), np.cos(row_pos), np.sin(col_pos), np.cos(col_pos)], 1)


def time_freq(t_value, width):
    half = width // 2
    freqs = jnp.exp(-math.log(10000.0) * jnp.arange(half, dtype=jnp.float32) / half)
    angles = (t_value * step_count)[:, None] * freqs[None, :]
    return jnp.concatenate([jnp.cos(angles), jnp.sin(angles)], -1)


def weight_grad(left, back):
    flat_left = left.reshape(-1, left.shape[-1])
    flat_back = back.reshape(-1, back.shape[-1])
    return lax.dot_general(
        flat_left, flat_back, (((0,), (0,)), ((), ())), preferred_element_type=jnp.float32
    )


MESH = pl.DeviceIdType.MESH
LINE = 4
PIECES = 4
PARTS = (6, 6, 3)
ORDER = (
    (0, 0), (0, 1), (0, 2), (1, 0), (9, 0), (0, 3), (1, 1), (9, 1), (0, 4), (1, 2), (9, 2), (0, 5), (1, 3),
    (2, 0), (9, 3), (0, 6), (1, 4), (0, 7), (2, 1), (9, 4), (1, 5), (0, 8), (3, 0), (1, 6), (9, 5), (2, 2),
    (0, 9), (1, 7), (3, 1), (1, 8), (9, 6), (2, 3), (0, 10), (0, 11), (1, 9), (2, 4), (9, 7), (3, 2), (4, 0),
    (0, 12), (9, 8), (1, 10), (1, 11), (2, 5), (3, 3), (2, 6), (9, 9), (3, 4), (4, 1), (0, 13), (1, 12), (2, 7),
    (9, 10), (4, 2), (6, 0), (3, 5), (0, 14), (2, 8), (3, 6), (9, 11), (4, 3), (0, 15), (4, 4), (2, 9), (3, 7),
    (9, 12), (6, 1), (7, 0), (0, 16), (3, 8), (2, 10), (6, 2), (4, 5), (0, 17), (4, 6), (3, 9), (2, 11), (6, 3),
    (7, 1), (8, 0), (0, 18), (3, 10), (6, 4), (0, 19), (2, 12), (3, 11), (4, 7), (4, 8), (4, 9), (4, 10), (5, 6),
    (6, 5), (1, 13), (9, 13), (7, 2), (7, 3), (7, 4), (8, 1), (0, 20), (3, 12), (0, 21), (0, 22), (4, 11),
    (6, 6), (5, 7), (7, 5), (8, 2), (8, 3), (8, 4), (1, 14), (9, 14), (5, 8), (1, 15), (1, 16), (5, 9), (2, 13),
    (5, 10), (8, 5), (6, 7), (7, 6), (4, 12), (9, 15), (5, 11), (2, 14), (6, 8), (3, 13), (8, 6), (6, 9),
    (9, 16), (6, 10), (7, 7), (6, 12), (3, 14), (2, 15), (6, 11), (7, 8), (8, 7), (4, 13), (2, 16), (7, 9),
    (8, 8), (4, 14), (7, 10), (8, 9), (7, 12), (6, 13), (3, 15), (8, 10), (5, 14), (8, 12), (7, 11), (3, 16),
    (7, 13), (4, 15), (6, 14), (8, 11), (8, 13), (4, 16), (5, 15), (7, 14), (5, 16), (8, 14), (6, 15), (6, 16),
    (7, 15), (8, 15), (7, 16), (8, 16),
)
BESIDE_AT = (84, 95, 107, 119, 131, 143, 155)
SQUARES_AT = (106, 119, 133)
SLOTS = 3
NN = (((1,), (0,)), ((), ()))
NT = (((1,), (1,)), ((), ()))
TN = (((0,), (0,)), ((), ()))


def mxu(left, right, kind):
    return lax.dot_general(left, right, kind, preferred_element_type=jnp.float32)


def blocks_of(total, size, body):
    def step(index, carry):
        body(pl.ds(pl.multiple_of(index * size, size), size))
        return carry

    lax.fori_loop(0, total // size, step, 0)


def heavy_chunks(width):
    half = width // 2
    fc2, fc1, kv = PARTS
    parts = [(0, 0, width, 4 * width // fc2 * k, 2 * width // fc2, False) for k in range(fc2)]
    parts += [(1, 4 * width // fc1 * k, 4 * width // fc1, 0, half, True) for k in range(fc1)]
    parts += [(2, 0, width, 0, half, False), (3, 0, width, 0, half, False)]
    parts += [(3, width + 2 * width // kv * k, 2 * width // kv, 0, half, True) for k in range(kv)]
    return tuple(parts)


def add_rows(target, left, right, rows):
    block = 16

    def body(index, carry):
        span = pl.ds(pl.multiple_of(index * block, block), block)
        target[span] = left[span] + right[span]
        return carry

    lax.fori_loop(0, rows // block, body, 0)


def step_kernel(lines, chunks, tables, in_cols, *refs):
    count = len(chunks)
    (in_far, out_far, w_in, w_out, state, target, weight_t, pos, head_t, embed, traits), refs = refs[:11], refs[11:]
    finals, refs = refs[:4], refs[4:]
    (d_in, d_head, d_two, d_full, d_one, few_sum, cond_full, time_act, all_traits, weight_sq), scratch = refs[:10], refs[10:]
    held, by_y, by_x, by_z = (scratch[k * count : (k + 1) * count] for k in range(4))
    send, recv, zsend, zrecv, wsend, wrecv = scratch[4 * count : 4 * count + 6]
    scratch = scratch[4 * count + 6 :]
    (stage_wide, stage_tall, land_wide, land_tall, free_wide, free_tall, fetch, weight_load, d_mod, d_fm, few), scratch = scratch[:11], scratch[11:]
    (
        stream, hat_one, hat_two, root_one, root_two, a_low, qkv_low, mixed, proj, b_low, active, mlp, d_mlp,
    ), scratch = scratch[:13], scratch[13:]
    (
        few_got, few_y, few_x, few_held, few_line, mod_got, fm_got, mod_sum, fm_sum, group_slot, part_own, part_slot,
        act_own, act_slot, pair_own, pair_got, line_in, line_rest, line_full,
        few_send, few_recv, group_send, group_recv, line_send, line_recv,
    ) = scratch[:25]
    gather_refs = scratch[25:]
    (in_starts, in_tiles), (head_starts, head_tiles), (embed_starts, embed_tiles), shards = tables
    time_one, modul, fmod, patch, last = gather_refs[:5]
    rep, shard = lax.axis_index("rep"), lax.axis_index("shard")
    place_here = lax.rem(rep, 2 * lines)
    base = rep - place_here
    x, z = lax.rem(place_here, 2), lax.div(place_here, 2)
    core, y = lax.rem(shard, 2), lax.div(shard, 2)
    to_core = (rep, shard + 1 - 2 * core)
    to_y = (rep, shard + 2 - 4 * y)
    to_x = (rep + 1 - 2 * x, shard)

    def line_peer(step):
        return (base + lax.rem(z + step, lines) * 2 + x, shard)

    barrier = pltpu.get_barrier_semaphore()
    to_far = (rep, shards - 1 - shard)
    for peer in (to_core, to_y, to_x, to_far):
        pl.semaphore_signal(barrier, inc=1, device_id=peer, device_id_type=MESH)
    for step in range(1, lines):
        pl.semaphore_signal(
            barrier, inc=1, device_id=line_peer(step), device_id_type=MESH
        )
    pl.semaphore_wait(barrier, 4 + lines - 1)

    width, tokens = head_t.shape[1], state.shape[0]
    in_blocks = [active.at[:, pl.ds(k * width, width)] for k in range(4)] + [d_mlp]

    def far_copy(k):
        return pltpu.make_async_copy(in_far.at[pl.ds(k * tokens, tokens), :], in_blocks[k], fetch.at[4 + k])

    stride = lines // PIECES
    owns = lax.rem(z, stride) == 0
    mine = lax.div(z, stride)
    def remote(source, target, send_sem, recv_sem, peer):
        return pltpu.make_async_remote_copy(
            src_ref=source,
            dst_ref=target,
            send_sem=send_sem,
            recv_sem=recv_sem,
            device_id=peer,
            device_id_type=MESH,
        )

    def rows_of(ref, start, size):
        return ref.at[pl.ds(pl.multiple_of(start, 16), size)]

    def lanes_at(index, ref, row, rows, which):
        _, _, _, lane, lanes, _ = chunks[index]
        return ref.at[
            pl.ds(pl.multiple_of(row, 16), rows), pl.ds(pl.multiple_of(lane + which * lanes, 128), lanes)
        ]

    turn = {i: sum(chunks[j][0] == 0 for j in range(i)) if chunks[i][0] == 0 else sum(chunks[j][0] != 0 for j in range(i)) for i in range(count)}

    def slot_of(i, wide, tall):
        if chunks[i][0] == 0:
            return wide.at[turn[i] % SLOTS]
        return tall.at[turn[i] % SLOTS, pl.ds(0, chunks[i][2])]

    def turn_away(i, steps):
        for j in range(count):
            if (chunks[j][0] == 0) == (chunks[i][0] == 0) and turn[j] == turn[i] + steps:
                return j
        return None

    def core_copy(i):
        return remote(
            slot_of(i, stage_wide, stage_tall), slot_of(i, land_wide, land_tall), send.at[i, 0], recv.at[i, 0], to_core
        )

    def free_of(i):
        return free_wide if chunks[i][0] == 0 else free_tall

    def y_copy(i):
        half = chunks[i][2] // 2
        return remote(
            rows_of(held[i], (1 - y) * half, half), by_y[i], send.at[i, 1], recv.at[i, 1], to_y
        )

    def x_copy(i):
        quarter = chunks[i][2] // 4
        return remote(
            rows_of(by_y[i], (1 - x) * quarter, quarter), by_x[i], send.at[i, 2], recv.at[i, 2], to_x
        )

    def z_copy(i, piece):
        size = chunks[i][2] // 4 // PIECES
        owner = piece * stride
        slot = lax.rem(z - owner - 1 + lines, lines)
        return remote(
            by_x[i].at[pl.ds(piece * size, size)],
            by_z[i].at[slot],
            zsend.at[i, piece],
            zrecv.at[i, slot],
            (base + owner * 2 + x, shard),
        )

    def final_rows(i, side, start, size, which):
        array, row, rows = chunks[i][:3]
        return lanes_at(i, finals[array], row + side * (rows // 2) + start, size, which)

    def cross_copy(i):
        quarter = chunks[i][2] // 4
        part = final_rows(i, 0, x * quarter, quarter, core)
        return remote(part, part, send.at[i, 3], recv.at[i, 3], to_y)

    def line_copy(i, which, side, step):
        size = chunks[i][2] // 4 // PIECES
        part = final_rows(i, side, (x * PIECES + mine) * size, size, core)
        return remote(
            part, part, wsend.at[i, which, step - 1], wrecv.at[i, which, mine], line_peer(step)
        )

    def line_arrival(i, which, side, piece):
        size = chunks[i][2] // 4 // PIECES
        part = final_rows(i, side, (x * PIECES + piece) * size, size, core)
        return remote(part, part, wsend.at[i, which, 0], wrecv.at[i, which, piece], to_core)

    def pair_copy(i, which, side, column):
        quarter = chunks[i][2] // 4
        part = final_rows(i, side, column * quarter, quarter, core)
        return remote(part, part, send.at[i, 4 + which], recv.at[i, 4 + which], to_x)

    def last_copy(i, which, side, half):
        rows = chunks[i][2] // 2
        part = final_rows(i, side, 0, rows, half)
        return remote(part, part, send.at[i, 6 + which], recv.at[i, 6 + which], to_core)

    def sides(i, action):
        if chunks[i][5]:

            @pl.when(y == 1)
            def _():
                action(0, 1)
                action(1, 0)

        else:
            action(0, y)

    def produce(i, left, right):
        rows, lanes = chunks[i][2], chunks[i][4]
        before, after = turn_away(i, -SLOTS), turn_away(i, SLOTS)
        if before is not None:
            core_copy(before).wait_send()
        staged = slot_of(i, stage_wide, stage_tall)

        def block(part):
            value = mxu(left[:, part], right[...], TN)
            first, second = value[:, :lanes], value[:, lanes:]
            held[i][part, :] = jnp.where(core == 0, first, second).astype(jnp.bfloat16)
            staged[part, :] = jnp.where(core == 0, second, first).astype(jnp.bfloat16)

        blocks_of(rows, 256, block)
        if before is not None:
            pl.semaphore_wait(free_of(i), 1)
        core_copy(i).start()

    def stage1(i):
        core_copy(i).wait_recv()
        add_rows(held[i], held[i], slot_of(i, land_wide, land_tall), chunks[i][2])
        if turn_away(i, SLOTS) is not None:
            pl.semaphore_signal(free_of(i), inc=1, device_id=to_core, device_id_type=MESH)

    def stage2(i):
        half = chunks[i][2] // 2
        y_copy(i).wait_recv()
        add_rows(by_y[i], by_y[i], rows_of(held[i], y * half, half), half)
        x_copy(i).start()

    def stage3(i):
        quarter = chunks[i][2] // 4
        x_copy(i).wait_recv()
        add_rows(by_x[i], by_x[i], rows_of(by_y[i], x * quarter, quarter), quarter)
        for piece in range(PIECES):

            @pl.when(z != piece * stride)
            def _():
                z_copy(i, piece).start()

    def stage4(i):
        size = chunks[i][2] // 4 // PIECES

        @pl.when(owns)
        def _():
            for slot in range(lines - 1):
                remote(
                    by_z[i].at[slot], by_z[i].at[slot], zsend.at[i, 0], zrecv.at[i, slot], to_core
                ).wait_recv()
            target = final_rows(i, y, (x * PIECES + mine) * size, size, core)

            def body(index, carry):
                total = by_x[i][
                    pl.ds(pl.multiple_of(mine * size + index * 16, 16), 16)
                ].astype(jnp.float32)
                for slot in range(lines - 1):
                    total += by_z[i][slot, pl.ds(pl.multiple_of(index * 16, 16), 16)].astype(jnp.float32)
                target[pl.ds(pl.multiple_of(index * 16, 16), 16)] = total.astype(jnp.bfloat16)
                return carry

            lax.fori_loop(0, size // 16, body, 0)
            for step in range(1, lines):
                line_copy(i, 0, y, step).start()

    def line_wait(i):
        for piece in range(PIECES):

            @pl.when(z != piece * stride)
            def _():
                line_arrival(i, 0, y, piece).wait_recv()

    def stage5(i):
        @pl.when(y == 0)
        def _():
            line_wait(i)
            cross_copy(i).start()

    def stage6(i):
        if chunks[i][5]:

            @pl.when(y == 1)
            def _():
                line_wait(i)
                pair_copy(i, 0, 1, x).start()
                cross_copy(i).wait_recv()
                pair_copy(i, 1, 0, x).start()

        else:
            line_wait(i)
            pair_copy(i, 0, y, x).start()

    def stage7(i):
        def action(which, side):
            pair_copy(i, which, side, 1 - x).wait_recv()
            last_copy(i, which, side, core).start()

        sides(i, action)

    def stage8(i):
        sides(i, lambda which, side: last_copy(i, which, side, 1 - core).wait_recv())


    mod_tiles, wide = 6 * width // 128, width // 128
    images = d_mod.shape[0]
    in_lanes, head_lanes, embed_lanes = in_tiles * 128, head_tiles * 128, embed_tiles * 128
    rest_lanes = 2 * head_lanes + embed_lanes
    head_places = [o for o in range(shards) if head_starts[o] < wide]
    mod_places = [o for o in range(shards) if in_starts[o] < mod_tiles]
    few_rows = few.shape[0] // 2
    half = pl.ds(pl.multiple_of(core * few_rows, 8), few_rows)
    other_half = pl.ds(pl.multiple_of((1 - core) * few_rows, 8), few_rows)

    def is_in(where, places):
        return functools.reduce(jnp.logical_or, [where == o for o in places])

    few_core = remote(few.at[other_half], few_got, few_send.at[0], few_recv.at[0], to_core)
    few_over_y = remote(few_held.at[0], few_y, few_send.at[1], few_recv.at[1], to_y)
    few_over_x = remote(few_held.at[1], few_x, few_send.at[2], few_recv.at[2], to_x)
    few_back = remote(few_sum.at[half], few_sum.at[half], few_send.at[3], few_recv.at[3], to_core)
    few_back_arrival = remote(few_sum.at[other_half], few_sum.at[other_half], few_send.at[3], few_recv.at[3], to_core)
    mod_core = remote(d_mod, mod_got, few_send.at[4], few_recv.at[4], to_core)
    fm_core = remote(d_fm, fm_got, few_send.at[5], few_recv.at[5], to_core)
    pair_copy_x = remote(pair_own, pair_got, few_send.at[6], few_recv.at[6], to_x)

    def few_line_copy(step):
        return remote(few_line.at[z], few_line.at[z], few_send.at[6 + step], few_recv.at[6 + step], line_peer(step))

    def few_line_arrival(step):
        origin = lax.rem(z + lines - step, lines)
        return remote(few_line.at[origin], few_line.at[origin], few_send.at[6 + step], few_recv.at[6 + step], to_core)

    def group_parts(place):
        parts = []
        tiles = min(in_tiles, mod_tiles - in_starts[place])
        if tiles > 0:
            parts.append((0, in_starts[place] * 128, 0, tiles * 128))
        first, final = max(head_starts[place], wide), min(head_starts[place] + head_tiles, 3 * wide)
        if final > first:
            lead = (first - head_starts[place]) * 128
            parts.append((1, (first - wide) * 128, in_lanes + lead, (final - first) * 128))
        return parts

    def group_copy(place, k):
        which, lane, own, lanes = group_parts(place)[k]
        return remote(
            (mod_sum, fm_sum)[which].at[:, pl.ds(lane, lanes)],
            group_slot.at[:, pl.ds(own, lanes)],
            group_send.at[k, 0],
            group_recv.at[k, 0],
            to_y,
        )

    def to_others(kind, source, slots, step):
        return remote(
            source,
            slots.at[shard],
            group_send.at[kind, step - 1],
            group_recv.at[kind, step - 1],
            (rep, lax.rem(shard + step, shards)),
        )

    def from_others(kind, slots, step):
        origin = lax.rem(shard + shards - step, shards)
        return remote(slots.at[origin], slots.at[origin], group_send.at[kind, 0], group_recv.at[kind, step - 1], to_core)

    slots_of = (line_rest, line_full, line_in)

    def line_copy_d(kind, step):
        slots = slots_of[kind]
        return remote(slots.at[z], slots.at[z], line_send.at[kind, step - 1], line_recv.at[kind, step - 1], line_peer(step))

    def line_arrival_d(kind, step):
        slots = slots_of[kind]
        origin = lax.rem(z + lines - step, lines)
        return remote(slots.at[origin], slots.at[origin], line_send.at[kind, 0], line_recv.at[kind, step - 1], to_core)

    def on_line(action):
        for step in range(1, lines):
            action(0, step)
            action(1, step)

            @pl.when(is_in(shard, mod_places))
            def _():
                action(2, step)

    def side0():
        mod_core.start()
        fm_core.start()
        few_core.start()

    def side1():
        mod_core.wait_recv()
        mod_sum[...] = d_mod[...] + mod_got[...]
        fm_core.wait_recv()
        fm_sum[...] = d_fm[...] + fm_got[...]
        for place in range(shards):

            @pl.when(to_y[1] == place)
            def _():
                for k in range(len(group_parts(place))):
                    group_copy(place, k).start()

        few_core.wait_recv()
        few_held[0] = few[half] + few_got[...]
        few_over_y.start()

    def side2():
        pair_own[...] = jnp.zeros_like(pair_own)
        for place in range(shards):

            @pl.when(shard == place)
            def _():
                for k, (which, lane, own, lanes) in enumerate(group_parts(place)):
                    group_copy(place, k).wait_recv()
                    pair_own[:, own : own + lanes] = (
                        (mod_sum, fm_sum)[which][:, lane : lane + lanes] + group_slot[:, own : own + lanes]
                    )

        part_own[...] = jnp.dot(
            pair_own[:, in_lanes : in_lanes + head_lanes].astype(jnp.bfloat16),
            head_t[...],
            preferred_element_type=jnp.float32,
        )

        @pl.when(is_in(shard, mod_places))
        def _():
            for k in range(len(in_blocks)):
                far_copy(k).wait()
                lanes = pair_own[:, k * tokens : (k + 1) * tokens].astype(jnp.bfloat16)
                part_own[...] += jnp.dot(lanes, in_blocks[k][...], preferred_element_type=jnp.float32)

        part_slot[shard] = part_own[...]
        for step in range(1, shards):
            to_others(2, part_own, part_slot, step).start()
        few_over_y.wait_recv()
        few_held[1] = few_held[0] + few_y[...]
        few_over_x.start()

    def side3():
        for step in range(1, shards):
            from_others(2, part_slot, step).wait_recv()
        d_cond = functools.reduce(jnp.add, [part_slot[o] for o in range(shards)])
        value = cond_full[pl.ds(pl.multiple_of(place_here * images, 8), images), :]
        gate = jax.nn.sigmoid(value)
        d_value = d_cond * (gate + value * gate * (1.0 - gate))
        for place in range(shards):

            @pl.when(shard == place)
            def _():
                first = embed_starts[place] * 128
                pair_own[:, in_lanes + rest_lanes :] = d_value[:, first : first + embed_lanes]
                if place in head_places:
                    lanes = min(head_tiles, wide - head_starts[place]) * 128
                    first = head_starts[place] * 128
                    start = in_lanes + head_lanes
                    d_two_own = d_value[:, first : first + lanes].astype(jnp.bfloat16)
                    pair_own[:, start : start + lanes] = d_two_own.astype(jnp.float32)
                    act_own[...] = jnp.dot(d_two_own, head_t[:lanes, :], preferred_element_type=jnp.float32)
                    act_slot[shard] = act_own[...]
                    for step in range(1, shards):
                        to_others(3, act_own, act_slot, step).start()

        few_over_x.wait_recv()
        few_line[z] = few_held[1] + few_x[...]
        for step in range(1, lines):
            few_line_copy(step).start()

    def side4():
        for step in range(1, shards):

            @pl.when(is_in(lax.rem(shard + shards - step, shards), head_places))
            def _():
                from_others(3, act_slot, step).wait_recv()

        value = time_one[pl.ds(pl.multiple_of(place_here * images, 8), images), :]
        gate = jax.nn.sigmoid(value)
        slope = gate + value * gate * (1.0 - gate)
        for place in range(shards):

            @pl.when(shard == place)
            def _():
                first = embed_starts[place] * 128
                d_act = functools.reduce(jnp.add, [act_slot[o, :, first : first + embed_lanes] for o in head_places])
                start = in_lanes + 2 * head_lanes
                pair_own[:, start : start + embed_lanes] = (slope * d_act).astype(jnp.bfloat16).astype(jnp.float32)

        pair_copy_x.start()
        for step in range(1, lines):
            few_line_arrival(step).wait_recv()
        few_sum[half] = functools.reduce(jnp.add, [few_line[at] for at in range(lines)])
        few_back.start()

    def side5():
        pair_copy_x.wait_recv()
        own, got = pair_own[...], pair_got[...]
        both = jnp.concatenate([jnp.where(x == 0, own, got), jnp.where(x == 0, got, own)], 0)
        line_in[z] = both[:, :in_lanes].astype(jnp.bfloat16)
        line_rest[z] = both[:, in_lanes : in_lanes + rest_lanes].astype(jnp.bfloat16)
        line_full[z] = both[:, in_lanes + rest_lanes :]
        on_line(lambda kind, step: line_copy_d(kind, step).start())

    def side6():
        on_line(lambda kind, step: line_arrival_d(kind, step).wait_recv())
        for at in range(lines):
            span = slice(at * 2 * images, (at + 1) * 2 * images)
            d_head[span, :] = line_rest[at, :, :head_lanes]
            d_two[span, :] = line_rest[at, :, head_lanes : 2 * head_lanes]
            d_one[span, :] = line_rest[at, :, 2 * head_lanes :]
            d_full[span, :] = line_full[at]
        d_in[...] = jnp.zeros_like(d_in)

        @pl.when(is_in(shard, mod_places))
        def _():
            for at in range(lines):
                d_in[at * 2 * images : (at + 1) * 2 * images, :] = line_in[at]

        few_back_arrival.wait_recv()

    def side_end():
        for copy in (few_core, few_over_y, few_over_x, few_back, mod_core, fm_core, pair_copy_x):
            copy.wait_send()
        for step in range(1, lines):
            few_line_copy(step).wait_send()
        on_line(lambda kind, step: line_copy_d(kind, step).wait_send())
        for place in range(shards):

            @pl.when(to_y[1] == place)
            def _():
                for k in range(len(group_parts(place))):
                    group_copy(place, k).wait_send()

        for step in range(1, shards):
            to_others(2, part_own, part_slot, step).wait_send()

        @pl.when(is_in(shard, head_places))
        def _():
            for step in range(1, shards):
                to_others(3, act_own, act_slot, step).wait_send()

    room = (stream, hat_one, hat_two, proj, mlp)
    rounds = []
    for source in (w_in,):
        blocks = [(start, min(tokens, source.shape[0] - start)) for start in range(0, source.shape[0], tokens)]
        rounds.append([(source.at[pl.ds(start, size), :], size) for start, size in blocks])
    rounds.append([(w_out.at[:, pl.ds(k * width, width)], w_out.shape[0]) for k in range(w_out.shape[1] // width)])

    def weight_copies(index):
        return [
            pltpu.make_async_copy(source, room[k].at[pl.ds(0, size), :], weight_load.at[k])
            for k, (source, size) in enumerate(rounds[index])
        ]

    def squares_step(index):
        if index > 0:
            total = jnp.zeros((1, width), jnp.float32)
            for k, copy in enumerate(weight_copies(index - 1)):
                copy.wait()
                size = rounds[index - 1][k][1]
                whole = size // 64 * 64

                def add(block, carry):
                    value = room[k][pl.ds(pl.multiple_of(block * 64, 64), 64), :]
                    return carry + jnp.sum(value * value, 0, keepdims=True)

                total = lax.fori_loop(0, size // 64, add, total)
                if whole < size:
                    value = room[k][whole:size, :]
                    total += jnp.sum(value * value, 0, keepdims=True)
            weight_sq[:, (index - 1) * width : index * width] = total
        if index < len(rounds):
            for copy in weight_copies(index):
                copy.start()

    beside = (side0, side1, side2, side3, side4, side5, side6)
    low = jnp.bfloat16
    per = tokens // TOK
    row = [shard * per + image for image in range(per)]
    span = [pl.ds(image * TOK, TOK) for image in range(per)]
    cut = 256

    def piece(ref, image, index):
        return ref[pl.ds(row[image], 1), pl.ds(index * width, width)]

    def normed(value):
        center = value - jnp.mean(value, -1, keepdims=True)
        root = lax.rsqrt(jnp.mean(center * center, -1, keepdims=True) + eps_norm)
        return center * root, root

    def norm_back(d_hat, hat, root):
        return root * (d_hat - jnp.mean(d_hat, -1, keepdims=True) - hat * jnp.mean(d_hat * hat, -1, keepdims=True))

    def put_row(ref, image, index, value):
        ref[pl.ds(row[image], 1), pl.ds(index * width, width)] = (
            jnp.sum(value, 0, keepdims=True).astype(low).astype(jnp.float32)
        )

    fc2, fc1, attn_out, qkv = finals
    segments = heavy_segments(width, in_cols, in_starts, out_far.shape[0], shards)
    plan = (segments,) + tables[:3] + (lines,)
    relay_tick, arrived, finish = gather_steps(
        plan, remote, line_peer, in_blocks, far_copy, out_far, in_far, head_t, embed, traits,
        *finals, cond_full, time_act, time_one, modul, fmod, patch, last, all_traits, *gather_refs[5:],
    )
    d_mod[...] = jnp.zeros_like(d_mod)
    d_fm[...] = jnp.zeros_like(d_fm)

    for image in range(per):
        value = mxu(state[span[image], :], patch[...], NN) + pos[...]
        stream[span[image], :] = value
        hat, root = normed(value)
        hat_one[span[image], :] = hat
        root_one[span[image], :] = root
        a_low[span[image], :] = (hat * (1.0 + piece(modul, image, 1)) + piece(modul, image, 0)).astype(low)

    def qkv_block(part):
        qkv_low[:, part] = mxu(a_low[...], qkv[part, :], NT).astype(low)

    relay_tick(4)
    arrived(3)
    blocks_of(3 * width, cut, qkv_block)
    relay_tick(5)
    lane = lax.broadcasted_iota(jnp.int32, (TOK, 128), 1)
    first = lane < 64
    scale = 0.125

    def softmax(query, key):
        score = mxu(query, key, NT) * scale
        expo = jnp.exp(score - jnp.max(score, -1, keepdims=True))
        return expo / jnp.sum(expo, -1, keepdims=True)

    def take(ref, image, start):
        return ref[span[image], pl.ds(pl.multiple_of(start, 128), 128)]

    def attend(pair, carry):
        for image in range(per):
            query, key, value = (take(qkv_low, image, index * width + pair * 128) for index in range(3))
            outs = []
            for side in (first, jnp.logical_not(first)):
                probs = softmax(jnp.where(side, query, jnp.zeros_like(query)), key)
                outs.append(mxu(probs.astype(low), value, NN))
            mixed[span[image], pl.ds(pl.multiple_of(pair * 128, 128), 128)] = jnp.where(first, outs[0], outs[1]).astype(low)
        return carry

    lax.fori_loop(0, width // 128, attend, 0)
    relay_tick(6)
    relay_tick(7)
    arrived(2)
    for image in range(per):
        got = mxu(mixed[span[image], :], attn_out[...], NT)
        proj[span[image], :] = got
        value = stream[span[image], :] + piece(modul, image, 2) * got
        stream[span[image], :] = value
        hat, root = normed(value)
        hat_two[span[image], :] = hat
        root_two[span[image], :] = root
        b_low[span[image], :] = (hat * (1.0 + piece(modul, image, 4)) + piece(modul, image, 3)).astype(low)

    def upper_block(part):
        value = mxu(b_low[...], fc1[part, :], NT)
        active[:, part] = (
            0.5 * value * (1.0 + jnp.tanh(0.7978845608 * (value + 0.044715 * value * value * value)))
        ).astype(low)

    arrived(1)
    blocks_of(4 * width, cut, upper_block)
    arrived(0)
    finish()

    def mlp_block(part):
        mlp[:, part] = mxu(active[...], fc2[part, :], NT)

    blocks_of(width, cut, mlp_block)
    loss = jnp.zeros((), jnp.float32)
    g_last = jnp.zeros((PATCH, width), jnp.float32)
    for image in range(per):
        value = stream[span[image], :] + piece(modul, image, 5) * mlp[span[image], :]
        hat, root = normed(value)
        gain = 1.0 + piece(fmod, image, 1)
        final = (hat * gain + piece(fmod, image, 0)).astype(low)
        diff = mxu(final, last[...], NT) - target[span[image], :]
        share = weight_t[span[image], :] * diff
        loss += 0.5 * jnp.sum(share * diff)
        d_out = share.astype(low)
        g_last += mxu(d_out, final, TN)
        d_final = mxu(d_out, last[...], NN)
        put_row(d_fm, image, 0, d_final)
        put_row(d_fm, image, 1, d_final * hat)
        d_value = norm_back(d_final * gain, hat, root)
        stream[span[image], :] = d_value
        put_row(d_mod, image, 5, d_value * mlp[span[image], :])
        d_mlp[span[image], :] = (piece(modul, image, 5) * d_value).astype(low)
    few[pl.ds(PATCH, 8), :] = jnp.full((8, width), loss, jnp.float32)
    few[pl.ds(PATCH + 8, PATCH), :] = g_last
    few[pl.ds(2 * PATCH + 8, 8), :] = jnp.zeros((8, width), jnp.float32)

    of_fc2 = [i for i in range(count) if chunks[i][0] == 0]
    of_fc1 = [i for i in range(count) if chunks[i][0] == 1]
    of_o = [i for i in range(count) if chunks[i][0] == 2]
    of_qkv = [i for i in range(count) if chunks[i][0] == 3]

    def fc2_step(i):
        first, lanes = chunks[i][3], 2 * chunks[i][4]
        part = pl.ds(first, lanes)
        value = mxu(b_low[...], fc1[part, :], NT)
        inner = jnp.tanh(0.7978845608 * (value + 0.044715 * value * value * value))
        slope = 0.5 * (1.0 + inner) + 0.5 * value * (1.0 - inner * inner) * 0.7978845608 * (
            1.0 + 3.0 * 0.044715 * value * value
        )
        d_upper = (slope * mxu(d_mlp[...], fc2[:, part], NN)).astype(low)
        produce(i, d_mlp, active.at[:, part])
        active[:, part] = d_upper

    def fc1_step(i):
        part = pl.ds(chunks[i][1], chunks[i][2])
        more = mxu(active[:, part], fc1[part, :], NN)
        if i == of_fc1[0]:
            mlp[...] = more
        else:
            mlp[...] += more
        produce(i, active.at[:, part], b_low)

    def o_step(i):
        for image in range(per):
            d_normed = mlp[span[image], :]
            hat = hat_two[span[image], :]
            put_row(d_mod, image, 3, d_normed)
            put_row(d_mod, image, 4, d_normed * hat)
            d_value = stream[span[image], :] + norm_back(
                d_normed * (1.0 + piece(modul, image, 4)), hat, root_two[span[image], :]
            )
            stream[span[image], :] = d_value
            put_row(d_mod, image, 2, d_value * proj[span[image], :])
            b_low[span[image], :] = (piece(modul, image, 2) * d_value).astype(low)
        active[:, pl.ds(0, width)] = mxu(b_low[...], attn_out[...], NN).astype(low)
        produce(i, b_low, mixed)

    def attend_back(pair):
        for image in range(per):
            query, key, value = (take(qkv_low, image, index * width + pair * 128) for index in range(3))
            d_out = take(active, image, pair * 128)
            d_query, d_key, d_value = [], [], []
            for side in (first, jnp.logical_not(first)):
                none = jnp.zeros_like(query)
                probs = softmax(jnp.where(side, query, none), key)
                d_prob = mxu(jnp.where(side, d_out, none), value, NT)
                d_score = (probs * (d_prob - jnp.sum(probs * d_prob, -1, keepdims=True))).astype(low)
                d_value.append(mxu(probs.astype(low), d_out, TN))
                d_query.append(mxu(d_score, key, NN) * scale)
                d_key.append(mxu(d_score, query, TN) * scale)
            for index, both in enumerate((d_query, d_key, d_value)):
                qkv_low[span[image], pl.ds(pl.multiple_of(index * width + pair * 128, 128), 128)] = jnp.where(
                    first, both[0], both[1]
                ).astype(low)

    def norm_one_step():
        @pl.when(is_in(shard, mod_places))
        def _():
            for k in range(len(in_blocks)):
                far_copy(k).start()

        g_patch = jnp.zeros((PATCH, width), jnp.float32)
        for image in range(per):
            d_normed = mxu(qkv_low[span[image], :], qkv[...], NN)
            hat = hat_one[span[image], :]
            put_row(d_mod, image, 0, d_normed)
            put_row(d_mod, image, 1, d_normed * hat)
            d_value = stream[span[image], :] + norm_back(
                d_normed * (1.0 + piece(modul, image, 1)), hat, root_one[span[image], :]
            )
            g_patch += mxu(state[span[image], :], d_value.astype(low), TN)
        few[pl.ds(0, PATCH), :] = g_patch

    def qkv_step(i):
        if i == of_qkv[0]:
            norm_one_step()
        produce(i, qkv_low.at[:, pl.ds(chunks[i][1], chunks[i][2])], a_low)

    def over_y(i):
        y_copy(i).start()

    stages = (None, stage1, stage2, stage3, stage4, stage5, stage6, stage7, stage8, over_y)
    steps = [(fc2_step, i) for i in of_fc2] + [(fc1_step, i) for i in of_fc1] + [(o_step, i) for i in of_o]
    steps += [(attend_back, pair) for pair in range(width // 128)] + [(qkv_step, i) for i in of_qkv]
    for j, (k, i) in enumerate(ORDER):
        if j in BESIDE_AT:
            beside[BESIDE_AT.index(j)]()
        if j in SQUARES_AT:
            squares_step(SQUARES_AT.index(j))
        if k == 0:
            step, arg = steps[i]
            step(arg)
        else:
            stages[k](i)

    side_end()
    for i in range(count):
        if turn_away(i, SLOTS) is None:
            core_copy(i).wait_send()
        y_copy(i).wait_send()
        x_copy(i).wait_send()
        for piece in range(PIECES):

            @pl.when(z != piece * stride)
            def _():
                z_copy(i, piece).wait_send()

        if chunks[i][5]:

            @pl.when(y == 0)
            def _():
                cross_copy(i).wait_send()

        @pl.when(owns)
        def _():
            for step in range(1, lines):
                line_copy(i, 0, y, step).wait_send()

        def action(which, side):
            pair_copy(i, which, side, x).wait_send()
            last_copy(i, which, side, core).wait_send()

        sides(i, action)


def step_call(lines, tables, in_cols, far, light):
    width = far[0].shape[1]
    chunks = heavy_chunks(width)
    count = len(chunks)
    low, full = jnp.bfloat16, jnp.float32
    (_, in_tiles), (_, head_tiles), (_, embed_tiles), shards = tables
    state, traits = light[0], light[6]
    tokens, group = state.shape[0], traits.shape[0]
    rows = 2 * lines * group
    modul_shape, fmod_shape = (group, 6 * width), (group, 2 * width)
    segments = heavy_segments(width, in_cols, tables[0][0], far[1].shape[0], shards)
    most = max(len(parts) for parts in segments)
    in_lanes, head_lanes, embed_lanes = in_tiles * 128, head_tiles * 128, embed_tiles * 128
    rest_lanes = 2 * head_lanes + embed_lanes
    few = (2 * PATCH + 16, width)
    few_half = (few[0] // 2, width)
    pair = (group, in_lanes + rest_lanes + embed_lanes)
    sizes = [(part_rows, part_lanes) for _, _, part_rows, _, part_lanes, _ in chunks]
    wide = [item for item, chunk in zip(sizes, chunks) if chunk[0] == 0][0]
    tall = max(item for item, chunk in zip(sizes, chunks) if chunk[0] != 0)
    dma = pltpu.SemaphoreType.DMA
    heavy = [(width, 4 * width), (4 * width, width), (width, width), (3 * width, width)]
    shapes = [(item, low) for item in heavy] + [
        ((rows, in_lanes), low),
        ((rows, head_lanes), low),
        ((rows, head_lanes), low),
        ((rows, embed_lanes), full),
        ((rows, embed_lanes), low),
        (few, full),
        ((rows, width), full),
        ((rows, width), low),
        ((rows, traits.shape[1]), full),
        ((1, 2 * width), full),
    ]
    pass_scratch = [
        ((tokens, width), full),
        ((tokens, width), full),
        ((tokens, width), full),
        ((tokens, 1), full),
        ((tokens, 1), full),
        ((tokens, width), low),
        ((tokens, 3 * width), low),
        ((tokens, width), low),
        ((tokens, width), full),
        ((tokens, width), low),
        ((tokens, 4 * width), low),
        ((tokens, width), full),
        ((tokens, width), low),
    ]
    scratch = [
        (few_half, full),
        (few_half, full),
        (few_half, full),
        ((2,) + few_half, full),
        ((lines,) + few_half, full),
        (modul_shape, full),
        (fmod_shape, full),
        (modul_shape, full),
        (fmod_shape, full),
        ((group, in_lanes + head_lanes), full),
        ((group, width), full),
        ((shards, group, width), full),
        ((group, width), full),
        ((shards, group, width), full),
        (pair, full),
        (pair, full),
        ((lines, 2 * group, in_lanes), low),
        ((lines, 2 * group, rest_lanes), low),
        ((lines, 2 * group, embed_lanes), full),
    ]
    gather_scratch = [
        ((rows, embed_lanes), full),
        (modul_shape, full),
        (fmod_shape, full),
        ((PATCH, width), low),
        ((PATCH, width), low),
        ((shards, rows, embed_lanes), low),
        ((shards, rows, embed_lanes), full),
        ((shards, PATCH, embed_lanes), low),
        ((shards, rows, head_lanes), full),
        ((rows, head_lanes), full),
        ((shards, group, in_lanes), full),
        ((group, in_lanes), full),
        ((shards, group, head_lanes), full),
        ((group, head_lanes), full),
        ((PATCH, width), low),
        ((shards,) + traits.shape, full),
        (traits.shape, full),
        (traits.shape, full),
        ((lines, 2 * group, traits.shape[1]), full),
    ]
    vmem, anywhere = pl.BlockSpec(memory_space=pltpu.VMEM), pl.BlockSpec(memory_space=pl.ANY)
    return pl.pallas_call(
        functools.partial(step_kernel, lines, chunks, tables, in_cols),
        out_shape=[jax.ShapeDtypeStruct(*item) for item in shapes],
        in_specs=[anywhere] * len(far) + [vmem] * len(light),
        out_specs=[vmem] * len(shapes),
        scratch_shapes=[pltpu.VMEM((r, c), low) for r, c in sizes]
        + [pltpu.VMEM((r // 2, c), low) for r, c in sizes]
        + [pltpu.VMEM((r // 4, c), low) for r, c in sizes]
        + [pltpu.VMEM((lines - 1, r // 4 // PIECES, c), low) for r, c in sizes]
        + [
            dma((count, 8)),
            dma((count, 8)),
            dma((count, PIECES)),
            dma((count, lines - 1)),
            dma((count, 2, lines - 1)),
            dma((count, 2, PIECES)),
        ]
        + [pltpu.VMEM((SLOTS,) + item, low) for item in (wide, tall)] * 2
        + [pltpu.SemaphoreType.REGULAR, pltpu.SemaphoreType.REGULAR, dma((9,)), dma((5,))]
        + [pltpu.VMEM(*item) for item in ((modul_shape, full), (fmod_shape, full), (few, full))]
        + [pltpu.VMEM(*item) for item in pass_scratch]
        + [pltpu.VMEM(*item) for item in scratch]
        + [
            dma((lines + 6,)),
            dma((lines + 6,)),
            dma((4, shards - 1)),
            dma((4, shards - 1)),
            dma((3, lines - 1)),
            dma((3, lines - 1)),
        ]
        + [pltpu.VMEM(*item) for item in gather_scratch]
        + [dma((most,)), dma((most,))]
        + [dma((most, 2))] * 4
        + [dma((most, 4))] * 2
        + [dma((most,)), dma((most,)), dma((8, shards - 1)), dma((8, shards - 1)), dma((most,)), dma((lines,)), dma((lines,))],
        compiler_params=pltpu.CompilerParams(
            collective_id=1, has_side_effects=True, vmem_limit_bytes=64 * 1024 * 1024 - 65536
        ),
    )(*far, *light)


def placed_traits(traits, lanes):
    lead = -(-(PATCH + FREQ) // 128) * 128
    lane = lax.broadcasted_iota(jnp.int32, (traits.shape[0], lead), 1)
    here = jnp.logical_and(lane >= PATCH, lane < PATCH + FREQ)
    freq = jnp.where(here, traits[:, :lead], 0.0).astype(jnp.bfloat16)
    named = lax.broadcasted_iota(jnp.int32, (traits.shape[0], lanes), 1).astype(jnp.float32)
    onehot = jnp.where(named == traits[:, lead : lead + 1], 1.0, 0.0).astype(jnp.bfloat16)
    return freq, onehot


def windows(cols, shards):
    starts = [place * cols // 128 for place in range(shards)]
    tiles = max(-(-(place + 1) * cols // 128) - start for place, start in enumerate(starts))
    return starts, tiles


def heavy_segments(width, in_cols, in_starts, out_rows, shards):
    every = []
    for place in range(shards):
        parts = []
        for array, low, high, most in ((3, 6 * width, 9 * width, 640), (1, 9 * width, 13 * width, 640)):
            first, last = max(low, place * in_cols), min(high, (place + 1) * in_cols)
            while first < last:
                rows = min(most, last - first)
                parts.append((0, first - in_starts[place] * 128, array, first - low, rows, 0, 0, width))
                first += rows
            if array == 3:
                parts.append((1, 0, 2, place * out_rows, out_rows, 0, 0, width))
        parts.append((1, 0, 0, place * out_rows, out_rows, width, 0, 4 * width))
        every.append(parts)
    return every


def gather_steps(
    plan, remote, line_peer, in_blocks, far_copy,
    out_t, in_t, head_t, embed, traits,
    fc2, fc1, attn_out, qkv, cond_full, time_act, time_one, modul, fmod, patch, last, all_traits,
    s1_slot, tab_slot, patch_slot, two_slot, two_own, mod_slot, mod_own, fm_slot, fm_own, last_own,
    trait_slot, trait_own, trait_got, line_slot,
    ysend, yrecv, xsend, xrecv, zsend, zrecv, csend, crecv, osend, orecv, small_send, small_recv, local_sem,
    trait_send, trait_recv,
):
    segments, (in_starts, in_tiles), (head_starts, head_tiles), (embed_starts, embed_tiles), lines = plan
    shards = len(segments)
    arrays = (fc2, fc1, attn_out, qkv)
    sources = (in_t, out_t)
    rep, shard = lax.axis_index("rep"), lax.axis_index("shard")
    place_here = lax.rem(rep, 2 * lines)
    x, z = lax.rem(place_here, 2), lax.div(place_here, 2)
    zb = lax.rem(z, 2)
    core, y = lax.rem(shard, 2), lax.div(shard, 2)
    to_core = (rep, shard + 1 - 2 * core)
    to_y = (rep, shard + 2 - 4 * y)
    to_x = (rep + 1 - 2 * x, shard)
    to_z = (rep + 2 - 4 * zb, shard)
    width = head_t.shape[1]
    others = [(rep, lax.rem(shard + step, shards)) for step in range(1, shards)]
    mod_places = [o for o in range(shards) if in_starts[o] * 128 < 6 * width]
    computes_mod = functools.reduce(jnp.logical_or, [shard == o for o in mod_places])

    @pl.when(computes_mod)
    def _():
        for k in range(len(in_blocks)):
            far_copy(k).start()

    def small(kind, source, slots, step):
        return remote(
            source, slots.at[shard], small_send.at[kind, step - 1], small_recv.at[kind, step - 1], others[step - 1]
        )

    def small_arrival(kind, slots, step):
        origin = lax.rem(shard + shards - step, shards)
        return remote(
            slots.at[origin], slots.at[origin], small_send.at[kind, step - 1], small_recv.at[kind, step - 1], to_core
        )

    def exchange(kind, source, slots, origins=None):
        for step in range(1, shards):
            if origins is None:
                small(kind, source, slots, step).start()
            else:
                sends = functools.reduce(jnp.logical_or, [shard == o for o in origins])

                @pl.when(sends)
                def _():
                    small(kind, source, slots, step).start()

    def arrive(kind, slots, origins=None):
        for step in range(1, shards):
            if origins is None:
                small_arrival(kind, slots, step).wait_recv()
            else:
                origin = lax.rem(shard + shards - step, shards)

                @pl.when(functools.reduce(jnp.logical_or, [origin == o for o in origins]))
                def _():
                    small_arrival(kind, slots, step).wait_recv()

    def sent(kind, source, slots, origins=None):
        for step in range(1, shards):
            if origins is None:
                small(kind, source, slots, step).wait_send()
            else:

                @pl.when(functools.reduce(jnp.logical_or, [shard == o for o in origins]))
                def _():
                    small(kind, source, slots, step).wait_send()

    def place_tiles(target, slots, starts, tiles, origins, dtype, first=0):
        total = target.shape[1] // 128
        for tile in range(total):
            parts = [
                slots[o, :, (tile + first - starts[o]) * 128 : (tile + first - starts[o] + 1) * 128]
                for o in origins
                if 0 <= tile + first - starts[o] < tiles
            ]
            target[:, tile * 128 : (tile + 1) * 128] = functools.reduce(jnp.add, parts).astype(dtype)

    def source_part(place, k):
        source, row, array, _, rows, lane, _, lanes = segments[place][k]
        return sources[source].at[pl.ds(row, rows), pl.ds(lane, lanes)]

    def target_part(place, k, start=0, rows=None):
        _, _, array, row, total, _, lane, lanes = segments[place][k]
        start = row + start
        if not isinstance(start, int):
            start = pl.multiple_of(start, 16)
        return arrays[array].at[pl.ds(start, total if rows is None else rows), pl.ds(lane, lanes)]

    def quarter(place, k, index):
        size = segments[place][k][4] // 4
        return target_part(place, k, index * size, size)

    def half_of(place, k, index, second):
        size = segments[place][k][4] // 4
        cut = -(-size // 32) * 16
        return target_part(place, k, index * size + (cut if second else 0), size - cut if second else cut)

    me = x * 2 + zb
    across_x, along_z, corner = (1 - x) * 2 + zb, x * 2 + 1 - zb, (1 - x) * 2 + 1 - zb

    def y_copy(place, k):
        size = segments[place][k][4] // 4
        source, row, _, _, _, lane, _, lanes = segments[place][k]
        part = sources[source].at[pl.ds(pl.multiple_of(row + me * size, 16), size), pl.ds(lane, lanes)]
        return remote(part, quarter(place, k, me), ysend.at[k], yrecv.at[k], to_y)

    def owner_copy(place, k):
        return remote(source_part(place, k), target_part(place, k), osend.at[k], orecv.at[k], to_core)

    def own_copy(place, k):
        return pltpu.make_async_copy(source_part(place, k), target_part(place, k), local_sem.at[k])

    def hop(part, sems, k, slot, peer):
        return remote(part, part, sems[0].at[k, slot], sems[1].at[k, slot], peer)

    xs, zs, cs = (xsend, xrecv), (zsend, zrecv), (csend, crecv)

    def begin(k, across):
        for place in range(shards):
            if k < len(segments[place]):

                @pl.when(shard == place)
                def _():
                    if across:
                        y_copy(place, k).start()
                    else:
                        owner_copy(place, k).start()
                        own_copy(place, k).start()

    def relay(place, stage, k):
        if stage == 0:
            y_copy(place, k).wait_recv()
            hop(quarter(place, k, me), xs, k, 0, to_x).start()
            hop(quarter(place, k, me), zs, k, 0, to_z).start()
            hop(quarter(place, k, me), cs, k, 0, to_core).start()
        elif stage == 1:
            hop(quarter(place, k, across_x), xs, k, 0, to_x).wait_recv()
            hop(half_of(place, k, across_x, False), zs, k, 1, to_z).start()
            hop(quarter(place, k, along_z), zs, k, 0, to_z).wait_recv()
            hop(half_of(place, k, along_z, True), xs, k, 1, to_x).start()
            hop(quarter(place, k, across_x), cs, k, 1, to_core).start()
            hop(quarter(place, k, along_z), cs, k, 2, to_core).start()
        else:
            hop(half_of(place, k, corner, False), zs, k, 1, to_z).wait_recv()
            hop(half_of(place, k, corner, True), xs, k, 1, to_x).wait_recv()
            hop(quarter(place, k, corner), cs, k, 3, to_core).start()

    def relay_tick(tick):
        for place in range(shards):

            @pl.when(to_y[1] == place)
            def _():
                for stage in range(3):
                    if 0 <= tick - stage < len(segments[place]):
                        relay(place, stage, tick - stage)

    def trait_line(step):
        return remote(
            line_slot.at[z], line_slot.at[z], trait_send.at[step], trait_recv.at[step], line_peer(step)
        )

    def trait_line_arrival(step):
        origin = lax.rem(z + lines - step, lines)
        return remote(line_slot.at[origin], line_slot.at[origin], trait_send.at[step], trait_recv.at[step], to_core)

    trait_pair = remote(trait_own, trait_got, trait_send.at[0], trait_recv.at[0], to_x)
    trait_slot[shard] = traits[...]
    exchange(7, traits, trait_slot)
    begin(0, True)
    arrive(7, trait_slot)
    trait_own[...] = functools.reduce(jnp.add, [trait_slot[o] for o in range(shards)])
    trait_pair.start()
    begin(1, True)
    trait_pair.wait_recv()
    own, got = trait_own[...], trait_got[...]
    line_slot[z] = jnp.concatenate([jnp.where(x == 0, own, got), jnp.where(x == 0, got, own)], 0)
    for step in range(1, lines):
        trait_line(step).start()
    relay_tick(0)
    begin(2, True)
    for step in range(1, lines):
        trait_line_arrival(step).wait_recv()
    count_in_line = 2 * traits.shape[0]
    for at in range(lines):
        all_traits[at * count_in_line : (at + 1) * count_in_line, :] = line_slot[at]
    freq, onehot = placed_traits(all_traits[...], embed.shape[1])

    nt = (((1,), (1,)), ((), ()))
    own_one = lax.dot_general(freq, embed[:, : freq.shape[1]], nt, preferred_element_type=jnp.float32)
    time_one[...] = own_one
    s1_slot[shard] = (own_one * jax.nn.sigmoid(own_one)).astype(jnp.bfloat16)
    tab_slot[shard] = lax.dot_general(onehot, embed[...], nt, preferred_element_type=jnp.float32)
    eye = lax.broadcasted_iota(jnp.int32, (PATCH, 128), 0) == lax.broadcasted_iota(jnp.int32, (PATCH, 128), 1)
    eye = jnp.where(eye, 1.0, 0.0).astype(jnp.bfloat16)
    patch_slot[shard] = lax.dot_general(eye, embed[:, :128], nt, preferred_element_type=jnp.float32).astype(jnp.bfloat16)
    exchange(0, s1_slot.at[shard], s1_slot)
    exchange(1, tab_slot.at[shard], tab_slot)
    exchange(2, patch_slot.at[shard], patch_slot)
    relay_tick(1)
    begin(3, True)
    last_place = [o for o in range(shards) if 0 <= 3 * width // 128 - head_starts[o] < head_tiles][-1]
    last_row = (3 * width // 128 - head_starts[last_place]) * 128
    last_own[...] = head_t[last_row : last_row + 16, :]

    @pl.when(shard == last_place)
    def _():
        last[...] = last_own[...]
        for step in range(1, shards):
            remote(last_own, last, small_send.at[6, step - 1], small_recv.at[6, 0], others[step - 1]).start()

    head_places = [o for o in range(shards) if head_starts[o] * 128 < width]
    fm_places = [o for o in range(shards) if (head_starts[o] + head_tiles) * 128 > width]
    group = modul.shape[0]

    arrive(0, s1_slot)
    place_tiles(time_act, s1_slot, embed_starts, embed_tiles, range(shards), jnp.bfloat16)
    two_own[...] = lax.dot_general(time_act[...], head_t[...], nt, preferred_element_type=jnp.float32)
    two_slot[shard] = two_own[...]
    exchange(3, two_own, two_slot, head_places)
    relay_tick(2)
    begin(4, True)
    arrive(1, tab_slot)
    arrive(3, two_slot, head_places)
    place_tiles(cond_full, tab_slot, embed_starts, embed_tiles, range(shards), jnp.float32)
    for tile in range(width // 128):
        span = slice(tile * 128, (tile + 1) * 128)
        for o in head_places:
            if 0 <= tile - head_starts[o] < head_tiles:
                cond_full[:, span] += two_slot[o, :, (tile - head_starts[o]) * 128 : (tile - head_starts[o] + 1) * 128]
    mine = cond_full[pl.ds(pl.multiple_of(place_here * group, 8), group), :]
    cond = (mine * jax.nn.sigmoid(mine)).astype(jnp.bfloat16)

    @pl.when(computes_mod)
    def _():
        for k, block in enumerate(in_blocks):
            far_copy(k).wait()
            span = slice(k * block.shape[0], (k + 1) * block.shape[0])
            mod_own[:, span] = lax.dot_general(cond, block[...], nt, preferred_element_type=jnp.float32)
        mod_slot[shard] = mod_own[...]

    exchange(4, mod_own, mod_slot, mod_places)
    fm_own[...] = lax.dot_general(cond, head_t[...], nt, preferred_element_type=jnp.float32)
    fm_slot[shard] = fm_own[...]
    exchange(5, fm_own, fm_slot, fm_places)
    relay_tick(3)
    begin(5, True)
    begin(0, False)
    begin(1, False)
    begin(2, False)
    begin(3, False)
    begin(4, False)
    begin(5, False)
    arrive(2, patch_slot)
    place_tiles(patch, patch_slot, embed_starts, embed_tiles, range(shards), jnp.bfloat16)
    arrive(4, mod_slot, mod_places)
    arrive(5, fm_slot, fm_places)
    place_tiles(modul, mod_slot, in_starts, in_tiles, mod_places, jnp.float32)
    place_tiles(fmod, fm_slot, head_starts, head_tiles, fm_places, jnp.float32, width // 128)

    @pl.when(shard != last_place)
    def _():
        remote(last_own, last, small_send.at[6, 0], small_recv.at[6, 0], to_core).wait_recv()

    def arrived(array):
        for place in range(shards):
            of_array = [k for k, part in enumerate(segments[place]) if part[2] == array]

            @pl.when(shard == place)
            def _():
                for k in of_array:
                    own_copy(place, k).wait()

            @pl.when(to_core[1] == place)
            def _():
                for k in of_array:
                    remote(target_part(place, k), target_part(place, k), osend.at[k], orecv.at[k], to_core).wait_recv()

            @pl.when(shards - 1 - shard == place)
            def _():
                for k in of_array:
                    for slot, index in enumerate((me, across_x, along_z, corner)):
                        part = quarter(place, k, index)
                        remote(part, part, csend.at[k, slot], crecv.at[k, slot], to_core).wait_recv()

    def finish():
        for place in range(shards):
            count = len(segments[place])

            @pl.when(shard == place)
            def _():
                for k in range(count):
                    y_copy(place, k).wait_send()
                    owner_copy(place, k).wait_send()

            @pl.when(to_y[1] == place)
            def _():
                for k in range(count):
                    hop(quarter(place, k, me), xs, k, 0, to_x).wait_send()
                    hop(quarter(place, k, me), zs, k, 0, to_z).wait_send()
                    hop(half_of(place, k, across_x, False), zs, k, 1, to_z).wait_send()
                    hop(half_of(place, k, along_z, True), xs, k, 1, to_x).wait_send()
                    for slot, index in enumerate((me, across_x, along_z, corner)):
                        hop(quarter(place, k, index), cs, k, slot, to_core).wait_send()

        trait_pair.wait_send()
        for step in range(1, lines):
            trait_line(step).wait_send()
        sent(7, traits, trait_slot)
        sent(0, s1_slot.at[shard], s1_slot)
        sent(1, tab_slot.at[shard], tab_slot)
        sent(2, patch_slot.at[shard], patch_slot)
        sent(3, two_own, two_slot, head_places)
        sent(4, mod_own, mod_slot, mod_places)
        sent(5, fm_own, fm_slot, fm_places)

        @pl.when(shard == last_place)
        def _():
            for step in range(1, shards):
                remote(last_own, last, small_send.at[6, step - 1], small_recv.at[6, 0], others[step - 1]).wait_send()

    return relay_tick, arrived, finish


def windowed(in_t, out_t, head_t, embed_t, shards):
    place = lax.axis_index("shard")
    width = head_t.shape[1]
    low = jnp.bfloat16

    def window(item_t, starts, tiles, lanes):
        rows = item_t.shape[0]
        most = max(o * rows - start * 128 for o, start in enumerate(starts))
        padded = jnp.pad(item_t, ((most, tiles * 128 - rows), (0, lanes - item_t.shape[1])))
        begin = most - lax.rem(place * rows, 128)
        return lax.dynamic_slice_in_dim(padded, begin, tiles * 128, 0).astype(low)

    in_cols, head_cols, embed_cols = in_t.shape[0], head_t.shape[0], embed_t.shape[0]
    in_starts, in_tiles = windows(in_cols, shards)
    head_starts, head_tiles = windows(head_cols, shards)
    embed_starts, embed_tiles = windows(embed_cols, shards)
    in_t = window(in_t, in_starts, in_tiles, width)
    head_t = window(head_t, head_starts, head_tiles, width)
    embed = window(embed_t, embed_starts, embed_tiles, -(-embed_t.shape[1] // 128) * 128)
    return in_t, out_t.astype(low), head_t, embed


def own_segments(width, in_cols, in_starts, out_rows, shards):
    every = []
    for place in range(shards):
        parts = []
        for array, low, high in ((3, 6 * width, 9 * width), (1, 9 * width, 13 * width)):
            first, last = max(low, place * in_cols), min(high, (place + 1) * in_cols)
            if first < last:
                parts.append((array, first - low, last - first, first - in_starts[place] * 128))
        every.append(parts)
    return every


def total_kernel(
    tables, segments, fc2, fc1, attn_out, qkv, w_in, w_out, w_head, w_embed,
    d_in, d_fin, d_two, d_one, d_full, few, cond_full, time_act, traits, weight_sq, c_in, c_out, c_head, c_embed,
    g_in, g_out, g_head, g_embed, n_in, n_out, n_head, n_embed, stats,
    own_t, own_out, grad_t, head_t, t_out, t_head, t_embed, v_head, v_embed,
    load, write, fetch,
):
    (in_starts, in_tiles), (head_starts, head_tiles), (embed_starts, embed_tiles), shards = tables
    arrays = (fc2, fc1, attn_out, qkv)
    shard = lax.axis_index("shard")
    width = cond_full.shape[1]
    in_cols, head_cols, embed_cols, out_cols = (item.shape[0] for item in (w_in, w_head, w_embed, w_out))
    full, low = jnp.float32, jnp.bfloat16
    span = lane_span(width, w_embed.shape[1])

    reads = [pltpu.make_async_copy(w_head, v_head, load.at[0]), pltpu.make_async_copy(w_embed, v_embed, load.at[1])]
    for copy in reads:
        copy.start()

    def heavy_copies(place):
        copies = []
        for k, (array, row, rows, at) in enumerate(segments[place]):
            copies.append(
                pltpu.make_async_copy(
                    arrays[array].at[pl.ds(row, rows), :], own_t.at[pl.ds(at, rows), :], fetch.at[k]
                )
            )
        for k, array in ((2, 2), (3, 0)):
            lane = 0 if array == 2 else width
            copies.append(
                pltpu.make_async_copy(
                    arrays[array].at[pl.ds(place * out_cols, out_cols), :],
                    own_out.at[:, pl.ds(lane, arrays[array].shape[1])],
                    fetch.at[k],
                )
            )
        return copies

    for place in range(shards):

        @pl.when(shard == place)
        def _():
            for copy in heavy_copies(place):
                copy.start()
            edges = [0]
            for _, _, rows, at in segments[place]:
                edges += [at, at + rows]
            edges.append(in_tiles * 128)
            for start, stop in zip(edges[0::2], edges[1::2]):
                if start < stop:
                    own_t[start:stop, :] = jnp.zeros((stop - start, width), low)

    def decayed(state, total, count):
        return decay * state + (1.0 - decay) * (total / count + eps_one)

    def to_lanes(column):
        return jnp.broadcast_to(column, (column.shape[0], 128)).T[:1, :]

    def to_column(lanes):
        return jnp.broadcast_to(lanes, (128, lanes.shape[1])).T[:, :1]

    def squares_of(value, state, fresh_out, start, size):
        square = value * value
        sums = to_lanes(jnp.sum(square, -1, keepdims=True))[:, :size]
        fresh = decayed(state[:, start : start + size], sums, value.shape[1])
        fresh_out[:, start : start + size] = fresh
        inverse = 1.0 / fresh
        if size < value.shape[0]:
            inverse = jnp.concatenate([inverse, jnp.zeros((1, value.shape[0] - size), full)], 1)
        return jnp.sum(square, 0, keepdims=True), jnp.sum(square * to_column(inverse), 0, keepdims=True)

    def put(start, plain, scaled):
        stats[:, start : start + plain.shape[1]] = plain
        stats[:, span + start : span + start + plain.shape[1]] = scaled

    def column_blocks(total):
        return [(start, min(128, total - start)) for start in range(0, total, 128)]

    def by_blocks(take, total, state, fresh_out, place):
        plain, scaled = jnp.zeros((1, width), full), jnp.zeros((1, width), full)
        for start, size in column_blocks(total):
            value = take(start, size)
            if size < 128:
                value = jnp.concatenate([value, jnp.zeros((128 - size, width), full)], 0)
            more, more_scaled = squares_of(value, state, fresh_out, start, size)
            plain, scaled = plain + more, scaled + more_scaled
        put(place, plain, scaled)

    cond = cond_full[...]
    cond = (cond * jax.nn.sigmoid(cond)).astype(low)

    lanes_all = -(-w_embed.shape[1] // 128) * 128
    freq, onehot = placed_traits(traits[...], lanes_all)
    square_one = lax.broadcasted_iota(jnp.int32, (PATCH, lanes_all), 0)
    eye = jnp.where(square_one == lax.broadcasted_iota(jnp.int32, (PATCH, lanes_all), 1), 1.0, 0.0).astype(low)

    def exact(value, picks):
        total = None
        for _ in range(3):
            part = value.astype(low)
            value = value - part.astype(full)
            term = mxu(part, picks, TN)
            total = term if total is None else total + term
        return total

    for place in range(shards):

        @pl.when(shard == place)
        def _():
            lead = place * embed_cols - embed_starts[place] * 128
            lanes = slice(embed_starts[place] * 128, (embed_starts[place] + embed_tiles) * 128)
            value = exact(d_full[...], onehot) + exact(few[0:PATCH, lanes], eye)
            value = value[lead : lead + embed_cols, :]
            time = mxu(d_one[...], freq, TN)[lead : lead + embed_cols, :]
            t_embed[:, : freq.shape[1]] = value[:, : freq.shape[1]] + time
            t_embed[:, freq.shape[1] :] = value[:, freq.shape[1] : w_embed.shape[1]]

    pltpu.make_async_copy(t_embed, g_embed, write.at[3]).start()
    value = jnp.concatenate([t_embed[...], jnp.zeros((embed_cols, lanes_all - w_embed.shape[1]), full)], 1)
    square = value * value
    fresh = decayed(c_embed[...], to_lanes(jnp.sum(square, -1, keepdims=True)), w_embed.shape[1])
    n_embed[...] = fresh
    put(7 * width, jnp.sum(square, 0, keepdims=True), jnp.sum(square * to_column(1.0 / fresh), 0, keepdims=True))

    head_t[...] = mxu(d_two[...], time_act[...], TN) + mxu(d_fin[...], cond, TN)
    last_place = [o for o in range(shards) if 0 <= 3 * width // 128 - head_starts[o] < head_tiles][-1]
    last_row = (3 * width // 128 - head_starts[last_place]) * 128

    @pl.when(shard == last_place)
    def _():
        head_t[last_row : last_row + PATCH, :] = few[PATCH + 8 : 2 * PATCH + 8, :]

    for place in range(shards):

        @pl.when(shard == place)
        def _():
            lead = place * head_cols - head_starts[place] * 128
            t_head[...] = head_t[lead : lead + head_cols, :]

    pltpu.make_async_copy(t_head, g_head, write.at[2]).start()
    by_blocks(lambda start, size: t_head[start : start + size, :], head_cols, c_head, n_head, 6 * width)

    for place in range(shards):

        @pl.when(shard == place)
        def _():
            for copy in heavy_copies(place):
                copy.wait()

    def light(index, carry):
        part = pl.ds(pl.multiple_of(index * 128, 128), 128)
        grad_t[part, :] = mxu(d_in[:, part], cond, TN) + own_t[part, :].astype(full)
        return carry

    lax.fori_loop(0, in_tiles, light, 0)
    lead = lax.rem(shard * in_cols, 128)
    write_in = pltpu.make_async_copy(grad_t.at[pl.ds(pl.multiple_of(lead, 64), in_cols), :], g_in, write.at[0])
    write_in.start()
    by_blocks(
        lambda start, size: grad_t[pl.ds(pl.multiple_of(lead + start, 64), size), :], in_cols, c_in, n_in, 0
    )

    sums = jnp.zeros((out_cols, 1), full)
    for index in range(5):
        value = own_out[:, index * width : (index + 1) * width].astype(full)
        t_out[:, index * width : (index + 1) * width] = value
        sums += jnp.sum(value * value, -1, keepdims=True)
    pltpu.make_async_copy(t_out, g_out, write.at[1]).start()
    fresh = decayed(c_out[...], to_lanes(sums), 5 * width)
    n_out[...] = fresh
    column = to_column(1.0 / fresh)
    for index in range(5):
        value = t_out[:, index * width : (index + 1) * width]
        square = value * value
        put(width + index * width, jnp.sum(square, 0, keepdims=True), jnp.sum(square * column, 0, keepdims=True))

    for copy in reads:
        copy.wait()
    squares = [weight_sq[:, k * width : (k + 1) * width] for k in (0, 1)]
    squares += [jnp.sum(value[...] * value[...], 0, keepdims=True) for value in (v_head, v_embed)]
    for k, total in enumerate(squares):
        start = 2 * span + k * 128
        stats[:, start : start + 128] = jnp.broadcast_to(jnp.sum(total, -1, keepdims=True) / 128.0, (1, 128))
    write_in.wait()
    for k, (source, target) in enumerate(((t_out, g_out), (t_head, g_head), (t_embed, g_embed))):
        pltpu.make_async_copy(source, target, write.at[k + 1]).wait()


def lane_span(width, embed_rows):
    return 7 * width + -(-embed_rows // 128) * 128


def total_call(tables, heavy, weights, light, cols):
    (in_starts, in_tiles), (_, head_tiles), _, shards = tables
    low, full = jnp.bfloat16, jnp.float32
    width = heavy[2].shape[0]
    w_in, w_out, w_head, w_embed = weights
    lanes = 2 * lane_span(width, w_embed.shape[1]) + 4 * 128
    segments = own_segments(width, w_in.shape[0], in_starts, w_out.shape[0], shards)
    shapes = [(item.shape, full) for item in weights] + [(item.shape, full) for item in cols] + [((1, lanes), full)]
    anywhere, vmem = pl.BlockSpec(memory_space=pl.ANY), pl.BlockSpec(memory_space=pltpu.VMEM)
    scratch = [
        ((in_tiles * 128, width), low),
        (w_out.shape, low),
        ((in_tiles * 128, width), full),
        ((head_tiles * 128, width), full),
    ]
    scratch += [(item.shape, full) for item in weights[1:]] + [(item.shape, full) for item in weights[2:]]
    return pl.pallas_call(
        functools.partial(total_kernel, tables, segments),
        out_shape=[jax.ShapeDtypeStruct(*item) for item in shapes],
        in_specs=[anywhere] * 8 + [vmem] * (len(light) + 4),
        out_specs=[anywhere] * 4 + [vmem] * 5,
        scratch_shapes=[pltpu.VMEM(*item) for item in scratch] + [pltpu.SemaphoreType.DMA((4,))] * 3,
        compiler_params=pltpu.CompilerParams(vmem_limit_bytes=60 * 1024 * 1024),
    )(*heavy, *weights, *light, *cols)


def finish_kernel(shards, sizes, own, r_in, r_out, r_head, r_embed, n_in, n_out, n_head, n_embed, s_in, s_out, s_head, s_embed, rms, slots, send, recv):
    rep, shard = lax.axis_index("rep"), lax.axis_index("shard")
    barrier = pltpu.get_barrier_semaphore()
    for step in range(1, shards):
        peer = (rep, lax.rem(shard + step, shards))
        pl.semaphore_signal(barrier, inc=1, device_id=peer, device_id_type=MESH)
    pl.semaphore_wait(barrier, shards - 1)

    def copy(step):
        return pltpu.make_async_remote_copy(
            src_ref=own,
            dst_ref=slots.at[shard],
            send_sem=send.at[step - 1],
            recv_sem=recv.at[step - 1],
            device_id=(rep, lax.rem(shard + step, shards)),
            device_id_type=MESH,
        )

    for step in range(1, shards):
        copy(step).start()
    slots[shard] = own[...]
    for step in range(1, shards):
        copy(step).wait()
    total = functools.reduce(jnp.add, [slots[o] for o in range(shards)])
    states, fresh, scales = (r_in, r_out, r_head, r_embed), (n_in, n_out, n_head, n_embed), (s_in, s_out, s_head, s_embed)
    starts, start = [], 0
    for rows, _ in sizes:
        starts.append(start)
        start += -(-rows // 128) * 128
    update, means = jnp.zeros((1, 1), jnp.float32), []
    for k, (rows, cols) in enumerate(sizes):
        row = decay * states[k][...] + (1.0 - decay) * (total[:, starts[k] : starts[k] + rows] / cols + eps_one)
        fresh[k][...] = row
        mean = jnp.mean(row, -1, keepdims=True)
        means.append(mean)
        update += mean * jnp.sum(total[:, start + starts[k] : start + starts[k] + rows] / row, -1, keepdims=True)
    update = jnp.sqrt(update / sum(rows * cols for rows, cols in sizes))
    rms[...] = jnp.broadcast_to(update, rms.shape)
    factor = jnp.maximum(1.0, update / clip_level)
    for k, (rows, cols) in enumerate(sizes):
        first = 2 * start + k * 128
        weight = jnp.sqrt(jnp.sum(total[:, first : first + 128], -1, keepdims=True) / (rows * cols))
        scales[k][...] = rate * jnp.maximum(eps_two, weight) / factor * lax.rsqrt(fresh[k][...] / means[k])


def finish_call(shards, sizes, stats, rows_old):
    full = jnp.float32
    shapes = [((1, rows), full) for rows, _ in sizes] * 2 + [((1, 128), full)]
    return pl.pallas_call(
        functools.partial(finish_kernel, shards, sizes),
        out_shape=[jax.ShapeDtypeStruct(*item) for item in shapes],
        in_specs=[pl.BlockSpec(memory_space=pltpu.VMEM)] * 5,
        out_specs=[pl.BlockSpec(memory_space=pltpu.VMEM)] * len(shapes),
        scratch_shapes=[
            pltpu.VMEM((shards,) + stats.shape, full),
            pltpu.SemaphoreType.DMA((shards - 1,)),
            pltpu.SemaphoreType.DMA((shards - 1,)),
        ],
        compiler_params=pltpu.CompilerParams(collective_id=3, has_side_effects=True),
    )(stats, *rows_old)


def on_device(
    latents,
    noises,
    velocity,
    times,
    labels,
    dropped,
    blocks_in,
    blocks_out,
    head_side,
    embed_side,
    state_in_row,
    state_in_col,
    state_out_row,
    state_out_col,
    state_head_row,
    state_head_col,
    state_embed_row,
    state_embed_col,
):
    images = latents.shape[0]
    width = head_side.shape[0]
    shard_count = lax.axis_size("shard")
    place = lax.axis_index("shard")
    in_cols = blocks_in.shape[2]
    head_cols = head_side.shape[1]
    embed_cols = embed_side.shape[1]
    group = images * shard_count
    weights = (blocks_in[0].T, blocks_out[0].T, head_side.T, embed_side.T)
    t_value = (times.astype(jnp.float32) + 1.0) / step_count
    classes = (PATCH + FREQ + jnp.where(dropped == 1, CLASSES - 1, labels)).astype(jnp.float32)
    lines = LINE
    lead = -(-(PATCH + FREQ) // 128) * 128
    own_traits = jnp.concatenate(
        [
            jnp.zeros((images, PATCH), jnp.float32),
            time_freq(t_value, FREQ),
            jnp.zeros((images, lead - PATCH - FREQ), jnp.float32),
            jnp.broadcast_to(classes[:, None], (images, 128)),
        ],
        1,
    )
    traits = lax.dynamic_update_slice(
        jnp.zeros((group, lead + 128), jnp.float32), own_traits, (place * images, 0)
    )
    in_t, out_t, head_t, embed = windowed(*weights, shard_count)
    tcol = t_value[:, None, None]
    state = (
        (1.0 - tcol) * latents.reshape(images, TOK, PATCH)
        + tcol * noises.reshape(images, TOK, PATCH)
    ).astype(jnp.bfloat16)
    tables = (
        windows(in_cols, shard_count),
        windows(head_cols, shard_count),
        windows(embed_cols, shard_count),
        shard_count,
    )
    sums = step_call(
        lines,
        tables,
        in_cols,
        [in_t, out_t] + list(weights[:2]),
        [
            state.reshape(images * TOK, PATCH),
            velocity.reshape(images * TOK, PATCH),
            jnp.repeat(t_value, TOK)[:, None],
            jnp.asarray(positions(GRID, width)),
            head_t,
            embed,
            traits,
        ],
    )
    d_in, d_fin, d_two, d_full, d_one, few_sum, cond_full, time_act, all_traits, weight_sq = sums[4:]
    loss_sum = few_sum[PATCH, 0]
    rows_old = (state_in_row, state_out_row, state_head_row[None], state_embed_row[None])
    cols_old = (state_in_col, state_out_col, state_head_col[None], state_embed_col[None])
    *outs, stats = total_call(
        tables,
        sums[:4],
        weights,
        [d_in, d_fin, d_two, d_one, d_full, few_sum, cond_full, time_act, all_traits, weight_sq],
        cols_old,
    )
    totals, cols_new = outs[:4], outs[4:]
    blocks = lax.axis_size("rep") // (2 * lines)
    if blocks > 1:
        apart = [[k * 2 * lines + j for k in range(blocks)] for j in range(2 * lines)]
        totals, loss_sum = lax.psum((totals, loss_sum), "rep", axis_index_groups=apart)
        cols_new, plain, scaled = [], [], []
        for gradient, col_state in zip(totals, cols_old):
            square = gradient * gradient
            fresh = decay * col_state + (1.0 - decay) * (jnp.mean(square, 1)[None] + eps_one)
            pad = (0, -gradient.shape[1] % 128)
            cols_new.append(fresh)
            plain.append(jnp.pad(jnp.sum(square, 0), pad))
            scaled.append(jnp.pad(jnp.sum(square / fresh[0][:, None], 0), pad))
        spans = sum(item.shape[0] for item in plain) * 2
        stats = jnp.concatenate(plain + scaled + [stats[0, spans:]])[None]
    sizes = [(weight.shape[1], weight.shape[0] * shard_count) for weight in weights]
    *outs, rms = finish_call(shard_count, sizes, stats, rows_old)
    rows_new, scales = outs[:4], outs[4:]
    update_rms = rms[0, 0]
    news = [
        (weight - gradient * scale * lax.rsqrt(col_next[0])[:, None]).T
        for weight, gradient, scale, col_next in zip(weights, totals, scales, cols_new)
    ]
    return (
        loss_sum,
        update_rms,
        totals[0].T[None],
        totals[1].T[None],
        totals[2].T,
        totals[3].T,
        rows_new[0],
        cols_new[0],
        rows_new[1],
        cols_new[1],
        rows_new[2][0],
        cols_new[2][0],
        rows_new[3][0],
        cols_new[3][0],
        news[0][None],
        news[1][None],
        news[2],
        news[3],
    )


def solution(mesh):
    placed = (
        P(("rep", "shard"), None),
        P(("rep", "shard"), None),
        P(("rep", "shard"), None),
        P(("rep", "shard")),
        P(("rep", "shard")),
        P(("rep", "shard")),
        P(None, None, "shard"),
        P(None, None, "shard"),
        P(None, "shard"),
        P(None, "shard"),
        P(),
        P(None, "shard"),
        P(),
        P(None, "shard"),
        P(),
        P("shard"),
        P(),
        P("shard"),
    )
    return jax.shard_map(
        on_device,
        mesh=mesh,
        in_specs=placed,
        out_specs=(
            P(),
            P(),
            P(None, None, "shard"),
            P(None, None, "shard"),
            P(None, "shard"),
            P(None, "shard"),
            P(),
            P(None, "shard"),
            P(),
            P(None, "shard"),
            P(),
            P("shard"),
            P(),
            P("shard"),
            P(None, None, "shard"),
            P(None, None, "shard"),
            P(None, "shard"),
            P(None, "shard"),
        ),
        check_vma=False,
    )
```

```python
import functools
import math

import jax
import jax.numpy as jnp
import numpy as np
from jax import lax
from jax.experimental import pallas as pl
from jax.experimental.pallas import tpu as pltpu
from jax.sharding import PartitionSpec as P

HEADS = 12
CLASSES = 1001
FREQ = 256
GRID = 16
PATCH = 16
LAYERS = 1
TOK = 256


decay = 0.5
eps_norm = 1e-06
eps_one = 1e-30
eps_two = 0.001
clip_level = 0.1
rate = 8.0
step_count = 1000.0


def silu(value):
    return value * jax.nn.sigmoid(value)


def positions(grid, width):
    quarter = width // 4
    omega = (1.0 / 10000.0 ** (np.arange(quarter, dtype=np.float32) / quarter)).astype(np.float32)
    index = np.arange(grid * grid)
    row_pos = (index // grid).astype(np.float32)[:, None] * omega[None, :]
    col_pos = (index % grid).astype(np.float32)[:, None] * omega[None, :]
    return np.concatenate([np.sin(row_pos), np.cos(row_pos), np.sin(col_pos), np.cos(col_pos)], 1)


def time_freq(t_value, width):
    half = width // 2
    freqs = jnp.exp(-math.log(10000.0) * jnp.arange(half, dtype=jnp.float32) / half)
    angles = (t_value * step_count)[:, None] * freqs[None, :]
    return jnp.concatenate([jnp.cos(angles), jnp.sin(angles)], -1)


def weight_grad(left, back):
    flat_left = left.reshape(-1, left.shape[-1])
    flat_back = back.reshape(-1, back.shape[-1])
    return lax.dot_general(
        flat_left, flat_back, (((0,), (0,)), ((), ())), preferred_element_type=jnp.float32
    )


MESH = pl.DeviceIdType.MESH
LINE = 4
PIECES = 4
PARTS = (6, 6, 3)
ORDER = (
    (0, 0), (0, 1), (0, 2), (1, 0), (9, 0), (0, 3), (1, 1), (9, 1), (0, 4), (1, 2), (9, 2), (0, 5), (1, 3),
    (2, 0), (9, 3), (0, 6), (1, 4), (0, 7), (2, 1), (9, 4), (1, 5), (0, 8), (3, 0), (1, 6), (9, 5), (2, 2),
    (0, 9), (1, 7), (3, 1), (1, 8), (9, 6), (2, 3), (0, 10), (0, 11), (1, 9), (2, 4), (9, 7), (3, 2), (4, 0),
    (0, 12), (9, 8), (1, 10), (1, 11), (2, 5), (3, 3), (2, 6), (9, 9), (3, 4), (4, 1), (0, 13), (1, 12), (2, 7),
    (9, 10), (4, 2), (6, 0), (3, 5), (0, 14), (2, 8), (3, 6), (9, 11), (4, 3), (0, 15), (4, 4), (2, 9), (3, 7),
    (9, 12), (6, 1), (7, 0), (0, 16), (3, 8), (2, 10), (6, 2), (4, 5), (0, 17), (4, 6), (3, 9), (2, 11), (6, 3),
    (7, 1), (8, 0), (0, 18), (3, 10), (6, 4), (0, 19), (2, 12), (3, 11), (4, 7), (4, 8), (4, 9), (4, 10), (5, 6),
    (6, 5), (1, 13), (9, 13), (7, 2), (7, 3), (7, 4), (8, 1), (0, 20), (3, 12), (0, 21), (0, 22), (4, 11),
    (6, 6), (5, 7), (7, 5), (8, 2), (8, 3), (8, 4), (1, 14), (9, 14), (5, 8), (1, 15), (1, 16), (5, 9), (2, 13),
    (5, 10), (8, 5), (6, 7), (7, 6), (4, 12), (9, 15), (5, 11), (2, 14), (6, 8), (3, 13), (8, 6), (6, 9),
    (9, 16), (6, 10), (7, 7), (6, 12), (3, 14), (2, 15), (6, 11), (7, 8), (8, 7), (4, 13), (2, 16), (7, 9),
    (8, 8), (4, 14), (7, 10), (8, 9), (7, 12), (6, 13), (3, 15), (8, 10), (5, 14), (8, 12), (7, 11), (3, 16),
    (7, 13), (4, 15), (6, 14), (8, 11), (8, 13), (4, 16), (5, 15), (7, 14), (5, 16), (8, 14), (6, 15), (6, 16),
    (7, 15), (8, 15), (7, 16), (8, 16),
)
BESIDE_AT = (84, 95, 107, 119, 131, 143, 155)
SQUARES_AT = (106, 119, 133)
SLOTS = 3
NN = (((1,), (0,)), ((), ()))
NT = (((1,), (1,)), ((), ()))
TN = (((0,), (0,)), ((), ()))


def mxu(left, right, kind):
    return lax.dot_general(left, right, kind, preferred_element_type=jnp.float32)


def blocks_of(total, size, body):
    def step(index, carry):
        body(pl.ds(pl.multiple_of(index * size, size), size))
        return carry

    lax.fori_loop(0, total // size, step, 0)


def heavy_chunks(width):
    half = width // 2
    fc2, fc1, kv = PARTS
    parts = [(0, 0, width, 4 * width // fc2 * k, 2 * width // fc2, False) for k in range(fc2)]
    parts += [(1, 4 * width // fc1 * k, 4 * width // fc1, 0, half, True) for k in range(fc1)]
    parts += [(2, 0, width, 0, half, False), (3, 0, width, 0, half, False)]
    parts += [(3, width + 2 * width // kv * k, 2 * width // kv, 0, half, True) for k in range(kv)]
    return tuple(parts)


def add_rows(target, left, right, rows):
    block = 16

    def body(index, carry):
        span = pl.ds(pl.multiple_of(index * block, block), block)
        target[span] = left[span] + right[span]
        return carry

    lax.fori_loop(0, rows // block, body, 0)


def step_kernel(lines, chunks, tables, in_cols, *refs):
    count = len(chunks)
    (in_far, out_far, w_in, w_out, state, target, weight_t, pos, head_t, embed, traits), refs = refs[:11], refs[11:]
    (own_t, own_out), refs = refs[:2], refs[2:]
    (d_in, d_head, d_two, d_full, d_one, few_sum, cond_full, time_act, all_traits, weight_sq), scratch = refs[:10], refs[10:]
    finals, scratch = scratch[:4], scratch[4:]
    held, by_y, by_x, by_z = (scratch[k * count : (k + 1) * count] for k in range(4))
    send, recv, zsend, zrecv, wsend, wrecv = scratch[4 * count : 4 * count + 6]
    scratch = scratch[4 * count + 6 :]
    (stage_wide, stage_tall, land_wide, land_tall, free_wide, free_tall, fetch, weight_load, d_mod, d_fm, few), scratch = scratch[:11], scratch[11:]
    (
        stream, hat_one, hat_two, root_one, root_two, a_low, qkv_low, mixed, proj, b_low, active, mlp, d_mlp,
    ), scratch = scratch[:13], scratch[13:]
    (
        few_got, few_y, few_x, few_held, few_line, mod_got, fm_got, mod_sum, fm_sum, group_slot, part_own, part_slot,
        act_own, act_slot, pair_own, pair_got, line_in, line_rest, line_full,
        few_send, few_recv, group_send, group_recv, line_send, line_recv,
    ) = scratch[:25]
    gather_refs = scratch[25:]
    (in_starts, in_tiles), (head_starts, head_tiles), (embed_starts, embed_tiles), shards = tables
    time_one, modul, fmod, patch, last = gather_refs[:5]
    rep, shard = lax.axis_index("rep"), lax.axis_index("shard")
    place_here = lax.rem(rep, 2 * lines)
    base = rep - place_here
    x, z = lax.rem(place_here, 2), lax.div(place_here, 2)
    core, y = lax.rem(shard, 2), lax.div(shard, 2)
    to_core = (rep, shard + 1 - 2 * core)
    to_y = (rep, shard + 2 - 4 * y)
    to_x = (rep + 1 - 2 * x, shard)

    def line_peer(step):
        return (base + lax.rem(z + step, lines) * 2 + x, shard)

    barrier = pltpu.get_barrier_semaphore()
    to_far = (rep, shards - 1 - shard)
    for peer in (to_core, to_y, to_x, to_far):
        pl.semaphore_signal(barrier, inc=1, device_id=peer, device_id_type=MESH)
    for step in range(1, lines):
        pl.semaphore_signal(
            barrier, inc=1, device_id=line_peer(step), device_id_type=MESH
        )
    pl.semaphore_wait(barrier, 4 + lines - 1)

    width, tokens = head_t.shape[1], state.shape[0]
    in_blocks = [active.at[:, pl.ds(k * width, width)] for k in range(4)] + [d_mlp]

    def far_copy(k):
        return pltpu.make_async_copy(in_far.at[pl.ds(k * tokens, tokens), :], in_blocks[k], fetch.at[4 + k])

    stride = lines // PIECES
    owns = lax.rem(z, stride) == 0
    mine = lax.div(z, stride)
    def remote(source, target, send_sem, recv_sem, peer):
        return pltpu.make_async_remote_copy(
            src_ref=source,
            dst_ref=target,
            send_sem=send_sem,
            recv_sem=recv_sem,
            device_id=peer,
            device_id_type=MESH,
        )

    def rows_of(ref, start, size):
        return ref.at[pl.ds(pl.multiple_of(start, 16), size)]

    def lanes_at(index, ref, row, rows, which):
        _, _, _, lane, lanes, _ = chunks[index]
        return ref.at[
            pl.ds(pl.multiple_of(row, 16), rows), pl.ds(pl.multiple_of(lane + which * lanes, 128), lanes)
        ]

    turn = {i: sum(chunks[j][0] == 0 for j in range(i)) if chunks[i][0] == 0 else sum(chunks[j][0] != 0 for j in range(i)) for i in range(count)}

    def slot_of(i, wide, tall):
        if chunks[i][0] == 0:
            return wide.at[turn[i] % SLOTS]
        return tall.at[turn[i] % SLOTS, pl.ds(0, chunks[i][2])]

    def turn_away(i, steps):
        for j in range(count):
            if (chunks[j][0] == 0) == (chunks[i][0] == 0) and turn[j] == turn[i] + steps:
                return j
        return None

    def core_copy(i):
        return remote(
            slot_of(i, stage_wide, stage_tall), slot_of(i, land_wide, land_tall), send.at[i, 0], recv.at[i, 0], to_core
        )

    def free_of(i):
        return free_wide if chunks[i][0] == 0 else free_tall

    def y_copy(i):
        half = chunks[i][2] // 2
        return remote(
            rows_of(held[i], (1 - y) * half, half), by_y[i], send.at[i, 1], recv.at[i, 1], to_y
        )

    def x_copy(i):
        quarter = chunks[i][2] // 4
        return remote(
            rows_of(by_y[i], (1 - x) * quarter, quarter), by_x[i], send.at[i, 2], recv.at[i, 2], to_x
        )

    def z_copy(i, piece):
        size = chunks[i][2] // 4 // PIECES
        owner = piece * stride
        slot = lax.rem(z - owner - 1 + lines, lines)
        return remote(
            by_x[i].at[pl.ds(piece * size, size)],
            by_z[i].at[slot],
            zsend.at[i, piece],
            zrecv.at[i, slot],
            (base + owner * 2 + x, shard),
        )

    def final_rows(i, side, start, size, which):
        array, row, rows = chunks[i][:3]
        return lanes_at(i, finals[array], row + side * (rows // 2) + start, size, which)

    def cross_copy(i):
        quarter = chunks[i][2] // 4
        part = final_rows(i, 0, x * quarter, quarter, core)
        return remote(part, part, send.at[i, 3], recv.at[i, 3], to_y)

    def line_copy(i, which, side, step):
        size = chunks[i][2] // 4 // PIECES
        part = final_rows(i, side, (x * PIECES + mine) * size, size, core)
        return remote(
            part, part, wsend.at[i, which, step - 1], wrecv.at[i, which, mine], line_peer(step)
        )

    def line_arrival(i, which, side, piece):
        size = chunks[i][2] // 4 // PIECES
        part = final_rows(i, side, (x * PIECES + piece) * size, size, core)
        return remote(part, part, wsend.at[i, which, 0], wrecv.at[i, which, piece], to_core)

    def pair_copy(i, which, side, column):
        quarter = chunks[i][2] // 4
        part = final_rows(i, side, column * quarter, quarter, core)
        return remote(part, part, send.at[i, 4 + which], recv.at[i, 4 + which], to_x)

    def last_copy(i, which, side, half):
        rows = chunks[i][2] // 2
        part = final_rows(i, side, 0, rows, half)
        return remote(part, part, send.at[i, 6 + which], recv.at[i, 6 + which], to_core)

    def sides(i, action):
        if chunks[i][5]:

            @pl.when(y == 1)
            def _():
                action(0, 1)
                action(1, 0)

        else:
            action(0, y)

    def produce(i, left, right):
        rows, lanes = chunks[i][2], chunks[i][4]
        before, after = turn_away(i, -SLOTS), turn_away(i, SLOTS)
        if before is not None:
            core_copy(before).wait_send()
        staged = slot_of(i, stage_wide, stage_tall)

        def block(part):
            value = mxu(left[:, part], right[...], TN)
            first, second = value[:, :lanes], value[:, lanes:]
            held[i][part, :] = jnp.where(core == 0, first, second).astype(jnp.bfloat16)
            staged[part, :] = jnp.where(core == 0, second, first).astype(jnp.bfloat16)

        blocks_of(rows, 256, block)
        if before is not None:
            pl.semaphore_wait(free_of(i), 1)
        core_copy(i).start()

    def stage1(i):
        core_copy(i).wait_recv()
        add_rows(held[i], held[i], slot_of(i, land_wide, land_tall), chunks[i][2])
        if turn_away(i, SLOTS) is not None:
            pl.semaphore_signal(free_of(i), inc=1, device_id=to_core, device_id_type=MESH)

    def stage2(i):
        half = chunks[i][2] // 2
        y_copy(i).wait_recv()
        add_rows(by_y[i], by_y[i], rows_of(held[i], y * half, half), half)
        x_copy(i).start()

    def stage3(i):
        quarter = chunks[i][2] // 4
        x_copy(i).wait_recv()
        add_rows(by_x[i], by_x[i], rows_of(by_y[i], x * quarter, quarter), quarter)
        for piece in range(PIECES):

            @pl.when(z != piece * stride)
            def _():
                z_copy(i, piece).start()

    def stage4(i):
        size = chunks[i][2] // 4 // PIECES

        @pl.when(owns)
        def _():
            for slot in range(lines - 1):
                remote(
                    by_z[i].at[slot], by_z[i].at[slot], zsend.at[i, 0], zrecv.at[i, slot], to_core
                ).wait_recv()
            target = final_rows(i, y, (x * PIECES + mine) * size, size, core)

            def body(index, carry):
                total = by_x[i][
                    pl.ds(pl.multiple_of(mine * size + index * 16, 16), 16)
                ].astype(jnp.float32)
                for slot in range(lines - 1):
                    total += by_z[i][slot, pl.ds(pl.multiple_of(index * 16, 16), 16)].astype(jnp.float32)
                target[pl.ds(pl.multiple_of(index * 16, 16), 16)] = total.astype(jnp.bfloat16)
                return carry

            lax.fori_loop(0, size // 16, body, 0)
            for step in range(1, lines):
                line_copy(i, 0, y, step).start()

    def line_wait(i):
        for piece in range(PIECES):

            @pl.when(z != piece * stride)
            def _():
                line_arrival(i, 0, y, piece).wait_recv()

    def stage5(i):
        @pl.when(y == 0)
        def _():
            line_wait(i)
            cross_copy(i).start()

    def stage6(i):
        if chunks[i][5]:

            @pl.when(y == 1)
            def _():
                line_wait(i)
                pair_copy(i, 0, 1, x).start()
                cross_copy(i).wait_recv()
                pair_copy(i, 1, 0, x).start()

        else:
            line_wait(i)
            pair_copy(i, 0, y, x).start()

    def stage7(i):
        def action(which, side):
            pair_copy(i, which, side, 1 - x).wait_recv()
            last_copy(i, which, side, core).start()

        sides(i, action)

    def stage8(i):
        sides(i, lambda which, side: last_copy(i, which, side, 1 - core).wait_recv())


    mod_tiles, wide = 6 * width // 128, width // 128
    images = d_mod.shape[0]
    in_lanes, head_lanes, embed_lanes = in_tiles * 128, head_tiles * 128, embed_tiles * 128
    rest_lanes = 2 * head_lanes + embed_lanes
    head_places = [o for o in range(shards) if head_starts[o] < wide]
    mod_places = [o for o in range(shards) if in_starts[o] < mod_tiles]
    few_rows = few.shape[0] // 2
    half = pl.ds(pl.multiple_of(core * few_rows, 8), few_rows)
    other_half = pl.ds(pl.multiple_of((1 - core) * few_rows, 8), few_rows)

    def is_in(where, places):
        return functools.reduce(jnp.logical_or, [where == o for o in places])

    few_core = remote(few.at[other_half], few_got, few_send.at[0], few_recv.at[0], to_core)
    few_over_y = remote(few_held.at[0], few_y, few_send.at[1], few_recv.at[1], to_y)
    few_over_x = remote(few_held.at[1], few_x, few_send.at[2], few_recv.at[2], to_x)
    few_back = remote(few_sum.at[half], few_sum.at[half], few_send.at[3], few_recv.at[3], to_core)
    few_back_arrival = remote(few_sum.at[other_half], few_sum.at[other_half], few_send.at[3], few_recv.at[3], to_core)
    mod_core = remote(d_mod, mod_got, few_send.at[4], few_recv.at[4], to_core)
    fm_core = remote(d_fm, fm_got, few_send.at[5], few_recv.at[5], to_core)
    pair_copy_x = remote(pair_own, pair_got, few_send.at[6], few_recv.at[6], to_x)

    def few_line_copy(step):
        return remote(few_line.at[z], few_line.at[z], few_send.at[6 + step], few_recv.at[6 + step], line_peer(step))

    def few_line_arrival(step):
        origin = lax.rem(z + lines - step, lines)
        return remote(few_line.at[origin], few_line.at[origin], few_send.at[6 + step], few_recv.at[6 + step], to_core)

    def group_parts(place):
        parts = []
        tiles = min(in_tiles, mod_tiles - in_starts[place])
        if tiles > 0:
            parts.append((0, in_starts[place] * 128, 0, tiles * 128))
        first, final = max(head_starts[place], wide), min(head_starts[place] + head_tiles, 3 * wide)
        if final > first:
            lead = (first - head_starts[place]) * 128
            parts.append((1, (first - wide) * 128, in_lanes + lead, (final - first) * 128))
        return parts

    def group_copy(place, k):
        which, lane, own, lanes = group_parts(place)[k]
        return remote(
            (mod_sum, fm_sum)[which].at[:, pl.ds(lane, lanes)],
            group_slot.at[:, pl.ds(own, lanes)],
            group_send.at[k, 0],
            group_recv.at[k, 0],
            to_y,
        )

    def to_others(kind, source, slots, step):
        return remote(
            source,
            slots.at[shard],
            group_send.at[kind, step - 1],
            group_recv.at[kind, step - 1],
            (rep, lax.rem(shard + step, shards)),
        )

    def from_others(kind, slots, step):
        origin = lax.rem(shard + shards - step, shards)
        return remote(slots.at[origin], slots.at[origin], group_send.at[kind, 0], group_recv.at[kind, step - 1], to_core)

    slots_of = (line_rest, line_full, line_in)

    def line_copy_d(kind, step):
        slots = slots_of[kind]
        return remote(slots.at[z], slots.at[z], line_send.at[kind, step - 1], line_recv.at[kind, step - 1], line_peer(step))

    def line_arrival_d(kind, step):
        slots = slots_of[kind]
        origin = lax.rem(z + lines - step, lines)
        return remote(slots.at[origin], slots.at[origin], line_send.at[kind, 0], line_recv.at[kind, step - 1], to_core)

    def on_line(action):
        for step in range(1, lines):
            action(0, step)
            action(1, step)

            @pl.when(is_in(shard, mod_places))
            def _():
                action(2, step)

    def side0():
        mod_core.start()
        fm_core.start()
        few_core.start()

    def side1():
        mod_core.wait_recv()
        mod_sum[...] = d_mod[...] + mod_got[...]
        fm_core.wait_recv()
        fm_sum[...] = d_fm[...] + fm_got[...]
        for place in range(shards):

            @pl.when(to_y[1] == place)
            def _():
                for k in range(len(group_parts(place))):
                    group_copy(place, k).start()

        few_core.wait_recv()
        few_held[0] = few[half] + few_got[...]
        few_over_y.start()

    def side2():
        pair_own[...] = jnp.zeros_like(pair_own)
        for place in range(shards):

            @pl.when(shard == place)
            def _():
                for k, (which, lane, own, lanes) in enumerate(group_parts(place)):
                    group_copy(place, k).wait_recv()
                    pair_own[:, own : own + lanes] = (
                        (mod_sum, fm_sum)[which][:, lane : lane + lanes] + group_slot[:, own : own + lanes]
                    )

        part_own[...] = jnp.dot(
            pair_own[:, in_lanes : in_lanes + head_lanes].astype(jnp.bfloat16),
            head_t[...],
            preferred_element_type=jnp.float32,
        )

        @pl.when(is_in(shard, mod_places))
        def _():
            for k in range(len(in_blocks)):
                far_copy(k).wait()
                lanes = pair_own[:, k * tokens : (k + 1) * tokens].astype(jnp.bfloat16)
                part_own[...] += jnp.dot(lanes, in_blocks[k][...], preferred_element_type=jnp.float32)

        part_slot[shard] = part_own[...]
        for step in range(1, shards):
            to_others(2, part_own, part_slot, step).start()
        few_over_y.wait_recv()
        few_held[1] = few_held[0] + few_y[...]
        few_over_x.start()

    def side3():
        for step in range(1, shards):
            from_others(2, part_slot, step).wait_recv()
        d_cond = functools.reduce(jnp.add, [part_slot[o] for o in range(shards)])
        value = cond_full[pl.ds(pl.multiple_of(place_here * images, 8), images), :]
        gate = jax.nn.sigmoid(value)
        d_value = d_cond * (gate + value * gate * (1.0 - gate))
        for place in range(shards):

            @pl.when(shard == place)
            def _():
                first = embed_starts[place] * 128
                pair_own[:, in_lanes + rest_lanes :] = d_value[:, first : first + embed_lanes]
                if place in head_places:
                    lanes = min(head_tiles, wide - head_starts[place]) * 128
                    first = head_starts[place] * 128
                    start = in_lanes + head_lanes
                    d_two_own = d_value[:, first : first + lanes].astype(jnp.bfloat16)
                    pair_own[:, start : start + lanes] = d_two_own.astype(jnp.float32)
                    act_own[...] = jnp.dot(d_two_own, head_t[:lanes, :], preferred_element_type=jnp.float32)
                    act_slot[shard] = act_own[...]
                    for step in range(1, shards):
                        to_others(3, act_own, act_slot, step).start()

        few_over_x.wait_recv()
        few_line[z] = few_held[1] + few_x[...]
        for step in range(1, lines):
            few_line_copy(step).start()

    def side4():
        for step in range(1, shards):

            @pl.when(is_in(lax.rem(shard + shards - step, shards), head_places))
            def _():
                from_others(3, act_slot, step).wait_recv()

        value = time_one[pl.ds(pl.multiple_of(place_here * images, 8), images), :]
        gate = jax.nn.sigmoid(value)
        slope = gate + value * gate * (1.0 - gate)
        for place in range(shards):

            @pl.when(shard == place)
            def _():
                first = embed_starts[place] * 128
                d_act = functools.reduce(jnp.add, [act_slot[o, :, first : first + embed_lanes] for o in head_places])
                start = in_lanes + 2 * head_lanes
                pair_own[:, start : start + embed_lanes] = (slope * d_act).astype(jnp.bfloat16).astype(jnp.float32)

        pair_copy_x.start()
        for step in range(1, lines):
            few_line_arrival(step).wait_recv()
        few_sum[half] = functools.reduce(jnp.add, [few_line[at] for at in range(lines)])
        few_back.start()

    def side5():
        pair_copy_x.wait_recv()
        own, got = pair_own[...], pair_got[...]
        both = jnp.concatenate([jnp.where(x == 0, own, got), jnp.where(x == 0, got, own)], 0)
        line_in[z] = both[:, :in_lanes].astype(jnp.bfloat16)
        line_rest[z] = both[:, in_lanes : in_lanes + rest_lanes].astype(jnp.bfloat16)
        line_full[z] = both[:, in_lanes + rest_lanes :]
        on_line(lambda kind, step: line_copy_d(kind, step).start())

    def side6():
        on_line(lambda kind, step: line_arrival_d(kind, step).wait_recv())
        for at in range(lines):
            span = slice(at * 2 * images, (at + 1) * 2 * images)
            d_head[span, :] = line_rest[at, :, :head_lanes]
            d_two[span, :] = line_rest[at, :, head_lanes : 2 * head_lanes]
            d_one[span, :] = line_rest[at, :, 2 * head_lanes :]
            d_full[span, :] = line_full[at]
        d_in[...] = jnp.zeros_like(d_in)

        @pl.when(is_in(shard, mod_places))
        def _():
            for at in range(lines):
                d_in[at * 2 * images : (at + 1) * 2 * images, :] = line_in[at]

        few_back_arrival.wait_recv()

    def side_end():
        for copy in (few_core, few_over_y, few_over_x, few_back, mod_core, fm_core, pair_copy_x):
            copy.wait_send()
        for step in range(1, lines):
            few_line_copy(step).wait_send()
        on_line(lambda kind, step: line_copy_d(kind, step).wait_send())
        for place in range(shards):

            @pl.when(to_y[1] == place)
            def _():
                for k in range(len(group_parts(place))):
                    group_copy(place, k).wait_send()

        for step in range(1, shards):
            to_others(2, part_own, part_slot, step).wait_send()

        @pl.when(is_in(shard, head_places))
        def _():
            for step in range(1, shards):
                to_others(3, act_own, act_slot, step).wait_send()

    room = (stream, hat_one, hat_two, proj, mlp)
    rounds = []
    for source in (w_in,):
        blocks = [(start, min(tokens, source.shape[0] - start)) for start in range(0, source.shape[0], tokens)]
        rounds.append([(source.at[pl.ds(start, size), :], size) for start, size in blocks])
    rounds.append([(w_out.at[:, pl.ds(k * width, width)], w_out.shape[0]) for k in range(w_out.shape[1] // width)])

    def weight_copies(index):
        return [
            pltpu.make_async_copy(source, room[k].at[pl.ds(0, size), :], weight_load.at[k])
            for k, (source, size) in enumerate(rounds[index])
        ]

    def squares_step(index):
        if index > 0:
            total = jnp.zeros((1, width), jnp.float32)
            for k, copy in enumerate(weight_copies(index - 1)):
                copy.wait()
                size = rounds[index - 1][k][1]
                whole = size // 64 * 64

                def add(block, carry):
                    value = room[k][pl.ds(pl.multiple_of(block * 64, 64), 64), :]
                    return carry + jnp.sum(value * value, 0, keepdims=True)

                total = lax.fori_loop(0, size // 64, add, total)
                if whole < size:
                    value = room[k][whole:size, :]
                    total += jnp.sum(value * value, 0, keepdims=True)
            weight_sq[:, (index - 1) * width : index * width] = total
        if index < len(rounds):
            for copy in weight_copies(index):
                copy.start()

    beside = (side0, side1, side2, side3, side4, side5, side6)
    low = jnp.bfloat16
    per = tokens // TOK
    row = [shard * per + image for image in range(per)]
    span = [pl.ds(image * TOK, TOK) for image in range(per)]
    cut = 256

    def piece(ref, image, index):
        return ref[pl.ds(row[image], 1), pl.ds(index * width, width)]

    def normed(value):
        center = value - jnp.mean(value, -1, keepdims=True)
        root = lax.rsqrt(jnp.mean(center * center, -1, keepdims=True) + eps_norm)
        return center * root, root

    def norm_back(d_hat, hat, root):
        return root * (d_hat - jnp.mean(d_hat, -1, keepdims=True) - hat * jnp.mean(d_hat * hat, -1, keepdims=True))

    def put_row(ref, image, index, value):
        ref[pl.ds(row[image], 1), pl.ds(index * width, width)] = (
            jnp.sum(value, 0, keepdims=True).astype(low).astype(jnp.float32)
        )

    fc2, fc1, attn_out, qkv = finals
    segments = heavy_segments(width, in_cols, in_starts, out_far.shape[0], shards)
    plan = (segments,) + tables[:3] + (lines,)
    relay_tick, arrived, finish = gather_steps(
        plan, remote, line_peer, in_blocks, far_copy, out_far, in_far, head_t, embed, traits,
        *finals, cond_full, time_act, time_one, modul, fmod, patch, last, all_traits, *gather_refs[5:],
    )
    d_mod[...] = jnp.zeros_like(d_mod)
    d_fm[...] = jnp.zeros_like(d_fm)

    for image in range(per):
        value = mxu(state[span[image], :], patch[...], NN) + pos[...]
        stream[span[image], :] = value
        hat, root = normed(value)
        hat_one[span[image], :] = hat
        root_one[span[image], :] = root
        a_low[span[image], :] = (hat * (1.0 + piece(modul, image, 1)) + piece(modul, image, 0)).astype(low)

    def qkv_block(part):
        qkv_low[:, part] = mxu(a_low[...], qkv[part, :], NT).astype(low)

    relay_tick(4)
    arrived(3)
    blocks_of(3 * width, cut, qkv_block)
    relay_tick(5)
    lane = lax.broadcasted_iota(jnp.int32, (TOK, 128), 1)
    first = lane < 64
    scale = 0.125

    def softmax(query, key):
        score = mxu(query, key, NT) * scale
        expo = jnp.exp(score - jnp.max(score, -1, keepdims=True))
        return expo / jnp.sum(expo, -1, keepdims=True)

    def take(ref, image, start):
        return ref[span[image], pl.ds(pl.multiple_of(start, 128), 128)]

    def attend(pair, carry):
        for image in range(per):
            query, key, value = (take(qkv_low, image, index * width + pair * 128) for index in range(3))
            outs = []
            for side in (first, jnp.logical_not(first)):
                probs = softmax(jnp.where(side, query, jnp.zeros_like(query)), key)
                outs.append(mxu(probs.astype(low), value, NN))
            mixed[span[image], pl.ds(pl.multiple_of(pair * 128, 128), 128)] = jnp.where(first, outs[0], outs[1]).astype(low)
        return carry

    lax.fori_loop(0, width // 128, attend, 0)
    relay_tick(6)
    relay_tick(7)
    arrived(2)
    for image in range(per):
        got = mxu(mixed[span[image], :], attn_out[...], NT)
        proj[span[image], :] = got
        value = stream[span[image], :] + piece(modul, image, 2) * got
        stream[span[image], :] = value
        hat, root = normed(value)
        hat_two[span[image], :] = hat
        root_two[span[image], :] = root
        b_low[span[image], :] = (hat * (1.0 + piece(modul, image, 4)) + piece(modul, image, 3)).astype(low)

    def upper_block(part):
        value = mxu(b_low[...], fc1[part, :], NT)
        active[:, part] = (
            0.5 * value * (1.0 + jnp.tanh(0.7978845608 * (value + 0.044715 * value * value * value)))
        ).astype(low)

    arrived(1)
    blocks_of(4 * width, cut, upper_block)
    arrived(0)
    finish()

    def mlp_block(part):
        mlp[:, part] = mxu(active[...], fc2[part, :], NT)

    blocks_of(width, cut, mlp_block)
    loss = jnp.zeros((), jnp.float32)
    g_last = jnp.zeros((PATCH, width), jnp.float32)
    for image in range(per):
        value = stream[span[image], :] + piece(modul, image, 5) * mlp[span[image], :]
        hat, root = normed(value)
        gain = 1.0 + piece(fmod, image, 1)
        final = (hat * gain + piece(fmod, image, 0)).astype(low)
        diff = mxu(final, last[...], NT) - target[span[image], :]
        share = weight_t[span[image], :] * diff
        loss += 0.5 * jnp.sum(share * diff)
        d_out = share.astype(low)
        g_last += mxu(d_out, final, TN)
        d_final = mxu(d_out, last[...], NN)
        put_row(d_fm, image, 0, d_final)
        put_row(d_fm, image, 1, d_final * hat)
        d_value = norm_back(d_final * gain, hat, root)
        stream[span[image], :] = d_value
        put_row(d_mod, image, 5, d_value * mlp[span[image], :])
        d_mlp[span[image], :] = (piece(modul, image, 5) * d_value).astype(low)
    few[pl.ds(PATCH, 8), :] = jnp.full((8, width), loss, jnp.float32)
    few[pl.ds(PATCH + 8, PATCH), :] = g_last
    few[pl.ds(2 * PATCH + 8, 8), :] = jnp.zeros((8, width), jnp.float32)

    of_fc2 = [i for i in range(count) if chunks[i][0] == 0]
    of_fc1 = [i for i in range(count) if chunks[i][0] == 1]
    of_o = [i for i in range(count) if chunks[i][0] == 2]
    of_qkv = [i for i in range(count) if chunks[i][0] == 3]

    def fc2_step(i):
        first, lanes = chunks[i][3], 2 * chunks[i][4]
        part = pl.ds(first, lanes)
        value = mxu(b_low[...], fc1[part, :], NT)
        inner = jnp.tanh(0.7978845608 * (value + 0.044715 * value * value * value))
        slope = 0.5 * (1.0 + inner) + 0.5 * value * (1.0 - inner * inner) * 0.7978845608 * (
            1.0 + 3.0 * 0.044715 * value * value
        )
        d_upper = (slope * mxu(d_mlp[...], fc2[:, part], NN)).astype(low)
        produce(i, d_mlp, active.at[:, part])
        active[:, part] = d_upper

    def fc1_step(i):
        part = pl.ds(chunks[i][1], chunks[i][2])
        more = mxu(active[:, part], fc1[part, :], NN)
        if i == of_fc1[0]:
            mlp[...] = more
        else:
            mlp[...] += more
        produce(i, active.at[:, part], b_low)

    def o_step(i):
        for image in range(per):
            d_normed = mlp[span[image], :]
            hat = hat_two[span[image], :]
            put_row(d_mod, image, 3, d_normed)
            put_row(d_mod, image, 4, d_normed * hat)
            d_value = stream[span[image], :] + norm_back(
                d_normed * (1.0 + piece(modul, image, 4)), hat, root_two[span[image], :]
            )
            stream[span[image], :] = d_value
            put_row(d_mod, image, 2, d_value * proj[span[image], :])
            b_low[span[image], :] = (piece(modul, image, 2) * d_value).astype(low)
        active[:, pl.ds(0, width)] = mxu(b_low[...], attn_out[...], NN).astype(low)
        produce(i, b_low, mixed)

    def attend_back(pair):
        for image in range(per):
            query, key, value = (take(qkv_low, image, index * width + pair * 128) for index in range(3))
            d_out = take(active, image, pair * 128)
            d_query, d_key, d_value = [], [], []
            for side in (first, jnp.logical_not(first)):
                none = jnp.zeros_like(query)
                probs = softmax(jnp.where(side, query, none), key)
                d_prob = mxu(jnp.where(side, d_out, none), value, NT)
                d_score = (probs * (d_prob - jnp.sum(probs * d_prob, -1, keepdims=True))).astype(low)
                d_value.append(mxu(probs.astype(low), d_out, TN))
                d_query.append(mxu(d_score, key, NN) * scale)
                d_key.append(mxu(d_score, query, TN) * scale)
            for index, both in enumerate((d_query, d_key, d_value)):
                qkv_low[span[image], pl.ds(pl.multiple_of(index * width + pair * 128, 128), 128)] = jnp.where(
                    first, both[0], both[1]
                ).astype(low)

    def norm_one_step():
        @pl.when(is_in(shard, mod_places))
        def _():
            for k in range(len(in_blocks)):
                far_copy(k).start()

        g_patch = jnp.zeros((PATCH, width), jnp.float32)
        for image in range(per):
            d_normed = mxu(qkv_low[span[image], :], qkv[...], NN)
            hat = hat_one[span[image], :]
            put_row(d_mod, image, 0, d_normed)
            put_row(d_mod, image, 1, d_normed * hat)
            d_value = stream[span[image], :] + norm_back(
                d_normed * (1.0 + piece(modul, image, 1)), hat, root_one[span[image], :]
            )
            g_patch += mxu(state[span[image], :], d_value.astype(low), TN)
        few[pl.ds(0, PATCH), :] = g_patch

    def qkv_step(i):
        if i == of_qkv[0]:
            norm_one_step()
        produce(i, qkv_low.at[:, pl.ds(chunks[i][1], chunks[i][2])], a_low)

    def over_y(i):
        y_copy(i).start()

    stages = (None, stage1, stage2, stage3, stage4, stage5, stage6, stage7, stage8, over_y)
    steps = [(fc2_step, i) for i in of_fc2] + [(fc1_step, i) for i in of_fc1] + [(o_step, i) for i in of_o]
    steps += [(attend_back, pair) for pair in range(width // 128)] + [(qkv_step, i) for i in of_qkv]
    for j, (k, i) in enumerate(ORDER):
        if j in BESIDE_AT:
            beside[BESIDE_AT.index(j)]()
        if j in SQUARES_AT:
            squares_step(SQUARES_AT.index(j))
        if k == 0:
            step, arg = steps[i]
            step(arg)
        else:
            stages[k](i)

    out_rows = out_far.shape[0]

    def own_copies(place):
        copies = [
            pltpu.make_async_copy(
                finals[array].at[pl.ds(row, rows), :], own_t.at[pl.ds(at, rows), :], fetch.at[n]
            )
            for n, (array, row, rows, at) in enumerate(own_segments(width, in_cols, in_starts, out_rows, shards)[place])
        ]
        for n, array, lane in ((2, 2, 0), (3, 0, width)):
            copies.append(
                pltpu.make_async_copy(
                    finals[array].at[pl.ds(place * out_rows, out_rows), :],
                    own_out.at[:, pl.ds(lane, finals[array].shape[1])],
                    fetch.at[n],
                )
            )
        return copies

    for place in range(shards):

        @pl.when(shard == place)
        def _():
            for copy in own_copies(place):
                copy.start()

    side_end()
    for i in range(count):
        if turn_away(i, SLOTS) is None:
            core_copy(i).wait_send()
        y_copy(i).wait_send()
        x_copy(i).wait_send()
        for piece in range(PIECES):

            @pl.when(z != piece * stride)
            def _():
                z_copy(i, piece).wait_send()

        if chunks[i][5]:

            @pl.when(y == 0)
            def _():
                cross_copy(i).wait_send()

        @pl.when(owns)
        def _():
            for step in range(1, lines):
                line_copy(i, 0, y, step).wait_send()

        def action(which, side):
            pair_copy(i, which, side, x).wait_send()
            last_copy(i, which, side, core).wait_send()

        sides(i, action)

    for place in range(shards):

        @pl.when(shard == place)
        def _():
            for copy in own_copies(place):
                copy.wait()


def step_call(lines, tables, in_cols, far, light):
    width = far[0].shape[1]
    chunks = heavy_chunks(width)
    count = len(chunks)
    low, full = jnp.bfloat16, jnp.float32
    (_, in_tiles), (_, head_tiles), (_, embed_tiles), shards = tables
    state, traits = light[0], light[6]
    tokens, group = state.shape[0], traits.shape[0]
    rows = 2 * lines * group
    modul_shape, fmod_shape = (group, 6 * width), (group, 2 * width)
    segments = heavy_segments(width, in_cols, tables[0][0], far[1].shape[0], shards)
    most = max(len(parts) for parts in segments)
    in_lanes, head_lanes, embed_lanes = in_tiles * 128, head_tiles * 128, embed_tiles * 128
    rest_lanes = 2 * head_lanes + embed_lanes
    few = (2 * PATCH + 16, width)
    few_half = (few[0] // 2, width)
    pair = (group, in_lanes + rest_lanes + embed_lanes)
    sizes = [(part_rows, part_lanes) for _, _, part_rows, _, part_lanes, _ in chunks]
    wide = [item for item, chunk in zip(sizes, chunks) if chunk[0] == 0][0]
    tall = max(item for item, chunk in zip(sizes, chunks) if chunk[0] != 0)
    dma = pltpu.SemaphoreType.DMA
    heavy = [(width, 4 * width), (4 * width, width), (width, width), (3 * width, width)]
    shapes = [((in_lanes, width), low), ((far[1].shape[0], 5 * width), low)] + [
        ((rows, in_lanes), low),
        ((rows, head_lanes), low),
        ((rows, head_lanes), low),
        ((rows, embed_lanes), full),
        ((rows, embed_lanes), low),
        (few, full),
        ((rows, width), full),
        ((rows, width), low),
        ((rows, traits.shape[1]), full),
        ((1, 2 * width), full),
    ]
    pass_scratch = [
        ((tokens, width), full),
        ((tokens, width), full),
        ((tokens, width), full),
        ((tokens, 1), full),
        ((tokens, 1), full),
        ((tokens, width), low),
        ((tokens, 3 * width), low),
        ((tokens, width), low),
        ((tokens, width), full),
        ((tokens, width), low),
        ((tokens, 4 * width), low),
        ((tokens, width), full),
        ((tokens, width), low),
    ]
    scratch = [
        (few_half, full),
        (few_half, full),
        (few_half, full),
        ((2,) + few_half, full),
        ((lines,) + few_half, full),
        (modul_shape, full),
        (fmod_shape, full),
        (modul_shape, full),
        (fmod_shape, full),
        ((group, in_lanes + head_lanes), full),
        ((group, width), full),
        ((shards, group, width), full),
        ((group, width), full),
        ((shards, group, width), full),
        (pair, full),
        (pair, full),
        ((lines, 2 * group, in_lanes), low),
        ((lines, 2 * group, rest_lanes), low),
        ((lines, 2 * group, embed_lanes), full),
    ]
    gather_scratch = [
        ((rows, embed_lanes), full),
        (modul_shape, full),
        (fmod_shape, full),
        ((PATCH, width), low),
        ((PATCH, width), low),
        ((shards, rows, embed_lanes), low),
        ((shards, rows, embed_lanes), full),
        ((shards, PATCH, embed_lanes), low),
        ((shards, rows, head_lanes), full),
        ((rows, head_lanes), full),
        ((shards, group, in_lanes), full),
        ((group, in_lanes), full),
        ((shards, group, head_lanes), full),
        ((group, head_lanes), full),
        ((PATCH, width), low),
        ((shards,) + traits.shape, full),
        (traits.shape, full),
        (traits.shape, full),
        ((lines, 2 * group, traits.shape[1]), full),
    ]
    vmem, anywhere = pl.BlockSpec(memory_space=pltpu.VMEM), pl.BlockSpec(memory_space=pl.ANY)
    return pl.pallas_call(
        functools.partial(step_kernel, lines, chunks, tables, in_cols),
        out_shape=[jax.ShapeDtypeStruct(*item) for item in shapes],
        in_specs=[anywhere] * len(far) + [vmem] * len(light),
        out_specs=[anywhere] * 2 + [vmem] * (len(shapes) - 2),
        scratch_shapes=[pltpu.VMEM(item, low) for item in heavy]
        + [pltpu.VMEM((r, c), low) for r, c in sizes]
        + [pltpu.VMEM((r // 2, c), low) for r, c in sizes]
        + [pltpu.VMEM((r // 4, c), low) for r, c in sizes]
        + [pltpu.VMEM((lines - 1, r // 4 // PIECES, c), low) for r, c in sizes]
        + [
            dma((count, 8)),
            dma((count, 8)),
            dma((count, PIECES)),
            dma((count, lines - 1)),
            dma((count, 2, lines - 1)),
            dma((count, 2, PIECES)),
        ]
        + [pltpu.VMEM((SLOTS,) + item, low) for item in (wide, tall)] * 2
        + [pltpu.SemaphoreType.REGULAR, pltpu.SemaphoreType.REGULAR, dma((9,)), dma((5,))]
        + [pltpu.VMEM(*item) for item in ((modul_shape, full), (fmod_shape, full), (few, full))]
        + [pltpu.VMEM(*item) for item in pass_scratch]
        + [pltpu.VMEM(*item) for item in scratch]
        + [
            dma((lines + 6,)),
            dma((lines + 6,)),
            dma((4, shards - 1)),
            dma((4, shards - 1)),
            dma((3, lines - 1)),
            dma((3, lines - 1)),
        ]
        + [pltpu.VMEM(*item) for item in gather_scratch]
        + [dma((most,)), dma((most,))]
        + [dma((most, 2))] * 4
        + [dma((most, 4))] * 2
        + [dma((most,)), dma((most,)), dma((8, shards - 1)), dma((8, shards - 1)), dma((most,)), dma((lines,)), dma((lines,))],
        compiler_params=pltpu.CompilerParams(
            collective_id=1, has_side_effects=True, vmem_limit_bytes=64 * 1024 * 1024 - 65536
        ),
    )(*far, *light)


def placed_traits(traits, lanes):
    lead = -(-(PATCH + FREQ) // 128) * 128
    lane = lax.broadcasted_iota(jnp.int32, (traits.shape[0], lead), 1)
    here = jnp.logical_and(lane >= PATCH, lane < PATCH + FREQ)
    freq = jnp.where(here, traits[:, :lead], 0.0).astype(jnp.bfloat16)
    named = lax.broadcasted_iota(jnp.int32, (traits.shape[0], lanes), 1).astype(jnp.float32)
    onehot = jnp.where(named == traits[:, lead : lead + 1], 1.0, 0.0).astype(jnp.bfloat16)
    return freq, onehot


def windows(cols, shards):
    starts = [place * cols // 128 for place in range(shards)]
    tiles = max(-(-(place + 1) * cols // 128) - start for place, start in enumerate(starts))
    return starts, tiles


def heavy_segments(width, in_cols, in_starts, out_rows, shards):
    every = []
    for place in range(shards):
        parts = []
        for array, low, high, most in ((3, 6 * width, 9 * width, 640), (1, 9 * width, 13 * width, 640)):
            first, last = max(low, place * in_cols), min(high, (place + 1) * in_cols)
            while first < last:
                rows = min(most, last - first)
                parts.append((0, first - in_starts[place] * 128, array, first - low, rows, 0, 0, width))
                first += rows
            if array == 3:
                parts.append((1, 0, 2, place * out_rows, out_rows, 0, 0, width))
        parts.append((1, 0, 0, place * out_rows, out_rows, width, 0, 4 * width))
        every.append(parts)
    return every


def gather_steps(
    plan, remote, line_peer, in_blocks, far_copy,
    out_t, in_t, head_t, embed, traits,
    fc2, fc1, attn_out, qkv, cond_full, time_act, time_one, modul, fmod, patch, last, all_traits,
    s1_slot, tab_slot, patch_slot, two_slot, two_own, mod_slot, mod_own, fm_slot, fm_own, last_own,
    trait_slot, trait_own, trait_got, line_slot,
    ysend, yrecv, xsend, xrecv, zsend, zrecv, csend, crecv, osend, orecv, small_send, small_recv, local_sem,
    trait_send, trait_recv,
):
    segments, (in_starts, in_tiles), (head_starts, head_tiles), (embed_starts, embed_tiles), lines = plan
    shards = len(segments)
    arrays = (fc2, fc1, attn_out, qkv)
    sources = (in_t, out_t)
    rep, shard = lax.axis_index("rep"), lax.axis_index("shard")
    place_here = lax.rem(rep, 2 * lines)
    x, z = lax.rem(place_here, 2), lax.div(place_here, 2)
    zb = lax.rem(z, 2)
    core, y = lax.rem(shard, 2), lax.div(shard, 2)
    to_core = (rep, shard + 1 - 2 * core)
    to_y = (rep, shard + 2 - 4 * y)
    to_x = (rep + 1 - 2 * x, shard)
    to_z = (rep + 2 - 4 * zb, shard)
    width = head_t.shape[1]
    others = [(rep, lax.rem(shard + step, shards)) for step in range(1, shards)]
    mod_places = [o for o in range(shards) if in_starts[o] * 128 < 6 * width]
    computes_mod = functools.reduce(jnp.logical_or, [shard == o for o in mod_places])

    @pl.when(computes_mod)
    def _():
        for k in range(len(in_blocks)):
            far_copy(k).start()

    def small(kind, source, slots, step):
        return remote(
            source, slots.at[shard], small_send.at[kind, step - 1], small_recv.at[kind, step - 1], others[step - 1]
        )

    def small_arrival(kind, slots, step):
        origin = lax.rem(shard + shards - step, shards)
        return remote(
            slots.at[origin], slots.at[origin], small_send.at[kind, step - 1], small_recv.at[kind, step - 1], to_core
        )

    def exchange(kind, source, slots, origins=None):
        for step in range(1, shards):
            if origins is None:
                small(kind, source, slots, step).start()
            else:
                sends = functools.reduce(jnp.logical_or, [shard == o for o in origins])

                @pl.when(sends)
                def _():
                    small(kind, source, slots, step).start()

    def arrive(kind, slots, origins=None):
        for step in range(1, shards):
            if origins is None:
                small_arrival(kind, slots, step).wait_recv()
            else:
                origin = lax.rem(shard + shards - step, shards)

                @pl.when(functools.reduce(jnp.logical_or, [origin == o for o in origins]))
                def _():
                    small_arrival(kind, slots, step).wait_recv()

    def sent(kind, source, slots, origins=None):
        for step in range(1, shards):
            if origins is None:
                small(kind, source, slots, step).wait_send()
            else:

                @pl.when(functools.reduce(jnp.logical_or, [shard == o for o in origins]))
                def _():
                    small(kind, source, slots, step).wait_send()

    def place_tiles(target, slots, starts, tiles, origins, dtype, first=0):
        total = target.shape[1] // 128
        for tile in range(total):
            parts = [
                slots[o, :, (tile + first - starts[o]) * 128 : (tile + first - starts[o] + 1) * 128]
                for o in origins
                if 0 <= tile + first - starts[o] < tiles
            ]
            target[:, tile * 128 : (tile + 1) * 128] = functools.reduce(jnp.add, parts).astype(dtype)

    def source_part(place, k):
        source, row, array, _, rows, lane, _, lanes = segments[place][k]
        return sources[source].at[pl.ds(row, rows), pl.ds(lane, lanes)]

    def target_part(place, k, start=0, rows=None):
        _, _, array, row, total, _, lane, lanes = segments[place][k]
        start = row + start
        if not isinstance(start, int):
            start = pl.multiple_of(start, 16)
        return arrays[array].at[pl.ds(start, total if rows is None else rows), pl.ds(lane, lanes)]

    def quarter(place, k, index):
        size = segments[place][k][4] // 4
        return target_part(place, k, index * size, size)

    def half_of(place, k, index, second):
        size = segments[place][k][4] // 4
        cut = -(-size // 32) * 16
        return target_part(place, k, index * size + (cut if second else 0), size - cut if second else cut)

    me = x * 2 + zb
    across_x, along_z, corner = (1 - x) * 2 + zb, x * 2 + 1 - zb, (1 - x) * 2 + 1 - zb

    def y_copy(place, k):
        size = segments[place][k][4] // 4
        source, row, _, _, _, lane, _, lanes = segments[place][k]
        part = sources[source].at[pl.ds(pl.multiple_of(row + me * size, 16), size), pl.ds(lane, lanes)]
        return remote(part, quarter(place, k, me), ysend.at[k], yrecv.at[k], to_y)

    def owner_copy(place, k):
        return remote(source_part(place, k), target_part(place, k), osend.at[k], orecv.at[k], to_core)

    def own_copy(place, k):
        return pltpu.make_async_copy(source_part(place, k), target_part(place, k), local_sem.at[k])

    def hop(part, sems, k, slot, peer):
        return remote(part, part, sems[0].at[k, slot], sems[1].at[k, slot], peer)

    xs, zs, cs = (xsend, xrecv), (zsend, zrecv), (csend, crecv)

    def begin(k, across):
        for place in range(shards):
            if k < len(segments[place]):

                @pl.when(shard == place)
                def _():
                    if across:
                        y_copy(place, k).start()
                    else:
                        owner_copy(place, k).start()
                        own_copy(place, k).start()

    def relay(place, stage, k):
        if stage == 0:
            y_copy(place, k).wait_recv()
            hop(quarter(place, k, me), xs, k, 0, to_x).start()
            hop(quarter(place, k, me), zs, k, 0, to_z).start()
            hop(quarter(place, k, me), cs, k, 0, to_core).start()
        elif stage == 1:
            hop(quarter(place, k, across_x), xs, k, 0, to_x).wait_recv()
            hop(half_of(place, k, across_x, False), zs, k, 1, to_z).start()
            hop(quarter(place, k, along_z), zs, k, 0, to_z).wait_recv()
            hop(half_of(place, k, along_z, True), xs, k, 1, to_x).start()
            hop(quarter(place, k, across_x), cs, k, 1, to_core).start()
            hop(quarter(place, k, along_z), cs, k, 2, to_core).start()
        else:
            hop(half_of(place, k, corner, False), zs, k, 1, to_z).wait_recv()
            hop(half_of(place, k, corner, True), xs, k, 1, to_x).wait_recv()
            hop(quarter(place, k, corner), cs, k, 3, to_core).start()

    def relay_tick(tick):
        for place in range(shards):

            @pl.when(to_y[1] == place)
            def _():
                for stage in range(3):
                    if 0 <= tick - stage < len(segments[place]):
                        relay(place, stage, tick - stage)

    def trait_line(step):
        return remote(
            line_slot.at[z], line_slot.at[z], trait_send.at[step], trait_recv.at[step], line_peer(step)
        )

    def trait_line_arrival(step):
        origin = lax.rem(z + lines - step, lines)
        return remote(line_slot.at[origin], line_slot.at[origin], trait_send.at[step], trait_recv.at[step], to_core)

    trait_pair = remote(trait_own, trait_got, trait_send.at[0], trait_recv.at[0], to_x)
    trait_slot[shard] = traits[...]
    exchange(7, traits, trait_slot)
    begin(0, True)
    arrive(7, trait_slot)
    trait_own[...] = functools.reduce(jnp.add, [trait_slot[o] for o in range(shards)])
    trait_pair.start()
    begin(1, True)
    trait_pair.wait_recv()
    own, got = trait_own[...], trait_got[...]
    line_slot[z] = jnp.concatenate([jnp.where(x == 0, own, got), jnp.where(x == 0, got, own)], 0)
    for step in range(1, lines):
        trait_line(step).start()
    relay_tick(0)
    begin(2, True)
    for step in range(1, lines):
        trait_line_arrival(step).wait_recv()
    count_in_line = 2 * traits.shape[0]
    for at in range(lines):
        all_traits[at * count_in_line : (at + 1) * count_in_line, :] = line_slot[at]
    freq, onehot = placed_traits(all_traits[...], embed.shape[1])

    nt = (((1,), (1,)), ((), ()))
    own_one = lax.dot_general(freq, embed[:, : freq.shape[1]], nt, preferred_element_type=jnp.float32)
    time_one[...] = own_one
    s1_slot[shard] = (own_one * jax.nn.sigmoid(own_one)).astype(jnp.bfloat16)
    tab_slot[shard] = lax.dot_general(onehot, embed[...], nt, preferred_element_type=jnp.float32)
    eye = lax.broadcasted_iota(jnp.int32, (PATCH, 128), 0) == lax.broadcasted_iota(jnp.int32, (PATCH, 128), 1)
    eye = jnp.where(eye, 1.0, 0.0).astype(jnp.bfloat16)
    patch_slot[shard] = lax.dot_general(eye, embed[:, :128], nt, preferred_element_type=jnp.float32).astype(jnp.bfloat16)
    exchange(0, s1_slot.at[shard], s1_slot)
    exchange(1, tab_slot.at[shard], tab_slot)
    exchange(2, patch_slot.at[shard], patch_slot)
    relay_tick(1)
    begin(3, True)
    last_place = [o for o in range(shards) if 0 <= 3 * width // 128 - head_starts[o] < head_tiles][-1]
    last_row = (3 * width // 128 - head_starts[last_place]) * 128
    last_own[...] = head_t[last_row : last_row + 16, :]

    @pl.when(shard == last_place)
    def _():
        last[...] = last_own[...]
        for step in range(1, shards):
            remote(last_own, last, small_send.at[6, step - 1], small_recv.at[6, 0], others[step - 1]).start()

    head_places = [o for o in range(shards) if head_starts[o] * 128 < width]
    fm_places = [o for o in range(shards) if (head_starts[o] + head_tiles) * 128 > width]
    group = modul.shape[0]

    arrive(0, s1_slot)
    place_tiles(time_act, s1_slot, embed_starts, embed_tiles, range(shards), jnp.bfloat16)
    two_own[...] = lax.dot_general(time_act[...], head_t[...], nt, preferred_element_type=jnp.float32)
    two_slot[shard] = two_own[...]
    exchange(3, two_own, two_slot, head_places)
    relay_tick(2)
    begin(4, True)
    arrive(1, tab_slot)
    arrive(3, two_slot, head_places)
    place_tiles(cond_full, tab_slot, embed_starts, embed_tiles, range(shards), jnp.float32)
    for tile in range(width // 128):
        span = slice(tile * 128, (tile + 1) * 128)
        for o in head_places:
            if 0 <= tile - head_starts[o] < head_tiles:
                cond_full[:, span] += two_slot[o, :, (tile - head_starts[o]) * 128 : (tile - head_starts[o] + 1) * 128]
    mine = cond_full[pl.ds(pl.multiple_of(place_here * group, 8), group), :]
    cond = (mine * jax.nn.sigmoid(mine)).astype(jnp.bfloat16)

    @pl.when(computes_mod)
    def _():
        for k, block in enumerate(in_blocks):
            far_copy(k).wait()
            span = slice(k * block.shape[0], (k + 1) * block.shape[0])
            mod_own[:, span] = lax.dot_general(cond, block[...], nt, preferred_element_type=jnp.float32)
        mod_slot[shard] = mod_own[...]

    exchange(4, mod_own, mod_slot, mod_places)
    fm_own[...] = lax.dot_general(cond, head_t[...], nt, preferred_element_type=jnp.float32)
    fm_slot[shard] = fm_own[...]
    exchange(5, fm_own, fm_slot, fm_places)
    relay_tick(3)
    begin(5, True)
    begin(0, False)
    begin(1, False)
    begin(2, False)
    begin(3, False)
    begin(4, False)
    begin(5, False)
    arrive(2, patch_slot)
    place_tiles(patch, patch_slot, embed_starts, embed_tiles, range(shards), jnp.bfloat16)
    arrive(4, mod_slot, mod_places)
    arrive(5, fm_slot, fm_places)
    place_tiles(modul, mod_slot, in_starts, in_tiles, mod_places, jnp.float32)
    place_tiles(fmod, fm_slot, head_starts, head_tiles, fm_places, jnp.float32, width // 128)

    @pl.when(shard != last_place)
    def _():
        remote(last_own, last, small_send.at[6, 0], small_recv.at[6, 0], to_core).wait_recv()

    def arrived(array):
        for place in range(shards):
            of_array = [k for k, part in enumerate(segments[place]) if part[2] == array]

            @pl.when(shard == place)
            def _():
                for k in of_array:
                    own_copy(place, k).wait()

            @pl.when(to_core[1] == place)
            def _():
                for k in of_array:
                    remote(target_part(place, k), target_part(place, k), osend.at[k], orecv.at[k], to_core).wait_recv()

            @pl.when(shards - 1 - shard == place)
            def _():
                for k in of_array:
                    for slot, index in enumerate((me, across_x, along_z, corner)):
                        part = quarter(place, k, index)
                        remote(part, part, csend.at[k, slot], crecv.at[k, slot], to_core).wait_recv()

    def finish():
        for place in range(shards):
            count = len(segments[place])

            @pl.when(shard == place)
            def _():
                for k in range(count):
                    y_copy(place, k).wait_send()
                    owner_copy(place, k).wait_send()

            @pl.when(to_y[1] == place)
            def _():
                for k in range(count):
                    hop(quarter(place, k, me), xs, k, 0, to_x).wait_send()
                    hop(quarter(place, k, me), zs, k, 0, to_z).wait_send()
                    hop(half_of(place, k, across_x, False), zs, k, 1, to_z).wait_send()
                    hop(half_of(place, k, along_z, True), xs, k, 1, to_x).wait_send()
                    for slot, index in enumerate((me, across_x, along_z, corner)):
                        hop(quarter(place, k, index), cs, k, slot, to_core).wait_send()

        trait_pair.wait_send()
        for step in range(1, lines):
            trait_line(step).wait_send()
        sent(7, traits, trait_slot)
        sent(0, s1_slot.at[shard], s1_slot)
        sent(1, tab_slot.at[shard], tab_slot)
        sent(2, patch_slot.at[shard], patch_slot)
        sent(3, two_own, two_slot, head_places)
        sent(4, mod_own, mod_slot, mod_places)
        sent(5, fm_own, fm_slot, fm_places)

        @pl.when(shard == last_place)
        def _():
            for step in range(1, shards):
                remote(last_own, last, small_send.at[6, step - 1], small_recv.at[6, 0], others[step - 1]).wait_send()

    return relay_tick, arrived, finish


def windowed(in_t, out_t, head_t, embed_t, shards):
    place = lax.axis_index("shard")
    width = head_t.shape[1]
    low = jnp.bfloat16

    def window(item_t, starts, tiles, lanes):
        rows = item_t.shape[0]
        most = max(o * rows - start * 128 for o, start in enumerate(starts))
        padded = jnp.pad(item_t, ((most, tiles * 128 - rows), (0, lanes - item_t.shape[1])))
        begin = most - lax.rem(place * rows, 128)
        return lax.dynamic_slice_in_dim(padded, begin, tiles * 128, 0).astype(low)

    in_cols, head_cols, embed_cols = in_t.shape[0], head_t.shape[0], embed_t.shape[0]
    in_starts, in_tiles = windows(in_cols, shards)
    head_starts, head_tiles = windows(head_cols, shards)
    embed_starts, embed_tiles = windows(embed_cols, shards)
    in_t = window(in_t, in_starts, in_tiles, width)
    head_t = window(head_t, head_starts, head_tiles, width)
    embed = window(embed_t, embed_starts, embed_tiles, -(-embed_t.shape[1] // 128) * 128)
    return in_t, out_t.astype(low), head_t, embed


def own_segments(width, in_cols, in_starts, out_rows, shards):
    every = []
    for place in range(shards):
        parts = []
        for array, low, high in ((3, 6 * width, 9 * width), (1, 9 * width, 13 * width)):
            first, last = max(low, place * in_cols), min(high, (place + 1) * in_cols)
            if first < last:
                parts.append((array, first - low, last - first, first - in_starts[place] * 128))
        every.append(parts)
    return every


def total_kernel(
    tables, segments, far_t, far_out, w_in, w_out, w_head, w_embed,
    d_in, d_fin, d_two, d_one, d_full, few, cond_full, time_act, traits, weight_sq, c_in, c_out, c_head, c_embed,
    g_in, g_out, g_head, g_embed, n_in, n_out, n_head, n_embed, stats, loss,
    own_t, own_out, grad_t, head_t, head_fresh, t_out, t_head, t_embed, v_head, v_embed,
    load, write, fetch,
):
    (in_starts, in_tiles), (head_starts, head_tiles), (embed_starts, embed_tiles), shards = tables
    shard = lax.axis_index("shard")
    width = cond_full.shape[1]
    in_cols, head_cols, embed_cols, out_cols = (item.shape[0] for item in (w_in, w_head, w_embed, w_out))
    full, low = jnp.float32, jnp.bfloat16
    span = lane_span(width, w_embed.shape[1])

    reads = [pltpu.make_async_copy(w_head, v_head, load.at[0]), pltpu.make_async_copy(w_embed, v_embed, load.at[1])]
    for copy in reads:
        copy.start()

    def heavy_copies(place):
        copies = [
            pltpu.make_async_copy(far_t.at[pl.ds(at, rows), :], own_t.at[pl.ds(at, rows), :], fetch.at[k])
            for k, (_, _, rows, at) in enumerate(segments[place])
        ]
        return copies + [pltpu.make_async_copy(far_out, own_out, fetch.at[2])]

    for place in range(shards):

        @pl.when(shard == place)
        def _():
            for copy in heavy_copies(place):
                copy.start()
            edges = [0]
            for _, _, rows, at in segments[place]:
                edges += [at, at + rows]
            edges.append(in_tiles * 128)
            for start, stop in zip(edges[0::2], edges[1::2]):
                if start < stop:
                    own_t[start:stop, :] = jnp.zeros((stop - start, width), low)

    def decayed(state, total, count):
        return decay * state + (1.0 - decay) * (total / count + eps_one)

    def to_lanes(column):
        return jnp.broadcast_to(column, (column.shape[0], 128)).T[:1, :]

    def to_column(lanes):
        return jnp.broadcast_to(lanes, (128, lanes.shape[1])).T[:, :1]

    def squares_of(value, state, fresh_out, start, size):
        square = value * value
        sums = to_lanes(jnp.sum(square, -1, keepdims=True))[:, :size]
        fresh = decayed(state[:, start : start + size], sums, value.shape[1])
        fresh_out[:, start : start + size] = fresh
        inverse = 1.0 / fresh
        if size < value.shape[0]:
            inverse = jnp.concatenate([inverse, jnp.zeros((1, value.shape[0] - size), full)], 1)
        return jnp.sum(square, 0, keepdims=True), jnp.sum(square * to_column(inverse), 0, keepdims=True)

    def put(start, plain, scaled):
        stats[:, start : start + plain.shape[1]] = plain
        stats[:, span + start : span + start + plain.shape[1]] = scaled

    def column_blocks(total):
        return [(start, min(128, total - start)) for start in range(0, total, 128)]

    def by_blocks(take, total, state, fresh_out, place):
        plain, scaled = jnp.zeros((1, width), full), jnp.zeros((1, width), full)
        for start, size in column_blocks(total):
            value = take(start, size)
            if size < 128:
                value = jnp.concatenate([value, jnp.zeros((128 - size, width), full)], 0)
            more, more_scaled = squares_of(value, state, fresh_out, start, size)
            plain, scaled = plain + more, scaled + more_scaled
        put(place, plain, scaled)

    cond = cond_full[...]
    cond = (cond * jax.nn.sigmoid(cond)).astype(low)

    lanes_all = -(-w_embed.shape[1] // 128) * 128
    freq, onehot = placed_traits(traits[...], lanes_all)
    square_one = lax.broadcasted_iota(jnp.int32, (PATCH, lanes_all), 0)
    eye = jnp.where(square_one == lax.broadcasted_iota(jnp.int32, (PATCH, lanes_all), 1), 1.0, 0.0).astype(low)

    def exact(value, picks):
        total = None
        for _ in range(3):
            part = value.astype(low)
            value = value - part.astype(full)
            term = mxu(part, picks, TN)
            total = term if total is None else total + term
        return total

    for place in range(shards):

        @pl.when(shard == place)
        def _():
            lead = place * embed_cols - embed_starts[place] * 128
            lanes = slice(embed_starts[place] * 128, (embed_starts[place] + embed_tiles) * 128)
            value = exact(d_full[...], onehot) + exact(few[0:PATCH, lanes], eye)
            value = value[lead : lead + embed_cols, :]
            time = mxu(d_one[...], freq, TN)[lead : lead + embed_cols, :]
            t_embed[:, : freq.shape[1]] = value[:, : freq.shape[1]] + time
            t_embed[:, freq.shape[1] :] = value[:, freq.shape[1] : w_embed.shape[1]]

    pltpu.make_async_copy(t_embed, g_embed, write.at[3]).start()
    value = jnp.concatenate([t_embed[...], jnp.zeros((embed_cols, lanes_all - w_embed.shape[1]), full)], 1)
    square = value * value
    fresh = decayed(c_embed[...].reshape(1, embed_cols), to_lanes(jnp.sum(square, -1, keepdims=True)), w_embed.shape[1])
    n_embed[...] = fresh.reshape(n_embed.shape)
    put(7 * width, jnp.sum(square, 0, keepdims=True), jnp.sum(square * to_column(1.0 / fresh), 0, keepdims=True))

    loss[0, 0] = few[PATCH : PATCH + 1, 0:1][0, 0]

    head_t[...] = mxu(d_two[...], time_act[...], TN) + mxu(d_fin[...], cond, TN)
    last_place = [o for o in range(shards) if 0 <= 3 * width // 128 - head_starts[o] < head_tiles][-1]
    last_row = (3 * width // 128 - head_starts[last_place]) * 128

    @pl.when(shard == last_place)
    def _():
        head_t[last_row : last_row + PATCH, :] = few[PATCH + 8 : 2 * PATCH + 8, :]

    for place in range(shards):

        @pl.when(shard == place)
        def _():
            lead = place * head_cols - head_starts[place] * 128
            t_head[...] = head_t[lead : lead + head_cols, :]

    pltpu.make_async_copy(t_head, g_head, write.at[2]).start()
    head_state = c_head[...].reshape(1, head_cols)
    by_blocks(lambda start, size: t_head[start : start + size, :], head_cols, head_state, head_fresh, 6 * width)
    n_head[...] = head_fresh[...].reshape(n_head.shape)

    for place in range(shards):

        @pl.when(shard == place)
        def _():
            for copy in heavy_copies(place):
                copy.wait()

    def light(index, carry):
        part = pl.ds(pl.multiple_of(index * 128, 128), 128)
        grad_t[part, :] = mxu(d_in[:, part], cond, TN) + own_t[part, :].astype(full)
        return carry

    lax.fori_loop(0, in_tiles, light, 0)
    lead = lax.rem(shard * in_cols, 128)
    write_in = pltpu.make_async_copy(grad_t.at[pl.ds(pl.multiple_of(lead, 64), in_cols), :], g_in, write.at[0])
    write_in.start()
    by_blocks(
        lambda start, size: grad_t[pl.ds(pl.multiple_of(lead + start, 64), size), :], in_cols, c_in, n_in, 0
    )

    sums = jnp.zeros((out_cols, 1), full)
    for index in range(5):
        value = own_out[:, index * width : (index + 1) * width].astype(full)
        t_out[:, index * width : (index + 1) * width] = value
        sums += jnp.sum(value * value, -1, keepdims=True)
    pltpu.make_async_copy(t_out, g_out, write.at[1]).start()
    fresh = decayed(c_out[...], to_lanes(sums), 5 * width)
    n_out[...] = fresh
    column = to_column(1.0 / fresh)
    for index in range(5):
        value = t_out[:, index * width : (index + 1) * width]
        square = value * value
        put(width + index * width, jnp.sum(square, 0, keepdims=True), jnp.sum(square * column, 0, keepdims=True))

    for copy in reads:
        copy.wait()
    squares = [weight_sq[:, k * width : (k + 1) * width] for k in (0, 1)]
    squares += [jnp.sum(value[...] * value[...], 0, keepdims=True) for value in (v_head, v_embed)]
    for k, total in enumerate(squares):
        start = 2 * span + k * 128
        stats[:, start : start + 128] = jnp.broadcast_to(jnp.sum(total, -1, keepdims=True) / 128.0, (1, 128))
    write_in.wait()
    for k, (source, target) in enumerate(((t_out, g_out), (t_head, g_head), (t_embed, g_embed))):
        pltpu.make_async_copy(source, target, write.at[k + 1]).wait()


def lane_span(width, embed_rows):
    return 7 * width + -(-embed_rows // 128) * 128


def total_call(tables, heavy, weights, light, cols):
    (in_starts, in_tiles), (_, head_tiles), _, shards = tables
    low, full = jnp.bfloat16, jnp.float32
    width = heavy[0].shape[1]
    w_in, w_out, w_head, w_embed = weights
    lanes = 2 * lane_span(width, w_embed.shape[1]) + 4 * 128
    segments = own_segments(width, w_in.shape[0], in_starts, w_out.shape[0], shards)
    shapes = [(item.shape, full) for item in weights] + [(item.shape, full) for item in cols] + [((1, lanes), full), ((1, 1), full)]
    anywhere, vmem = pl.BlockSpec(memory_space=pl.ANY), pl.BlockSpec(memory_space=pltpu.VMEM)
    scratch = [
        ((in_tiles * 128, width), low),
        (w_out.shape, low),
        ((in_tiles * 128, width), full),
        ((head_tiles * 128, width), full),
        ((1, w_head.shape[0]), full),
    ]
    scratch += [(item.shape, full) for item in weights[1:]] + [(item.shape, full) for item in weights[2:]]
    return pl.pallas_call(
        functools.partial(total_kernel, tables, segments),
        out_shape=[jax.ShapeDtypeStruct(*item) for item in shapes],
        in_specs=[anywhere] * 6 + [vmem] * (len(light) + 4),
        out_specs=[anywhere] * 4 + [vmem] * 5 + [pl.BlockSpec(memory_space=pltpu.SMEM)],
        scratch_shapes=[pltpu.VMEM(*item) for item in scratch] + [pltpu.SemaphoreType.DMA((4,))] * 3,
        compiler_params=pltpu.CompilerParams(vmem_limit_bytes=60 * 1024 * 1024),
    )(*heavy, *weights, *light, *cols)


def finish_kernel(shards, sizes, own, r_in, r_out, r_head, r_embed, n_in, n_out, n_head, n_embed, s_in, s_out, s_head, s_embed, rms, slots, send, recv):
    rep, shard = lax.axis_index("rep"), lax.axis_index("shard")
    barrier = pltpu.get_barrier_semaphore()
    for step in range(1, shards):
        peer = (rep, lax.rem(shard + step, shards))
        pl.semaphore_signal(barrier, inc=1, device_id=peer, device_id_type=MESH)
    pl.semaphore_wait(barrier, shards - 1)

    def copy(step):
        return pltpu.make_async_remote_copy(
            src_ref=own,
            dst_ref=slots.at[shard],
            send_sem=send.at[step - 1],
            recv_sem=recv.at[step - 1],
            device_id=(rep, lax.rem(shard + step, shards)),
            device_id_type=MESH,
        )

    for step in range(1, shards):
        copy(step).start()
    slots[shard] = own[...]
    for step in range(1, shards):
        copy(step).wait()
    total = functools.reduce(jnp.add, [slots[o] for o in range(shards)])
    states, fresh, scales = (r_in, r_out, r_head, r_embed), (n_in, n_out, n_head, n_embed), (s_in, s_out, s_head, s_embed)
    starts, start = [], 0
    for rows, _ in sizes:
        starts.append(start)
        start += -(-rows // 128) * 128
    update, means, news = jnp.zeros((1, 1), jnp.float32), [], []
    for k, (rows, cols) in enumerate(sizes):
        row = decay * states[k][...].reshape(1, rows) + (1.0 - decay) * (
            total[:, starts[k] : starts[k] + rows] / cols + eps_one
        )
        fresh[k][...] = row.reshape(fresh[k].shape)
        news.append(row)
        mean = jnp.mean(row, -1, keepdims=True)
        means.append(mean)
        update += mean * jnp.sum(total[:, start + starts[k] : start + starts[k] + rows] / row, -1, keepdims=True)
    update = jnp.sqrt(update / sum(rows * cols for rows, cols in sizes))
    rms[0, 0] = update[0, 0]
    factor = jnp.maximum(1.0, update / clip_level)
    for k, (rows, cols) in enumerate(sizes):
        first = 2 * start + k * 128
        weight = jnp.sqrt(jnp.sum(total[:, first : first + 128], -1, keepdims=True) / (rows * cols))
        scales[k][...] = rate * jnp.maximum(eps_two, weight) / factor * lax.rsqrt(news[k] / means[k])


def finish_call(shards, sizes, stats, rows_old):
    full = jnp.float32
    shapes = [(item.shape, full) for item in rows_old] + [((1, rows), full) for rows, _ in sizes] + [((1, 1), full)]
    return pl.pallas_call(
        functools.partial(finish_kernel, shards, sizes),
        out_shape=[jax.ShapeDtypeStruct(*item) for item in shapes],
        in_specs=[pl.BlockSpec(memory_space=pltpu.VMEM)] * 5,
        out_specs=[pl.BlockSpec(memory_space=pltpu.VMEM)] * (len(shapes) - 1) + [pl.BlockSpec(memory_space=pltpu.SMEM)],
        scratch_shapes=[
            pltpu.VMEM((shards,) + stats.shape, full),
            pltpu.SemaphoreType.DMA((shards - 1,)),
            pltpu.SemaphoreType.DMA((shards - 1,)),
        ],
        compiler_params=pltpu.CompilerParams(collective_id=3, has_side_effects=True),
    )(stats, *rows_old)


def on_device(
    latents,
    noises,
    velocity,
    times,
    labels,
    dropped,
    blocks_in,
    blocks_out,
    head_side,
    embed_side,
    state_in_row,
    state_in_col,
    state_out_row,
    state_out_col,
    state_head_row,
    state_head_col,
    state_embed_row,
    state_embed_col,
):
    images = latents.shape[0]
    width = head_side.shape[0]
    shard_count = lax.axis_size("shard")
    place = lax.axis_index("shard")
    in_cols = blocks_in.shape[2]
    head_cols = head_side.shape[1]
    embed_cols = embed_side.shape[1]
    group = images * shard_count
    weights = (blocks_in[0].T, blocks_out[0].T, head_side.T, embed_side.T)
    t_value = (times.astype(jnp.float32) + 1.0) / step_count
    classes = (PATCH + FREQ + jnp.where(dropped == 1, CLASSES - 1, labels)).astype(jnp.float32)
    lines = LINE
    lead = -(-(PATCH + FREQ) // 128) * 128
    own_traits = jnp.concatenate(
        [
            jnp.zeros((images, PATCH), jnp.float32),
            time_freq(t_value, FREQ),
            jnp.zeros((images, lead - PATCH - FREQ), jnp.float32),
            jnp.broadcast_to(classes[:, None], (images, 128)),
        ],
        1,
    )
    traits = lax.dynamic_update_slice(
        jnp.zeros((group, lead + 128), jnp.float32), own_traits, (place * images, 0)
    )
    in_t, out_t, head_t, embed = windowed(*weights, shard_count)
    tcol = t_value[:, None, None]
    state = (
        (1.0 - tcol) * latents.reshape(images, TOK, PATCH)
        + tcol * noises.reshape(images, TOK, PATCH)
    ).astype(jnp.bfloat16)
    tables = (
        windows(in_cols, shard_count),
        windows(head_cols, shard_count),
        windows(embed_cols, shard_count),
        shard_count,
    )
    sums = step_call(
        lines,
        tables,
        in_cols,
        [in_t, out_t] + list(weights[:2]),
        [
            state.reshape(images * TOK, PATCH),
            velocity.reshape(images * TOK, PATCH),
            jnp.repeat(t_value, TOK)[:, None],
            jnp.asarray(positions(GRID, width)),
            head_t,
            embed,
            traits,
        ],
    )
    d_in, d_fin, d_two, d_full, d_one, few_sum, cond_full, time_act, all_traits, weight_sq = sums[2:]
    rows_old = (state_in_row, state_out_row, state_head_row, state_embed_row)
    cols_old = (state_in_col, state_out_col, state_head_col, state_embed_col)
    *outs, stats, loss = total_call(
        tables,
        sums[:2],
        weights,
        [d_in, d_fin, d_two, d_one, d_full, few_sum, cond_full, time_act, all_traits, weight_sq],
        cols_old,
    )
    totals, cols_new = outs[:4], outs[4:]
    loss_sum = loss.reshape(())
    blocks = lax.axis_size("rep") // (2 * lines)
    if blocks > 1:
        apart = [[k * 2 * lines + j for k in range(blocks)] for j in range(2 * lines)]
        totals, loss_sum = lax.psum((totals, loss_sum), "rep", axis_index_groups=apart)
        cols_new, plain, scaled = [], [], []
        for gradient, col_state in zip(totals, cols_old):
            square = gradient * gradient
            fresh = decay * col_state + (1.0 - decay) * (jnp.mean(square, 1).reshape(col_state.shape) + eps_one)
            pad = (0, -gradient.shape[1] % 128)
            cols_new.append(fresh)
            plain.append(jnp.pad(jnp.sum(square, 0), pad))
            scaled.append(jnp.pad(jnp.sum(square / fresh.reshape(-1)[:, None], 0), pad))
        spans = sum(item.shape[0] for item in plain) * 2
        stats = jnp.concatenate(plain + scaled + [stats[0, spans:]])[None]
    sizes = [(weight.shape[1], weight.shape[0] * shard_count) for weight in weights]
    *outs, rms = finish_call(shard_count, sizes, stats, rows_old)
    rows_new, scales = outs[:4], outs[4:]
    update_rms = rms.reshape(())
    news = [
        (weight - gradient * scale * lax.rsqrt(col_next.reshape(-1))[:, None]).T
        for weight, gradient, scale, col_next in zip(weights, totals, scales, cols_new)
    ]
    return (
        loss_sum,
        update_rms,
        totals[0].T[None],
        totals[1].T[None],
        totals[2].T,
        totals[3].T,
        rows_new[0],
        cols_new[0],
        rows_new[1],
        cols_new[1],
        rows_new[2],
        cols_new[2],
        rows_new[3],
        cols_new[3],
        news[0][None],
        news[1][None],
        news[2],
        news[3],
    )


def solution(mesh):
    placed = (
        P(("rep", "shard"), None),
        P(("rep", "shard"), None),
        P(("rep", "shard"), None),
        P(("rep", "shard")),
        P(("rep", "shard")),
        P(("rep", "shard")),
        P(None, None, "shard"),
        P(None, None, "shard"),
        P(None, "shard"),
        P(None, "shard"),
        P(),
        P(None, "shard"),
        P(),
        P(None, "shard"),
        P(),
        P("shard"),
        P(),
        P("shard"),
    )
    return jax.shard_map(
        on_device,
        mesh=mesh,
        in_specs=placed,
        out_specs=(
            P(),
            P(),
            P(None, None, "shard"),
            P(None, None, "shard"),
            P(None, "shard"),
            P(None, "shard"),
            P(),
            P(None, "shard"),
            P(),
            P(None, "shard"),
            P(),
            P("shard"),
            P(),
            P("shard"),
            P(None, None, "shard"),
            P(None, None, "shard"),
            P(None, "shard"),
            P(None, "shard"),
        ),
        check_vma=False,
    )
```

```python
import functools
import math

import jax
import jax.numpy as jnp
import numpy as np
from jax import lax
from jax.experimental import pallas as pl
from jax.experimental.pallas import tpu as pltpu
from jax.sharding import PartitionSpec as P

HEADS = 12
CLASSES = 1001
FREQ = 256
GRID = 16
PATCH = 16
LAYERS = 1
TOK = 256


decay = 0.5
eps_norm = 1e-06
eps_one = 1e-30
eps_two = 0.001
clip_level = 0.1
rate = 8.0
step_count = 1000.0


def silu(value):
    return value * jax.nn.sigmoid(value)


def positions(grid, width):
    quarter = width // 4
    omega = (1.0 / 10000.0 ** (np.arange(quarter, dtype=np.float32) / quarter)).astype(np.float32)
    index = np.arange(grid * grid)
    row_pos = (index // grid).astype(np.float32)[:, None] * omega[None, :]
    col_pos = (index % grid).astype(np.float32)[:, None] * omega[None, :]
    return np.concatenate([np.sin(row_pos), np.cos(row_pos), np.sin(col_pos), np.cos(col_pos)], 1)


def time_freq(t_value, width):
    half = width // 2
    freqs = jnp.exp(-math.log(10000.0) * jnp.arange(half, dtype=jnp.float32) / half)
    angles = (t_value * step_count)[:, None] * freqs[None, :]
    return jnp.concatenate([jnp.cos(angles), jnp.sin(angles)], -1)


def weight_grad(left, back):
    flat_left = left.reshape(-1, left.shape[-1])
    flat_back = back.reshape(-1, back.shape[-1])
    return lax.dot_general(
        flat_left, flat_back, (((0,), (0,)), ((), ())), preferred_element_type=jnp.float32
    )


MESH = pl.DeviceIdType.MESH
LINE = 4
PIECES = 4
PARTS = (6, 6, 3)
ORDER = (
    (0, 0), (0, 1), (0, 2), (1, 0), (9, 0), (0, 3), (1, 1), (9, 1), (0, 4), (1, 2), (9, 2), (0, 5), (1, 3),
    (2, 0), (9, 3), (0, 6), (1, 4), (0, 7), (2, 1), (9, 4), (1, 5), (0, 8), (3, 0), (1, 6), (9, 5), (2, 2),
    (0, 9), (1, 7), (3, 1), (1, 8), (9, 6), (2, 3), (0, 10), (0, 11), (1, 9), (2, 4), (9, 7), (3, 2), (4, 0),
    (0, 12), (9, 8), (1, 10), (1, 11), (2, 5), (3, 3), (2, 6), (9, 9), (3, 4), (4, 1), (0, 13), (1, 12), (2, 7),
    (9, 10), (4, 2), (6, 0), (3, 5), (0, 14), (2, 8), (3, 6), (9, 11), (4, 3), (0, 15), (4, 4), (2, 9), (3, 7),
    (9, 12), (6, 1), (7, 0), (0, 16), (3, 8), (2, 10), (6, 2), (4, 5), (0, 17), (4, 6), (3, 9), (2, 11), (6, 3),
    (7, 1), (8, 0), (0, 18), (3, 10), (6, 4), (0, 19), (2, 12), (3, 11), (4, 7), (4, 8), (4, 9), (4, 10), (5, 6),
    (6, 5), (1, 13), (9, 13), (7, 2), (7, 3), (7, 4), (8, 1), (0, 20), (3, 12), (0, 21), (0, 22), (4, 11),
    (6, 6), (5, 7), (7, 5), (8, 2), (8, 3), (8, 4), (1, 14), (9, 14), (5, 8), (1, 15), (1, 16), (5, 9), (2, 13),
    (5, 10), (8, 5), (6, 7), (7, 6), (4, 12), (9, 15), (5, 11), (2, 14), (6, 8), (3, 13), (8, 6), (6, 9),
    (9, 16), (6, 10), (7, 7), (6, 12), (3, 14), (2, 15), (6, 11), (7, 8), (8, 7), (4, 13), (2, 16), (7, 9),
    (8, 8), (4, 14), (7, 10), (8, 9), (7, 12), (6, 13), (3, 15), (8, 10), (5, 14), (8, 12), (7, 11), (3, 16),
    (7, 13), (4, 15), (6, 14), (8, 11), (8, 13), (4, 16), (5, 15), (7, 14), (5, 16), (8, 14), (6, 15), (6, 16),
    (7, 15), (8, 15), (7, 16), (8, 16),
)
BESIDE_AT = (84, 95, 107, 119, 131, 143, 155)
SQUARES_AT = (106, 119, 133)
SLOTS = 3
NN = (((1,), (0,)), ((), ()))
NT = (((1,), (1,)), ((), ()))
TN = (((0,), (0,)), ((), ()))


def mxu(left, right, kind):
    return lax.dot_general(left, right, kind, preferred_element_type=jnp.float32)


def blocks_of(total, size, body):
    def step(index, carry):
        body(pl.ds(pl.multiple_of(index * size, size), size))
        return carry

    lax.fori_loop(0, total // size, step, 0)


def heavy_chunks(width):
    half = width // 2
    fc2, fc1, kv = PARTS
    parts = [(0, 0, width, 4 * width // fc2 * k, 2 * width // fc2, False) for k in range(fc2)]
    parts += [(1, 4 * width // fc1 * k, 4 * width // fc1, 0, half, True) for k in range(fc1)]
    parts += [(2, 0, width, 0, half, False), (3, 0, width, 0, half, False)]
    parts += [(3, width + 2 * width // kv * k, 2 * width // kv, 0, half, True) for k in range(kv)]
    return tuple(parts)


def add_rows(target, left, right, rows):
    block = 16

    def body(index, carry):
        span = pl.ds(pl.multiple_of(index * block, block), block)
        target[span] = left[span] + right[span]
        return carry

    lax.fori_loop(0, rows // block, body, 0)


def step_kernel(lines, chunks, tables, in_cols, *refs):
    count = len(chunks)
    (in_far, out_far, w_in, w_out, state, target, weight_t, pos, head_t, embed, traits), refs = refs[:11], refs[11:]
    (own_t, own_out), refs = refs[:2], refs[2:]
    (d_in, d_head, d_two, d_full, d_one, few_sum, cond_full, time_act, all_traits, weight_sq), scratch = refs[:10], refs[10:]
    finals, scratch = scratch[:4], scratch[4:]
    held, by_y, by_x, by_z = (scratch[k * count : (k + 1) * count] for k in range(4))
    send, recv, zsend, zrecv, wsend, wrecv = scratch[4 * count : 4 * count + 6]
    scratch = scratch[4 * count + 6 :]
    (stage_wide, stage_tall, land_wide, land_tall, free_wide, free_tall, fetch, weight_load, d_mod, d_fm, few), scratch = scratch[:11], scratch[11:]
    (
        stream, hat_one, hat_two, root_one, root_two, a_low, qkv_low, mixed, proj, b_low, active, mlp, d_mlp,
    ), scratch = scratch[:13], scratch[13:]
    (
        few_got, few_y, few_x, few_held, few_line, mod_got, fm_got, mod_sum, fm_sum, group_slot, part_own, part_slot,
        act_own, act_slot, pair_own, pair_got, line_in, line_rest, line_full,
        few_send, few_recv, group_send, group_recv, line_send, line_recv,
    ) = scratch[:25]
    gather_refs = scratch[25:]
    (in_starts, in_tiles), (head_starts, head_tiles), (embed_starts, embed_tiles), shards = tables
    time_one, modul, fmod, patch, last = gather_refs[:5]
    rep, shard = lax.axis_index("rep"), lax.axis_index("shard")
    place_here = lax.rem(rep, 2 * lines)
    base = rep - place_here
    x, z = lax.rem(place_here, 2), lax.div(place_here, 2)
    core, y = lax.rem(shard, 2), lax.div(shard, 2)
    to_core = (rep, shard + 1 - 2 * core)
    to_y = (rep, shard + 2 - 4 * y)
    to_x = (rep + 1 - 2 * x, shard)

    def line_peer(step):
        return (base + lax.rem(z + step, lines) * 2 + x, shard)

    barrier = pltpu.get_barrier_semaphore()
    to_far = (rep, shards - 1 - shard)
    for peer in (to_core, to_y, to_x, to_far):
        pl.semaphore_signal(barrier, inc=1, device_id=peer, device_id_type=MESH)
    for step in range(1, lines):
        pl.semaphore_signal(
            barrier, inc=1, device_id=line_peer(step), device_id_type=MESH
        )
    pl.semaphore_wait(barrier, 4 + lines - 1)

    width, tokens = head_t.shape[1], state.shape[0]
    in_blocks = [active.at[:, pl.ds(k * width, width)] for k in range(4)] + [d_mlp]

    def far_copy(k):
        return pltpu.make_async_copy(in_far.at[pl.ds(k * tokens, tokens), :], in_blocks[k], fetch.at[4 + k])

    stride = lines // PIECES
    owns = lax.rem(z, stride) == 0
    mine = lax.div(z, stride)
    def remote(source, target, send_sem, recv_sem, peer):
        return pltpu.make_async_remote_copy(
            src_ref=source,
            dst_ref=target,
            send_sem=send_sem,
            recv_sem=recv_sem,
            device_id=peer,
            device_id_type=MESH,
        )

    def rows_of(ref, start, size):
        return ref.at[pl.ds(pl.multiple_of(start, 16), size)]

    def lanes_at(index, ref, row, rows, which):
        _, _, _, lane, lanes, _ = chunks[index]
        return ref.at[
            pl.ds(pl.multiple_of(row, 16), rows), pl.ds(pl.multiple_of(lane + which * lanes, 128), lanes)
        ]

    turn = {i: sum(chunks[j][0] == 0 for j in range(i)) if chunks[i][0] == 0 else sum(chunks[j][0] != 0 for j in range(i)) for i in range(count)}

    def slot_of(i, wide, tall):
        if chunks[i][0] == 0:
            return wide.at[turn[i] % SLOTS]
        return tall.at[turn[i] % SLOTS, pl.ds(0, chunks[i][2])]

    def turn_away(i, steps):
        for j in range(count):
            if (chunks[j][0] == 0) == (chunks[i][0] == 0) and turn[j] == turn[i] + steps:
                return j
        return None

    def core_copy(i):
        return remote(
            slot_of(i, stage_wide, stage_tall), slot_of(i, land_wide, land_tall), send.at[i, 0], recv.at[i, 0], to_core
        )

    def free_of(i):
        return free_wide if chunks[i][0] == 0 else free_tall

    def y_copy(i):
        half = chunks[i][2] // 2
        return remote(
            rows_of(held[i], (1 - y) * half, half), by_y[i], send.at[i, 1], recv.at[i, 1], to_y
        )

    def x_copy(i):
        quarter = chunks[i][2] // 4
        return remote(
            rows_of(by_y[i], (1 - x) * quarter, quarter), by_x[i], send.at[i, 2], recv.at[i, 2], to_x
        )

    def z_copy(i, piece):
        size = chunks[i][2] // 4 // PIECES
        owner = piece * stride
        slot = lax.rem(z - owner - 1 + lines, lines)
        return remote(
            by_x[i].at[pl.ds(piece * size, size)],
            by_z[i].at[slot],
            zsend.at[i, piece],
            zrecv.at[i, slot],
            (base + owner * 2 + x, shard),
        )

    def final_rows(i, side, start, size, which):
        array, row, rows = chunks[i][:3]
        return lanes_at(i, finals[array], row + side * (rows // 2) + start, size, which)

    def cross_copy(i):
        quarter = chunks[i][2] // 4
        part = final_rows(i, 0, x * quarter, quarter, core)
        return remote(part, part, send.at[i, 3], recv.at[i, 3], to_y)

    def line_copy(i, which, side, step):
        size = chunks[i][2] // 4 // PIECES
        part = final_rows(i, side, (x * PIECES + mine) * size, size, core)
        return remote(
            part, part, wsend.at[i, which, step - 1], wrecv.at[i, which, mine], line_peer(step)
        )

    def line_arrival(i, which, side, piece):
        size = chunks[i][2] // 4 // PIECES
        part = final_rows(i, side, (x * PIECES + piece) * size, size, core)
        return remote(part, part, wsend.at[i, which, 0], wrecv.at[i, which, piece], to_core)

    def pair_copy(i, which, side, column):
        quarter = chunks[i][2] // 4
        part = final_rows(i, side, column * quarter, quarter, core)
        return remote(part, part, send.at[i, 4 + which], recv.at[i, 4 + which], to_x)

    def last_copy(i, which, side, half):
        rows = chunks[i][2] // 2
        part = final_rows(i, side, 0, rows, half)
        return remote(part, part, send.at[i, 6 + which], recv.at[i, 6 + which], to_core)

    def sides(i, action):
        if chunks[i][5]:

            @pl.when(y == 1)
            def _():
                action(0, 1)
                action(1, 0)

        else:
            action(0, y)

    def produce(i, left, right):
        rows, lanes = chunks[i][2], chunks[i][4]
        before, after = turn_away(i, -SLOTS), turn_away(i, SLOTS)
        if before is not None:
            core_copy(before).wait_send()
        staged = slot_of(i, stage_wide, stage_tall)

        def block(part):
            value = mxu(left[:, part], right[...], TN)
            first, second = value[:, :lanes], value[:, lanes:]
            held[i][part, :] = jnp.where(core == 0, first, second).astype(jnp.bfloat16)
            staged[part, :] = jnp.where(core == 0, second, first).astype(jnp.bfloat16)

        blocks_of(rows, 256, block)
        if before is not None:
            pl.semaphore_wait(free_of(i), 1)
        core_copy(i).start()

    def stage1(i):
        core_copy(i).wait_recv()
        add_rows(held[i], held[i], slot_of(i, land_wide, land_tall), chunks[i][2])
        if turn_away(i, SLOTS) is not None:
            pl.semaphore_signal(free_of(i), inc=1, device_id=to_core, device_id_type=MESH)

    def stage2(i):
        half = chunks[i][2] // 2
        y_copy(i).wait_recv()
        add_rows(by_y[i], by_y[i], rows_of(held[i], y * half, half), half)
        x_copy(i).start()

    def stage3(i):
        quarter = chunks[i][2] // 4
        x_copy(i).wait_recv()
        add_rows(by_x[i], by_x[i], rows_of(by_y[i], x * quarter, quarter), quarter)
        for piece in range(PIECES):

            @pl.when(z != piece * stride)
            def _():
                z_copy(i, piece).start()

    def stage4(i):
        size = chunks[i][2] // 4 // PIECES

        @pl.when(owns)
        def _():
            for slot in range(lines - 1):
                remote(
                    by_z[i].at[slot], by_z[i].at[slot], zsend.at[i, 0], zrecv.at[i, slot], to_core
                ).wait_recv()
            target = final_rows(i, y, (x * PIECES + mine) * size, size, core)

            def body(index, carry):
                total = by_x[i][
                    pl.ds(pl.multiple_of(mine * size + index * 16, 16), 16)
                ].astype(jnp.float32)
                for slot in range(lines - 1):
                    total += by_z[i][slot, pl.ds(pl.multiple_of(index * 16, 16), 16)].astype(jnp.float32)
                target[pl.ds(pl.multiple_of(index * 16, 16), 16)] = total.astype(jnp.bfloat16)
                return carry

            lax.fori_loop(0, size // 16, body, 0)
            for step in range(1, lines):
                line_copy(i, 0, y, step).start()

    def line_wait(i):
        for piece in range(PIECES):

            @pl.when(z != piece * stride)
            def _():
                line_arrival(i, 0, y, piece).wait_recv()

    def stage5(i):
        @pl.when(y == 0)
        def _():
            line_wait(i)
            cross_copy(i).start()

    def stage6(i):
        if chunks[i][5]:

            @pl.when(y == 1)
            def _():
                line_wait(i)
                pair_copy(i, 0, 1, x).start()
                cross_copy(i).wait_recv()
                pair_copy(i, 1, 0, x).start()

        else:
            line_wait(i)
            pair_copy(i, 0, y, x).start()

    def stage7(i):
        def action(which, side):
            pair_copy(i, which, side, 1 - x).wait_recv()
            last_copy(i, which, side, core).start()

        sides(i, action)

    def stage8(i):
        sides(i, lambda which, side: last_copy(i, which, side, 1 - core).wait_recv())


    mod_tiles, wide = 6 * width // 128, width // 128
    images = d_mod.shape[0]
    in_lanes, head_lanes, embed_lanes = in_tiles * 128, head_tiles * 128, embed_tiles * 128
    rest_lanes = 2 * head_lanes + embed_lanes
    head_places = [o for o in range(shards) if head_starts[o] < wide]
    mod_places = [o for o in range(shards) if in_starts[o] < mod_tiles]
    few_rows = few.shape[0] // 2
    half = pl.ds(pl.multiple_of(core * few_rows, 8), few_rows)
    other_half = pl.ds(pl.multiple_of((1 - core) * few_rows, 8), few_rows)

    def is_in(where, places):
        return functools.reduce(jnp.logical_or, [where == o for o in places])

    few_core = remote(few.at[other_half], few_got, few_send.at[0], few_recv.at[0], to_core)
    few_over_y = remote(few_held.at[0], few_y, few_send.at[1], few_recv.at[1], to_y)
    few_over_x = remote(few_held.at[1], few_x, few_send.at[2], few_recv.at[2], to_x)
    few_back = remote(few_sum.at[half], few_sum.at[half], few_send.at[3], few_recv.at[3], to_core)
    few_back_arrival = remote(few_sum.at[other_half], few_sum.at[other_half], few_send.at[3], few_recv.at[3], to_core)
    mod_core = remote(d_mod, mod_got, few_send.at[4], few_recv.at[4], to_core)
    fm_core = remote(d_fm, fm_got, few_send.at[5], few_recv.at[5], to_core)
    pair_copy_x = remote(pair_own, pair_got, few_send.at[6], few_recv.at[6], to_x)

    def few_line_copy(step):
        return remote(few_line.at[z], few_line.at[z], few_send.at[6 + step], few_recv.at[6 + step], line_peer(step))

    def few_line_arrival(step):
        origin = lax.rem(z + lines - step, lines)
        return remote(few_line.at[origin], few_line.at[origin], few_send.at[6 + step], few_recv.at[6 + step], to_core)

    def group_parts(place):
        parts = []
        tiles = min(in_tiles, mod_tiles - in_starts[place])
        if tiles > 0:
            parts.append((0, in_starts[place] * 128, 0, tiles * 128))
        first, final = max(head_starts[place], wide), min(head_starts[place] + head_tiles, 3 * wide)
        if final > first:
            lead = (first - head_starts[place]) * 128
            parts.append((1, (first - wide) * 128, in_lanes + lead, (final - first) * 128))
        return parts

    def group_copy(place, k):
        which, lane, own, lanes = group_parts(place)[k]
        return remote(
            (mod_sum, fm_sum)[which].at[:, pl.ds(lane, lanes)],
            group_slot.at[:, pl.ds(own, lanes)],
            group_send.at[k, 0],
            group_recv.at[k, 0],
            to_y,
        )

    def to_others(kind, source, slots, step):
        return remote(
            source,
            slots.at[shard],
            group_send.at[kind, step - 1],
            group_recv.at[kind, step - 1],
            (rep, lax.rem(shard + step, shards)),
        )

    def from_others(kind, slots, step):
        origin = lax.rem(shard + shards - step, shards)
        return remote(slots.at[origin], slots.at[origin], group_send.at[kind, 0], group_recv.at[kind, step - 1], to_core)

    slots_of = (line_rest, line_full, line_in)

    def line_copy_d(kind, step):
        slots = slots_of[kind]
        return remote(slots.at[z], slots.at[z], line_send.at[kind, step - 1], line_recv.at[kind, step - 1], line_peer(step))

    def line_arrival_d(kind, step):
        slots = slots_of[kind]
        origin = lax.rem(z + lines - step, lines)
        return remote(slots.at[origin], slots.at[origin], line_send.at[kind, 0], line_recv.at[kind, step - 1], to_core)

    def on_line(action):
        for step in range(1, lines):
            action(0, step)
            action(1, step)

            @pl.when(is_in(shard, mod_places))
            def _():
                action(2, step)

    def side0():
        mod_core.start()
        fm_core.start()
        few_core.start()

    def side1():
        mod_core.wait_recv()
        mod_sum[...] = d_mod[...] + mod_got[...]
        fm_core.wait_recv()
        fm_sum[...] = d_fm[...] + fm_got[...]
        for place in range(shards):

            @pl.when(to_y[1] == place)
            def _():
                for k in range(len(group_parts(place))):
                    group_copy(place, k).start()

        few_core.wait_recv()
        few_held[0] = few[half] + few_got[...]
        few_over_y.start()

    def side2():
        pair_own[...] = jnp.zeros_like(pair_own)
        for place in range(shards):

            @pl.when(shard == place)
            def _():
                for k, (which, lane, own, lanes) in enumerate(group_parts(place)):
                    group_copy(place, k).wait_recv()
                    pair_own[:, own : own + lanes] = (
                        (mod_sum, fm_sum)[which][:, lane : lane + lanes] + group_slot[:, own : own + lanes]
                    )

        part_own[...] = jnp.dot(
            pair_own[:, in_lanes : in_lanes + head_lanes].astype(jnp.bfloat16),
            head_t[...],
            preferred_element_type=jnp.float32,
        )

        @pl.when(is_in(shard, mod_places))
        def _():
            for k in range(len(in_blocks)):
                far_copy(k).wait()
                lanes = pair_own[:, k * tokens : (k + 1) * tokens].astype(jnp.bfloat16)
                part_own[...] += jnp.dot(lanes, in_blocks[k][...], preferred_element_type=jnp.float32)

        part_slot[shard] = part_own[...]
        for step in range(1, shards):
            to_others(2, part_own, part_slot, step).start()
        few_over_y.wait_recv()
        few_held[1] = few_held[0] + few_y[...]
        few_over_x.start()

    def side3():
        for step in range(1, shards):
            from_others(2, part_slot, step).wait_recv()
        d_cond = functools.reduce(jnp.add, [part_slot[o] for o in range(shards)])
        value = cond_full[pl.ds(pl.multiple_of(place_here * images, 8), images), :]
        gate = jax.nn.sigmoid(value)
        d_value = d_cond * (gate + value * gate * (1.0 - gate))
        for place in range(shards):

            @pl.when(shard == place)
            def _():
                first = embed_starts[place] * 128
                pair_own[:, in_lanes + rest_lanes :] = d_value[:, first : first + embed_lanes]
                if place in head_places:
                    lanes = min(head_tiles, wide - head_starts[place]) * 128
                    first = head_starts[place] * 128
                    start = in_lanes + head_lanes
                    d_two_own = d_value[:, first : first + lanes].astype(jnp.bfloat16)
                    pair_own[:, start : start + lanes] = d_two_own.astype(jnp.float32)
                    act_own[...] = jnp.dot(d_two_own, head_t[:lanes, :], preferred_element_type=jnp.float32)
                    act_slot[shard] = act_own[...]
                    for step in range(1, shards):
                        to_others(3, act_own, act_slot, step).start()

        few_over_x.wait_recv()
        few_line[z] = few_held[1] + few_x[...]
        for step in range(1, lines):
            few_line_copy(step).start()

    def side4():
        for step in range(1, shards):

            @pl.when(is_in(lax.rem(shard + shards - step, shards), head_places))
            def _():
                from_others(3, act_slot, step).wait_recv()

        value = time_one[pl.ds(pl.multiple_of(place_here * images, 8), images), :]
        gate = jax.nn.sigmoid(value)
        slope = gate + value * gate * (1.0 - gate)
        for place in range(shards):

            @pl.when(shard == place)
            def _():
                first = embed_starts[place] * 128
                d_act = functools.reduce(jnp.add, [act_slot[o, :, first : first + embed_lanes] for o in head_places])
                start = in_lanes + 2 * head_lanes
                pair_own[:, start : start + embed_lanes] = (slope * d_act).astype(jnp.bfloat16).astype(jnp.float32)

        pair_copy_x.start()
        for step in range(1, lines):
            few_line_arrival(step).wait_recv()
        few_sum[half] = functools.reduce(jnp.add, [few_line[at] for at in range(lines)])
        few_back.start()

    def side5():
        pair_copy_x.wait_recv()
        own, got = pair_own[...], pair_got[...]
        both = jnp.concatenate([jnp.where(x == 0, own, got), jnp.where(x == 0, got, own)], 0)
        line_in[z] = both[:, :in_lanes].astype(jnp.bfloat16)
        line_rest[z] = both[:, in_lanes : in_lanes + rest_lanes].astype(jnp.bfloat16)
        line_full[z] = both[:, in_lanes + rest_lanes :]
        on_line(lambda kind, step: line_copy_d(kind, step).start())

    def side6():
        on_line(lambda kind, step: line_arrival_d(kind, step).wait_recv())
        for at in range(lines):
            span = slice(at * 2 * images, (at + 1) * 2 * images)
            d_head[span, :] = line_rest[at, :, :head_lanes]
            d_two[span, :] = line_rest[at, :, head_lanes : 2 * head_lanes]
            d_one[span, :] = line_rest[at, :, 2 * head_lanes :]
            d_full[span, :] = line_full[at]
        d_in[...] = jnp.zeros_like(d_in)

        @pl.when(is_in(shard, mod_places))
        def _():
            for at in range(lines):
                d_in[at * 2 * images : (at + 1) * 2 * images, :] = line_in[at]

        few_back_arrival.wait_recv()

    def side_end():
        for copy in (few_core, few_over_y, few_over_x, few_back, mod_core, fm_core, pair_copy_x):
            copy.wait_send()
        for step in range(1, lines):
            few_line_copy(step).wait_send()
        on_line(lambda kind, step: line_copy_d(kind, step).wait_send())
        for place in range(shards):

            @pl.when(to_y[1] == place)
            def _():
                for k in range(len(group_parts(place))):
                    group_copy(place, k).wait_send()

        for step in range(1, shards):
            to_others(2, part_own, part_slot, step).wait_send()

        @pl.when(is_in(shard, head_places))
        def _():
            for step in range(1, shards):
                to_others(3, act_own, act_slot, step).wait_send()

    room = (stream, hat_one, hat_two, proj, mlp)
    rounds = []
    for source in (w_in,):
        blocks = [(start, min(tokens, source.shape[0] - start)) for start in range(0, source.shape[0], tokens)]
        rounds.append([(source.at[pl.ds(start, size), :], size) for start, size in blocks])
    rounds.append([(w_out.at[:, pl.ds(k * width, width)], w_out.shape[0]) for k in range(w_out.shape[1] // width)])

    def weight_copies(index):
        return [
            pltpu.make_async_copy(source, room[k].at[pl.ds(0, size), :], weight_load.at[k])
            for k, (source, size) in enumerate(rounds[index])
        ]

    def squares_step(index):
        if index > 0:
            total = jnp.zeros((1, width), jnp.float32)
            for k, copy in enumerate(weight_copies(index - 1)):
                copy.wait()
                size = rounds[index - 1][k][1]
                whole = size // 64 * 64

                def add(block, carry):
                    value = room[k][pl.ds(pl.multiple_of(block * 64, 64), 64), :]
                    return carry + jnp.sum(value * value, 0, keepdims=True)

                total = lax.fori_loop(0, size // 64, add, total)
                if whole < size:
                    value = room[k][whole:size, :]
                    total += jnp.sum(value * value, 0, keepdims=True)
            weight_sq[:, (index - 1) * width : index * width] = total
        if index < len(rounds):
            for copy in weight_copies(index):
                copy.start()

    beside = (side0, side1, side2, side3, side4, side5, side6)
    low = jnp.bfloat16
    per = tokens // TOK
    row = [shard * per + image for image in range(per)]
    span = [pl.ds(image * TOK, TOK) for image in range(per)]
    cut = 256

    def piece(ref, image, index):
        return ref[pl.ds(row[image], 1), pl.ds(index * width, width)]

    def normed(value):
        center = value - jnp.mean(value, -1, keepdims=True)
        root = lax.rsqrt(jnp.mean(center * center, -1, keepdims=True) + eps_norm)
        return center * root, root

    def norm_back(d_hat, hat, root):
        return root * (d_hat - jnp.mean(d_hat, -1, keepdims=True) - hat * jnp.mean(d_hat * hat, -1, keepdims=True))

    def put_row(ref, image, index, value):
        ref[pl.ds(row[image], 1), pl.ds(index * width, width)] = (
            jnp.sum(value, 0, keepdims=True).astype(low).astype(jnp.float32)
        )

    fc2, fc1, attn_out, qkv = finals
    segments = heavy_segments(width, in_cols, in_starts, out_far.shape[0], shards)
    plan = (segments,) + tables[:3] + (lines,)
    relay_tick, arrived, finish = gather_steps(
        plan, remote, line_peer, in_blocks, far_copy, out_far, in_far, head_t, embed, traits,
        *finals, cond_full, time_act, time_one, modul, fmod, patch, last, all_traits, *gather_refs[5:],
    )
    d_mod[...] = jnp.zeros_like(d_mod)
    d_fm[...] = jnp.zeros_like(d_fm)

    for image in range(per):
        value = mxu(state[span[image], :], patch[...], NN) + pos[...]
        stream[span[image], :] = value
        hat, root = normed(value)
        hat_one[span[image], :] = hat
        root_one[span[image], :] = root
        a_low[span[image], :] = (hat * (1.0 + piece(modul, image, 1)) + piece(modul, image, 0)).astype(low)

    def qkv_block(part):
        qkv_low[:, part] = mxu(a_low[...], qkv[part, :], NT).astype(low)

    relay_tick(4)
    arrived(3)
    blocks_of(3 * width, width, qkv_block)
    relay_tick(5)
    lane = lax.broadcasted_iota(jnp.int32, (TOK, 128), 1)
    first = lane < 64
    scale = 0.125

    def softmax(query, key):
        score = mxu(query, key, NT) * scale
        expo = jnp.exp(score - jnp.max(score, -1, keepdims=True))
        return expo / jnp.sum(expo, -1, keepdims=True)

    def take(ref, image, start):
        return ref[span[image], pl.ds(pl.multiple_of(start, 128), 128)]

    def attend(pair, carry):
        for image in range(per):
            query, key, value = (take(qkv_low, image, index * width + pair * 128) for index in range(3))
            outs = []
            for side in (first, jnp.logical_not(first)):
                probs = softmax(jnp.where(side, query, jnp.zeros_like(query)), key)
                outs.append(mxu(probs.astype(low), value, NN))
            mixed[span[image], pl.ds(pl.multiple_of(pair * 128, 128), 128)] = jnp.where(first, outs[0], outs[1]).astype(low)
        return carry

    lax.fori_loop(0, width // 128, attend, 0)
    relay_tick(6)
    relay_tick(7)
    arrived(2)
    for image in range(per):
        got = mxu(mixed[span[image], :], attn_out[...], NT)
        proj[span[image], :] = got
        value = stream[span[image], :] + piece(modul, image, 2) * got
        stream[span[image], :] = value
        hat, root = normed(value)
        hat_two[span[image], :] = hat
        root_two[span[image], :] = root
        b_low[span[image], :] = (hat * (1.0 + piece(modul, image, 4)) + piece(modul, image, 3)).astype(low)

    def upper_block(part):
        value = mxu(b_low[...], fc1[part, :], NT)
        active[:, part] = (
            0.5 * value * (1.0 + jnp.tanh(0.7978845608 * (value + 0.044715 * value * value * value)))
        ).astype(low)

    arrived(1)
    blocks_of(4 * width, 2 * cut, upper_block)
    arrived(0)
    finish()

    def mlp_block(part):
        mlp[:, part] = mxu(active[...], fc2[part, :], NT)

    blocks_of(width, width, mlp_block)
    loss = jnp.zeros((), jnp.float32)
    g_last = jnp.zeros((PATCH, width), jnp.float32)
    for image in range(per):
        value = stream[span[image], :] + piece(modul, image, 5) * mlp[span[image], :]
        hat, root = normed(value)
        gain = 1.0 + piece(fmod, image, 1)
        final = (hat * gain + piece(fmod, image, 0)).astype(low)
        diff = mxu(final, last[...], NT) - target[span[image], :]
        share = weight_t[span[image], :] * diff
        loss += 0.5 * jnp.sum(share * diff)
        d_out = share.astype(low)
        g_last += mxu(d_out, final, TN)
        d_final = mxu(d_out, last[...], NN)
        put_row(d_fm, image, 0, d_final)
        put_row(d_fm, image, 1, d_final * hat)
        d_value = norm_back(d_final * gain, hat, root)
        stream[span[image], :] = d_value
        put_row(d_mod, image, 5, d_value * mlp[span[image], :])
        d_mlp[span[image], :] = (piece(modul, image, 5) * d_value).astype(low)
    few[pl.ds(PATCH, 8), :] = jnp.full((8, width), loss, jnp.float32)
    few[pl.ds(PATCH + 8, PATCH), :] = g_last
    few[pl.ds(2 * PATCH + 8, 8), :] = jnp.zeros((8, width), jnp.float32)

    of_fc2 = [i for i in range(count) if chunks[i][0] == 0]
    of_fc1 = [i for i in range(count) if chunks[i][0] == 1]
    of_o = [i for i in range(count) if chunks[i][0] == 2]
    of_qkv = [i for i in range(count) if chunks[i][0] == 3]

    def fc2_step(i):
        first, lanes = chunks[i][3], 2 * chunks[i][4]
        part = pl.ds(first, lanes)
        value = mxu(b_low[...], fc1[part, :], NT)
        inner = jnp.tanh(0.7978845608 * (value + 0.044715 * value * value * value))
        slope = 0.5 * (1.0 + inner) + 0.5 * value * (1.0 - inner * inner) * 0.7978845608 * (
            1.0 + 3.0 * 0.044715 * value * value
        )
        d_upper = (slope * mxu(d_mlp[...], fc2[:, part], NN)).astype(low)
        produce(i, d_mlp, active.at[:, part])
        active[:, part] = d_upper

    def fc1_step(i):
        part = pl.ds(chunks[i][1], chunks[i][2])
        more = mxu(active[:, part], fc1[part, :], NN)
        if i == of_fc1[0]:
            mlp[...] = more
        else:
            mlp[...] += more
        produce(i, active.at[:, part], b_low)

    def o_step(i):
        for image in range(per):
            d_normed = mlp[span[image], :]
            hat = hat_two[span[image], :]
            put_row(d_mod, image, 3, d_normed)
            put_row(d_mod, image, 4, d_normed * hat)
            d_value = stream[span[image], :] + norm_back(
                d_normed * (1.0 + piece(modul, image, 4)), hat, root_two[span[image], :]
            )
            stream[span[image], :] = d_value
            put_row(d_mod, image, 2, d_value * proj[span[image], :])
            b_low[span[image], :] = (piece(modul, image, 2) * d_value).astype(low)
        active[:, pl.ds(0, width)] = mxu(b_low[...], attn_out[...], NN).astype(low)
        produce(i, b_low, mixed)

    def attend_back(pair):
        for image in range(per):
            query, key, value = (take(qkv_low, image, index * width + pair * 128) for index in range(3))
            d_out = take(active, image, pair * 128)
            d_query, d_key, d_value = [], [], []
            for side in (first, jnp.logical_not(first)):
                none = jnp.zeros_like(query)
                probs = softmax(jnp.where(side, query, none), key)
                d_prob = mxu(jnp.where(side, d_out, none), value, NT)
                d_score = (probs * (d_prob - jnp.sum(probs * d_prob, -1, keepdims=True))).astype(low)
                d_value.append(mxu(probs.astype(low), d_out, TN))
                d_query.append(mxu(d_score, key, NN) * scale)
                d_key.append(mxu(d_score, query, TN) * scale)
            for index, both in enumerate((d_query, d_key, d_value)):
                qkv_low[span[image], pl.ds(pl.multiple_of(index * width + pair * 128, 128), 128)] = jnp.where(
                    first, both[0], both[1]
                ).astype(low)

    def norm_one_step():
        @pl.when(is_in(shard, mod_places))
        def _():
            for k in range(len(in_blocks)):
                far_copy(k).start()

        g_patch = jnp.zeros((PATCH, width), jnp.float32)
        for image in range(per):
            d_normed = mxu(qkv_low[span[image], :], qkv[...], NN)
            hat = hat_one[span[image], :]
            put_row(d_mod, image, 0, d_normed)
            put_row(d_mod, image, 1, d_normed * hat)
            d_value = stream[span[image], :] + norm_back(
                d_normed * (1.0 + piece(modul, image, 1)), hat, root_one[span[image], :]
            )
            g_patch += mxu(state[span[image], :], d_value.astype(low), TN)
        few[pl.ds(0, PATCH), :] = g_patch

    def qkv_step(i):
        if i == of_qkv[0]:
            norm_one_step()
        produce(i, qkv_low.at[:, pl.ds(chunks[i][1], chunks[i][2])], a_low)

    def over_y(i):
        y_copy(i).start()

    stages = (None, stage1, stage2, stage3, stage4, stage5, stage6, stage7, stage8, over_y)
    steps = [(fc2_step, i) for i in of_fc2] + [(fc1_step, i) for i in of_fc1] + [(o_step, i) for i in of_o]
    steps += [(attend_back, pair) for pair in range(width // 128)] + [(qkv_step, i) for i in of_qkv]
    for j, (k, i) in enumerate(ORDER):
        if j in BESIDE_AT:
            beside[BESIDE_AT.index(j)]()
        if j in SQUARES_AT:
            squares_step(SQUARES_AT.index(j))
        if k == 0:
            step, arg = steps[i]
            step(arg)
        else:
            stages[k](i)

    out_rows = out_far.shape[0]

    def own_copies(place):
        copies = [
            pltpu.make_async_copy(
                finals[array].at[pl.ds(row, rows), :], own_t.at[pl.ds(at, rows), :], fetch.at[n]
            )
            for n, (array, row, rows, at) in enumerate(own_segments(width, in_cols, in_starts, out_rows, shards)[place])
        ]
        for n, array, lane in ((2, 2, 0), (3, 0, width)):
            copies.append(
                pltpu.make_async_copy(
                    finals[array].at[pl.ds(place * out_rows, out_rows), :],
                    own_out.at[:, pl.ds(lane, finals[array].shape[1])],
                    fetch.at[n],
                )
            )
        return copies

    for place in range(shards):

        @pl.when(shard == place)
        def _():
            for copy in own_copies(place):
                copy.start()

    side_end()
    for i in range(count):
        if turn_away(i, SLOTS) is None:
            core_copy(i).wait_send()
        y_copy(i).wait_send()
        x_copy(i).wait_send()
        for piece in range(PIECES):

            @pl.when(z != piece * stride)
            def _():
                z_copy(i, piece).wait_send()

        if chunks[i][5]:

            @pl.when(y == 0)
            def _():
                cross_copy(i).wait_send()

        @pl.when(owns)
        def _():
            for step in range(1, lines):
                line_copy(i, 0, y, step).wait_send()

        def action(which, side):
            pair_copy(i, which, side, x).wait_send()
            last_copy(i, which, side, core).wait_send()

        sides(i, action)

    for place in range(shards):

        @pl.when(shard == place)
        def _():
            for copy in own_copies(place):
                copy.wait()


def step_call(lines, tables, in_cols, far, light):
    width = far[0].shape[1]
    chunks = heavy_chunks(width)
    count = len(chunks)
    low, full = jnp.bfloat16, jnp.float32
    (_, in_tiles), (_, head_tiles), (_, embed_tiles), shards = tables
    state, traits = light[0], light[6]
    tokens, group = state.shape[0], traits.shape[0]
    rows = 2 * lines * group
    modul_shape, fmod_shape = (group, 6 * width), (group, 2 * width)
    segments = heavy_segments(width, in_cols, tables[0][0], far[1].shape[0], shards)
    most = max(len(parts) for parts in segments)
    in_lanes, head_lanes, embed_lanes = in_tiles * 128, head_tiles * 128, embed_tiles * 128
    rest_lanes = 2 * head_lanes + embed_lanes
    few = (2 * PATCH + 16, width)
    few_half = (few[0] // 2, width)
    pair = (group, in_lanes + rest_lanes + embed_lanes)
    sizes = [(part_rows, part_lanes) for _, _, part_rows, _, part_lanes, _ in chunks]
    wide = [item for item, chunk in zip(sizes, chunks) if chunk[0] == 0][0]
    tall = max(item for item, chunk in zip(sizes, chunks) if chunk[0] != 0)
    dma = pltpu.SemaphoreType.DMA
    heavy = [(width, 4 * width), (4 * width, width), (width, width), (3 * width, width)]
    shapes = [((in_lanes, width), low), ((far[1].shape[0], 5 * width), low)] + [
        ((rows, in_lanes), low),
        ((rows, head_lanes), low),
        ((rows, head_lanes), low),
        ((rows, embed_lanes), full),
        ((rows, embed_lanes), low),
        (few, full),
        ((rows, width), full),
        ((rows, width), low),
        ((rows, traits.shape[1]), full),
        ((1, 2 * width), full),
    ]
    pass_scratch = [
        ((tokens, width), full),
        ((tokens, width), full),
        ((tokens, width), full),
        ((tokens, 1), full),
        ((tokens, 1), full),
        ((tokens, width), low),
        ((tokens, 3 * width), low),
        ((tokens, width), low),
        ((tokens, width), full),
        ((tokens, width), low),
        ((tokens, 4 * width), low),
        ((tokens, width), full),
        ((tokens, width), low),
    ]
    scratch = [
        (few_half, full),
        (few_half, full),
        (few_half, full),
        ((2,) + few_half, full),
        ((lines,) + few_half, full),
        (modul_shape, full),
        (fmod_shape, full),
        (modul_shape, full),
        (fmod_shape, full),
        ((group, in_lanes + head_lanes), full),
        ((group, width), full),
        ((shards, group, width), full),
        ((group, width), full),
        ((shards, group, width), full),
        (pair, full),
        (pair, full),
        ((lines, 2 * group, in_lanes), low),
        ((lines, 2 * group, rest_lanes), low),
        ((lines, 2 * group, embed_lanes), full),
    ]
    gather_scratch = [
        ((rows, embed_lanes), full),
        (modul_shape, full),
        (fmod_shape, full),
        ((PATCH, width), low),
        ((PATCH, width), low),
        ((shards, rows, embed_lanes), low),
        ((shards, rows, embed_lanes), full),
        ((shards, PATCH, embed_lanes), low),
        ((shards, rows, head_lanes), full),
        ((rows, head_lanes), full),
        ((shards, group, in_lanes), full),
        ((group, in_lanes), full),
        ((shards, group, head_lanes), full),
        ((group, head_lanes), full),
        ((PATCH, width), low),
        ((shards,) + traits.shape, full),
        (traits.shape, full),
        (traits.shape, full),
        ((lines, 2 * group, traits.shape[1]), full),
    ]
    vmem, anywhere = pl.BlockSpec(memory_space=pltpu.VMEM), pl.BlockSpec(memory_space=pl.ANY)
    return pl.pallas_call(
        functools.partial(step_kernel, lines, chunks, tables, in_cols),
        out_shape=[jax.ShapeDtypeStruct(*item) for item in shapes],
        in_specs=[anywhere] * len(far) + [vmem] * len(light),
        out_specs=[anywhere] * 2 + [vmem] * (len(shapes) - 2),
        scratch_shapes=[pltpu.VMEM(item, low) for item in heavy]
        + [pltpu.VMEM((r, c), low) for r, c in sizes]
        + [pltpu.VMEM((r // 2, c), low) for r, c in sizes]
        + [pltpu.VMEM((r // 4, c), low) for r, c in sizes]
        + [pltpu.VMEM((lines - 1, r // 4 // PIECES, c), low) for r, c in sizes]
        + [
            dma((count, 8)),
            dma((count, 8)),
            dma((count, PIECES)),
            dma((count, lines - 1)),
            dma((count, 2, lines - 1)),
            dma((count, 2, PIECES)),
        ]
        + [pltpu.VMEM((SLOTS,) + item, low) for item in (wide, tall)] * 2
        + [pltpu.SemaphoreType.REGULAR, pltpu.SemaphoreType.REGULAR, dma((9,)), dma((5,))]
        + [pltpu.VMEM(*item) for item in ((modul_shape, full), (fmod_shape, full), (few, full))]
        + [pltpu.VMEM(*item) for item in pass_scratch]
        + [pltpu.VMEM(*item) for item in scratch]
        + [
            dma((lines + 6,)),
            dma((lines + 6,)),
            dma((4, shards - 1)),
            dma((4, shards - 1)),
            dma((3, lines - 1)),
            dma((3, lines - 1)),
        ]
        + [pltpu.VMEM(*item) for item in gather_scratch]
        + [dma((most,)), dma((most,))]
        + [dma((most, 2))] * 4
        + [dma((most, 4))] * 2
        + [dma((most,)), dma((most,)), dma((8, shards - 1)), dma((8, shards - 1)), dma((most,)), dma((lines,)), dma((lines,))],
        compiler_params=pltpu.CompilerParams(
            collective_id=1, has_side_effects=True, vmem_limit_bytes=64 * 1024 * 1024 - 65536
        ),
    )(*far, *light)


def placed_traits(traits, lanes):
    lead = -(-(PATCH + FREQ) // 128) * 128
    lane = lax.broadcasted_iota(jnp.int32, (traits.shape[0], lead), 1)
    here = jnp.logical_and(lane >= PATCH, lane < PATCH + FREQ)
    freq = jnp.where(here, traits[:, :lead], 0.0).astype(jnp.bfloat16)
    named = lax.broadcasted_iota(jnp.int32, (traits.shape[0], lanes), 1).astype(jnp.float32)
    onehot = jnp.where(named == traits[:, lead : lead + 1], 1.0, 0.0).astype(jnp.bfloat16)
    return freq, onehot


def windows(cols, shards):
    starts = [place * cols // 128 for place in range(shards)]
    tiles = max(-(-(place + 1) * cols // 128) - start for place, start in enumerate(starts))
    return starts, tiles


def heavy_segments(width, in_cols, in_starts, out_rows, shards):
    every = []
    for place in range(shards):
        parts = []
        for array, low, high, most in ((3, 6 * width, 9 * width, 640), (1, 9 * width, 13 * width, 640)):
            first, last = max(low, place * in_cols), min(high, (place + 1) * in_cols)
            while first < last:
                rows = min(most, last - first)
                parts.append((0, first - in_starts[place] * 128, array, first - low, rows, 0, 0, width))
                first += rows
            if array == 3:
                parts.append((1, 0, 2, place * out_rows, out_rows, 0, 0, width))
        parts.append((1, 0, 0, place * out_rows, out_rows, width, 0, 4 * width))
        every.append(parts)
    return every


def gather_steps(
    plan, remote, line_peer, in_blocks, far_copy,
    out_t, in_t, head_t, embed, traits,
    fc2, fc1, attn_out, qkv, cond_full, time_act, time_one, modul, fmod, patch, last, all_traits,
    s1_slot, tab_slot, patch_slot, two_slot, two_own, mod_slot, mod_own, fm_slot, fm_own, last_own,
    trait_slot, trait_own, trait_got, line_slot,
    ysend, yrecv, xsend, xrecv, zsend, zrecv, csend, crecv, osend, orecv, small_send, small_recv, local_sem,
    trait_send, trait_recv,
):
    segments, (in_starts, in_tiles), (head_starts, head_tiles), (embed_starts, embed_tiles), lines = plan
    shards = len(segments)
    arrays = (fc2, fc1, attn_out, qkv)
    sources = (in_t, out_t)
    rep, shard = lax.axis_index("rep"), lax.axis_index("shard")
    place_here = lax.rem(rep, 2 * lines)
    x, z = lax.rem(place_here, 2), lax.div(place_here, 2)
    zb = lax.rem(z, 2)
    core, y = lax.rem(shard, 2), lax.div(shard, 2)
    to_core = (rep, shard + 1 - 2 * core)
    to_y = (rep, shard + 2 - 4 * y)
    to_x = (rep + 1 - 2 * x, shard)
    to_z = (rep + 2 - 4 * zb, shard)
    width = head_t.shape[1]
    others = [(rep, lax.rem(shard + step, shards)) for step in range(1, shards)]
    mod_places = [o for o in range(shards) if in_starts[o] * 128 < 6 * width]
    computes_mod = functools.reduce(jnp.logical_or, [shard == o for o in mod_places])

    @pl.when(computes_mod)
    def _():
        for k in range(len(in_blocks)):
            far_copy(k).start()

    def small(kind, source, slots, step):
        return remote(
            source, slots.at[shard], small_send.at[kind, step - 1], small_recv.at[kind, step - 1], others[step - 1]
        )

    def small_arrival(kind, slots, step):
        origin = lax.rem(shard + shards - step, shards)
        return remote(
            slots.at[origin], slots.at[origin], small_send.at[kind, step - 1], small_recv.at[kind, step - 1], to_core
        )

    def exchange(kind, source, slots, origins=None):
        for step in range(1, shards):
            if origins is None:
                small(kind, source, slots, step).start()
            else:
                sends = functools.reduce(jnp.logical_or, [shard == o for o in origins])

                @pl.when(sends)
                def _():
                    small(kind, source, slots, step).start()

    def arrive(kind, slots, origins=None):
        for step in range(1, shards):
            if origins is None:
                small_arrival(kind, slots, step).wait_recv()
            else:
                origin = lax.rem(shard + shards - step, shards)

                @pl.when(functools.reduce(jnp.logical_or, [origin == o for o in origins]))
                def _():
                    small_arrival(kind, slots, step).wait_recv()

    def sent(kind, source, slots, origins=None):
        for step in range(1, shards):
            if origins is None:
                small(kind, source, slots, step).wait_send()
            else:

                @pl.when(functools.reduce(jnp.logical_or, [shard == o for o in origins]))
                def _():
                    small(kind, source, slots, step).wait_send()

    def place_tiles(target, slots, starts, tiles, origins, dtype, first=0):
        total = target.shape[1] // 128
        for tile in range(total):
            parts = [
                slots[o, :, (tile + first - starts[o]) * 128 : (tile + first - starts[o] + 1) * 128]
                for o in origins
                if 0 <= tile + first - starts[o] < tiles
            ]
            target[:, tile * 128 : (tile + 1) * 128] = functools.reduce(jnp.add, parts).astype(dtype)

    def source_part(place, k):
        source, row, array, _, rows, lane, _, lanes = segments[place][k]
        return sources[source].at[pl.ds(row, rows), pl.ds(lane, lanes)]

    def target_part(place, k, start=0, rows=None):
        _, _, array, row, total, _, lane, lanes = segments[place][k]
        start = row + start
        if not isinstance(start, int):
            start = pl.multiple_of(start, 16)
        return arrays[array].at[pl.ds(start, total if rows is None else rows), pl.ds(lane, lanes)]

    def quarter(place, k, index):
        size = segments[place][k][4] // 4
        return target_part(place, k, index * size, size)

    def half_of(place, k, index, second):
        size = segments[place][k][4] // 4
        cut = -(-size // 32) * 16
        return target_part(place, k, index * size + (cut if second else 0), size - cut if second else cut)

    me = x * 2 + zb
    across_x, along_z, corner = (1 - x) * 2 + zb, x * 2 + 1 - zb, (1 - x) * 2 + 1 - zb

    def y_copy(place, k):
        size = segments[place][k][4] // 4
        source, row, _, _, _, lane, _, lanes = segments[place][k]
        part = sources[source].at[pl.ds(pl.multiple_of(row + me * size, 16), size), pl.ds(lane, lanes)]
        return remote(part, quarter(place, k, me), ysend.at[k], yrecv.at[k], to_y)

    def owner_copy(place, k):
        return remote(source_part(place, k), target_part(place, k), osend.at[k], orecv.at[k], to_core)

    def own_copy(place, k):
        return pltpu.make_async_copy(source_part(place, k), target_part(place, k), local_sem.at[k])

    def hop(part, sems, k, slot, peer):
        return remote(part, part, sems[0].at[k, slot], sems[1].at[k, slot], peer)

    xs, zs, cs = (xsend, xrecv), (zsend, zrecv), (csend, crecv)

    def begin(k, across):
        for place in range(shards):
            if k < len(segments[place]):

                @pl.when(shard == place)
                def _():
                    if across:
                        y_copy(place, k).start()
                    else:
                        owner_copy(place, k).start()
                        own_copy(place, k).start()

    def relay(place, stage, k):
        if stage == 0:
            y_copy(place, k).wait_recv()
            hop(quarter(place, k, me), xs, k, 0, to_x).start()
            hop(quarter(place, k, me), zs, k, 0, to_z).start()
            hop(quarter(place, k, me), cs, k, 0, to_core).start()
        elif stage == 1:
            hop(quarter(place, k, across_x), xs, k, 0, to_x).wait_recv()
            hop(half_of(place, k, across_x, False), zs, k, 1, to_z).start()
            hop(quarter(place, k, along_z), zs, k, 0, to_z).wait_recv()
            hop(half_of(place, k, along_z, True), xs, k, 1, to_x).start()
            hop(quarter(place, k, across_x), cs, k, 1, to_core).start()
            hop(quarter(place, k, along_z), cs, k, 2, to_core).start()
        else:
            hop(half_of(place, k, corner, False), zs, k, 1, to_z).wait_recv()
            hop(half_of(place, k, corner, True), xs, k, 1, to_x).wait_recv()
            hop(quarter(place, k, corner), cs, k, 3, to_core).start()

    def relay_tick(tick):
        for place in range(shards):

            @pl.when(to_y[1] == place)
            def _():
                for stage in range(3):
                    if 0 <= tick - stage < len(segments[place]):
                        relay(place, stage, tick - stage)

    def trait_line(step):
        return remote(
            line_slot.at[z], line_slot.at[z], trait_send.at[step], trait_recv.at[step], line_peer(step)
        )

    def trait_line_arrival(step):
        origin = lax.rem(z + lines - step, lines)
        return remote(line_slot.at[origin], line_slot.at[origin], trait_send.at[step], trait_recv.at[step], to_core)

    trait_pair = remote(trait_own, trait_got, trait_send.at[0], trait_recv.at[0], to_x)
    trait_slot[shard] = traits[...]
    exchange(7, traits, trait_slot)
    begin(0, True)
    arrive(7, trait_slot)
    trait_own[...] = functools.reduce(jnp.add, [trait_slot[o] for o in range(shards)])
    trait_pair.start()
    begin(1, True)
    trait_pair.wait_recv()
    own, got = trait_own[...], trait_got[...]
    line_slot[z] = jnp.concatenate([jnp.where(x == 0, own, got), jnp.where(x == 0, got, own)], 0)
    for step in range(1, lines):
        trait_line(step).start()
    relay_tick(0)
    begin(2, True)
    for step in range(1, lines):
        trait_line_arrival(step).wait_recv()
    count_in_line = 2 * traits.shape[0]
    for at in range(lines):
        all_traits[at * count_in_line : (at + 1) * count_in_line, :] = line_slot[at]
    freq, onehot = placed_traits(all_traits[...], embed.shape[1])

    nt = (((1,), (1,)), ((), ()))
    own_one = lax.dot_general(freq, embed[:, : freq.shape[1]], nt, preferred_element_type=jnp.float32)
    time_one[...] = own_one
    s1_slot[shard] = (own_one * jax.nn.sigmoid(own_one)).astype(jnp.bfloat16)
    tab_slot[shard] = lax.dot_general(onehot, embed[...], nt, preferred_element_type=jnp.float32)
    eye = lax.broadcasted_iota(jnp.int32, (PATCH, 128), 0) == lax.broadcasted_iota(jnp.int32, (PATCH, 128), 1)
    eye = jnp.where(eye, 1.0, 0.0).astype(jnp.bfloat16)
    patch_slot[shard] = lax.dot_general(eye, embed[:, :128], nt, preferred_element_type=jnp.float32).astype(jnp.bfloat16)
    exchange(0, s1_slot.at[shard], s1_slot)
    exchange(1, tab_slot.at[shard], tab_slot)
    exchange(2, patch_slot.at[shard], patch_slot)
    relay_tick(1)
    begin(3, True)
    last_place = [o for o in range(shards) if 0 <= 3 * width // 128 - head_starts[o] < head_tiles][-1]
    last_row = (3 * width // 128 - head_starts[last_place]) * 128
    last_own[...] = head_t[last_row : last_row + 16, :]

    @pl.when(shard == last_place)
    def _():
        last[...] = last_own[...]
        for step in range(1, shards):
            remote(last_own, last, small_send.at[6, step - 1], small_recv.at[6, 0], others[step - 1]).start()

    head_places = [o for o in range(shards) if head_starts[o] * 128 < width]
    fm_places = [o for o in range(shards) if (head_starts[o] + head_tiles) * 128 > width]
    group = modul.shape[0]

    arrive(0, s1_slot)
    place_tiles(time_act, s1_slot, embed_starts, embed_tiles, range(shards), jnp.bfloat16)
    two_own[...] = lax.dot_general(time_act[...], head_t[...], nt, preferred_element_type=jnp.float32)
    two_slot[shard] = two_own[...]
    exchange(3, two_own, two_slot, head_places)
    relay_tick(2)
    begin(4, True)
    arrive(1, tab_slot)
    arrive(3, two_slot, head_places)
    place_tiles(cond_full, tab_slot, embed_starts, embed_tiles, range(shards), jnp.float32)
    for tile in range(width // 128):
        span = slice(tile * 128, (tile + 1) * 128)
        for o in head_places:
            if 0 <= tile - head_starts[o] < head_tiles:
                cond_full[:, span] += two_slot[o, :, (tile - head_starts[o]) * 128 : (tile - head_starts[o] + 1) * 128]
    mine = cond_full[pl.ds(pl.multiple_of(place_here * group, 8), group), :]
    cond = (mine * jax.nn.sigmoid(mine)).astype(jnp.bfloat16)

    @pl.when(computes_mod)
    def _():
        for k, block in enumerate(in_blocks):
            far_copy(k).wait()
            span = slice(k * block.shape[0], (k + 1) * block.shape[0])
            mod_own[:, span] = lax.dot_general(cond, block[...], nt, preferred_element_type=jnp.float32)
        mod_slot[shard] = mod_own[...]

    exchange(4, mod_own, mod_slot, mod_places)
    fm_own[...] = lax.dot_general(cond, head_t[...], nt, preferred_element_type=jnp.float32)
    fm_slot[shard] = fm_own[...]
    exchange(5, fm_own, fm_slot, fm_places)
    relay_tick(3)
    begin(5, True)
    begin(0, False)
    begin(1, False)
    begin(2, False)
    begin(3, False)
    begin(4, False)
    begin(5, False)
    arrive(2, patch_slot)
    place_tiles(patch, patch_slot, embed_starts, embed_tiles, range(shards), jnp.bfloat16)
    arrive(4, mod_slot, mod_places)
    arrive(5, fm_slot, fm_places)
    place_tiles(modul, mod_slot, in_starts, in_tiles, mod_places, jnp.float32)
    place_tiles(fmod, fm_slot, head_starts, head_tiles, fm_places, jnp.float32, width // 128)

    @pl.when(shard != last_place)
    def _():
        remote(last_own, last, small_send.at[6, 0], small_recv.at[6, 0], to_core).wait_recv()

    def arrived(array):
        for place in range(shards):
            of_array = [k for k, part in enumerate(segments[place]) if part[2] == array]

            @pl.when(shard == place)
            def _():
                for k in of_array:
                    own_copy(place, k).wait()

            @pl.when(to_core[1] == place)
            def _():
                for k in of_array:
                    remote(target_part(place, k), target_part(place, k), osend.at[k], orecv.at[k], to_core).wait_recv()

            @pl.when(shards - 1 - shard == place)
            def _():
                for k in of_array:
                    for slot, index in enumerate((me, across_x, along_z, corner)):
                        part = quarter(place, k, index)
                        remote(part, part, csend.at[k, slot], crecv.at[k, slot], to_core).wait_recv()

    def finish():
        for place in range(shards):
            count = len(segments[place])

            @pl.when(shard == place)
            def _():
                for k in range(count):
                    y_copy(place, k).wait_send()
                    owner_copy(place, k).wait_send()

            @pl.when(to_y[1] == place)
            def _():
                for k in range(count):
                    hop(quarter(place, k, me), xs, k, 0, to_x).wait_send()
                    hop(quarter(place, k, me), zs, k, 0, to_z).wait_send()
                    hop(half_of(place, k, across_x, False), zs, k, 1, to_z).wait_send()
                    hop(half_of(place, k, along_z, True), xs, k, 1, to_x).wait_send()
                    for slot, index in enumerate((me, across_x, along_z, corner)):
                        hop(quarter(place, k, index), cs, k, slot, to_core).wait_send()

        trait_pair.wait_send()
        for step in range(1, lines):
            trait_line(step).wait_send()
        sent(7, traits, trait_slot)
        sent(0, s1_slot.at[shard], s1_slot)
        sent(1, tab_slot.at[shard], tab_slot)
        sent(2, patch_slot.at[shard], patch_slot)
        sent(3, two_own, two_slot, head_places)
        sent(4, mod_own, mod_slot, mod_places)
        sent(5, fm_own, fm_slot, fm_places)

        @pl.when(shard == last_place)
        def _():
            for step in range(1, shards):
                remote(last_own, last, small_send.at[6, step - 1], small_recv.at[6, 0], others[step - 1]).wait_send()

    return relay_tick, arrived, finish


def windowed(in_t, out_t, head_t, embed_t, shards):
    place = lax.axis_index("shard")
    width = head_t.shape[1]
    low = jnp.bfloat16

    def window(item_t, starts, tiles, lanes):
        rows = item_t.shape[0]
        most = max(o * rows - start * 128 for o, start in enumerate(starts))
        padded = jnp.pad(item_t, ((most, tiles * 128 - rows), (0, lanes - item_t.shape[1])))
        begin = most - lax.rem(place * rows, 128)
        return lax.dynamic_slice_in_dim(padded, begin, tiles * 128, 0).astype(low)

    in_cols, head_cols, embed_cols = in_t.shape[0], head_t.shape[0], embed_t.shape[0]
    in_starts, in_tiles = windows(in_cols, shards)
    head_starts, head_tiles = windows(head_cols, shards)
    embed_starts, embed_tiles = windows(embed_cols, shards)
    in_t = window(in_t, in_starts, in_tiles, width)
    head_t = window(head_t, head_starts, head_tiles, width)
    embed = window(embed_t, embed_starts, embed_tiles, -(-embed_t.shape[1] // 128) * 128)
    return in_t, out_t.astype(low), head_t, embed


def own_segments(width, in_cols, in_starts, out_rows, shards):
    every = []
    for place in range(shards):
        parts = []
        for array, low, high in ((3, 6 * width, 9 * width), (1, 9 * width, 13 * width)):
            first, last = max(low, place * in_cols), min(high, (place + 1) * in_cols)
            if first < last:
                parts.append((array, first - low, last - first, first - in_starts[place] * 128))
        every.append(parts)
    return every


def total_kernel(
    tables, segments, far_t, far_out, w_in, w_out, w_head, w_embed,
    d_in, d_fin, d_two, d_one, d_full, few, cond_full, time_act, traits, weight_sq, c_in, c_out, c_head, c_embed,
    g_in, g_out, g_head, g_embed, n_in, n_out, n_head, n_embed, stats, loss,
    own_t, own_out, grad_t, head_t, head_fresh, t_out, t_head, t_embed, v_head, v_embed,
    load, write, fetch,
):
    (in_starts, in_tiles), (head_starts, head_tiles), (embed_starts, embed_tiles), shards = tables
    shard = lax.axis_index("shard")
    width = cond_full.shape[1]
    in_cols, head_cols, embed_cols, out_cols = (item.shape[0] for item in (w_in, w_head, w_embed, w_out))
    full, low = jnp.float32, jnp.bfloat16
    span = lane_span(width, w_embed.shape[1])

    reads = [pltpu.make_async_copy(w_head, v_head, load.at[0]), pltpu.make_async_copy(w_embed, v_embed, load.at[1])]
    for copy in reads:
        copy.start()

    def heavy_copies(place):
        copies = [
            pltpu.make_async_copy(far_t.at[pl.ds(at, rows), :], own_t.at[pl.ds(at, rows), :], fetch.at[k])
            for k, (_, _, rows, at) in enumerate(segments[place])
        ]
        return copies + [pltpu.make_async_copy(far_out, own_out, fetch.at[2])]

    for place in range(shards):

        @pl.when(shard == place)
        def _():
            for copy in heavy_copies(place):
                copy.start()
            edges = [0]
            for _, _, rows, at in segments[place]:
                edges += [at, at + rows]
            edges.append(in_tiles * 128)
            for start, stop in zip(edges[0::2], edges[1::2]):
                if start < stop:
                    own_t[start:stop, :] = jnp.zeros((stop - start, width), low)

    def decayed(state, total, count):
        return decay * state + (1.0 - decay) * (total / count + eps_one)

    def to_lanes(column):
        return jnp.broadcast_to(column, (column.shape[0], 128)).T[:1, :]

    def to_column(lanes):
        return jnp.broadcast_to(lanes, (128, lanes.shape[1])).T[:, :1]

    def squares_of(value, state, fresh_out, start, size):
        square = value * value
        sums = to_lanes(jnp.sum(square, -1, keepdims=True))[:, :size]
        fresh = decayed(state[:, start : start + size], sums, value.shape[1])
        fresh_out[:, start : start + size] = fresh
        inverse = 1.0 / fresh
        if size < value.shape[0]:
            inverse = jnp.concatenate([inverse, jnp.zeros((1, value.shape[0] - size), full)], 1)
        return jnp.sum(square, 0, keepdims=True), jnp.sum(square * to_column(inverse), 0, keepdims=True)

    def put(start, plain, scaled):
        stats[:, start : start + plain.shape[1]] = plain
        stats[:, span + start : span + start + plain.shape[1]] = scaled

    def column_blocks(total):
        return [(start, min(128, total - start)) for start in range(0, total, 128)]

    def by_blocks(take, total, state, fresh_out, place):
        plain, scaled = jnp.zeros((1, width), full), jnp.zeros((1, width), full)
        for start, size in column_blocks(total):
            value = take(start, size)
            if size < 128:
                value = jnp.concatenate([value, jnp.zeros((128 - size, width), full)], 0)
            more, more_scaled = squares_of(value, state, fresh_out, start, size)
            plain, scaled = plain + more, scaled + more_scaled
        put(place, plain, scaled)

    cond = cond_full[...]
    cond = (cond * jax.nn.sigmoid(cond)).astype(low)

    lanes_all = -(-w_embed.shape[1] // 128) * 128
    freq, onehot = placed_traits(traits[...], lanes_all)
    square_one = lax.broadcasted_iota(jnp.int32, (PATCH, lanes_all), 0)
    eye = jnp.where(square_one == lax.broadcasted_iota(jnp.int32, (PATCH, lanes_all), 1), 1.0, 0.0).astype(low)

    def exact(value, picks):
        total = None
        for _ in range(3):
            part = value.astype(low)
            value = value - part.astype(full)
            term = mxu(part, picks, TN)
            total = term if total is None else total + term
        return total

    for place in range(shards):

        @pl.when(shard == place)
        def _():
            lead = place * embed_cols - embed_starts[place] * 128
            lanes = slice(embed_starts[place] * 128, (embed_starts[place] + embed_tiles) * 128)
            value = exact(d_full[...], onehot) + exact(few[0:PATCH, lanes], eye)
            value = value[lead : lead + embed_cols, :]
            time = mxu(d_one[...], freq, TN)[lead : lead + embed_cols, :]
            t_embed[:, : freq.shape[1]] = value[:, : freq.shape[1]] + time
            t_embed[:, freq.shape[1] :] = value[:, freq.shape[1] : w_embed.shape[1]]

    pltpu.make_async_copy(t_embed, g_embed, write.at[3]).start()
    value = jnp.concatenate([t_embed[...], jnp.zeros((embed_cols, lanes_all - w_embed.shape[1]), full)], 1)
    square = value * value
    fresh = decayed(c_embed[...].reshape(1, embed_cols), to_lanes(jnp.sum(square, -1, keepdims=True)), w_embed.shape[1])
    n_embed[...] = fresh.reshape(n_embed.shape)
    put(7 * width, jnp.sum(square, 0, keepdims=True), jnp.sum(square * to_column(1.0 / fresh), 0, keepdims=True))

    loss[0, 0] = few[PATCH : PATCH + 1, 0:1][0, 0]

    head_t[...] = mxu(d_two[...], time_act[...], TN) + mxu(d_fin[...], cond, TN)
    last_place = [o for o in range(shards) if 0 <= 3 * width // 128 - head_starts[o] < head_tiles][-1]
    last_row = (3 * width // 128 - head_starts[last_place]) * 128

    @pl.when(shard == last_place)
    def _():
        head_t[last_row : last_row + PATCH, :] = few[PATCH + 8 : 2 * PATCH + 8, :]

    for place in range(shards):

        @pl.when(shard == place)
        def _():
            lead = place * head_cols - head_starts[place] * 128
            t_head[...] = head_t[lead : lead + head_cols, :]

    pltpu.make_async_copy(t_head, g_head, write.at[2]).start()
    head_state = c_head[...].reshape(1, head_cols)
    by_blocks(lambda start, size: t_head[start : start + size, :], head_cols, head_state, head_fresh, 6 * width)
    n_head[...] = head_fresh[...].reshape(n_head.shape)

    for place in range(shards):

        @pl.when(shard == place)
        def _():
            for copy in heavy_copies(place):
                copy.wait()

    def light(index, carry):
        part = pl.ds(pl.multiple_of(index * 128, 128), 128)
        grad_t[part, :] = mxu(d_in[:, part], cond, TN) + own_t[part, :].astype(full)
        return carry

    lax.fori_loop(0, in_tiles, light, 0)
    lead = lax.rem(shard * in_cols, 128)
    write_in = pltpu.make_async_copy(grad_t.at[pl.ds(pl.multiple_of(lead, 64), in_cols), :], g_in, write.at[0])
    write_in.start()

    sums = jnp.zeros((out_cols, 1), full)
    for index in range(5):
        value = own_out[:, index * width : (index + 1) * width].astype(full)
        t_out[:, index * width : (index + 1) * width] = value
        sums += jnp.sum(value * value, -1, keepdims=True)
    pltpu.make_async_copy(t_out, g_out, write.at[1]).start()
    fresh = decayed(c_out[...], to_lanes(sums), 5 * width)
    n_out[...] = fresh
    column = to_column(1.0 / fresh)
    for index in range(5):
        value = t_out[:, index * width : (index + 1) * width]
        square = value * value
        put(width + index * width, jnp.sum(square, 0, keepdims=True), jnp.sum(square * column, 0, keepdims=True))

    by_blocks(
        lambda start, size: grad_t[pl.ds(pl.multiple_of(lead + start, 64), size), :], in_cols, c_in, n_in, 0
    )

    for copy in reads:
        copy.wait()
    squares = [weight_sq[:, k * width : (k + 1) * width] for k in (0, 1)]
    squares += [jnp.sum(value[...] * value[...], 0, keepdims=True) for value in (v_head, v_embed)]
    for k, total in enumerate(squares):
        start = 2 * span + k * 128
        stats[:, start : start + 128] = jnp.broadcast_to(jnp.sum(total, -1, keepdims=True) / 128.0, (1, 128))
    write_in.wait()
    for k, (source, target) in enumerate(((t_out, g_out), (t_head, g_head), (t_embed, g_embed))):
        pltpu.make_async_copy(source, target, write.at[k + 1]).wait()


def lane_span(width, embed_rows):
    return 7 * width + -(-embed_rows // 128) * 128


def total_call(tables, heavy, weights, light, cols):
    (in_starts, in_tiles), (_, head_tiles), _, shards = tables
    low, full = jnp.bfloat16, jnp.float32
    width = heavy[0].shape[1]
    w_in, w_out, w_head, w_embed = weights
    lanes = 2 * lane_span(width, w_embed.shape[1]) + 4 * 128
    segments = own_segments(width, w_in.shape[0], in_starts, w_out.shape[0], shards)
    shapes = [(item.shape, full) for item in weights] + [(item.shape, full) for item in cols] + [((1, lanes), full), ((1, 1), full)]
    anywhere, vmem = pl.BlockSpec(memory_space=pl.ANY), pl.BlockSpec(memory_space=pltpu.VMEM)
    scratch = [
        ((in_tiles * 128, width), low),
        (w_out.shape, low),
        ((in_tiles * 128, width), full),
        ((head_tiles * 128, width), full),
        ((1, w_head.shape[0]), full),
    ]
    scratch += [(item.shape, full) for item in weights[1:]] + [(item.shape, full) for item in weights[2:]]
    return pl.pallas_call(
        functools.partial(total_kernel, tables, segments),
        out_shape=[jax.ShapeDtypeStruct(*item) for item in shapes],
        in_specs=[anywhere] * 6 + [vmem] * (len(light) + 4),
        out_specs=[anywhere] * 4 + [vmem] * 5 + [pl.BlockSpec(memory_space=pltpu.SMEM)],
        scratch_shapes=[pltpu.VMEM(*item) for item in scratch] + [pltpu.SemaphoreType.DMA((4,))] * 3,
        compiler_params=pltpu.CompilerParams(vmem_limit_bytes=60 * 1024 * 1024),
    )(*heavy, *weights, *light, *cols)


def finish_kernel(shards, sizes, own, r_in, r_out, r_head, r_embed, n_in, n_out, n_head, n_embed, s_in, s_out, s_head, s_embed, rms, slots, send, recv):
    rep, shard = lax.axis_index("rep"), lax.axis_index("shard")
    barrier = pltpu.get_barrier_semaphore()
    for step in range(1, shards):
        peer = (rep, lax.rem(shard + step, shards))
        pl.semaphore_signal(barrier, inc=1, device_id=peer, device_id_type=MESH)
    pl.semaphore_wait(barrier, shards - 1)

    def copy(step):
        return pltpu.make_async_remote_copy(
            src_ref=own,
            dst_ref=slots.at[shard],
            send_sem=send.at[step - 1],
            recv_sem=recv.at[step - 1],
            device_id=(rep, lax.rem(shard + step, shards)),
            device_id_type=MESH,
        )

    for step in range(1, shards):
        copy(step).start()
    slots[shard] = own[...]
    for step in range(1, shards):
        copy(step).wait()
    total = functools.reduce(jnp.add, [slots[o] for o in range(shards)])
    states, fresh, scales = (r_in, r_out, r_head, r_embed), (n_in, n_out, n_head, n_embed), (s_in, s_out, s_head, s_embed)
    starts, start = [], 0
    for rows, _ in sizes:
        starts.append(start)
        start += -(-rows // 128) * 128
    update, means, news = jnp.zeros((1, 1), jnp.float32), [], []
    for k, (rows, cols) in enumerate(sizes):
        row = decay * states[k][...].reshape(1, rows) + (1.0 - decay) * (
            total[:, starts[k] : starts[k] + rows] / cols + eps_one
        )
        fresh[k][...] = row.reshape(fresh[k].shape)
        news.append(row)
        mean = jnp.mean(row, -1, keepdims=True)
        means.append(mean)
        update += mean * jnp.sum(total[:, start + starts[k] : start + starts[k] + rows] / row, -1, keepdims=True)
    update = jnp.sqrt(update / sum(rows * cols for rows, cols in sizes))
    rms[0, 0] = update[0, 0]
    factor = jnp.maximum(1.0, update / clip_level)
    for k, (rows, cols) in enumerate(sizes):
        first = 2 * start + k * 128
        weight = jnp.sqrt(jnp.sum(total[:, first : first + 128], -1, keepdims=True) / (rows * cols))
        scales[k][...] = rate * jnp.maximum(eps_two, weight) / factor * lax.rsqrt(news[k] / means[k])


def finish_call(shards, sizes, stats, rows_old):
    full = jnp.float32
    shapes = [(item.shape, full) for item in rows_old] + [((1, rows), full) for rows, _ in sizes] + [((1, 1), full)]
    return pl.pallas_call(
        functools.partial(finish_kernel, shards, sizes),
        out_shape=[jax.ShapeDtypeStruct(*item) for item in shapes],
        in_specs=[pl.BlockSpec(memory_space=pltpu.VMEM)] * 5,
        out_specs=[pl.BlockSpec(memory_space=pltpu.VMEM)] * (len(shapes) - 1) + [pl.BlockSpec(memory_space=pltpu.SMEM)],
        scratch_shapes=[
            pltpu.VMEM((shards,) + stats.shape, full),
            pltpu.SemaphoreType.DMA((shards - 1,)),
            pltpu.SemaphoreType.DMA((shards - 1,)),
        ],
        compiler_params=pltpu.CompilerParams(collective_id=3, has_side_effects=True),
    )(stats, *rows_old)


def on_device(
    latents,
    noises,
    velocity,
    times,
    labels,
    dropped,
    blocks_in,
    blocks_out,
    head_side,
    embed_side,
    state_in_row,
    state_in_col,
    state_out_row,
    state_out_col,
    state_head_row,
    state_head_col,
    state_embed_row,
    state_embed_col,
):
    images = latents.shape[0]
    width = head_side.shape[0]
    shard_count = lax.axis_size("shard")
    place = lax.axis_index("shard")
    in_cols = blocks_in.shape[2]
    head_cols = head_side.shape[1]
    embed_cols = embed_side.shape[1]
    group = images * shard_count
    weights = (blocks_in[0].T, blocks_out[0].T, head_side.T, embed_side.T)
    t_value = (times.astype(jnp.float32) + 1.0) / step_count
    classes = (PATCH + FREQ + jnp.where(dropped == 1, CLASSES - 1, labels)).astype(jnp.float32)
    lines = LINE
    lead = -(-(PATCH + FREQ) // 128) * 128
    own_traits = jnp.concatenate(
        [
            jnp.zeros((images, PATCH), jnp.float32),
            time_freq(t_value, FREQ),
            jnp.zeros((images, lead - PATCH - FREQ), jnp.float32),
            jnp.broadcast_to(classes[:, None], (images, 128)),
        ],
        1,
    )
    traits = lax.dynamic_update_slice(
        jnp.zeros((group, lead + 128), jnp.float32), own_traits, (place * images, 0)
    )
    in_t, out_t, head_t, embed = windowed(*weights, shard_count)
    tcol = t_value[:, None, None]
    state = (
        (1.0 - tcol) * latents.reshape(images, TOK, PATCH)
        + tcol * noises.reshape(images, TOK, PATCH)
    ).astype(jnp.bfloat16)
    tables = (
        windows(in_cols, shard_count),
        windows(head_cols, shard_count),
        windows(embed_cols, shard_count),
        shard_count,
    )
    sums = step_call(
        lines,
        tables,
        in_cols,
        [in_t, out_t] + list(weights[:2]),
        [
            state.reshape(images * TOK, PATCH),
            velocity.reshape(images * TOK, PATCH),
            jnp.repeat(t_value, TOK)[:, None],
            jnp.asarray(positions(GRID, width)),
            head_t,
            embed,
            traits,
        ],
    )
    d_in, d_fin, d_two, d_full, d_one, few_sum, cond_full, time_act, all_traits, weight_sq = sums[2:]
    rows_old = (state_in_row, state_out_row, state_head_row, state_embed_row)
    cols_old = (state_in_col, state_out_col, state_head_col, state_embed_col)
    *outs, stats, loss = total_call(
        tables,
        sums[:2],
        weights,
        [d_in, d_fin, d_two, d_one, d_full, few_sum, cond_full, time_act, all_traits, weight_sq],
        cols_old,
    )
    totals, cols_new = outs[:4], outs[4:]
    loss_sum = loss.reshape(())
    blocks = lax.axis_size("rep") // (2 * lines)
    if blocks > 1:
        apart = [[k * 2 * lines + j for k in range(blocks)] for j in range(2 * lines)]
        totals, loss_sum = lax.psum((totals, loss_sum), "rep", axis_index_groups=apart)
        cols_new, plain, scaled = [], [], []
        for gradient, col_state in zip(totals, cols_old):
            square = gradient * gradient
            fresh = decay * col_state + (1.0 - decay) * (jnp.mean(square, 1).reshape(col_state.shape) + eps_one)
            pad = (0, -gradient.shape[1] % 128)
            cols_new.append(fresh)
            plain.append(jnp.pad(jnp.sum(square, 0), pad))
            scaled.append(jnp.pad(jnp.sum(square / fresh.reshape(-1)[:, None], 0), pad))
        spans = sum(item.shape[0] for item in plain) * 2
        stats = jnp.concatenate(plain + scaled + [stats[0, spans:]])[None]
    sizes = [(weight.shape[1], weight.shape[0] * shard_count) for weight in weights]
    *outs, rms = finish_call(shard_count, sizes, stats, rows_old)
    rows_new, scales = outs[:4], outs[4:]
    update_rms = rms.reshape(())
    news = [
        (weight - gradient * scale * lax.rsqrt(col_next.reshape(-1))[:, None]).T
        for weight, gradient, scale, col_next in zip(weights, totals, scales, cols_new)
    ]
    return (
        loss_sum,
        update_rms,
        totals[0].T[None],
        totals[1].T[None],
        totals[2].T,
        totals[3].T,
        rows_new[0],
        cols_new[0],
        rows_new[1],
        cols_new[1],
        rows_new[2],
        cols_new[2],
        rows_new[3],
        cols_new[3],
        news[0][None],
        news[1][None],
        news[2],
        news[3],
    )


def solution(mesh):
    placed = (
        P(("rep", "shard"), None),
        P(("rep", "shard"), None),
        P(("rep", "shard"), None),
        P(("rep", "shard")),
        P(("rep", "shard")),
        P(("rep", "shard")),
        P(None, None, "shard"),
        P(None, None, "shard"),
        P(None, "shard"),
        P(None, "shard"),
        P(),
        P(None, "shard"),
        P(),
        P(None, "shard"),
        P(),
        P("shard"),
        P(),
        P("shard"),
    )
    return jax.shard_map(
        on_device,
        mesh=mesh,
        in_specs=placed,
        out_specs=(
            P(),
            P(),
            P(None, None, "shard"),
            P(None, None, "shard"),
            P(None, "shard"),
            P(None, "shard"),
            P(),
            P(None, "shard"),
            P(),
            P(None, "shard"),
            P(),
            P("shard"),
            P(),
            P("shard"),
            P(None, None, "shard"),
            P(None, None, "shard"),
            P(None, "shard"),
            P(None, "shard"),
        ),
        check_vma=False,
    )
```
